32 devices in a mesh: member: 4 (over z), band: 8 (over y, x, core).
Axes of the slice: x: 2, y: 2, z: 4, core: 2. Of those that a mesh axis runs over, the one named last changes fastest.
Arguments:
- hidden: bfloat16 [8, 512, 1024], P('member', 'band'), may hold values from -6 to 6
- queries: bfloat16 [2048, 1024], P('band'), may hold values from -6 to 6
- kv_weight: bfloat16 [1024, 2048], replicated, may hold values from -0.1875 to 0.1875
- out_weight: bfloat16 [1024, 1024], replicated, may hold values from -0.1875 to 0.1875
- head_projection: bfloat16 [1024, 100], replicated, may hold values from -0.1875 to 0.1875
- initial_state: float32 [100, 2048], P(None, 'band'), may hold values from -6 to 6
- truth: float32 [100, 2048], P(None, 'band'), may hold values from -8 to 8
- latitude_weight: float32 [2048], P('band'), may hold values from 0.1 to 2
- channel_loss_weight: float32 [100], replicated, may hold values from 0.3 to 3
- sources: int32 [3, 2048], P(None, 'band'), may hold values from 0 to 127, as said below
- halo_rows: int32 [16, 32], P('band'), may hold values from 0 to 63, as said below
Outputs:
- hidden_grad: float32 [8, 512, 1024], P('member', 'band')
- kv_grad: float32 [1024, 2048], P(('member', 'band'))
- out_grad: float32 [1024, 1024], P(('member', 'band'))
- head_grad: float32 [1024, 100], P(('member', 'band'))
The draws below stay inside these ranges and needn't reach their ends.
Inputs may be any that keep to these rules, and one draw needn't show every extreme that they name: sources[e, t] names a row of the extended list of point t's band: rows below 64 are the band's own nodes, the next 32 those received from the band below, the last 32 those from the band above; the 3 rows of one point are distinct; the first band names no row from below and the last band none from above. `halo_rows`: rows 2 b and 2 b + 1 list the nodes of band b sent to the band below and to the band above; each node of a band stands once in the two rows together.
All inputs are finite; a program needn't handle non-finite values.
Results may differ from the reference program's by a relative error of at most 0.019.
Values may be sent and summed in bfloat16 or wider, within the bound.
No kernel may reach another device: no remote copies, remote signals or barrier semaphores. Data moves between devices by JAX's collectives and lax.ppermute only.
A program may use at most 128 MiB of HBM per device.

```python
import math
import jax
import jax.numpy as jnp
from jax import lax

C = 1024
HEAD_DIM = 64
HEADS = 16
CH = 100
EDGES = 3
MEMBERS = 8
G_DEV = 256
HN_DEV = 64
HALO = 32
NGRID = 2048
HNODES = 512
N_BAND = 8
DEVICES = 32


def shuffled_half(band_key):
    return jax.random.permutation(band_key, HN_DEV // 2).astype(jnp.int32)


def draw_latitude_weight(key, part):
    key = jax.random.fold_in(key, 5)
    point_count = G_DEV * N_BAND
    position = (jnp.arange(point_count, dtype=jnp.float32) + 0.5) / point_count
    smooth = 0.35 + 0.65 * jnp.sin(jnp.pi * position)
    rough_part = jax.random.uniform(key, (point_count,), jnp.float32, 0.6, 1.4)
    return smooth * rough_part


def draw_sources(key, part):
    key = jax.random.fold_in(key, 11)
    point_count = G_DEV * N_BAND
    point_index = jnp.arange(point_count, dtype=jnp.int32)
    band_index = point_index // G_DEV
    local_index = point_index % G_DEV
    base_node = local_index * (HN_DEV - 5 * EDGES) // G_DEV
    jitter = jax.random.randint(key, (EDGES, point_count), 0, 5, dtype=jnp.int32)
    jitter = jnp.where(local_index[None, :] == 0, 0, jitter)
    offsets = jnp.arange(EDGES, dtype=jnp.int32)[:, None] * 5
    nearby = base_node[None, :] + offsets + jitter
    halo_pick = jax.random.randint(jax.random.fold_in(key, 1), (point_count,), 0, HALO, dtype=jnp.int32)
    rim_points = G_DEV // 8
    halo_pick = jnp.where(local_index == rim_points - 1, HALO - 1, halo_pick)
    halo_pick = jnp.where(local_index == G_DEV - rim_points, HALO - 1, halo_pick)
    lower_rim = (local_index < rim_points) & (band_index > 0)
    upper_rim = (local_index >= G_DEV - rim_points) & (band_index < N_BAND - 1)
    first_edge = jnp.where(lower_rim, HN_DEV + halo_pick, jnp.where(upper_rim, HN_DEV + HALO + halo_pick, nearby[0]))
    return jnp.concatenate([first_edge[None, :], nearby[1:]], axis=0).astype(jnp.int32)


def draw_halo_rows(key, part):
    key = jax.random.fold_in(key, 23)
    band_keys = jax.random.split(key, 2 * N_BAND)
    picked = jax.vmap(shuffled_half)(band_keys)
    offsets = jnp.arange(2 * N_BAND, dtype=jnp.int32) % 2 * (HN_DEV // 2)
    return (picked + offsets[:, None]).astype(jnp.int32)


def with_spikes(result, key, source, target, parts, factor):
    def block_of(dim):
        return (jnp.arange(result.shape[dim]) // (result.shape[dim] // parts)).reshape((-1,) + (1,) * (result.ndim - 1 - dim))

    first = jax.random.permutation(key, parts)[block_of(target)]
    second = (block_of(target) + parts // 2) % parts
    return jnp.where((block_of(source) == first) | (block_of(source) == second), factor * result, result)


def steps_of(key, shape, pieces, low, top_value):
    factor_of = 1.0
    for dim, parts in pieces:
        draws = jax.random.uniform(jax.random.fold_in(jax.random.fold_in(key, 6), dim), (parts,), jnp.float32, low / len(pieces), top_value / len(pieces))
        factor_of = factor_of * jnp.repeat(jnp.exp(draws), shape[dim] // parts).reshape((-1,) + (1,) * (len(shape) - 1 - dim))
    return factor_of


def gaussian(rng, shape, deviation, bound, cuts=(), held_as=jnp.bfloat16):
    values = deviation * jax.random.normal(rng, shape, jnp.float32)
    if cuts:
        values = values * steps_of(rng, shape, cuts, -0.22, 0.18)
    return jnp.clip(values, -bound, bound).astype(held_as)


def heavy_noise(stream_key, shape, scale, bound, shards, heavy, kind=jnp.bfloat16):
    result = scale * jax.random.normal(stream_key, shape, jnp.float32)
    if shards:
        result = result * steps_of(stream_key, shape, shards, -0.22, 0.18)
    return jnp.clip(with_spikes(result, jax.random.fold_in(stream_key, 3), *heavy), -bound, bound).astype(kind)


def setup_inputs(seed: int = 0) -> dict:
    splits = jax.random.split(jax.random.key(seed), 12)
    hidden = heavy_noise(splits[0], (MEMBERS, HNODES, C), 1.0, 6.0, ((0, 4), (1, 8)), (1, 2, 8, 2.0))
    queries = gaussian(splits[1], (NGRID, C), 1.0, 6.0, ((0, 8),))
    kv_weight = gaussian(splits[2], (C, 2 * C), C ** -0.5, 0.1875)
    out_weight = gaussian(splits[3], (C, C), C ** -0.5, 0.1875)
    head_projection = gaussian(splits[4], (C, CH), C ** -0.5, 0.1875)
    initial_state = gaussian(splits[5], (CH, NGRID), 1.0, 6.0, ((1, 8),), jnp.float32)
    truth = gaussian(splits[6], (CH, NGRID), 1.5, 8.0, ((1, 8),), jnp.float32)
    latitude_weight = draw_latitude_weight(jax.random.fold_in(splits[11], 71), 0)
    channel_loss_weight = jnp.clip(jnp.exp(jax.random.uniform(splits[8], (CH,), jnp.float32, math.log(0.3), math.log(3.0))), 0.3, 3.0)
    sources = draw_sources(jax.random.fold_in(splits[11], 71), 0)
    halo_rows = draw_halo_rows(jax.random.fold_in(splits[11], 71), 0)
    return {"hidden": hidden, "queries": queries, "kv_weight": kv_weight, "out_weight": out_weight, "head_projection": head_projection, "initial_state": initial_state, "truth": truth, "latitude_weight": latitude_weight, "channel_loss_weight": channel_loss_weight, "sources": sources, "halo_rows": halo_rows}


ALPHA = 0.95
SOFTENING = 0.5

def pick_rows(node_rows, index_list):
    return node_rows[index_list]

def add_back(local_rows, index_list, lower_rows, upper_rows):
    return local_rows.at[index_list[0]].add(lower_rows).at[index_list[1]].add(upper_rows)

def reference(hidden, queries, kv_weight, out_weight, head_projection, initial_state, truth, latitude_weight, channel_loss_weight, sources, halo_rows):
    band_of_point = (jnp.arange(NGRID, dtype=jnp.int32) // G_DEV).astype(jnp.int32)
    node_ids = (sources + band_of_point[None, :] * (2 * HN_DEV)).astype(jnp.int32)
    index_lists = halo_rows.reshape(N_BAND, 2, HALO)
    query_heads = queries.reshape(NGRID, HEADS, HEAD_DIM)
    score_scale = HEAD_DIM ** (-0.5)

    def extend_nodes(ensemble_rows):
        band_rows = ensemble_rows.reshape(N_BAND, HN_DEV, C)
        picked = jax.vmap(pick_rows)(band_rows, index_lists)
        zero_block = jnp.zeros((1, HALO, C), jnp.bfloat16)
        from_below = jnp.concatenate([zero_block, picked[:-1, 1]], axis=0)
        from_above = jnp.concatenate([picked[1:, 0], zero_block], axis=0)
        return jnp.concatenate([band_rows, from_below, from_above], axis=1).reshape(N_BAND * 2 * HN_DEV, C)

    def member_forward_pass(ensemble_rows):
        extended_nodes = extend_nodes(ensemble_rows)
        key_value = jnp.dot(extended_nodes, kv_weight, preferred_element_type=jnp.float32).astype(jnp.bfloat16)
        key_value = lax.optimization_barrier(key_value)
        edge_rows = key_value[node_ids]
        edge_keys = edge_rows[..., :C].reshape(EDGES, NGRID, HEADS, HEAD_DIM)
        edge_messages = edge_rows[..., C:].reshape(EDGES, NGRID, HEADS, HEAD_DIM)
        scores = jnp.einsum('kthd,thd->kth', edge_keys.astype(jnp.float32), query_heads.astype(jnp.float32)) * score_scale
        gate_activations = jax.nn.sigmoid(scores)
        gate_lowprecision = lax.optimization_barrier(gate_activations.astype(jnp.bfloat16))
        combined_nodes = jnp.einsum('kth,kthd->thd', gate_lowprecision.astype(jnp.float32), edge_messages.astype(jnp.float32))
        combined_nodes = combined_nodes.reshape(NGRID, C).astype(jnp.bfloat16)
        updated = queries.astype(jnp.float32) + jnp.dot(combined_nodes, out_weight, preferred_element_type=jnp.float32)
        updated_lowprecision = updated.astype(jnp.bfloat16)
        prediction = initial_state + lax.dot_general(head_projection, updated_lowprecision, (((0,), (1,)), ((), ())), preferred_element_type=jnp.float32)
        return (extended_nodes, edge_messages, gate_activations, gate_lowprecision, combined_nodes, updated_lowprecision, prediction)

    def produce_prediction(ensemble_rows):
        return member_forward_pass(ensemble_rows)[-1]
    predictions = lax.map(produce_prediction, hidden)
    score_weight = channel_loss_weight[:, None] * latitude_weight[None, :]
    spread = (1.0 - (1.0 - ALPHA) / MEMBERS) / (MEMBERS * (MEMBERS - 1))

    def pairwise_terms(local_rows):
        member_differences = local_rows[None] - predictions
        gap_root = jnp.sqrt(member_differences * member_differences + SOFTENING * SOFTENING)
        slope_sum = lax.optimization_barrier(jnp.sum(member_differences / gap_root, axis=0))
        truth_gap = local_rows - truth
        truth_root = jnp.sqrt(truth_gap * truth_gap + SOFTENING * SOFTENING)
        return score_weight * (truth_gap / truth_root / MEMBERS - spread * slope_sum)
    loss_gradient_list = lax.map(pairwise_terms, predictions)
    grad_rounded = loss_gradient_list.astype(jnp.bfloat16)

    def member_step(running, inputs):
        ensemble_rows, member_grad = inputs
        kv_sum, out_sum, head_sum = running
        extended_nodes, edge_messages, gate_activations, gate_lowprecision, combined_nodes, updated_lowprecision, prediction = member_forward_pass(ensemble_rows)
        head_part = lax.dot_general(updated_lowprecision, member_grad, (((0,), (1,)), ((), ())), preferred_element_type=jnp.float32)
        update_grad = lax.dot_general(member_grad, head_projection, (((0,), (1,)), ((), ())), preferred_element_type=jnp.float32).astype(jnp.bfloat16)
        out_part = lax.dot_general(combined_nodes, update_grad, (((0,), (0,)), ((), ())), preferred_element_type=jnp.float32)
        merged_grad = lax.dot_general(update_grad, out_weight, (((1,), (1,)), ((), ())), preferred_element_type=jnp.float32).astype(jnp.bfloat16)
        merged_grad = lax.optimization_barrier(merged_grad).reshape(NGRID, HEADS, HEAD_DIM)
        gate_grad = jnp.einsum('thd,kthd->kth', merged_grad.astype(jnp.float32), edge_messages.astype(jnp.float32))
        score_grad = gate_grad * gate_activations * (1.0 - gate_activations) * score_scale
        value_grad = gate_lowprecision.astype(jnp.float32)[..., None] * merged_grad.astype(jnp.float32)[None]
        key_grad = score_grad[..., None] * query_heads.astype(jnp.float32)[None]
        edge_grad = jnp.concatenate([key_grad.reshape(EDGES, NGRID, C), value_grad.reshape(EDGES, NGRID, C)], axis=-1)
        node_grad = jax.ops.segment_sum(edge_grad.reshape(EDGES * NGRID, 2 * C), node_ids.reshape(-1), num_segments=N_BAND * 2 * HN_DEV)
        node_grad = node_grad.astype(jnp.bfloat16)
        kv_part = lax.dot_general(extended_nodes, node_grad, (((0,), (0,)), ((), ())), preferred_element_type=jnp.float32)
        extended_grad = lax.dot_general(node_grad, kv_weight, (((1,), (1,)), ((), ())), preferred_element_type=jnp.float32)
        band_grad = extended_grad.reshape(N_BAND, 2 * HN_DEV, C)
        own_grad = band_grad[:, :HN_DEV]
        below_grad = band_grad[:, HN_DEV:HN_DEV + HALO]
        above_grad = band_grad[:, HN_DEV + HALO:]
        zero_block = jnp.zeros((1, HALO, C), jnp.float32)
        to_upper_list = jnp.concatenate([below_grad[1:], zero_block], axis=0)
        to_lower_list = jnp.concatenate([zero_block, above_grad[:-1]], axis=0)
        hidden_part = jax.vmap(add_back)(own_grad, index_lists, to_lower_list, to_upper_list).reshape(HNODES, C)
        return ((kv_sum + kv_part, out_sum + out_part, head_sum + head_part), hidden_part)
    start_sums = (jnp.zeros((C, 2 * C), jnp.float32), jnp.zeros((C, C), jnp.float32), jnp.zeros((C, CH), jnp.float32))
    totals, hidden_grad = lax.scan(member_step, start_sums, (hidden, grad_rounded))
    kv_grad = totals[0] / DEVICES
    out_grad = totals[1] / DEVICES
    head_grad = totals[2] / DEVICES
    return (hidden_grad, kv_grad, out_grad, head_grad)
```

```python
import functools

import jax
import jax.numpy as jnp
from jax import lax
from jax.experimental import pallas as pl
from jax.experimental.pallas import tpu as pltpu
from jax.sharding import PartitionSpec as P

HEAD_DIM = 64
LANES = 128
ALPHA = 0.95
SOFTENING = 0.5
BF = jnp.bfloat16
F32 = jnp.float32
NN = (((1,), (0,)), ((), ()))
NT = (((1,), (1,)), ((), ()))
TN = (((0,), (0,)), ((), ()))


def mm(a, b, dims=NN):
    return lax.dot_general(a, b, dims, preferred_element_type=F32)


def call(body, out_shape, args, scratch=(), flops=0, nbytes=0, limit=40):
    return pl.pallas_call(
        body,
        out_shape=out_shape,
        in_specs=[pl.BlockSpec(memory_space=pltpu.VMEM) for _ in args],
        out_specs=jax.tree.map(lambda _: pl.BlockSpec(memory_space=pltpu.VMEM), out_shape),
        scratch_shapes=list(scratch),
        compiler_params=pltpu.CompilerParams(vmem_limit_bytes=limit * 1024 * 1024),
        cost_estimate=pl.CostEstimate(flops=flops, bytes_accessed=nbytes, transcendentals=0),
    )(*args)


def sds(shape, dtype):
    return jax.ShapeDtypeStruct(shape, dtype)


def one_hot_rows(halo_ref, row, node_count):
    rim = halo_ref.shape[1]
    nodes = lax.broadcasted_iota(jnp.int32, (node_count, rim), 0)
    return (nodes == halo_ref[row : row + 1, :]).astype(F32).astype(BF)


def pick_body(hidden_ref, halo_ref, down_ref, up_ref):
    members, nodes, _ = hidden_ref.shape
    rim = halo_ref.shape[1]
    for row, out_ref in ((0, down_ref), (1, up_ref)):
        hot = one_hot_rows(halo_ref, row, nodes)
        for m in range(members):
            out_ref[m * rim : (m + 1) * rim, :] = mm(hot, hidden_ref[m], TN).astype(BF)


def prepare_body(
    hidden_ref, kvw_ref, wo_ref, hp_ref, q_ref, init_ref, chw_ref, lat_ref,
    kv_ref, pt_ref, p_ref, base_ref, weight_ref, hp_pad,
):
    channels = hp_ref.shape[1]
    hp_pad[...] = jnp.zeros_like(hp_pad)
    hp_pad[:, 0:channels] = hp_ref[...].astype(F32)
    hp = hp_pad[...]
    hp_t = hp.T.astype(BF)
    pt = mm(wo_ref[...], hp.astype(BF))
    pt_ref[...] = pt.astype(BF)
    p_ref[...] = pt.T.astype(BF)
    base_ref[...] = mm(hp_t, q_ref[...], NT)
    base_ref[0:channels, :] = base_ref[0:channels, :] + init_ref[...]
    weight_ref[...] = chw_ref[...] * lat_ref[...]
    kv_ref[...] = mm(hidden_ref[...], kvw_ref[...]).astype(BF)


def split_heads(block):
    low = lax.broadcasted_iota(jnp.int32, block.shape, 1) < HEAD_DIM
    zero = jnp.zeros_like(block)
    return jnp.concatenate([jnp.where(low, block, zero), jnp.where(low, zero, block)], axis=0)


def forward_body(
    below_ref, above_ref, own_ref, kvw_ref, q_ref, src_ref, p_ref,
    kv_ref, gate_ref, slope_ref, merged_ref, part_ref, send_ref,
):
    members, ext, width2 = kv_ref.shape
    width = width2 // 2
    points = q_ref.shape[0]
    nodes = own_ref.shape[0] // members
    rim = below_ref.shape[0] // members
    halo = mm(jnp.concatenate([below_ref[...], above_ref[...]], axis=0), kvw_ref[...]).astype(BF)
    for m in range(members):
        kv_ref[m, 0:nodes, :] = own_ref[m * nodes : (m + 1) * nodes, :]
        kv_ref[m, nodes : nodes + rim, :] = halo[m * rim : (m + 1) * rim]
        kv_ref[m, nodes + rim : ext, :] = halo[(members + m) * rim : (members + m + 1) * rim]
    rows = lax.broadcasted_iota(jnp.int32, (ext, points), 0)
    mask = rows == src_ref[0:1, :]
    for e in range(1, src_ref.shape[0]):
        mask = mask | (rows == src_ref[e : e + 1, :])
    mask = mask.astype(F32)
    mask = jnp.concatenate([mask, mask], axis=0)
    scale = HEAD_DIM ** (-0.5)
    for pair in range(width // LANES):
        cols = slice(pair * LANES, (pair + 1) * LANES)
        vcols = slice(width + pair * LANES, width + (pair + 1) * LANES)
        q = q_ref[:, cols]
        for m in range(members):
            th = jnp.tanh(mm(split_heads(kv_ref[m, :, cols]), q, NT) * (0.5 * scale))
            gate = ((0.5 * th + 0.5) * mask).astype(BF)
            gate_ref[pair, m] = gate
            slope_ref[pair, m] = ((0.25 * scale) * mask * (1.0 - th * th)).astype(BF)
            merged_ref[m, cols, :] = mm(split_heads(kv_ref[m, :, vcols]), gate, TN).astype(BF)
    send_rows = send_ref.shape[1]
    for m in range(members):
        part = mm(p_ref[...], merged_ref[m])
        part_ref[m] = part
        send_ref[m] = part[0:send_rows].astype(BF)


def destination_rows(member, band, n_member, n_band, rw):
    chip, core = band // 2, band % 2
    for rel_core in (1, 0):
        for rel_chip in range(n_band // 2):
            to_band = (chip ^ rel_chip) * 2 + (core ^ rel_core)
            for rel_member in range(n_member):
                yield pl.multiple_of(((member ^ rel_member) * n_band + to_band) * rw, rw)


def reorder(src_ref, n_member, n_band):
    rw = src_ref.shape[0] // (n_member * n_band)
    member, band = lax.axis_index("member"), lax.axis_index("band")
    starts = destination_rows(member, band, n_member, n_band, rw)
    return jnp.concatenate([src_ref[pl.ds(start, rw), :] for start in starts], axis=0)


def transpose_body(n_member, n_band, hidden_ref, below_ref, above_ref, out_ref, turned):
    members, nodes, _ = hidden_ref.shape
    rim = below_ref.shape[0] // members
    parts = []
    for m in range(members):
        parts.append(hidden_ref[m])
        parts.append(below_ref[m * rim : (m + 1) * rim, :])
        parts.append(above_ref[m * rim : (m + 1) * rim, :])
    turned[...] = jnp.concatenate(parts, axis=0).astype(F32).T
    out_ref[...] = reorder(turned, n_member, n_band).astype(BF)


def select_heads(block):
    half = block.shape[0] // 2
    low = lax.broadcasted_iota(jnp.int32, (half, block.shape[1]), 1) < HEAD_DIM
    return jnp.where(low, block[:half], block[half:])


def soft_slope(v):
    return v * lax.rsqrt(v * v + SOFTENING * SOFTENING)


def backward_body(n_member, n_band, n_recv, *refs):
    recv_refs = refs[:n_recv]
    (part_ref, base_ref, truth_ref, weight_ref, pt_ref, merged_ref, gate_ref, slope_ref,
     kv_ref, q_ref, ext_ref, wo_ref) = refs[n_recv : n_recv + 12]
    outs = refs[n_recv + 12 :]
    n_out = n_band
    ng_ref = outs[0]
    part_outs = outs[1 : 1 + n_out]
    grad, turned = outs[1 + n_out :]
    members, ext, width2 = kv_ref.shape
    width = width2 // 2
    channels = truth_ref.shape[0]
    total = members * n_member
    spread = (1.0 - (1.0 - ALPHA) / total) / (total * (total - 1))

    grad[...] = jnp.zeros_like(grad)
    own = [part_ref[m, 0:channels, :] for m in range(members)]
    for m in range(members):
        slopes = jnp.zeros_like(own[m])
        for k in range(members):
            if k != m:
                slopes = slopes + soft_slope(own[m] - own[k])
        for ref in recv_refs:
            for k in range(members):
                slopes = slopes + soft_slope(own[m] - ref[k, 0:channels, :].astype(F32))
        gap = soft_slope(own[m] + base_ref[0:channels, :] - truth_ref[...])
        grad[m, 0:channels, :] = (weight_ref[...] * (gap / total - spread * slopes)).astype(BF)

    merged_t = [mm(pt_ref[...], grad[m]).astype(BF) for m in range(members)]

    for pair in range(width // LANES):
        cols = slice(pair * LANES, (pair + 1) * LANES)
        vcols = slice(width + pair * LANES, width + (pair + 1) * LANES)
        q = q_ref[:, cols]
        for m in range(members):
            dm = merged_t[m][cols]
            dgate = mm(split_heads(kv_ref[m, :, vcols]), dm)
            dscore = (dgate * slope_ref[pair, m].astype(F32)).astype(BF)
            ng_ref[m * ext : (m + 1) * ext, cols] = select_heads(mm(dscore, q)).astype(BF)
            ng_ref[m * ext : (m + 1) * ext, vcols] = select_heads(mm(gate_ref[pair, m], dm, NT)).astype(BF)

    step = 512
    block = part_outs[0].shape[0]
    for start in range(0, width2, step):
        product = mm(ext_ref[...], ng_ref[:, start : start + step]).astype(BF)
        for i, ref in enumerate(part_outs):
            ref[:, start : start + step] = product[i * block : (i + 1) * block]

    m_t = sum(mm(grad[m], merged_ref[m], NT) for m in range(members))
    head_t = sum(mm(grad[m], q_ref[...]) for m in range(members)) + mm(m_t.astype(BF), wo_ref[...])
    turned[...] = jnp.concatenate([m_t, head_t], axis=0).T
    small = reorder(turned, n_member, n_band).astype(BF)
    for i, ref in enumerate(part_outs):
        ref[:, width2:] = small[i * block : (i + 1) * block]


def extended_grad_body(members, nodes, rim, ng_ref, kvw_ref, own_ref, down_ref, up_ref):
    ext = nodes + 2 * rim
    for m in range(members):
        rows = mm(ng_ref[m * ext : (m + 1) * ext, :], kvw_ref[...], NT)
        own_ref[m] = rows[0:nodes]
        down_ref[m * rim : (m + 1) * rim, :] = rows[nodes : nodes + rim].astype(BF)
        up_ref[m * rim : (m + 1) * rim, :] = rows[nodes + rim :].astype(BF)


def hidden_body(own_ref, from_below_ref, from_above_ref, halo_ref, out_ref):
    members, nodes, _ = own_ref.shape
    rim = halo_ref.shape[1]
    low = one_hot_rows(halo_ref, 0, nodes)
    high = one_hot_rows(halo_ref, 1, nodes)
    for m in range(members):
        rows = slice(m * rim, (m + 1) * rim)
        out_ref[m] = own_ref[m] + mm(low, from_below_ref[rows, :]) + mm(high, from_above_ref[rows, :])


def finish_body(devices, *refs):
    parts = refs[:-4]
    hp_ref, kv_ref, out_ref, head_ref = refs[-4:]
    width2 = kv_ref.shape[1]
    channels = hp_ref.shape[1]
    total = parts[0][...].astype(F32)
    for ref in parts[1:]:
        total = total + ref[...].astype(F32)
    total = total * (1.0 / devices)
    kv_ref[...] = total[:, 0:width2]
    m_rows = total[:, width2 : width2 + channels]
    high = m_rows.astype(BF)
    low = (m_rows - high.astype(F32)).astype(BF)
    out_ref[...] = mm(high, hp_ref[...], NT) + mm(low, hp_ref[...], NT)
    head_ref[...] = total[:, width2 + LANES : width2 + LANES + channels]


def add_up(*parts):
    return functools.reduce(lambda a, b: a + b, [p.astype(F32) for p in parts])


def shards(
    n_member, n_band,
    hidden, queries, kv_weight, out_weight, head_projection, initial_state, truth,
    latitude_weight, channel_loss_weight, sources, halo_rows,
):
    members, nodes, width = hidden.shape
    points = queries.shape[0]
    channels = head_projection.shape[1]
    rim = halo_rows.shape[1]
    ext = nodes + 2 * rim
    pairs = width // LANES
    devices = n_member * n_band
    chips = n_band // 2
    rw = width // devices
    send_rows = -(-channels // 16) * 16
    to_above = [(i, i + 1) for i in range(n_band - 1)]
    to_below = [(i + 1, i) for i in range(n_band - 1)]

    down, up = call(
        pick_body, [sds((members * rim, width), BF)] * 2, (hidden, halo_rows), flops=10**7, nbytes=10**6
    )
    below = lax.ppermute(up, "band", to_above)
    above = lax.ppermute(down, "band", to_below)

    own_kv, pt, p, base, weight = call(
        prepare_body,
        [
            sds((members * nodes, 2 * width), BF),
            sds((width, LANES), BF),
            sds((LANES, width), BF),
            sds((LANES, points), F32),
            sds((channels, points), F32),
        ],
        (
            hidden.reshape(members * nodes, width), kv_weight, out_weight, head_projection, queries,
            initial_state, channel_loss_weight[:, None], latitude_weight[None, :],
        ),
        [pltpu.VMEM((width, LANES), F32)],
        flops=10**9, nbytes=8 * 10**6,
    )

    kv, gates, slopes, merged, part, sent = call(
        forward_body,
        [
            sds((members, ext, 2 * width), BF),
            sds((pairs, members, 2 * ext, points), BF),
            sds((pairs, members, 2 * ext, points), BF),
            sds((members, width, points), BF),
            sds((members, LANES, points), F32),
            sds((members, send_rows, points), BF),
        ],
        (below, above, own_kv, kv_weight, queries, sources, p),
        flops=4 * 10**9, nbytes=16 * 10**6,
    )

    received = [
        lax.ppermute(sent, "member", [(i, i ^ s) for i in range(n_member)]) for s in range(1, n_member)
    ]

    ext_t = call(
        functools.partial(transpose_body, n_member, n_band),
        sds((width, members * ext), BF),
        (hidden, below, above),
        [pltpu.VMEM((width, members * ext), F32)],
        flops=10**8, nbytes=2 * 10**6,
    )

    extra = 2 * LANES
    results = call(
        functools.partial(backward_body, n_member, n_band, n_member - 1),
        [sds((members * ext, 2 * width), BF)]
        + [sds((n_member * rw, 2 * width + extra), BF)] * n_band,
        (*received, part, base, truth, weight, pt, merged, gates, slopes, kv, queries, ext_t, out_weight),
        [pltpu.VMEM((members, LANES, points), BF), pltpu.VMEM((width, extra), F32)],
        flops=8 * 10**9, nbytes=24 * 10**6,
    )
    node_grad, send, keep = results[0], results[1 : 1 + chips], results[1 + chips :]

    swap = [(i, i ^ 1) for i in range(n_band)]
    crossed = [None] * chips
    for s in list(range(1, chips)) + [0]:
        crossed[s] = lax.ppermute(send[s], "band", swap)

    own_grad, back_down, back_up = call(
        functools.partial(extended_grad_body, members, nodes, rim),
        [sds((members, nodes, width), F32)] + [sds((members * rim, width), BF)] * 2,
        (node_grad, kv_weight),
        flops=2 * 10**9, nbytes=8 * 10**6,
    )

    gathered = []
    for s in range(1, chips):
        chip_sum = add_up(keep[s], crossed[s]).astype(BF)
        gathered.append(
            lax.ppermute(chip_sum, "band", [(i, ((i // 2) ^ s) * 2 + i % 2) for i in range(n_band)])
        )

    from_above = lax.ppermute(back_down, "band", to_below)
    from_below = lax.ppermute(back_up, "band", to_above)
    hidden_grad = call(
        hidden_body,
        sds((members, nodes, width), F32),
        (own_grad, from_below, from_above, halo_rows),
        flops=10**7, nbytes=2 * 10**6,
    )

    plane = add_up(keep[0], crossed[0], *gathered).astype(BF)
    last = [plane[0:rw]]
    for s in range(1, n_member):
        last.append(
            lax.ppermute(plane[s * rw : (s + 1) * rw], "member", [(i, i ^ s) for i in range(n_member)])
        )
    kv_grad, out_grad, head_grad = call(
        functools.partial(finish_body, devices),
        [sds((rw, 2 * width), F32), sds((rw, width), F32), sds((rw, channels), F32)],
        (*last, head_projection),
        flops=10**7, nbytes=10**6,
    )
    return hidden_grad, kv_grad, out_grad, head_grad


def solution(mesh):
    placed = (
        P("member", "band", None),
        P("band", None),
        P(),
        P(),
        P(),
        P(None, "band"),
        P(None, "band"),
        P("band"),
        P(),
        P(None, "band"),
        P("band", None),
    )
    return jax.shard_map(
        functools.partial(shards, mesh.shape["member"], mesh.shape["band"]),
        mesh=mesh,
        in_specs=placed,
        out_specs=(
            P("member", "band", None),
            P(("member", "band"), None),
            P(("member", "band"), None),
            P(("member", "band"), None),
        ),
        check_vma=False,
    )
```

```python
import functools

import jax
import jax.numpy as jnp
from jax import lax
from jax.experimental import pallas as pl
from jax.experimental.pallas import tpu as pltpu
from jax.sharding import PartitionSpec as P

HEAD_DIM = 64
LANES = 128
ALPHA = 0.95
SOFTENING = 0.5
BF = jnp.bfloat16
F32 = jnp.float32
NN = (((1,), (0,)), ((), ()))
NT = (((1,), (1,)), ((), ()))
TN = (((0,), (0,)), ((), ()))


def mm(a, b, dims=NN):
    return lax.dot_general(a, b, dims, preferred_element_type=F32)


def call(body, out_shape, args, scratch=(), flops=0, nbytes=0, hbm=(), limit=40):
    return pl.pallas_call(
        body,
        out_shape=out_shape,
        in_specs=[
            pl.BlockSpec(memory_space=pltpu.HBM if i in hbm else pltpu.VMEM) for i in range(len(args))
        ],
        out_specs=jax.tree.map(lambda _: pl.BlockSpec(memory_space=pltpu.VMEM), out_shape),
        scratch_shapes=list(scratch),
        compiler_params=pltpu.CompilerParams(vmem_limit_bytes=limit * 1024 * 1024),
        cost_estimate=pl.CostEstimate(flops=flops, bytes_accessed=nbytes, transcendentals=0),
    )(*args)


def sds(shape, dtype):
    return jax.ShapeDtypeStruct(shape, dtype)


def one_hot_rows(rows, node_count):
    nodes = lax.broadcasted_iota(jnp.int32, (node_count, rows.shape[1]), 0).astype(rows.dtype)
    return (nodes == rows).astype(F32).astype(BF)


def start_copies(pairs, sems):
    copies = [pltpu.make_async_copy(src, dst, sems.at[i]) for i, (src, dst) in enumerate(pairs)]
    for copy in copies:
        copy.start()
    return copies


def pick_body(hidden_hbm, halo_hbm, hidden_ref, halo_ref, down_ref, up_ref, plus_ref, row_ref, sems):
    for copy in start_copies([(hidden_hbm, hidden_ref), (halo_hbm, halo_ref)], sems):
        copy.wait()
    members, nodes, _ = hidden_ref.shape
    rim = halo_ref.shape[1]
    for row, out_ref in ((0, down_ref), (1, up_ref)):
        hot = one_hot_rows(halo_ref[row : row + 1, :], nodes)
        for m in range(members):
            out_ref[m * rim : (m + 1) * rim, :] = mm(hot, hidden_ref[m], TN).astype(BF)
    for m in range(members):
        plus_ref[m * nodes : (m + 1) * nodes, :] = hidden_ref[m]
    row_ref[...] = jnp.zeros_like(row_ref)
    row_ref[0:2, 0:rim] = halo_ref[...].astype(F32)
    plus_ref[members * nodes :, :] = row_ref[...].astype(BF)


def prepare_body(
    hidden_ref, wo_hbm, hp_hbm, q_hbm, kvw_hbm, init_hbm, chw_hbm, lat_hbm, src_hbm, truth_hbm,
    kv_ref, pt_ref, p_ref, base_ref, weight_ref, wo_ref, hp_ref, q_ref, kvw_ref, src_ref, truth_ref,
    init_ref, chw_ref, lat_ref, chw_pad, hp_pad, sems,
):
    channels = hp_ref.shape[0]
    members, nodes, width = hidden_ref.shape
    w, h, q, k, i, c, l, s, t = start_copies(
        [
            (wo_hbm, wo_ref), (hp_hbm, hp_ref), (q_hbm, q_ref), (kvw_hbm, kvw_ref), (init_hbm, init_ref),
            (chw_hbm, chw_ref), (lat_hbm, lat_ref), (src_hbm, src_ref), (truth_hbm, truth_ref),
        ],
        sems,
    )
    hp_pad[...] = jnp.zeros_like(hp_pad)
    h.wait()
    hp_pad[0:channels, :] = hp_ref[...].astype(F32)
    hp_t = hp_pad[...].astype(BF)
    c.wait()
    l.wait()
    chw_pad[:, 0:channels] = jnp.broadcast_to(chw_ref[...], (8, channels))
    column = chw_pad[...].T
    weight_ref[...] = column[0:channels, 0:1] * lat_ref[...]
    q.wait()
    i.wait()
    base_ref[...] = mm(hp_t, q_ref[...], NT)
    base_ref[0:channels, :] = base_ref[0:channels, :] + init_ref[...]
    w.wait()
    p = mm(hp_t, wo_ref[...], NT)
    p_ref[...] = p.astype(BF)
    pt_ref[...] = p.T.astype(BF)
    k.wait()
    for m in range(members):
        kv_ref[m * nodes : (m + 1) * nodes, :] = mm(hidden_ref[m], kvw_ref[...]).astype(BF)
    s.wait()
    t.wait()


def split_heads(block):
    low = lax.broadcasted_iota(jnp.int32, block.shape, 1) < HEAD_DIM
    zero = jnp.zeros_like(block)
    return jnp.concatenate([jnp.where(low, block, zero), jnp.where(low, zero, block)], axis=0)


def forward_body(
    below_ref, above_ref, own_ref, kvw_ref, q_ref, src_ref, p_ref,
    kv_ref, gate_ref, slope_ref, merged_ref, part_ref, send_ref,
):
    members, ext, width2 = kv_ref.shape
    width = width2 // 2
    points = q_ref.shape[0]
    nodes = own_ref.shape[0] // members
    rim = below_ref.shape[0] // members
    halo = mm(jnp.concatenate([below_ref[...], above_ref[...]], axis=0), kvw_ref[...]).astype(BF)
    for m in range(members):
        kv_ref[m, 0:nodes, :] = own_ref[m * nodes : (m + 1) * nodes, :]
        kv_ref[m, nodes : nodes + rim, :] = halo[m * rim : (m + 1) * rim]
        kv_ref[m, nodes + rim : ext, :] = halo[(members + m) * rim : (members + m + 1) * rim]
    rows = lax.broadcasted_iota(jnp.int32, (ext, points), 0)
    mask = rows == src_ref[0:1, :]
    for e in range(1, src_ref.shape[0]):
        mask = mask | (rows == src_ref[e : e + 1, :])
    mask = mask.astype(F32)
    mask = jnp.concatenate([mask, mask], axis=0)
    scale = HEAD_DIM ** (-0.5)
    for pair in range(width // LANES):
        cols = slice(pair * LANES, (pair + 1) * LANES)
        vcols = slice(width + pair * LANES, width + (pair + 1) * LANES)
        q = q_ref[:, cols]
        for m in range(members):
            th = jnp.tanh(mm(split_heads(kv_ref[m, :, cols]), q, NT) * (0.5 * scale))
            gate = ((0.5 * th + 0.5) * mask).astype(BF)
            gate_ref[pair, m] = gate
            slope_ref[pair, m] = ((0.25 * scale) * mask * (1.0 - th * th)).astype(BF)
            merged_ref[m, cols, :] = mm(split_heads(kv_ref[m, :, vcols]), gate, TN).astype(BF)
    send_rows = send_ref.shape[1]
    for m in range(members):
        part = mm(p_ref[...], merged_ref[m])
        part_ref[m] = part
        send_ref[m] = part[0:send_rows].astype(BF)


def plane_body(all_ref, turned_ref, hot_ref):
    bands, nodes2, rim = all_ref.shape[0], turned_ref.shape[1] // all_ref.shape[0], hot_ref.shape[3]
    for band in range(bands):
        rows = all_ref[band, 0:nodes2, :].astype(F32)
        turned_ref[:, band * nodes2 : (band + 1) * nodes2] = rows.T.astype(BF)
        halo = all_ref[band, nodes2:, 0:LANES].astype(F32)
        for side in range(2):
            hot_ref[band, side] = one_hot_rows(halo[side : side + 1, 0:rim], hot_ref.shape[2])


def select_heads(block):
    half = block.shape[0] // 2
    low = lax.broadcasted_iota(jnp.int32, (half, block.shape[1]), 1) < HEAD_DIM
    return jnp.where(low, block[:half], block[half:])


def soft_slope(v):
    return v * lax.rsqrt(v * v + SOFTENING * SOFTENING)


def column_blocks(width, block):
    for pair in range(width // LANES):
        for side in range(2):
            flat = (2 * pair + side) * LANES
            yield pair, side, flat // block, flat % block


def backward_body(n_member, n_band, n_recv, *refs):
    recv_refs = refs[:n_recv]
    (part_ref, base_ref, truth_ref, weight_ref, pt_ref, merged_ref, gate_ref, slope_ref,
     kv_ref, q_ref, wo_ref, ng_ref, small_ref, grad, turned) = refs[n_recv:]
    members, ext, width2 = kv_ref.shape
    width = width2 // 2
    block = ng_ref.shape[2]
    channels = truth_ref.shape[0]
    total = members * n_member
    spread = (1.0 - (1.0 - ALPHA) / total) / (total * (total - 1))

    grad[...] = jnp.zeros_like(grad)
    own = [part_ref[m, 0:channels, :] for m in range(members)]
    for m in range(members):
        slopes = jnp.zeros_like(own[m])
        for k in range(members):
            if k != m:
                slopes = slopes + soft_slope(own[m] - own[k])
        for ref in recv_refs:
            for k in range(members):
                slopes = slopes + soft_slope(own[m] - ref[k, 0:channels, :].astype(F32))
        gap = soft_slope(own[m] + base_ref[0:channels, :] - truth_ref[...])
        grad[m, 0:channels, :] = (weight_ref[...] * (gap / total - spread * slopes)).astype(BF)

    merged_t = [mm(pt_ref[...], grad[m]).astype(BF) for m in range(members)]

    for pair, side, where, offset in column_blocks(width, block):
        cols = slice(pair * LANES, (pair + 1) * LANES)
        vcols = slice(width + pair * LANES, width + (pair + 1) * LANES)
        for m in range(members):
            dm = merged_t[m][cols]
            if side == 0:
                dgate = mm(split_heads(kv_ref[m, :, vcols]), dm)
                dscore = (dgate * slope_ref[pair, m].astype(F32)).astype(BF)
                result = mm(dscore, q_ref[:, cols])
            else:
                result = mm(gate_ref[pair, m], dm, NT)
            rows = slice(m * ext, (m + 1) * ext)
            ng_ref[where, rows, offset : offset + LANES] = select_heads(result).astype(BF)

    m_t = sum(mm(grad[m], merged_ref[m], NT) for m in range(members))
    head_t = sum(mm(grad[m], q_ref[...]) for m in range(members)) + mm(m_t.astype(BF), wo_ref[...])
    turned[...] = jnp.concatenate([m_t, head_t], axis=0).T
    rw = turned.shape[0] // (n_member * n_band)
    for band in range(n_band):
        starts = [(m * n_band + band) * rw for m in range(n_member)]
        small_ref[band] = jnp.concatenate([turned[i : i + rw, :] for i in starts], axis=0).astype(BF)


def block_body(rim, got_ref, turned_ref, hot_ref, out_ref, owned):
    bands, rows, block = got_ref.shape
    nodes = hot_ref.shape[2]
    ext = nodes + 2 * rim
    members = rows // ext
    for band in range(bands):
        for m in range(members):
            at = m * ext
            total = got_ref[band, at : at + nodes, :].astype(F32)
            if band > 0:
                total = total + mm(hot_ref[band, 0], got_ref[band - 1, at + nodes + rim : at + ext, :])
            if band < bands - 1:
                total = total + mm(hot_ref[band, 1], got_ref[band + 1, at + nodes : at + nodes + rim, :])
            first = (band * members + m) * nodes
            owned[first : first + nodes, :] = total.astype(BF)
    out_ref[...] = mm(turned_ref[...], owned[...]).astype(BF)


def extended_grad_body(members, nodes, rim, ng_ref, kvw_ref, own_ref, down_ref, up_ref):
    ext = nodes + 2 * rim
    width = kvw_ref.shape[0]
    block = ng_ref.shape[2]
    places = list(column_blocks(width, block))
    ordered = [p for p in places if p[1] == 0] + [p for p in places if p[1] == 1]
    for m in range(members):
        at = slice(m * ext, (m + 1) * ext)
        grads = jnp.concatenate([ng_ref[w, at, o : o + LANES] for _, _, w, o in ordered], axis=1)
        rows = mm(grads, kvw_ref[...], NT)
        own_ref[m] = rows[0:nodes]
        down_ref[m * rim : (m + 1) * rim, :] = rows[nodes : nodes + rim].astype(BF)
        up_ref[m * rim : (m + 1) * rim, :] = rows[nodes + rim :].astype(BF)


def hidden_body(own_ref, from_below_ref, from_above_ref, halo_ref, out_ref):
    members, nodes, _ = own_ref.shape
    rim = halo_ref.shape[1]
    low = one_hot_rows(halo_ref[0:1, :], nodes)
    high = one_hot_rows(halo_ref[1:2, :], nodes)
    for m in range(members):
        rows = slice(m * rim, (m + 1) * rim)
        out_ref[m] = own_ref[m] + mm(low, from_below_ref[rows, :]) + mm(high, from_above_ref[rows, :])


def finish_body(n_member, n_band, blocks_ref, small_ref, hp_ref, kv_ref, out_ref, head_ref):
    width = kv_ref.shape[1] // 2
    channels = hp_ref.shape[0]
    scale = 1.0 / (n_member * n_band)
    block = blocks_ref.shape[2]
    sums = []
    for band in range(n_band):
        total = blocks_ref[band].astype(F32)
        for m in range(1, n_member):
            total = total + blocks_ref[m * n_band + band].astype(F32)
        sums.append(total * scale)
    for pair, side, where, offset in column_blocks(width, block):
        at = side * width + pair * LANES
        kv_ref[:, at : at + LANES] = sums[where][:, offset : offset + LANES]
    total = small_ref[0].astype(F32)
    for m in range(1, n_member):
        total = total + small_ref[m].astype(F32)
    total = total * scale
    m_rows = total[:, 0:channels]
    high = m_rows.astype(BF)
    low = (m_rows - high.astype(F32)).astype(BF)
    out_ref[...] = mm(high, hp_ref[...]) + mm(low, hp_ref[...])
    head_ref[...] = total[:, LANES : LANES + channels]


def shards(
    n_member, n_band,
    hidden, queries, kv_weight, out_weight, head_projection, initial_state, truth,
    latitude_weight, channel_loss_weight, sources, halo_rows,
):
    members, nodes, width = hidden.shape
    points = queries.shape[0]
    channels = head_projection.shape[1]
    rim = halo_rows.shape[1]
    ext = nodes + 2 * rim
    pairs = width // LANES
    devices = n_member * n_band
    rw = width // devices
    block = 2 * width // n_band
    send_rows = -(-channels // 16) * 16
    to_above = [(i, i + 1) for i in range(n_band - 1)]
    to_below = [(i + 1, i) for i in range(n_band - 1)]

    own_hidden, halo, down, up, plus = call(
        pick_body,
        [sds(hidden.shape, BF), sds(halo_rows.shape, jnp.int32)]
        + [sds((members * rim, width), BF)] * 2
        + [sds((members * nodes + 16, width), BF)],
        (hidden, halo_rows),
        [pltpu.VMEM((16, width), F32), pltpu.SemaphoreType.DMA((2,))],
        flops=10**7, nbytes=10**6, hbm=(0, 1),
    )
    below = lax.ppermute(up, "band", to_above)
    above = lax.ppermute(down, "band", to_below)
    whole_plane = lax.all_gather(plus, "band", axis=0)

    args = (
        own_hidden, out_weight, head_projection.T, queries, kv_weight, initial_state,
        channel_loss_weight[None, :], latitude_weight[None, :], sources, truth,
    )
    own_kv, pt, p, base, weight, wo, hp, q, kvw, src, true = call(
        prepare_body,
        [
            sds((members * nodes, 2 * width), BF),
            sds((width, LANES), BF),
            sds((LANES, width), BF),
            sds((LANES, points), F32),
            sds((channels, points), F32),
        ]
        + [sds(args[i].shape, args[i].dtype) for i in (1, 2, 3, 4, 8, 9)],
        args,
        [
            pltpu.VMEM((channels, points), F32),
            pltpu.VMEM((1, channels), F32),
            pltpu.VMEM((1, points), F32),
            pltpu.VMEM((8, LANES), F32),
            pltpu.VMEM((LANES, width), F32),
            pltpu.SemaphoreType.DMA((9,)),
        ],
        flops=10**9, nbytes=8 * 10**6, hbm=tuple(range(1, 10)),
    )

    kv, gates, slopes, merged, part, sent = call(
        forward_body,
        [
            sds((members, ext, 2 * width), BF),
            sds((pairs, members, 2 * ext, points), BF),
            sds((pairs, members, 2 * ext, points), BF),
            sds((members, width, points), BF),
            sds((members, LANES, points), F32),
            sds((members, send_rows, points), BF),
        ],
        (below, above, own_kv, kvw, q, src, p),
        flops=4 * 10**9, nbytes=16 * 10**6,
    )

    received = [
        lax.ppermute(sent, "member", [(i, i ^ s) for i in range(n_member)]) for s in range(1, n_member)
    ]

    node_grad, small = call(
        functools.partial(backward_body, n_member, n_band, n_member - 1),
        [sds((n_band, members * ext, block), BF), sds((n_band, n_member * rw, 2 * LANES), BF)],
        (*received, part, base, true, weight, pt, merged, gates, slopes, kv, q, wo),
        [pltpu.VMEM((members, LANES, points), BF), pltpu.VMEM((width, 2 * LANES), F32)],
        flops=6 * 10**9, nbytes=24 * 10**6,
    )
    traded = lax.all_to_all(node_grad, "band", 0, 0, tiled=True)
    small = lax.all_to_all(small, "band", 0, 0, tiled=True)

    own_grad, back_down, back_up = call(
        functools.partial(extended_grad_body, members, nodes, rim),
        [sds((members, nodes, width), F32)] + [sds((members * rim, width), BF)] * 2,
        (node_grad, kvw),
        flops=2 * 10**9, nbytes=8 * 10**6,
    )
    from_above = lax.ppermute(back_down, "band", to_below)
    from_below = lax.ppermute(back_up, "band", to_above)

    turned, hot = call(
        plane_body,
        [sds((width, n_band * members * nodes), BF), sds((n_band, 2, nodes, rim), BF)],
        (whole_plane,),
        flops=10**8, nbytes=2 * 10**6,
    )
    kv_part = call(
        functools.partial(block_body, rim),
        sds((width, block), BF),
        (traded, turned, hot),
        [pltpu.VMEM((n_band * members * nodes, block), BF)],
        flops=10**9, nbytes=4 * 10**6,
    )
    blocks = lax.all_to_all(kv_part.reshape(devices, rw, block), ("member", "band"), 0, 0, tiled=True)
    small = jnp.sum(small.astype(F32), axis=0).astype(BF).reshape(n_member, rw, 2 * LANES)
    small = lax.all_to_all(small, "member", 0, 0, tiled=True)

    hidden_grad = call(
        hidden_body,
        sds((members, nodes, width), F32),
        (own_grad, from_below, from_above, halo),
        flops=10**7, nbytes=2 * 10**6,
    )
    kv_grad, out_grad, head_grad = call(
        functools.partial(finish_body, n_member, n_band),
        [sds((rw, 2 * width), F32), sds((rw, width), F32), sds((rw, channels), F32)],
        (blocks, small, hp),
        flops=10**7, nbytes=10**6,
    )
    return hidden_grad, kv_grad, out_grad, head_grad


def solution(mesh):
    placed = (
        P("member", "band", None),
        P("band", None),
        P(),
        P(),
        P(),
        P(None, "band"),
        P(None, "band"),
        P("band"),
        P(),
        P(None, "band"),
        P("band", None),
    )
    return jax.shard_map(
        functools.partial(shards, mesh.shape["member"], mesh.shape["band"]),
        mesh=mesh,
        in_specs=placed,
        out_specs=(
            P("member", "band", None),
            P(("member", "band"), None),
            P(("member", "band"), None),
            P(("member", "band"), None),
        ),
        check_vma=False,
    )
```

```python
import functools

import jax
import jax.numpy as jnp
from jax import lax
from jax.experimental import pallas as pl
from jax.experimental.pallas import tpu as pltpu
from jax.sharding import PartitionSpec as P

HEAD_DIM = 64
LANES = 128
KV_COPIES = 4
ALPHA = 0.95
SOFTENING = 0.5
BF = jnp.bfloat16
F32 = jnp.float32
NN = (((1,), (0,)), ((), ()))
NT = (((1,), (1,)), ((), ()))
TN = (((0,), (0,)), ((), ()))


def mm(a, b, dims=NN):
    return lax.dot_general(a, b, dims, preferred_element_type=F32)


def call(body, out_shape, args, scratch=(), hbm=(), limit=40):
    args = [pltpu.with_memory_space_constraint(x, pltpu.HBM) if i in hbm else x for i, x in enumerate(args)]
    return pl.pallas_call(
        body,
        out_shape=out_shape,
        in_specs=[
            pl.BlockSpec(memory_space=pltpu.HBM if i in hbm else pltpu.VMEM) for i in range(len(args))
        ],
        out_specs=jax.tree.map(lambda _: pl.BlockSpec(memory_space=pltpu.VMEM), out_shape),
        scratch_shapes=list(scratch),
        compiler_params=pltpu.CompilerParams(vmem_limit_bytes=limit * 1024 * 1024),
        cost_estimate=pl.CostEstimate(flops=1, bytes_accessed=1, transcendentals=0),
    )(*args)


def sds(shape, dtype):
    return jax.ShapeDtypeStruct(shape, dtype)


def one_hot_rows(rows, node_count):
    nodes = lax.broadcasted_iota(jnp.int32, (node_count, rows.shape[1]), 0).astype(rows.dtype)
    return (nodes == rows).astype(F32).astype(BF)


def start_copies(pairs, sems):
    copies = [pltpu.make_async_copy(src, dst, sems.at[i]) for i, (src, dst) in enumerate(pairs)]
    for copy in copies:
        copy.start()
    return copies


def pick_body(hidden_hbm, halo_hbm, hidden_ref, halo_ref, down_ref, up_ref, sems):
    for copy in start_copies([(hidden_hbm, hidden_ref), (halo_hbm, halo_ref)], sems):
        copy.wait()
    members, nodes, _ = hidden_ref.shape
    rim = halo_ref.shape[1]
    for row, out_ref in ((0, down_ref), (1, up_ref)):
        hot = one_hot_rows(halo_ref[row : row + 1, :], nodes)
        for m in range(members):
            out_ref[m * rim : (m + 1) * rim, :] = mm(hot, hidden_ref[m], TN).astype(BF)


def prepare_body(
    hidden_ref, wo_hbm, hp_hbm, q_hbm, kvw_hbm, init_hbm, chw_hbm, lat_hbm, src_hbm, truth_hbm,
    kv_ref, pt_ref, p_ref, base_ref, weight_ref, wo_ref, hp_ref, q_ref, kvw_ref, src_ref, truth_ref,
    init_ref, chw_ref, lat_ref, chw_pad, hp_pad, sems,
):
    channels = hp_ref.shape[0]
    members, nodes, width = hidden_ref.shape
    step = kvw_ref.shape[1] // KV_COPIES
    pieces = [slice(j * step, (j + 1) * step) for j in range(KV_COPIES)]
    h, q, i, w, c, l, s, t, *k = start_copies(
        [
            (hp_hbm, hp_ref), (q_hbm, q_ref), (init_hbm, init_ref), (wo_hbm, wo_ref), (chw_hbm, chw_ref),
            (lat_hbm, lat_ref), (src_hbm, src_ref), (truth_hbm, truth_ref),
        ]
        + [(kvw_hbm.at[:, piece], kvw_ref.at[:, piece]) for piece in pieces],
        sems,
    )
    hp_pad[...] = jnp.zeros_like(hp_pad)
    h.wait()
    hp_pad[0:channels, :] = hp_ref[...].astype(F32)
    hp_t = hp_pad[...].astype(BF)
    c.wait()
    l.wait()
    chw_pad[:, 0:channels] = jnp.broadcast_to(chw_ref[...], (8, channels))
    column = chw_pad[...].T
    weight_ref[...] = column[0:channels, 0:1] * lat_ref[...]
    q.wait()
    i.wait()
    base_ref[...] = mm(hp_t, q_ref[...], NT)
    base_ref[0:channels, :] = base_ref[0:channels, :] + init_ref[...]
    w.wait()
    p = mm(hp_t, wo_ref[...], NT)
    p_ref[...] = p.astype(BF)
    pt_ref[...] = p.T.astype(BF)
    hidden = jnp.concatenate([hidden_ref[m] for m in range(members)], axis=0)
    for piece, copy in zip(pieces, k):
        copy.wait()
        kv_ref[:, piece] = mm(hidden, kvw_ref[:, piece]).astype(BF)
    s.wait()
    t.wait()


def split_heads(block):
    low = lax.broadcasted_iota(jnp.int32, block.shape, 1) < HEAD_DIM
    zero = jnp.zeros_like(block)
    return jnp.concatenate([jnp.where(low, block, zero), jnp.where(low, zero, block)], axis=0)


def forward_body(
    below_ref, above_ref, own_ref, kvw_ref, q_ref, src_ref, p_ref,
    kv_ref, gate_ref, slope_ref, merged_ref, part_ref, send_ref,
):
    members, ext, width2 = kv_ref.shape
    width = width2 // 2
    points = q_ref.shape[0]
    nodes = own_ref.shape[0] // members
    rim = below_ref.shape[0] // members
    halo = mm(jnp.concatenate([below_ref[...], above_ref[...]], axis=0), kvw_ref[...]).astype(BF)
    for m in range(members):
        kv_ref[m, 0:nodes, :] = own_ref[m * nodes : (m + 1) * nodes, :]
        kv_ref[m, nodes : nodes + rim, :] = halo[m * rim : (m + 1) * rim]
        kv_ref[m, nodes + rim : ext, :] = halo[(members + m) * rim : (members + m + 1) * rim]
    rows = lax.broadcasted_iota(jnp.int32, (ext, points), 0)
    mask = rows == src_ref[0:1, :]
    for e in range(1, src_ref.shape[0]):
        mask = mask | (rows == src_ref[e : e + 1, :])
    mask = mask.astype(F32)
    mask = jnp.concatenate([mask, mask], axis=0)
    scale = HEAD_DIM ** (-0.5)
    for pair in range(width // LANES):
        cols = slice(pair * LANES, (pair + 1) * LANES)
        vcols = slice(width + pair * LANES, width + (pair + 1) * LANES)
        q = q_ref[:, cols]
        for m in range(members):
            th = jnp.tanh(mm(split_heads(kv_ref[m, :, cols]), q, NT) * (0.5 * scale))
            gate = ((0.5 * th + 0.5) * mask).astype(BF)
            gate_ref[pair, m] = gate
            slope_ref[pair, m] = ((0.25 * scale) * mask * (1.0 - th * th)).astype(BF)
            merged_ref[m, cols, :] = mm(split_heads(kv_ref[m, :, vcols]), gate, TN).astype(BF)
    send_rows = send_ref.shape[1]
    for m in range(members):
        part = mm(p_ref[...], merged_ref[m])
        part_ref[m] = part
        send_ref[m] = part[0:send_rows].astype(BF)


def chip_orders(chips):
    bits = range(chips.bit_length() - 1)
    orders = []
    for order in (list(bits), list(bits)[::-1]):
        orders.append(sorted(range(chips), key=lambda s: [-(s >> bit & 1) for bit in order]))
    return orders


def destination_rows(member, band, n_member, n_band, rw):
    chip, core = band // 2, band % 2
    for rel_core in (1, 0):
        for rel_chip in range(n_band // 2):
            to_band = (chip ^ rel_chip) * 2 + (core ^ rel_core)
            for rel_member in range(n_member):
                yield pl.multiple_of(((member ^ rel_member) * n_band + to_band) * rw, rw)


def reorder(src_ref, n_member, n_band):
    rw = src_ref.shape[0] // (n_member * n_band)
    member, band = lax.axis_index("member"), lax.axis_index("band")
    starts = destination_rows(member, band, n_member, n_band, rw)
    return jnp.concatenate([src_ref[pl.ds(start, rw), :] for start in starts], axis=0)


def store_parts(rows, chips, half, at, out_refs):
    block = rows.shape[0] // (2 * chips)
    for core, ref in enumerate(out_refs):
        for place, chip in enumerate(chip_orders(chips)[half]):
            start = (core * chips + chip) * block
            ref[place * block : (place + 1) * block, at : at + rows.shape[1]] = rows[start : start + block]


def transpose_body(n_member, n_band, hidden_ref, below_ref, above_ref, out_ref, turned):
    members, nodes, _ = hidden_ref.shape
    rim = below_ref.shape[0] // members
    parts = []
    for m in range(members):
        parts.append(hidden_ref[m])
        parts.append(below_ref[m * rim : (m + 1) * rim, :])
        parts.append(above_ref[m * rim : (m + 1) * rim, :])
    turned[...] = jnp.concatenate(parts, axis=0).astype(F32).T
    out_ref[...] = reorder(turned, n_member, n_band).astype(BF)


def select_heads(block):
    half = block.shape[0] // 2
    low = lax.broadcasted_iota(jnp.int32, (half, block.shape[1]), 1) < HEAD_DIM
    return jnp.where(low, block[:half], block[half:])


def soft_slope(v):
    return v * lax.rsqrt(v * v + SOFTENING * SOFTENING)


def kv_products(chips, ext_ref, ng_ref, out_refs):
    step = ng_ref.shape[1] // 2
    for half in range(2):
        product = mm(ext_ref[...], ng_ref[:, half * step : (half + 1) * step]).astype(BF)
        store_parts(product, chips, half, half * (out_refs[0].shape[1] // 2), out_refs)


def value_body(n_member, n_band, *refs):
    recv_refs = refs[: n_member - 1]
    part_ref, base_ref, truth_ref, weight_ref, pt_ref, gate_ref, ext_ref = refs[n_member - 1 : n_member + 6]
    grad_ref, dm_ref, ng_ref, *out_refs = refs[n_member + 6 :]
    members, width, _ = dm_ref.shape
    ext = ng_ref.shape[0] // members
    channels = truth_ref.shape[0]
    total = members * n_member
    spread = (1.0 - (1.0 - ALPHA) / total) / (total * (total - 1))

    grad_ref[...] = jnp.zeros_like(grad_ref)
    own = [part_ref[m, 0:channels, :] for m in range(members)]
    for m in range(members):
        slopes = jnp.zeros_like(own[m])
        for k in range(members):
            if k != m:
                slopes = slopes + soft_slope(own[m] - own[k])
        for ref in recv_refs:
            for k in range(members):
                slopes = slopes + soft_slope(own[m] - ref[k, 0:channels, :].astype(F32))
        gap = soft_slope(own[m] + base_ref[0:channels, :] - truth_ref[...])
        grad_ref[m, 0:channels, :] = (weight_ref[...] * (gap / total - spread * slopes)).astype(BF)
    for m in range(members):
        dm_ref[m] = mm(pt_ref[...], grad_ref[m]).astype(BF)
    for pair in range(width // LANES):
        cols = slice(pair * LANES, (pair + 1) * LANES)
        for m in range(members):
            result = mm(gate_ref[pair, m], dm_ref[m, cols, :], NT)
            ng_ref[m * ext : (m + 1) * ext, cols] = select_heads(result).astype(BF)
    kv_products(n_band // 2, ext_ref, ng_ref, out_refs)


def small_body(n_member, n_band, grad_ref, merged_ref, q_ref, wo_ref, out_ref, turned):
    members = grad_ref.shape[0]
    m_t = sum(mm(grad_ref[m], merged_ref[m], NT) for m in range(members))
    head_t = sum(mm(grad_ref[m], q_ref[...]) for m in range(members)) + mm(m_t.astype(BF), wo_ref[...])
    turned[...] = jnp.concatenate([m_t, head_t], axis=0).T
    out_ref[...] = reorder(turned, n_member, n_band).astype(BF)


def key_body(chips, dm_ref, kv_ref, slope_ref, q_ref, ext_ref, small_ref, ng_ref, *out_refs):
    members, ext, width2 = kv_ref.shape
    width = width2 // 2
    for pair in range(width // LANES):
        cols = slice(pair * LANES, (pair + 1) * LANES)
        vcols = slice(width + pair * LANES, width + (pair + 1) * LANES)
        for m in range(members):
            dgate = mm(split_heads(kv_ref[m, :, vcols]), dm_ref[m, cols, :])
            dscore = (dgate * slope_ref[pair, m].astype(F32)).astype(BF)
            ng_ref[m * ext : (m + 1) * ext, cols] = select_heads(mm(dscore, q_ref[:, cols])).astype(BF)
    kv_products(chips, ext_ref, ng_ref, out_refs)
    half_width = out_refs[0].shape[1] // 2
    for half in range(2):
        part = small_ref[:, half * LANES : (half + 1) * LANES]
        store_parts(part, chips, half, (half + 1) * half_width - LANES, out_refs)


def extended_grad_body(members, nodes, rim, ngk_ref, ngv_ref, kvw_ref, own_ref, down_ref, up_ref):
    ext = nodes + 2 * rim
    width = kvw_ref.shape[0]
    for m in range(members):
        at = slice(m * ext, (m + 1) * ext)
        rows = mm(ngk_ref[at, :], kvw_ref[:, 0:width], NT) + mm(ngv_ref[at, :], kvw_ref[:, width:], NT)
        own_ref[m] = rows[0:nodes]
        down_ref[m * rim : (m + 1) * rim, :] = rows[nodes : nodes + rim].astype(BF)
        up_ref[m * rim : (m + 1) * rim, :] = rows[nodes + rim :].astype(BF)


def hidden_body(own_ref, from_below_ref, from_above_ref, halo_ref, out_ref):
    members, nodes, _ = own_ref.shape
    rim = halo_ref.shape[1]
    low = one_hot_rows(halo_ref[0:1, :], nodes)
    high = one_hot_rows(halo_ref[1:2, :], nodes)
    for m in range(members):
        rows = slice(m * rim, (m + 1) * rim)
        out_ref[m] = own_ref[m] + mm(low, from_below_ref[rows, :]) + mm(high, from_above_ref[rows, :])


def finish_body(devices, n_member, *refs):
    value_refs, key_refs = refs[:n_member], refs[n_member : 2 * n_member]
    hp_ref, kv_ref, out_ref, head_ref = refs[2 * n_member :]
    width = kv_ref.shape[1] // 2
    channels = hp_ref.shape[0]

    def summed(parts):
        total = parts[0][...].astype(F32)
        for ref in parts[1:]:
            total = total + ref[...].astype(F32)
        return total * (1.0 / devices)

    kv_ref[:, width:] = summed(value_refs)
    total = summed(key_refs)
    half = width // 2
    kv_ref[:, 0:half] = total[:, 0:half]
    kv_ref[:, half:width] = total[:, half + LANES : width + LANES]
    m_rows = total[:, half : half + channels]
    high = m_rows.astype(BF)
    low = (m_rows - high.astype(F32)).astype(BF)
    out_ref[...] = mm(high, hp_ref[...]) + mm(low, hp_ref[...])
    head_ref[...] = total[:, width + LANES : width + LANES + channels]


def add_up(*parts):
    return functools.reduce(lambda a, b: a + b, [p.astype(F32) for p in parts])


def swap_cores(send, keep, n_band):
    arrived = lax.ppermute(send, "band", [(i, i ^ 1) for i in range(n_band)])
    half = send.shape[1] // 2
    return [[t[:, i * half : (i + 1) * half] for t in (keep, arrived)] for i in range(2)]


def outgoing_sums(halves):
    return [add_up(*[t[: t.shape[0] // 2] for t in terms]).astype(BF) for terms in halves]


def reduce_plane(halves, outgoing, n_band):
    bits = list(range((n_band // 2).bit_length() - 1))
    orders = (bits, bits[::-1])
    for step in range(len(bits)):
        if step:
            outgoing = outgoing_sums(halves)
        arrived = [
            lax.ppermute(out, "band", [(i, i ^ (2 << order[step])) for i in range(n_band)])
            for out, order in zip(outgoing, orders)
        ]
        halves = [[t[t.shape[0] // 2 :] for t in terms] + [new] for terms, new in zip(halves, arrived)]
    return halves


def plane_sum(halves):
    return jnp.concatenate([add_up(*terms) for terms in halves], axis=1).astype(BF)


def swap_members(plane, n_member):
    rw = plane.shape[0] // n_member
    return [plane[0:rw]] + [
        lax.ppermute(plane[s * rw : (s + 1) * rw], "member", [(i, i ^ s) for i in range(n_member)])
        for s in range(1, n_member)
    ]


def shards(
    n_member, n_band,
    hidden, queries, kv_weight, out_weight, head_projection, initial_state, truth,
    latitude_weight, channel_loss_weight, sources, halo_rows,
):
    members, nodes, width = hidden.shape
    points = queries.shape[0]
    channels = head_projection.shape[1]
    rim = halo_rows.shape[1]
    ext = nodes + 2 * rim
    pairs = width // LANES
    devices = n_member * n_band
    rw = width // devices
    chips = n_band // 2
    send_rows = -(-channels // 16) * 16
    to_above = [(i, i + 1) for i in range(n_band - 1)]
    to_below = [(i + 1, i) for i in range(n_band - 1)]

    own_hidden, halo, down, up = call(
        pick_body,
        [sds(hidden.shape, BF), sds(halo_rows.shape, jnp.int32)] + [sds((members * rim, width), BF)] * 2,
        (hidden, halo_rows),
        [pltpu.SemaphoreType.DMA((2,))],
        hbm=(0, 1),
    )
    below = lax.ppermute(up, "band", to_above)
    above = lax.ppermute(down, "band", to_below)

    args = (
        own_hidden, out_weight, head_projection.T, queries, kv_weight, initial_state,
        channel_loss_weight[None, :], latitude_weight[None, :], sources, truth,
    )
    own_kv, pt, p, base, weight, wo, hp, q, kvw, src, true = call(
        prepare_body,
        [
            sds((members * nodes, 2 * width), BF),
            sds((width, LANES), BF),
            sds((LANES, width), BF),
            sds((LANES, points), F32),
            sds((channels, points), F32),
        ]
        + [sds(args[i].shape, args[i].dtype) for i in (1, 2, 3, 4, 8, 9)],
        args,
        [
            pltpu.VMEM((channels, points), F32),
            pltpu.VMEM((1, channels), F32),
            pltpu.VMEM((1, points), F32),
            pltpu.VMEM((8, LANES), F32),
            pltpu.VMEM((LANES, width), F32),
            pltpu.SemaphoreType.DMA((8 + KV_COPIES,)),
        ],
        hbm=tuple(range(1, 10)),
    )

    kv, gates, slopes, merged, part, sent = call(
        forward_body,
        [
            sds((members, ext, 2 * width), BF),
            sds((pairs, members, 2 * ext, points), BF),
            sds((pairs, members, 2 * ext, points), BF),
            sds((members, width, points), BF),
            sds((members, LANES, points), F32),
            sds((members, send_rows, points), BF),
        ],
        (below, above, own_kv, kvw, q, src, p),
    )

    received = [
        lax.ppermute(sent, "member", [(i, i ^ s) for i in range(n_member)]) for s in range(1, n_member)
    ]

    ext_t = call(
        functools.partial(transpose_body, n_member, n_band),
        sds((width, members * ext), BF),
        (own_hidden, below, above),
        [pltpu.VMEM((width, members * ext), F32)],
    )

    extra = 2 * LANES
    grad, dm, ng_value, send, keep = call(
        functools.partial(value_body, n_member, n_band),
        [sds((members, LANES, points), BF), sds((members, width, points), BF), sds((members * ext, width), BF)]
        + [sds((width // 2, width), BF)] * 2,
        (*received, part, base, true, weight, pt, gates, ext_t),
    )
    small = call(
        functools.partial(small_body, n_member, n_band),
        sds((width, extra), BF),
        (grad, merged, q, wo),
        [pltpu.VMEM((width, extra), F32)],
    )
    value_halves = swap_cores(send, keep, n_band)
    outgoing = outgoing_sums(value_halves)

    outgoing, dm, small = lax.optimization_barrier((outgoing, dm, small))
    value_halves = reduce_plane(value_halves, outgoing, n_band)
    ng_key, send, keep = call(
        functools.partial(key_body, chips),
        [sds((members * ext, width), BF)] + [sds((width // 2, width + extra), BF)] * 2,
        (dm, kv, slopes, q, ext_t, small),
    )
    key_halves = swap_cores(send, keep, n_band)
    outgoing = outgoing_sums(key_halves)

    outgoing, ng_key = lax.optimization_barrier((outgoing, ng_key))
    key_halves = reduce_plane(key_halves, outgoing, n_band)
    own_grad, back_down, back_up = call(
        functools.partial(extended_grad_body, members, nodes, rim),
        [sds((members, nodes, width), F32)] + [sds((members * rim, width), BF)] * 2,
        (ng_key, ng_value, kvw),
    )
    from_above = lax.ppermute(back_down, "band", to_below)
    from_below = lax.ppermute(back_up, "band", to_above)
    hidden_grad = call(
        hidden_body,
        sds((members, nodes, width), F32),
        (own_grad, from_below, from_above, halo),
    )

    last_v = swap_members(plane_sum(value_halves), n_member)
    hidden_grad, key_halves = lax.optimization_barrier((hidden_grad, key_halves))
    last_k = swap_members(plane_sum(key_halves), n_member)

    kv_grad, out_grad, head_grad = call(
        functools.partial(finish_body, devices, n_member),
        [sds((rw, 2 * width), F32), sds((rw, width), F32), sds((rw, channels), F32)],
        (*last_v, *last_k, hp),
    )
    return hidden_grad, kv_grad, out_grad, head_grad


def solution(mesh):
    placed = (
        P("member", "band", None),
        P("band", None),
        P(),
        P(),
        P(),
        P(None, "band"),
        P(None, "band"),
        P("band"),
        P(),
        P(None, "band"),
        P("band", None),
    )
    return jax.shard_map(
        functools.partial(shards, mesh.shape["member"], mesh.shape["band"]),
        mesh=mesh,
        in_specs=placed,
        out_specs=(
            P("member", "band", None),
            P(("member", "band"), None),
            P(("member", "band"), None),
            P(("member", "band"), None),
        ),
        check_vma=False,
    )
```

```python
import functools

import jax
import jax.numpy as jnp
from jax import lax
from jax.experimental import pallas as pl
from jax.experimental.pallas import tpu as pltpu
from jax.sharding import PartitionSpec as P

HEAD_DIM = 64
LANES = 128
GROUPS = 3
ALPHA = 0.95
SOFTENING = 0.5
BF = jnp.bfloat16
F32 = jnp.float32
NN = (((1,), (0,)), ((), ()))
NT = (((1,), (1,)), ((), ()))
TN = (((0,), (0,)), ((), ()))


def mm(a, b, dims=NN):
    return lax.dot_general(a, b, dims, preferred_element_type=F32)


def call(body, out_shape, args, scratch=(), hbm=(), limit=24, flops=1):
    args = [pltpu.with_memory_space_constraint(x, pltpu.HBM) if i in hbm else x for i, x in enumerate(args)]
    return pl.pallas_call(
        body,
        out_shape=out_shape,
        in_specs=[
            pl.BlockSpec(memory_space=pltpu.HBM if i in hbm else pltpu.VMEM) for i in range(len(args))
        ],
        out_specs=jax.tree.map(lambda _: pl.BlockSpec(memory_space=pltpu.VMEM), out_shape),
        scratch_shapes=list(scratch),
        compiler_params=pltpu.CompilerParams(vmem_limit_bytes=limit * 1024 * 1024),
        cost_estimate=pl.CostEstimate(flops=flops, bytes_accessed=1, transcendentals=0),
    )(*args)


def sds(shape, dtype):
    return jax.ShapeDtypeStruct(shape, dtype)


def one_hot_rows(rows, node_count):
    nodes = lax.broadcasted_iota(jnp.int32, (node_count, rows.shape[1]), 0).astype(rows.dtype)
    return (nodes == rows).astype(F32).astype(BF)


def start_copies(pairs, sems):
    copies = [pltpu.make_async_copy(src, dst, sems.at[i]) for i, (src, dst) in enumerate(pairs)]
    for copy in copies:
        copy.start()
    return copies


def pick_body(hidden_hbm, halo_hbm, hidden_ref, halo_ref, down_ref, up_ref, sems):
    for copy in start_copies([(hidden_hbm, hidden_ref), (halo_hbm, halo_ref)], sems):
        copy.wait()
    members, nodes, _ = hidden_ref.shape
    rim = halo_ref.shape[1]
    for row, out_ref in ((0, down_ref), (1, up_ref)):
        hot = one_hot_rows(halo_ref[row : row + 1, :], nodes)
        for m in range(members):
            out_ref[m * rim : (m + 1) * rim, :] = mm(hot, hidden_ref[m], TN).astype(BF)


def prepare_body(
    hidden_ref, wo_ref, hp_ref, q_ref, kvw_ref, init_ref, chw_ref, lat_ref,
    kv_ref, pt_ref, p_ref, base_ref, weight_ref, chw_pad, hp_pad,
):
    channels = hp_ref.shape[0]
    hp_pad[...] = jnp.zeros_like(hp_pad)
    hp_pad[0:channels, :] = hp_ref[...].astype(F32)
    hp_t = hp_pad[...].astype(BF)
    chw_pad[:, 0:channels] = jnp.broadcast_to(chw_ref[...], (8, channels))
    weight_ref[...] = chw_pad[...].T[0:channels, 0:1] * lat_ref[...]
    base_ref[...] = mm(hp_t, q_ref[...], NT)
    base_ref[0:channels, :] = base_ref[0:channels, :] + init_ref[...]
    p = mm(hp_t, wo_ref[...], NT)
    p_ref[...] = p.astype(BF)
    pt_ref[...] = p.T.astype(BF)
    hidden = jnp.concatenate([hidden_ref[m] for m in range(hidden_ref.shape[0])], axis=0)
    kv_ref[...] = mm(hidden, kvw_ref[...]).astype(BF)


def split_heads(block):
    low = lax.broadcasted_iota(jnp.int32, block.shape, 1) < HEAD_DIM
    zero = jnp.zeros_like(block)
    return jnp.concatenate([jnp.where(low, block, zero), jnp.where(low, zero, block)], axis=0)


def forward_body(
    send_rows,
    below_ref, above_ref, own_ref, kvw_ref, q_ref, src_ref, p_ref,
    kv_ref, gate_ref, slope_ref, merged_ref, part_ref, send_ref,
):
    members, ext, width2 = kv_ref.shape
    width = width2 // 2
    points = q_ref.shape[0]
    nodes = own_ref.shape[0] // members
    rim = below_ref.shape[0] // members
    halo = mm(jnp.concatenate([below_ref[...], above_ref[...]], axis=0), kvw_ref[...]).astype(BF)
    for m in range(members):
        kv_ref[m, 0:nodes, :] = own_ref[m * nodes : (m + 1) * nodes, :]
        kv_ref[m, nodes : nodes + rim, :] = halo[m * rim : (m + 1) * rim]
        kv_ref[m, nodes + rim : ext, :] = halo[(members + m) * rim : (members + m + 1) * rim]
    rows = lax.broadcasted_iota(jnp.int32, (ext, points), 0)
    mask = rows == src_ref[0:1, :]
    for e in range(1, src_ref.shape[0]):
        mask = mask | (rows == src_ref[e : e + 1, :])
    mask = mask.astype(F32)
    mask = jnp.concatenate([mask, mask], axis=0)
    scale = HEAD_DIM ** (-0.5)
    for pair in range(width // LANES):
        cols = slice(pair * LANES, (pair + 1) * LANES)
        vcols = slice(width + pair * LANES, width + (pair + 1) * LANES)
        q = q_ref[:, cols]
        for m in range(members):
            th = jnp.tanh(mm(split_heads(kv_ref[m, :, cols]), q, NT) * (0.5 * scale))
            gate = ((0.5 * th + 0.5) * mask).astype(BF)
            gate_ref[pair, m] = gate
            slope_ref[pair, m] = ((0.25 * scale) * mask * (1.0 - th * th)).astype(BF)
            merged_ref[m, cols, :] = mm(split_heads(kv_ref[m, :, vcols]), gate, TN).astype(BF)
    sent = []
    for m in range(members):
        part = mm(p_ref[...], merged_ref[m])
        part_ref[m] = part
        sent.append(part[0:send_rows])
    filler = send_ref.shape[0] - members * send_rows
    if filler:
        sent.append(jnp.zeros((filler, points), F32))
    send_ref[...] = jnp.concatenate(sent, axis=0).astype(BF)


def halving_orders(n_member, n_band):
    chips = [("band", bit) for bit in range(1, n_band.bit_length() - 1)]
    member = [("member", bit) for bit in range(n_member.bit_length() - 1)]
    turn = chips + member[:1]
    return [turn[i:] + turn[:i] for i in range(GROUPS)], member[1:]


def unit_order(order, n_member, n_band):
    def key(unit):
        return [-((2 * unit[0] if axis == "band" else unit[1]) >> bit & 1) for axis, bit in order]

    return sorted([(c, m) for c in range(n_band // 2) for m in range(n_member)], key=key)


def destination_rows(member, band, n_member, n_band, rw):
    chip, core = band // 2, band % 2
    for rel_core in (1, 0):
        for rel_chip in range(n_band // 2):
            to_band = (chip ^ rel_chip) * 2 + (core ^ rel_core)
            for rel_member in range(n_member):
                yield pl.multiple_of(((member ^ rel_member) * n_band + to_band) * rw, rw)


def reorder(src_ref, n_member, n_band):
    rw = src_ref.shape[0] // (n_member * n_band)
    member, band = lax.axis_index("member"), lax.axis_index("band")
    starts = destination_rows(member, band, n_member, n_band, rw)
    return jnp.concatenate([src_ref[pl.ds(start, rw), :] for start in starts], axis=0)


def store_group(rows, group, n_member, n_band, at, out_refs):
    orders, rest = halving_orders(n_member, n_band)
    units = unit_order(orders[group] + rest, n_member, n_band)
    rw = rows.shape[0] // (n_member * n_band)
    for core, ref in enumerate(out_refs):
        starts = [((core * (n_band // 2) + chip) * n_member + member) * rw for chip, member in units]
        ordered = jnp.concatenate([rows[i : i + rw] for i in starts], axis=0)
        ref[:, at : at + rows.shape[1]] = ordered.astype(BF)


def transpose_body(n_member, n_band, hidden_ref, below_ref, above_ref, out_ref, turned):
    members, nodes, _ = hidden_ref.shape
    rim = below_ref.shape[0] // members
    parts = []
    for m in range(members):
        parts.append(hidden_ref[m])
        parts.append(below_ref[m * rim : (m + 1) * rim, :])
        parts.append(above_ref[m * rim : (m + 1) * rim, :])
    turned[...] = jnp.concatenate(parts, axis=0).astype(F32).T
    out_ref[...] = reorder(turned, n_member, n_band).astype(BF)


def select_heads(block):
    half = block.shape[0] // 2
    low = lax.broadcasted_iota(jnp.int32, (half, block.shape[1]), 1) < HEAD_DIM
    return jnp.where(low, block[:half], block[half:])


def soft_slope(v):
    return v * lax.rsqrt(v * v + SOFTENING * SOFTENING)


def value_body(n_member, n_band, *refs):
    recv_refs = refs[: n_member - 1]
    part_ref, base_ref, truth_ref, weight_ref, pt_ref, gate_ref, ext_ref = refs[n_member - 1 : n_member + 6]
    grad_ref, dm_ref, ng_ref, *out_refs = refs[n_member + 6 :]
    group_width = out_refs[0].shape[1]
    members, width, _ = dm_ref.shape
    ext = ng_ref.shape[0] // members
    channels = truth_ref.shape[0]
    total = members * n_member
    spread = (1.0 - (1.0 - ALPHA) / total) / (total * (total - 1))

    grad_ref[...] = jnp.zeros_like(grad_ref)
    own = [part_ref[m, 0:channels, :] for m in range(members)]
    sent_rows = -(-channels // 8) * 8
    others = []
    for ref in recv_refs:
        rows = ref[...].astype(F32)
        others += [rows[k * sent_rows : k * sent_rows + channels] for k in range(members)]
    for m in range(members):
        slopes = jnp.zeros_like(own[m])
        for k in range(members):
            if k != m:
                slopes = slopes + soft_slope(own[m] - own[k])
        for other in others:
            slopes = slopes + soft_slope(own[m] - other)
        gap = soft_slope(own[m] + base_ref[0:channels, :] - truth_ref[...])
        grad_ref[m, 0:channels, :] = (weight_ref[...] * (gap / total - spread * slopes)).astype(BF)
    for m in range(members):
        dm_ref[m] = mm(pt_ref[...], grad_ref[m]).astype(BF)
    for pair in range(width // LANES):
        cols = slice(pair * LANES, (pair + 1) * LANES)
        for m in range(members):
            result = mm(gate_ref[pair, m], dm_ref[m, cols, :], NT)
            ng_ref[m * ext : (m + 1) * ext, cols] = select_heads(result).astype(BF)
    store_group(mm(ext_ref[...], ng_ref[:, 0:group_width]), 0, n_member, n_band, 0, out_refs)


def key_body(
    n_member, n_band, grad_ref, dm_ref, kv_ref, slope_ref, q_ref, merged_ref, wo_ref, ext_ref, ngv_ref,
    ng_ref, *refs
):
    out_refs, turned = refs[:-1], refs[-1]
    members, ext, width2 = kv_ref.shape
    width = width2 // 2
    group_width = out_refs[0].shape[1]
    for pair in range(width // LANES):
        cols = slice(pair * LANES, (pair + 1) * LANES)
        vcols = slice(width + pair * LANES, width + (pair + 1) * LANES)
        for m in range(members):
            dgate = mm(split_heads(kv_ref[m, :, vcols]), dm_ref[m, cols, :])
            dscore = (dgate * slope_ref[pair, m].astype(F32)).astype(BF)
            ng_ref[m * ext : (m + 1) * ext, cols] = select_heads(mm(dscore, q_ref[:, cols])).astype(BF)
    m_t = sum(mm(grad_ref[m], merged_ref[m], NT) for m in range(members))
    head_t = sum(mm(grad_ref[m], q_ref[...]) for m in range(members)) + mm(m_t.astype(BF), wo_ref[...])
    turned[...] = jnp.concatenate([m_t, head_t], axis=0).T
    pieces = [(ngv_ref, group_width, width), (ng_ref, 0, width), (None, 0, 2 * LANES)]
    at = group_width
    for ref, first, last in pieces:
        while first < last:
            group, offset = at // group_width, at % group_width
            take = min(last - first, group_width - offset)
            if ref is None:
                rows = reorder(turned, n_member, n_band)
            else:
                rows = mm(ext_ref[...], ref[:, first : first + take])
            outs = out_refs[2 * (group - 1) : 2 * group]
            store_group(rows, group, n_member, n_band, offset, outs)
            first, at = first + take, at + take


def extended_grad_body(members, nodes, rim, ngk_ref, ngv_ref, kvw_ref, own_ref, down_ref, up_ref):
    ext = nodes + 2 * rim
    width = kvw_ref.shape[0]
    rows = mm(ngk_ref[...], kvw_ref[:, 0:width], NT) + mm(ngv_ref[...], kvw_ref[:, width:], NT)
    for m in range(members):
        at = m * ext
        own_ref[m] = rows[at : at + nodes]
        down_ref[m * rim : (m + 1) * rim, :] = rows[at + nodes : at + nodes + rim].astype(BF)
        up_ref[m * rim : (m + 1) * rim, :] = rows[at + nodes + rim : at + ext].astype(BF)


def hidden_body(own_ref, from_below_ref, from_above_ref, halo_ref, out_ref):
    members, nodes, _ = own_ref.shape
    rim = halo_ref.shape[1]
    low = one_hot_rows(halo_ref[0:1, :], nodes)
    high = one_hot_rows(halo_ref[1:2, :], nodes)
    for m in range(members):
        rows = slice(m * rim, (m + 1) * rim)
        out_ref[m] = own_ref[m] + mm(low, from_below_ref[rows, :]) + mm(high, from_above_ref[rows, :])


def finish_body(devices, own_ref, arrived_ref, hp_ref, kv_ref, out_ref, head_ref):
    width = kv_ref.shape[1] // 2
    channels = hp_ref.shape[0]
    total = (own_ref[...] + arrived_ref[...].astype(F32)) * (1.0 / devices)
    kv_ref[:, width:] = total[:, 0:width]
    kv_ref[:, 0:width] = total[:, width : 2 * width]
    m_rows = total[:, 2 * width : 2 * width + channels]
    high = m_rows.astype(BF)
    low = (m_rows - high.astype(F32)).astype(BF)
    out_ref[...] = mm(high, hp_ref[...]) + mm(low, hp_ref[...])
    head_ref[...] = total[:, 2 * width + LANES : 2 * width + LANES + channels]


def add_up(*parts):
    return functools.reduce(lambda a, b: a + b, [p.astype(F32) for p in parts])


def swap(rows, axis, bit, count):
    return lax.ppermute(rows, axis, [(i, i ^ (1 << bit)) for i in range(count)])


def upper(terms):
    return [t[: t.shape[0] // 2] for t in terms]


def lower(terms):
    return [t[t.shape[0] // 2 :] for t in terms]


def shards(
    n_member, n_band,
    hidden, queries, kv_weight, out_weight, head_projection, initial_state, truth,
    latitude_weight, channel_loss_weight, sources, halo_rows,
):
    members, nodes, width = hidden.shape
    points = queries.shape[0]
    channels = head_projection.shape[1]
    rim = halo_rows.shape[1]
    ext = nodes + 2 * rim
    pairs = width // LANES
    devices = n_member * n_band
    rw = width // devices
    chips = n_band // 2
    send_rows = -(-channels // 8) * 8
    to_above = [(i, i + 1) for i in range(n_band - 1)]
    to_below = [(i + 1, i) for i in range(n_band - 1)]

    own_hidden, halo, down, up = call(
        pick_body,
        [sds(hidden.shape, BF), sds(halo_rows.shape, jnp.int32)] + [sds((members * rim, width), BF)] * 2,
        (hidden, halo_rows),
        [pltpu.SemaphoreType.DMA((2,))],
        hbm=(0, 1),
        flops=10**10,
    )
    below = lax.ppermute(up, "band", to_above)
    above = lax.ppermute(down, "band", to_below)

    hp = head_projection.T
    own_kv, pt, p, base, weight = call(
        prepare_body,
        [
            sds((members * nodes, 2 * width), BF),
            sds((width, LANES), BF),
            sds((LANES, width), BF),
            sds((LANES, points), F32),
            sds((channels, points), F32),
        ],
        (
            own_hidden, out_weight, hp, queries, kv_weight, initial_state,
            channel_loss_weight[None, :], latitude_weight[None, :],
        ),
        [pltpu.VMEM((8, LANES), F32), pltpu.VMEM((LANES, width), F32)],
    )

    kv, gates, slopes, merged, part, sent = call(
        functools.partial(forward_body, send_rows),
        [
            sds((members, ext, 2 * width), BF),
            sds((pairs, members, 2 * ext, points), BF),
            sds((pairs, members, 2 * ext, points), BF),
            sds((members, width, points), BF),
            sds((members, LANES, points), F32),
            sds((-(-members * send_rows // 16) * 16, points), BF),
        ],
        (below, above, own_kv, kv_weight, queries, sources, p),
    )

    received = [
        lax.ppermute(sent, "member", [(i, i ^ s) for i in range(n_member)]) for s in range(1, n_member)
    ]

    ext_t = call(
        functools.partial(transpose_body, n_member, n_band),
        sds((width, members * ext), BF),
        (own_hidden, below, above),
        [pltpu.VMEM((width, members * ext), F32)],
    )

    extra = 2 * LANES
    group_width = (2 * width + extra) // GROUPS
    grad, dm, ng_value, send, keep = call(
        functools.partial(value_body, n_member, n_band),
        [sds((members, LANES, points), BF), sds((members, width, points), BF), sds((members * ext, width), BF)]
        + [sds((width // 2, group_width), BF)] * 2,
        (*received, part, base, truth, weight, pt, gates, ext_t),
    )
    groups = [[keep, swap(send, "band", 0, n_band)]]
    ng_key, *outs = call(
        functools.partial(key_body, n_member, n_band),
        [sds((members * ext, width), BF)] + [sds((width // 2, group_width), BF)] * (2 * (GROUPS - 1)),
        (grad, dm, kv, slopes, queries, merged, out_weight, ext_t, ng_value),
        [pltpu.VMEM((width, extra), F32)],
    )
    for i in range(GROUPS - 1):
        groups.append([outs[2 * i + 1], swap(outs[2 * i], "band", 0, n_band)])

    count = {"member": n_member, "band": n_band}
    turns, rest = halving_orders(n_member, n_band)
    for step in range(len(turns[0])):
        outgoing = [add_up(*upper(terms)).astype(BF) for terms in groups]
        if step == 0:
            outgoing[0], groups[1:] = lax.optimization_barrier((outgoing[0], groups[1:]))
            outgoing[1:] = [add_up(*upper(terms)).astype(BF) for terms in groups[1:]]
            outgoing, ng_key = lax.optimization_barrier((outgoing, ng_key))
            own_grad, back_down, back_up = call(
                functools.partial(extended_grad_body, members, nodes, rim),
                [sds((members, nodes, width), F32)] + [sds((members * rim, width), BF)] * 2,
                (ng_key, ng_value, kv_weight),
            )
            from_above = lax.ppermute(back_down, "band", to_below)
            from_below = lax.ppermute(back_up, "band", to_above)
        arrived = [swap(out, *turn[step], count[turn[step][0]]) for out, turn in zip(outgoing, turns)]
        if step == 0:
            arrived, from_above, from_below = lax.optimization_barrier((arrived, from_above, from_below))
        groups = [lower(terms) + [new] for terms, new in zip(groups, arrived)]
    hidden_grad = call(
        hidden_body,
        sds((members, nodes, width), F32),
        (own_grad, from_below, from_above, halo),
    )
    terms = [jnp.concatenate([add_up(*group) for group in groups], axis=1)]
    for axis, bit in rest:
        arrived = swap(add_up(*upper(terms)).astype(BF), axis, bit, count[axis])
        terms = lower(terms) + [arrived]

    kv_grad, out_grad, head_grad = call(
        functools.partial(finish_body, devices),
        [sds((rw, 2 * width), F32), sds((rw, width), F32), sds((rw, channels), F32)],
        (add_up(*terms[:-1]), terms[-1], hp),
    )
    return hidden_grad, kv_grad, out_grad, head_grad


def solution(mesh):
    placed = (
        P("member", "band", None),
        P("band", None),
        P(),
        P(),
        P(),
        P(None, "band"),
        P(None, "band"),
        P("band"),
        P(),
        P(None, "band"),
        P("band", None),
    )
    return jax.shard_map(
        functools.partial(shards, mesh.shape["member"], mesh.shape["band"]),
        mesh=mesh,
        in_specs=placed,
        out_specs=(
            P("member", "band", None),
            P(("member", "band"), None),
            P(("member", "band"), None),
            P(("member", "band"), None),
        ),
        check_vma=False,
    )
```

```python
import functools

import jax
import jax.numpy as jnp
from jax import lax
from jax.experimental import pallas as pl
from jax.experimental.pallas import tpu as pltpu
from jax.sharding import PartitionSpec as P

HEAD_DIM = 64
LANES = 128
GROUPS = 3
ALPHA = 0.95
SOFTENING = 0.5
BF = jnp.bfloat16
F32 = jnp.float32
NN = (((1,), (0,)), ((), ()))
NT = (((1,), (1,)), ((), ()))
TN = (((0,), (0,)), ((), ()))


def mm(a, b, dims=NN):
    return lax.dot_general(a, b, dims, preferred_element_type=F32)


def call(body, out_shape, args, scratch=(), hbm=(), limit=24, flops=1):
    args = [pltpu.with_memory_space_constraint(x, pltpu.HBM) if i in hbm else x for i, x in enumerate(args)]
    return pl.pallas_call(
        body,
        out_shape=out_shape,
        in_specs=[
            pl.BlockSpec(memory_space=pltpu.HBM if i in hbm else pltpu.VMEM) for i in range(len(args))
        ],
        out_specs=jax.tree.map(lambda _: pl.BlockSpec(memory_space=pltpu.VMEM), out_shape),
        scratch_shapes=list(scratch),
        compiler_params=pltpu.CompilerParams(vmem_limit_bytes=limit * 1024 * 1024),
        cost_estimate=pl.CostEstimate(flops=flops, bytes_accessed=1, transcendentals=0),
    )(*args)


def sds(shape, dtype):
    return jax.ShapeDtypeStruct(shape, dtype)


def one_hot_rows(rows, node_count):
    nodes = lax.broadcasted_iota(jnp.int32, (node_count, rows.shape[1]), 0).astype(rows.dtype)
    return (nodes == rows).astype(F32).astype(BF)


def start_copies(pairs, sems):
    copies = [pltpu.make_async_copy(src, dst, sems.at[i]) for i, (src, dst) in enumerate(pairs)]
    for copy in copies:
        copy.start()
    return copies


def halo_lists(halo_ref):
    even = lax.axis_index("band") % 2 == 0
    down, up = halo_ref[0:1, :], halo_ref[1:2, :]
    return jnp.where(even, up, down), jnp.where(even, down, up)


def pick_body(hidden_hbm, halo_hbm, hidden_ref, halo_ref, mate_ref, other_ref, sems):
    for copy in start_copies([(hidden_hbm, hidden_ref), (halo_hbm, halo_ref)], sems):
        copy.wait()
    members, nodes, _ = hidden_ref.shape
    rim = halo_ref.shape[1]
    for rows, out_ref in zip(halo_lists(halo_ref), (mate_ref, other_ref)):
        hot = one_hot_rows(rows, nodes)
        for m in range(members):
            out_ref[m * rim : (m + 1) * rim, :] = mm(hot, hidden_ref[m], TN).astype(BF)


def prepare_body(
    hidden_ref, wo_ref, hp_ref, q_ref, kvw_ref, init_ref, chw_ref, lat_ref,
    kv_ref, pt_ref, p_ref, base_ref, weight_ref, chw_pad, hp_pad,
):
    channels = hp_ref.shape[0]
    hp_pad[...] = jnp.zeros_like(hp_pad)
    hp_pad[0:channels, :] = hp_ref[...].astype(F32)
    hp_t = hp_pad[...].astype(BF)
    chw_pad[:, 0:channels] = jnp.broadcast_to(chw_ref[...], (8, channels))
    weight_ref[...] = chw_pad[...].T[0:channels, 0:1] * lat_ref[...]
    base_ref[...] = mm(hp_t, q_ref[...], NT)
    base_ref[0:channels, :] = base_ref[0:channels, :] + init_ref[...]
    p = mm(hp_t, wo_ref[...], NT)
    p_ref[...] = p.astype(BF)
    pt_ref[...] = p.T.astype(BF)
    hidden = jnp.concatenate([hidden_ref[m] for m in range(hidden_ref.shape[0])], axis=0)
    kv_ref[...] = mm(hidden, kvw_ref[...]).astype(BF)


def split_heads(block):
    low = lax.broadcasted_iota(jnp.int32, block.shape, 1) < HEAD_DIM
    zero = jnp.zeros_like(block)
    return jnp.concatenate([jnp.where(low, block, zero), jnp.where(low, zero, block)], axis=0)


def forward_body(
    send_rows,
    mate_ref, other_ref, own_ref, kvw_ref, q_ref, src_ref, p_ref,
    kv_ref, gate_ref, slope_ref, merged_ref, part_ref, send_ref,
):
    members, ext, width2 = kv_ref.shape
    width = width2 // 2
    points = q_ref.shape[0]
    nodes = own_ref.shape[0] // members
    rim = mate_ref.shape[0] // members
    halo = mm(jnp.concatenate([mate_ref[...], other_ref[...]], axis=0), kvw_ref[...]).astype(BF)
    for m in range(members):
        kv_ref[m, 0:nodes, :] = own_ref[m * nodes : (m + 1) * nodes, :]
        kv_ref[m, nodes : nodes + rim, :] = halo[m * rim : (m + 1) * rim]
        kv_ref[m, nodes + rim : ext, :] = halo[(members + m) * rim : (members + m + 1) * rim]
    rows = lax.broadcasted_iota(jnp.int32, (ext, points), 0)
    src = src_ref[...]
    even = lax.axis_index("band") % 2 == 0
    shift = jnp.where(src >= nodes + rim, -rim, jnp.where(src >= nodes, rim, 0))
    src = src + jnp.where(even, shift, 0)
    mask = rows == src[0:1, :]
    for e in range(1, src.shape[0]):
        mask = mask | (rows == src[e : e + 1, :])
    mask = mask.astype(F32)
    mask = jnp.concatenate([mask, mask], axis=0)
    scale = HEAD_DIM ** (-0.5)
    for pair in range(width // LANES):
        cols = slice(pair * LANES, (pair + 1) * LANES)
        vcols = slice(width + pair * LANES, width + (pair + 1) * LANES)
        q = q_ref[:, cols]
        for m in range(members):
            th = jnp.tanh(mm(split_heads(kv_ref[m, :, cols]), q, NT) * (0.5 * scale))
            gate = ((0.5 * th + 0.5) * mask).astype(BF)
            gate_ref[pair, m] = gate
            slope_ref[pair, m] = ((0.25 * scale) * mask * (1.0 - th * th)).astype(BF)
            merged_ref[m, cols, :] = mm(split_heads(kv_ref[m, :, vcols]), gate, TN).astype(BF)
    sent = []
    for m in range(members):
        part = mm(p_ref[...], merged_ref[m])
        part_ref[m] = part
        sent.append(part[0:send_rows])
    filler = send_ref.shape[0] - members * send_rows
    if filler:
        sent.append(jnp.zeros((filler, points), F32))
    send_ref[...] = jnp.concatenate(sent, axis=0).astype(BF)


def halving_orders(n_member, n_band):
    chips = [("band", bit) for bit in range(1, n_band.bit_length() - 1)]
    member = [("member", bit) for bit in range(n_member.bit_length() - 1)]
    turn = chips + member[:1]
    return [turn[i:] + turn[:i] for i in range(GROUPS)], member[1:]


def unit_order(order, n_member, n_band):
    def key(unit):
        return [-((2 * unit[0] if axis == "band" else unit[1]) >> bit & 1) for axis, bit in order]

    return sorted([(c, m) for c in range(n_band // 2) for m in range(n_member)], key=key)


def destination_rows(member, band, n_member, n_band, rw):
    chip, core = band // 2, band % 2
    for rel_core in (1, 0):
        for rel_chip in range(n_band // 2):
            to_band = (chip ^ rel_chip) * 2 + (core ^ rel_core)
            for rel_member in range(n_member):
                yield pl.multiple_of(((member ^ rel_member) * n_band + to_band) * rw, rw)


def reorder(src_ref, n_member, n_band):
    rw = src_ref.shape[0] // (n_member * n_band)
    member, band = lax.axis_index("member"), lax.axis_index("band")
    starts = destination_rows(member, band, n_member, n_band, rw)
    return jnp.concatenate([src_ref[pl.ds(start, rw), :] for start in starts], axis=0)


def store_group(rows, group, n_member, n_band, at, out_refs):
    orders, rest = halving_orders(n_member, n_band)
    units = unit_order(orders[group] + rest, n_member, n_band)
    rw = rows.shape[0] // (n_member * n_band)
    for core, ref in enumerate(out_refs):
        starts = [((core * (n_band // 2) + chip) * n_member + member) * rw for chip, member in units]
        ordered = jnp.concatenate([rows[i : i + rw] for i in starts], axis=0)
        ref[:, at : at + rows.shape[1]] = ordered.astype(BF)


def transpose_body(n_member, n_band, hidden_ref, mate_ref, other_ref, out_ref, turned):
    members, nodes, _ = hidden_ref.shape
    rim = mate_ref.shape[0] // members
    parts = []
    for m in range(members):
        parts.append(hidden_ref[m])
        parts.append(mate_ref[m * rim : (m + 1) * rim, :])
        parts.append(other_ref[m * rim : (m + 1) * rim, :])
    turned[...] = jnp.concatenate(parts, axis=0).astype(F32).T
    out_ref[...] = reorder(turned, n_member, n_band).astype(BF)


def select_heads(block):
    half = block.shape[0] // 2
    low = lax.broadcasted_iota(jnp.int32, (half, block.shape[1]), 1) < HEAD_DIM
    return jnp.where(low, block[:half], block[half:])


def soft_slope(v):
    return v * lax.rsqrt(v * v + SOFTENING * SOFTENING)


def value_body(n_member, n_band, *refs):
    recv_refs = refs[: n_member - 1]
    part_ref, base_ref, truth_ref, weight_ref, pt_ref, gate_ref, ext_ref = refs[n_member - 1 : n_member + 6]
    grad_ref, dm_ref, ng_ref, *out_refs = refs[n_member + 6 :]
    group_width = out_refs[0].shape[1]
    members, width, _ = dm_ref.shape
    ext = ng_ref.shape[0] // members
    channels = truth_ref.shape[0]
    total = members * n_member
    spread = (1.0 - (1.0 - ALPHA) / total) / (total * (total - 1))

    grad_ref[...] = jnp.zeros_like(grad_ref)
    own = [part_ref[m, 0:channels, :] for m in range(members)]
    sent_rows = -(-channels // 8) * 8
    others = []
    for ref in recv_refs:
        rows = ref[...].astype(F32)
        others += [rows[k * sent_rows : k * sent_rows + channels] for k in range(members)]
    for m in range(members):
        slopes = jnp.zeros_like(own[m])
        for k in range(members):
            if k != m:
                slopes = slopes + soft_slope(own[m] - own[k])
        for other in others:
            slopes = slopes + soft_slope(own[m] - other)
        gap = soft_slope(own[m] + base_ref[0:channels, :] - truth_ref[...])
        grad_ref[m, 0:channels, :] = (weight_ref[...] * (gap / total - spread * slopes)).astype(BF)
    for m in range(members):
        dm_ref[m] = mm(pt_ref[...], grad_ref[m]).astype(BF)
    for pair in range(width // LANES):
        cols = slice(pair * LANES, (pair + 1) * LANES)
        for m in range(members):
            result = mm(gate_ref[pair, m], dm_ref[m, cols, :], NT)
            ng_ref[m * ext : (m + 1) * ext, cols] = select_heads(result).astype(BF)
    store_group(mm(ext_ref[...], ng_ref[:, 0:group_width]), 0, n_member, n_band, 0, out_refs)


def key_body(
    n_member, n_band, grad_ref, dm_ref, kv_ref, slope_ref, q_ref, merged_ref, wo_ref, ext_ref, ngv_ref,
    ng_ref, *refs
):
    out_refs, turned = refs[:-1], refs[-1]
    members, ext, width2 = kv_ref.shape
    width = width2 // 2
    group_width = out_refs[0].shape[1]
    for pair in range(width // LANES):
        cols = slice(pair * LANES, (pair + 1) * LANES)
        vcols = slice(width + pair * LANES, width + (pair + 1) * LANES)
        for m in range(members):
            dgate = mm(split_heads(kv_ref[m, :, vcols]), dm_ref[m, cols, :])
            dscore = (dgate * slope_ref[pair, m].astype(F32)).astype(BF)
            ng_ref[m * ext : (m + 1) * ext, cols] = select_heads(mm(dscore, q_ref[:, cols])).astype(BF)
    m_t = sum(mm(grad_ref[m], merged_ref[m], NT) for m in range(members))
    head_t = sum(mm(grad_ref[m], q_ref[...]) for m in range(members)) + mm(m_t.astype(BF), wo_ref[...])
    turned[...] = jnp.concatenate([m_t, head_t], axis=0).T
    pieces = [(ngv_ref, group_width, width), (ng_ref, 0, width), (None, 0, 2 * LANES)]
    at = group_width
    for ref, first, last in pieces:
        while first < last:
            group, offset = at // group_width, at % group_width
            take = min(last - first, group_width - offset)
            if ref is None:
                rows = reorder(turned, n_member, n_band)
            else:
                rows = mm(ext_ref[...], ref[:, first : first + take])
            outs = out_refs[2 * (group - 1) : 2 * group]
            store_group(rows, group, n_member, n_band, offset, outs)
            first, at = first + take, at + take


def extended_grad_body(members, nodes, rim, ngk_ref, ngv_ref, kvw_ref, own_ref, mate_ref, other_ref):
    ext = nodes + 2 * rim
    width = kvw_ref.shape[0]
    rows = mm(ngk_ref[...], kvw_ref[:, 0:width], NT) + mm(ngv_ref[...], kvw_ref[:, width:], NT)
    for m in range(members):
        at = m * ext
        own_ref[m] = rows[at : at + nodes]
        mate_ref[m * rim : (m + 1) * rim, :] = rows[at + nodes : at + nodes + rim].astype(BF)
        other_ref[m * rim : (m + 1) * rim, :] = rows[at + nodes + rim : at + ext].astype(BF)


def hidden_body(own_ref, from_mate_ref, from_other_ref, halo_ref, out_ref):
    members, nodes, _ = own_ref.shape
    rim = halo_ref.shape[1]
    mate, other = [one_hot_rows(rows, nodes) for rows in halo_lists(halo_ref)]
    for m in range(members):
        rows = slice(m * rim, (m + 1) * rim)
        out_ref[m] = own_ref[m] + mm(mate, from_mate_ref[rows, :]) + mm(other, from_other_ref[rows, :])


def finish_body(devices, own_ref, arrived_ref, hp_ref, kv_ref, out_ref, head_ref):
    width = kv_ref.shape[1] // 2
    channels = hp_ref.shape[0]
    total = (own_ref[...] + arrived_ref[...].astype(F32)) * (1.0 / devices)
    kv_ref[:, width:] = total[:, 0:width]
    kv_ref[:, 0:width] = total[:, width : 2 * width]
    m_rows = total[:, 2 * width : 2 * width + channels]
    high = m_rows.astype(BF)
    low = (m_rows - high.astype(F32)).astype(BF)
    out_ref[...] = mm(high, hp_ref[...]) + mm(low, hp_ref[...])
    head_ref[...] = total[:, 2 * width + LANES : 2 * width + LANES + channels]


def add_up(*parts):
    return functools.reduce(lambda a, b: a + b, [p.astype(F32) for p in parts])


def swap(rows, axis, bit, count):
    return lax.ppermute(rows, axis, [(i, i ^ (1 << bit)) for i in range(count)])


def upper(terms):
    return [t[: t.shape[0] // 2] for t in terms]


def lower(terms):
    return [t[t.shape[0] // 2 :] for t in terms]


def shards(
    n_member, n_band,
    hidden, queries, kv_weight, out_weight, head_projection, initial_state, truth,
    latitude_weight, channel_loss_weight, sources, halo_rows,
):
    members, nodes, width = hidden.shape
    points = queries.shape[0]
    channels = head_projection.shape[1]
    rim = halo_rows.shape[1]
    ext = nodes + 2 * rim
    pairs = width // LANES
    devices = n_member * n_band
    rw = width // devices
    chips = n_band // 2
    send_rows = -(-channels // 8) * 8
    mates = [(i, i ^ 1) for i in range(n_band)]
    others = [(i, i + 1 if i % 2 else i - 1) for i in range(1, n_band - 1)]

    own_hidden, halo, for_mate, for_other = call(
        pick_body,
        [sds(hidden.shape, BF), sds(halo_rows.shape, jnp.int32)] + [sds((members * rim, width), BF)] * 2,
        (hidden, halo_rows),
        [pltpu.SemaphoreType.DMA((2,))],
        hbm=(0, 1),
        flops=10**10,
    )
    mate = lax.ppermute(for_mate, "band", mates)
    other = lax.ppermute(for_other, "band", others)

    hp = head_projection.T
    own_kv, pt, p, base, weight = call(
        prepare_body,
        [
            sds((members * nodes, 2 * width), BF),
            sds((width, LANES), BF),
            sds((LANES, width), BF),
            sds((LANES, points), F32),
            sds((channels, points), F32),
        ],
        (
            own_hidden, out_weight, hp, queries, kv_weight, initial_state,
            channel_loss_weight[None, :], latitude_weight[None, :],
        ),
        [pltpu.VMEM((8, LANES), F32), pltpu.VMEM((LANES, width), F32)],
    )

    kv, gates, slopes, merged, part, sent = call(
        functools.partial(forward_body, send_rows),
        [
            sds((members, ext, 2 * width), BF),
            sds((pairs, members, 2 * ext, points), BF),
            sds((pairs, members, 2 * ext, points), BF),
            sds((members, width, points), BF),
            sds((members, LANES, points), F32),
            sds((-(-members * send_rows // 16) * 16, points), BF),
        ],
        (mate, other, own_kv, kv_weight, queries, sources, p),
    )

    received = [
        lax.ppermute(sent, "member", [(i, i ^ s) for i in range(n_member)]) for s in range(1, n_member)
    ]

    ext_t = call(
        functools.partial(transpose_body, n_member, n_band),
        sds((width, members * ext), BF),
        (own_hidden, mate, other),
        [pltpu.VMEM((width, members * ext), F32)],
    )

    extra = 2 * LANES
    group_width = (2 * width + extra) // GROUPS
    grad, dm, ng_value, send, keep = call(
        functools.partial(value_body, n_member, n_band),
        [sds((members, LANES, points), BF), sds((members, width, points), BF), sds((members * ext, width), BF)]
        + [sds((width // 2, group_width), BF)] * 2,
        (*received, part, base, truth, weight, pt, gates, ext_t),
    )
    groups = [[keep, swap(send, "band", 0, n_band)]]
    ng_key, *outs = call(
        functools.partial(key_body, n_member, n_band),
        [sds((members * ext, width), BF)] + [sds((width // 2, group_width), BF)] * (2 * (GROUPS - 1)),
        (grad, dm, kv, slopes, queries, merged, out_weight, ext_t, ng_value),
        [pltpu.VMEM((width, extra), F32)],
    )
    for i in range(GROUPS - 1):
        groups.append([outs[2 * i + 1], swap(outs[2 * i], "band", 0, n_band)])

    count = {"member": n_member, "band": n_band}
    turns, rest = halving_orders(n_member, n_band)
    for step in range(len(turns[0])):
        outgoing = [add_up(*upper(terms)).astype(BF) for terms in groups]
        if step == 0:
            outgoing[0], groups[1:] = lax.optimization_barrier((outgoing[0], groups[1:]))
            outgoing[1:] = [add_up(*upper(terms)).astype(BF) for terms in groups[1:]]
            outgoing, ng_key = lax.optimization_barrier((outgoing, ng_key))
            own_grad, back_mate, back_other = call(
                functools.partial(extended_grad_body, members, nodes, rim),
                [sds((members, nodes, width), F32)] + [sds((members * rim, width), BF)] * 2,
                (ng_key, ng_value, kv_weight),
            )
        arrived = [swap(out, *turn[step], count[turn[step][0]]) for out, turn in zip(outgoing, turns)]
        if step == 0:
            arrived, back_mate, back_other = lax.optimization_barrier((arrived, back_mate, back_other))
            from_mate = lax.ppermute(back_mate, "band", mates)
            from_other = lax.ppermute(back_other, "band", others)
        groups = [lower(terms) + [new] for terms, new in zip(groups, arrived)]
    hidden_grad = call(
        hidden_body,
        sds((members, nodes, width), F32),
        (own_grad, from_mate, from_other, halo),
    )
    terms = [jnp.concatenate([add_up(*group) for group in groups], axis=1)]
    for axis, bit in rest:
        arrived = swap(add_up(*upper(terms)).astype(BF), axis, bit, count[axis])
        terms = lower(terms) + [arrived]

    kv_grad, out_grad, head_grad = call(
        functools.partial(finish_body, devices),
        [sds((rw, 2 * width), F32), sds((rw, width), F32), sds((rw, channels), F32)],
        (add_up(*terms[:-1]), terms[-1], hp),
    )
    return hidden_grad, kv_grad, out_grad, head_grad


def solution(mesh):
    placed = (
        P("member", "band", None),
        P("band", None),
        P(),
        P(),
        P(),
        P(None, "band"),
        P(None, "band"),
        P("band"),
        P(),
        P(None, "band"),
        P("band", None),
    )
    return jax.shard_map(
        functools.partial(shards, mesh.shape["member"], mesh.shape["band"]),
        mesh=mesh,
        in_specs=placed,
        out_specs=(
            P("member", "band", None),
            P(("member", "band"), None),
            P(("member", "band"), None),
            P(("member", "band"), None),
        ),
        check_vma=False,
    )
```

```python
import functools

import jax
import jax.numpy as jnp
from jax import lax
from jax.experimental import pallas as pl
from jax.experimental.pallas import tpu as pltpu
from jax.sharding import PartitionSpec as P

HEAD_DIM = 64
LANES = 128
GROUPS = 3
ALPHA = 0.95
SOFTENING = 0.5
BF = jnp.bfloat16
F32 = jnp.float32
NN = (((1,), (0,)), ((), ()))
NT = (((1,), (1,)), ((), ()))
TN = (((0,), (0,)), ((), ()))


def mm(a, b, dims=NN):
    return lax.dot_general(a, b, dims, preferred_element_type=F32)


def call(body, out_shape, args, scratch=(), hbm=(), limit=24, flops=1):
    args = [pltpu.with_memory_space_constraint(x, pltpu.HBM) if i in hbm else x for i, x in enumerate(args)]
    return pl.pallas_call(
        body,
        out_shape=out_shape,
        in_specs=[
            pl.BlockSpec(memory_space=pltpu.HBM if i in hbm else pltpu.VMEM) for i in range(len(args))
        ],
        out_specs=jax.tree.map(lambda _: pl.BlockSpec(memory_space=pltpu.VMEM), out_shape),
        scratch_shapes=list(scratch),
        compiler_params=pltpu.CompilerParams(vmem_limit_bytes=limit * 1024 * 1024),
        cost_estimate=pl.CostEstimate(flops=flops, bytes_accessed=1, transcendentals=0),
    )(*args)


def sds(shape, dtype):
    return jax.ShapeDtypeStruct(shape, dtype)


def one_hot_rows(rows, node_count):
    nodes = lax.broadcasted_iota(jnp.int32, (node_count, rows.shape[1]), 0).astype(rows.dtype)
    return (nodes == rows).astype(F32).astype(BF)


def start_copies(pairs, sems):
    copies = [pltpu.make_async_copy(src, dst, sems.at[i]) for i, (src, dst) in enumerate(pairs)]
    for copy in copies:
        copy.start()
    return copies


def halo_lists(halo_ref):
    even = lax.axis_index("band") % 2 == 0
    down, up = halo_ref[0:1, :], halo_ref[1:2, :]
    return jnp.where(even, up, down), jnp.where(even, down, up)


def pick_body(hidden_hbm, halo_hbm, hidden_ref, halo_ref, mate_ref, other_ref, sems):
    for copy in start_copies([(hidden_hbm, hidden_ref), (halo_hbm, halo_ref)], sems):
        copy.wait()
    members, nodes, _ = hidden_ref.shape
    rim = halo_ref.shape[1]
    for rows, out_ref in zip(halo_lists(halo_ref), (mate_ref, other_ref)):
        hot = one_hot_rows(rows, nodes)
        for m in range(members):
            out_ref[m * rim : (m + 1) * rim, :] = mm(hot, hidden_ref[m], TN).astype(BF)


def prepare_body(
    hidden_ref, wo_ref, hp_ref, q_ref, kvw_ref, init_ref, chw_ref, lat_ref,
    kv_ref, pt_ref, p_ref, base_ref, weight_ref, chw_pad, hp_pad,
):
    channels = hp_ref.shape[0]
    hp_pad[...] = jnp.zeros_like(hp_pad)
    hp_pad[0:channels, :] = hp_ref[...].astype(F32)
    hp_t = hp_pad[...].astype(BF)
    chw_pad[:, 0:channels] = jnp.broadcast_to(chw_ref[...], (8, channels))
    weight_ref[...] = chw_pad[...].T[0:channels, 0:1] * lat_ref[...]
    base_ref[...] = mm(hp_t, q_ref[...], NT)
    base_ref[0:channels, :] = base_ref[0:channels, :] + init_ref[...]
    p = mm(hp_t, wo_ref[...], NT)
    p_ref[...] = p.astype(BF)
    pt_ref[...] = p.T.astype(BF)
    hidden = jnp.concatenate([hidden_ref[m] for m in range(hidden_ref.shape[0])], axis=0)
    kv_ref[...] = mm(hidden, kvw_ref[...]).astype(BF)


def split_heads(block):
    low = lax.broadcasted_iota(jnp.int32, block.shape, 1) < HEAD_DIM
    zero = jnp.zeros_like(block)
    return jnp.concatenate([jnp.where(low, block, zero), jnp.where(low, zero, block)], axis=0)


def forward_body(
    send_rows,
    mate_ref, other_ref, own_ref, kvw_ref, q_ref, src_ref, p_ref,
    kv_ref, gate_ref, slope_ref, merged_ref, part_ref, send_ref,
):
    members, ext, width2 = kv_ref.shape
    width = width2 // 2
    points = q_ref.shape[0]
    nodes = own_ref.shape[0] // members
    rim = mate_ref.shape[0] // members
    halo = mm(jnp.concatenate([mate_ref[...], other_ref[...]], axis=0), kvw_ref[...]).astype(BF)
    for m in range(members):
        kv_ref[m, 0:nodes, :] = own_ref[m * nodes : (m + 1) * nodes, :]
        kv_ref[m, nodes : nodes + rim, :] = halo[m * rim : (m + 1) * rim]
        kv_ref[m, nodes + rim : ext, :] = halo[(members + m) * rim : (members + m + 1) * rim]
    rows = lax.broadcasted_iota(jnp.int32, (ext, points), 0)
    src = src_ref[...]
    even = lax.axis_index("band") % 2 == 0
    shift = jnp.where(src >= nodes + rim, -rim, jnp.where(src >= nodes, rim, 0))
    src = src + jnp.where(even, shift, 0)
    mask = rows == src[0:1, :]
    for e in range(1, src.shape[0]):
        mask = mask | (rows == src[e : e + 1, :])
    mask = mask.astype(F32)
    mask = jnp.concatenate([mask, mask], axis=0)
    scale = HEAD_DIM ** (-0.5)
    for pair in range(width // LANES):
        cols = slice(pair * LANES, (pair + 1) * LANES)
        vcols = slice(width + pair * LANES, width + (pair + 1) * LANES)
        q = q_ref[:, cols]
        for m in range(members):
            th = jnp.tanh(mm(split_heads(kv_ref[m, :, cols]), q, NT) * (0.5 * scale))
            gate = ((0.5 * th + 0.5) * mask).astype(BF)
            gate_ref[pair, m] = gate
            slope_ref[pair, m] = ((0.25 * scale) * mask * (1.0 - th * th)).astype(BF)
            merged_ref[m, cols, :] = mm(split_heads(kv_ref[m, :, vcols]), gate, TN).astype(BF)
    sent = []
    for m in range(members):
        part = mm(p_ref[...], merged_ref[m])
        part_ref[m] = part
        sent.append(part[0:send_rows])
    filler = send_ref.shape[0] - members * send_rows
    if filler:
        sent.append(jnp.zeros((filler, points), F32))
    send_ref[...] = jnp.concatenate(sent, axis=0).astype(BF)


def halving_orders(n_member, n_band):
    chips = [("band", bit) for bit in range(1, n_band.bit_length() - 1)]
    member = [("member", bit) for bit in range(n_member.bit_length() - 1)]
    turn = chips + member[:1]
    return [turn[i:] + turn[:i] for i in range(GROUPS)], member[1:]


def unit_order(order, n_member, n_band):
    def key(unit):
        return [-((2 * unit[0] if axis == "band" else unit[1]) >> bit & 1) for axis, bit in order]

    return sorted([(c, m) for c in range(n_band // 2) for m in range(n_member)], key=key)


def destination_rows(member, band, n_member, n_band, rw):
    chip, core = band // 2, band % 2
    for rel_core in (1, 0):
        for rel_chip in range(n_band // 2):
            to_band = (chip ^ rel_chip) * 2 + (core ^ rel_core)
            for rel_member in range(n_member):
                yield pl.multiple_of(((member ^ rel_member) * n_band + to_band) * rw, rw)


def reorder(src_ref, n_member, n_band):
    rw = src_ref.shape[0] // (n_member * n_band)
    member, band = lax.axis_index("member"), lax.axis_index("band")
    starts = destination_rows(member, band, n_member, n_band, rw)
    return jnp.concatenate([src_ref[pl.ds(start, rw), :] for start in starts], axis=0)


def store_group(rows, group, n_member, n_band, at, out_refs):
    orders, rest = halving_orders(n_member, n_band)
    units = unit_order(orders[group] + rest, n_member, n_band)
    rw = rows.shape[0] // (n_member * n_band)
    for core, ref in enumerate(out_refs):
        starts = [((core * (n_band // 2) + chip) * n_member + member) * rw for chip, member in units]
        ordered = jnp.concatenate([rows[i : i + rw] for i in starts], axis=0)
        ref[:, at : at + rows.shape[1]] = ordered.astype(BF)


def transpose_body(n_member, n_band, hidden_ref, mate_ref, other_ref, out_ref, turned):
    members, nodes, _ = hidden_ref.shape
    rim = mate_ref.shape[0] // members
    parts = []
    for m in range(members):
        parts.append(hidden_ref[m])
        parts.append(mate_ref[m * rim : (m + 1) * rim, :])
        parts.append(other_ref[m * rim : (m + 1) * rim, :])
    turned[...] = jnp.concatenate(parts, axis=0).astype(F32).T
    out_ref[...] = reorder(turned, n_member, n_band).astype(BF)


def select_heads(block):
    half = block.shape[0] // 2
    low = lax.broadcasted_iota(jnp.int32, (half, block.shape[1]), 1) < HEAD_DIM
    return jnp.where(low, block[:half], block[half:])


def soft_slope(v):
    return v * lax.rsqrt(v * v + SOFTENING * SOFTENING)


def value_body(n_member, n_band, *refs):
    recv_refs = refs[: n_member - 1]
    part_ref, base_ref, truth_ref, weight_ref, pt_ref, gate_ref, ext_ref = refs[n_member - 1 : n_member + 6]
    grad_ref, dm_ref, ng_ref, *out_refs = refs[n_member + 6 :]
    group_width = out_refs[0].shape[1]
    members, width, _ = dm_ref.shape
    ext = ng_ref.shape[0] // members
    channels = truth_ref.shape[0]
    total = members * n_member
    spread = (1.0 - (1.0 - ALPHA) / total) / (total * (total - 1))

    grad_ref[...] = jnp.zeros_like(grad_ref)
    own = [part_ref[m, 0:channels, :] for m in range(members)]
    sent_rows = -(-channels // 8) * 8
    others = []
    for ref in recv_refs:
        rows = ref[...].astype(F32)
        others += [rows[k * sent_rows : k * sent_rows + channels] for k in range(members)]
    for m in range(members):
        slopes = jnp.zeros_like(own[m])
        for k in range(members):
            if k != m:
                slopes = slopes + soft_slope(own[m] - own[k])
        for other in others:
            slopes = slopes + soft_slope(own[m] - other)
        gap = soft_slope(own[m] + base_ref[0:channels, :] - truth_ref[...])
        grad_ref[m, 0:channels, :] = (weight_ref[...] * (gap / total - spread * slopes)).astype(BF)
    for m in range(members):
        dm_ref[m] = mm(pt_ref[...], grad_ref[m]).astype(BF)
    for pair in range(width // LANES):
        cols = slice(pair * LANES, (pair + 1) * LANES)
        for m in range(members):
            result = mm(gate_ref[pair, m], dm_ref[m, cols, :], NT)
            ng_ref[m * ext : (m + 1) * ext, cols] = select_heads(result).astype(BF)
    store_group(mm(ext_ref[...], ng_ref[:, 0:group_width]), 0, n_member, n_band, 0, out_refs)


def key_body(
    n_member, n_band, grad_ref, dm_ref, kv_ref, slope_ref, q_ref, merged_ref, wo_ref, ext_ref, ngv_ref,
    ng_ref, *refs
):
    out_refs, turned = refs[:-1], refs[-1]
    members, ext, width2 = kv_ref.shape
    width = width2 // 2
    group_width = out_refs[0].shape[1]
    for pair in range(width // LANES):
        cols = slice(pair * LANES, (pair + 1) * LANES)
        vcols = slice(width + pair * LANES, width + (pair + 1) * LANES)
        for m in range(members):
            dgate = mm(split_heads(kv_ref[m, :, vcols]), dm_ref[m, cols, :])
            dscore = (dgate * slope_ref[pair, m].astype(F32)).astype(BF)
            ng_ref[m * ext : (m + 1) * ext, cols] = select_heads(mm(dscore, q_ref[:, cols])).astype(BF)
    m_t = sum(mm(grad_ref[m], merged_ref[m], NT) for m in range(members))
    head_t = sum(mm(grad_ref[m], q_ref[...]) for m in range(members)) + mm(m_t.astype(BF), wo_ref[...])
    turned[...] = jnp.concatenate([m_t, head_t], axis=0).T
    pieces = [(ngv_ref, group_width, width), (ng_ref, 0, width), (None, 0, 2 * LANES)]
    at = group_width
    for ref, first, last in pieces:
        while first < last:
            group, offset = at // group_width, at % group_width
            take = min(last - first, group_width - offset)
            if ref is None:
                rows = reorder(turned, n_member, n_band)
            else:
                rows = mm(ext_ref[...], ref[:, first : first + take])
            outs = out_refs[2 * (group - 1) : 2 * group]
            store_group(rows, group, n_member, n_band, offset, outs)
            first, at = first + take, at + take


def extended_grad_body(members, nodes, rim, ngk_ref, ngv_ref, kvw_ref, own_ref, mate_ref, other_ref):
    ext = nodes + 2 * rim
    width = kvw_ref.shape[0]
    rows = mm(ngk_ref[...], kvw_ref[:, 0:width], NT) + mm(ngv_ref[...], kvw_ref[:, width:], NT)
    for m in range(members):
        at = m * ext
        own_ref[m] = rows[at : at + nodes]
        mate_ref[m * rim : (m + 1) * rim, :] = rows[at + nodes : at + nodes + rim].astype(BF)
        other_ref[m * rim : (m + 1) * rim, :] = rows[at + nodes + rim : at + ext].astype(BF)


def hidden_body(own_ref, from_mate_ref, from_other_ref, halo_ref, out_ref):
    members, nodes, _ = own_ref.shape
    rim = halo_ref.shape[1]
    mate, other = [one_hot_rows(rows, nodes) for rows in halo_lists(halo_ref)]
    for m in range(members):
        rows = slice(m * rim, (m + 1) * rim)
        out_ref[m] = own_ref[m] + mm(mate, from_mate_ref[rows, :]) + mm(other, from_other_ref[rows, :])


def finish_body(devices, own_ref, arrived_ref, hp_ref, kv_ref, out_ref, head_ref):
    width = kv_ref.shape[1] // 2
    channels = hp_ref.shape[0]
    total = (own_ref[...] + arrived_ref[...].astype(F32)) * (1.0 / devices)
    kv_ref[:, width:] = total[:, 0:width]
    kv_ref[:, 0:width] = total[:, width : 2 * width]
    m_rows = total[:, 2 * width : 2 * width + channels]
    high = m_rows.astype(BF)
    low = (m_rows - high.astype(F32)).astype(BF)
    out_ref[...] = mm(high, hp_ref[...]) + mm(low, hp_ref[...])
    head_ref[...] = total[:, 2 * width + LANES : 2 * width + LANES + channels]


def add_up(*parts):
    return functools.reduce(lambda a, b: a + b, [p.astype(F32) for p in parts])


def swap(rows, axis, bit, count):
    return lax.ppermute(rows, axis, [(i, i ^ (1 << bit)) for i in range(count)])


def upper(terms):
    return [t[: t.shape[0] // 2] for t in terms]


def lower(terms):
    return [t[t.shape[0] // 2 :] for t in terms]


def shards(
    n_member, n_band,
    hidden, queries, kv_weight, out_weight, head_projection, initial_state, truth,
    latitude_weight, channel_loss_weight, sources, halo_rows,
):
    members, nodes, width = hidden.shape
    points = queries.shape[0]
    channels = head_projection.shape[1]
    rim = halo_rows.shape[1]
    ext = nodes + 2 * rim
    pairs = width // LANES
    devices = n_member * n_band
    rw = width // devices
    chips = n_band // 2
    send_rows = -(-channels // 8) * 8
    mates = [(i, i ^ 1) for i in range(n_band)]
    others = [(i, (i + 1 if i % 2 else i - 1) % n_band) for i in range(n_band)]

    own_hidden, halo, for_mate, for_other = call(
        pick_body,
        [sds(hidden.shape, BF), sds(halo_rows.shape, jnp.int32)] + [sds((members * rim, width), BF)] * 2,
        (hidden, halo_rows),
        [pltpu.SemaphoreType.DMA((2,))],
        hbm=(0, 1),
        flops=10**10,
    )
    mate = lax.ppermute(for_mate, "band", mates)
    other = lax.ppermute(for_other, "band", others)

    hp = head_projection.T
    own_kv, pt, p, base, weight = call(
        prepare_body,
        [
            sds((members * nodes, 2 * width), BF),
            sds((width, LANES), BF),
            sds((LANES, width), BF),
            sds((LANES, points), F32),
            sds((channels, points), F32),
        ],
        (
            own_hidden, out_weight, hp, queries, kv_weight, initial_state,
            channel_loss_weight[None, :], latitude_weight[None, :],
        ),
        [pltpu.VMEM((8, LANES), F32), pltpu.VMEM((LANES, width), F32)],
    )

    kv, gates, slopes, merged, part, sent = call(
        functools.partial(forward_body, send_rows),
        [
            sds((members, ext, 2 * width), BF),
            sds((pairs, members, 2 * ext, points), BF),
            sds((pairs, members, 2 * ext, points), BF),
            sds((members, width, points), BF),
            sds((members, LANES, points), F32),
            sds((-(-members * send_rows // 16) * 16, points), BF),
        ],
        (mate, other, own_kv, kv_weight, queries, sources, p),
    )

    received = [
        lax.ppermute(sent, "member", [(i, i ^ s) for i in range(n_member)]) for s in range(n_member - 1, 0, -1)
    ]

    ext_t = call(
        functools.partial(transpose_body, n_member, n_band),
        sds((width, members * ext), BF),
        (own_hidden, mate, other),
        [pltpu.VMEM((width, members * ext), F32)],
    )

    extra = 2 * LANES
    group_width = (2 * width + extra) // GROUPS
    grad, dm, ng_value, send, keep = call(
        functools.partial(value_body, n_member, n_band),
        [sds((members, LANES, points), BF), sds((members, width, points), BF), sds((members * ext, width), BF)]
        + [sds((width // 2, group_width), BF)] * 2,
        (*received, part, base, truth, weight, pt, gates, ext_t),
    )
    groups = [[keep, swap(send, "band", 0, n_band)]]
    ng_key, *outs = call(
        functools.partial(key_body, n_member, n_band),
        [sds((members * ext, width), BF)] + [sds((width // 2, group_width), BF)] * (2 * (GROUPS - 1)),
        (grad, dm, kv, slopes, queries, merged, out_weight, ext_t, ng_value),
        [pltpu.VMEM((width, extra), F32)],
    )
    for i in range(GROUPS - 1):
        groups.append([outs[2 * i + 1], swap(outs[2 * i], "band", 0, n_band)])

    count = {"member": n_member, "band": n_band}
    turns, rest = halving_orders(n_member, n_band)
    for step in range(len(turns[0])):
        outgoing = [add_up(*upper(terms)).astype(BF) for terms in groups]
        if step == 0:
            outgoing[0], groups[1:] = lax.optimization_barrier((outgoing[0], groups[1:]))
            outgoing[1:] = [add_up(*upper(terms)).astype(BF) for terms in groups[1:]]
            outgoing, ng_key = lax.optimization_barrier((outgoing, ng_key))
            own_grad, back_mate, back_other = call(
                functools.partial(extended_grad_body, members, nodes, rim),
                [sds((members, nodes, width), F32)] + [sds((members * rim, width), BF)] * 2,
                (ng_key, ng_value, kv_weight),
            )
        arrived = [swap(out, *turn[step], count[turn[step][0]]) for out, turn in zip(outgoing, turns)]
        if step == 0:
            from_mate = lax.ppermute(back_mate, "band", mates)
            from_other = lax.ppermute(back_other, "band", others)
            arrived, from_mate, from_other = lax.optimization_barrier((arrived, from_mate, from_other))
        groups = [lower(terms) + [new] for terms, new in zip(groups, arrived)]
    hidden_grad = call(
        hidden_body,
        sds((members, nodes, width), F32),
        (own_grad, from_mate, from_other, halo),
    )
    terms = [jnp.concatenate([add_up(*group) for group in groups], axis=1)]
    for axis, bit in rest:
        arrived = swap(add_up(*upper(terms)).astype(BF), axis, bit, count[axis])
        terms = lower(terms) + [arrived]

    kv_grad, out_grad, head_grad = call(
        functools.partial(finish_body, devices),
        [sds((rw, 2 * width), F32), sds((rw, width), F32), sds((rw, channels), F32)],
        (add_up(*terms[:-1]), terms[-1], hp),
    )
    return hidden_grad, kv_grad, out_grad, head_grad


def solution(mesh):
    placed = (
        P("member", "band", None),
        P("band", None),
        P(),
        P(),
        P(),
        P(None, "band"),
        P(None, "band"),
        P("band"),
        P(),
        P(None, "band"),
        P("band", None),
    )
    return jax.shard_map(
        functools.partial(shards, mesh.shape["member"], mesh.shape["band"]),
        mesh=mesh,
        in_specs=placed,
        out_specs=(
            P("member", "band", None),
            P(("member", "band"), None),
            P(("member", "band"), None),
            P(("member", "band"), None),
        ),
        check_vma=False,
    )
```

```python
import functools

import jax
import jax.numpy as jnp
from jax import lax
from jax.experimental import pallas as pl
from jax.experimental.pallas import tpu as pltpu
from jax.sharding import PartitionSpec as P

HEAD_DIM = 64
LANES = 128
GROUPS = 3
ALPHA = 0.95
SOFTENING = 0.5
BF = jnp.bfloat16
F32 = jnp.float32
NN = (((1,), (0,)), ((), ()))
NT = (((1,), (1,)), ((), ()))
TN = (((0,), (0,)), ((), ()))


def mm(a, b, dims=NN):
    return lax.dot_general(a, b, dims, preferred_element_type=F32)


def call(body, out_shape, args, scratch=(), hbm=(), limit=24, flops=1):
    args = [pltpu.with_memory_space_constraint(x, pltpu.HBM) if i in hbm else x for i, x in enumerate(args)]
    return pl.pallas_call(
        body,
        out_shape=out_shape,
        in_specs=[
            pl.BlockSpec(memory_space=pltpu.HBM if i in hbm else pltpu.VMEM) for i in range(len(args))
        ],
        out_specs=jax.tree.map(lambda _: pl.BlockSpec(memory_space=pltpu.VMEM), out_shape),
        scratch_shapes=list(scratch),
        compiler_params=pltpu.CompilerParams(vmem_limit_bytes=limit * 1024 * 1024),
        cost_estimate=pl.CostEstimate(flops=flops, bytes_accessed=1, transcendentals=0),
    )(*args)


def sds(shape, dtype):
    return jax.ShapeDtypeStruct(shape, dtype)


def one_hot_rows(rows, node_count):
    nodes = lax.broadcasted_iota(jnp.int32, (node_count, rows.shape[1]), 0).astype(rows.dtype)
    return (nodes == rows).astype(F32).astype(BF)


def start_copies(pairs, sems):
    copies = [pltpu.make_async_copy(src, dst, sems.at[i]) for i, (src, dst) in enumerate(pairs)]
    for copy in copies:
        copy.start()
    return copies


def halo_lists(halo_ref):
    even = lax.axis_index("band") % 2 == 0
    down, up = halo_ref[0:1, :], halo_ref[1:2, :]
    return jnp.where(even, up, down), jnp.where(even, down, up)


def pick_body(hidden_hbm, halo_hbm, hidden_ref, halo_ref, mate_ref, other_ref, sems):
    for copy in start_copies([(hidden_hbm, hidden_ref), (halo_hbm, halo_ref)], sems):
        copy.wait()
    members, nodes, _ = hidden_ref.shape
    rim = halo_ref.shape[1]
    for rows, out_ref in zip(halo_lists(halo_ref), (mate_ref, other_ref)):
        hot = one_hot_rows(rows, nodes)
        for m in range(members):
            out_ref[m * rim : (m + 1) * rim, :] = mm(hot, hidden_ref[m], TN).astype(BF)


def prepare_body(
    hidden_ref, wo_ref, hp_ref, q_ref, kvw_ref, init_ref, chw_ref, lat_ref,
    kv_ref, pt_ref, p_ref, base_ref, weight_ref, chw_pad, hp_pad,
):
    channels = hp_ref.shape[0]
    hp_pad[...] = jnp.zeros_like(hp_pad)
    hp_pad[0:channels, :] = hp_ref[...].astype(F32)
    hp_t = hp_pad[...].astype(BF)
    chw_pad[:, 0:channels] = jnp.broadcast_to(chw_ref[...], (8, channels))
    weight_ref[...] = chw_pad[...].T[0:channels, 0:1] * lat_ref[...]
    base_ref[...] = mm(hp_t, q_ref[...], NT)
    base_ref[0:channels, :] = base_ref[0:channels, :] + init_ref[...]
    p = mm(hp_t, wo_ref[...], NT)
    p_ref[...] = p.astype(BF)
    pt_ref[...] = p.T.astype(BF)
    hidden = jnp.concatenate([hidden_ref[m] for m in range(hidden_ref.shape[0])], axis=0)
    kv_ref[...] = mm(hidden, kvw_ref[...]).astype(BF)


def split_heads(block):
    low = lax.broadcasted_iota(jnp.int32, block.shape, 1) < HEAD_DIM
    zero = jnp.zeros_like(block)
    return jnp.concatenate([jnp.where(low, block, zero), jnp.where(low, zero, block)], axis=0)


def forward_body(
    send_rows, mate_ref, other_ref, own_ref, kvw_ref, q_ref, src_ref, p_ref,
    value_ref, gate_ref, slope_ref, merged_ref, part_ref, send_ref,
):
    members, ext, width = value_ref.shape
    points = q_ref.shape[0]
    nodes = own_ref.shape[0] // members
    rim = mate_ref.shape[0] // members
    step = 2 * LANES
    halo_rows = jnp.concatenate([mate_ref[...], other_ref[...]], axis=0)

    def project(start):
        halo = mm(halo_rows, kvw_ref[:, start : start + step]).astype(BF)
        result = []
        for m in range(members):
            own = own_ref[m * nodes : (m + 1) * nodes, start : start + step]
            mate = halo[m * rim : (m + 1) * rim]
            other = halo[(members + m) * rim : (members + m + 1) * rim]
            result.append(jnp.concatenate([own, mate, other], axis=0))
        return result

    rows = lax.broadcasted_iota(jnp.int32, (ext, points), 0)
    src = src_ref[...]
    even = lax.axis_index("band") % 2 == 0
    shift = jnp.where(src >= nodes + rim, -rim, jnp.where(src >= nodes, rim, 0))
    src = src + jnp.where(even, shift, 0)
    mask = rows == src[0:1, :]
    for e in range(1, src.shape[0]):
        mask = mask | (rows == src[e : e + 1, :])
    half_mask = jnp.where(mask, 0.5, 0.0).astype(F32)
    half_mask = jnp.concatenate([half_mask, half_mask], axis=0)
    half_scale = 0.5 * HEAD_DIM ** (-0.5)
    low_rows = lax.broadcasted_iota(jnp.int32, (LANES, ext), 0) < HEAD_DIM

    keys, values = {}, {}

    def prepare(block):
        start = block * step
        for m, rows in enumerate(project(start)):
            keys[block, m] = rows
        for m, rows in enumerate(project(width + start)):
            values[block, m] = rows
            value_ref[m, :, start : start + step] = rows

    def scores(pair, m):
        block, at = pair * LANES // step, pair * LANES % step
        q = (q_ref[:, pair * LANES : (pair + 1) * LANES].astype(F32) * half_scale).astype(BF)
        return mm(split_heads(keys[block, m][:, at : at + LANES]), q, NT)

    tasks = [(pair, m) for pair in range(width // LANES) for m in range(members)]
    prepare(0)
    ahead = scores(*tasks[0])
    for i, (pair, m) in enumerate(tasks):
        block, at = pair * LANES // step, pair * LANES % step
        current = ahead
        if at == 0 and m == 0 and (block + 1) * step < width:
            prepare(block + 1)
        if i + 1 < len(tasks):
            ahead = scores(*tasks[i + 1])
        value_t = values[block, m][:, at : at + LANES].astype(F32).T
        zero = jnp.zeros_like(value_t)
        value_t = jnp.concatenate(
            [jnp.where(low_rows, value_t, zero), jnp.where(low_rows, zero, value_t)], axis=1
        ).astype(BF)
        gate = jnp.tanh(current) * half_mask + half_mask
        rounded = gate.astype(BF)
        gate_ref[pair, m] = rounded
        slope_ref[pair, m] = (gate - gate * gate).astype(BF)
        merged_ref[m, pair * LANES : (pair + 1) * LANES, :] = mm(value_t, rounded).astype(BF)
    sent = []
    for m in range(members):
        part = mm(p_ref[...], merged_ref[m])
        part_ref[m] = part
        sent.append(part[0:send_rows])
    filler = send_ref.shape[0] - members * send_rows
    if filler:
        sent.append(jnp.zeros((filler, points), F32))
    send_ref[...] = jnp.concatenate(sent, axis=0).astype(BF)


def halving_orders(n_member, n_band):
    chips = [("band", bit) for bit in range(1, n_band.bit_length() - 1)]
    member = [("member", bit) for bit in range(n_member.bit_length() - 1)]
    turn = chips + member[:1]
    return [turn[i:] + turn[:i] for i in range(GROUPS)], member[1:]


def unit_order(order, n_member, n_band):
    def key(unit):
        return [-((2 * unit[0] if axis == "band" else unit[1]) >> bit & 1) for axis, bit in order]

    return sorted([(c, m) for c in range(n_band // 2) for m in range(n_member)], key=key)


def destination_rows(member, band, n_member, n_band, rw):
    chip, core = band // 2, band % 2
    for rel_core in (1, 0):
        for rel_chip in range(n_band // 2):
            to_band = (chip ^ rel_chip) * 2 + (core ^ rel_core)
            for rel_member in range(n_member):
                yield pl.multiple_of(((member ^ rel_member) * n_band + to_band) * rw, rw)


def reorder(src_ref, n_member, n_band):
    rw = src_ref.shape[0] // (n_member * n_band)
    member, band = lax.axis_index("member"), lax.axis_index("band")
    starts = destination_rows(member, band, n_member, n_band, rw)
    return jnp.concatenate([src_ref[pl.ds(start, rw), :] for start in starts], axis=0)


def store_group(rows, group, n_member, n_band, at, out_refs):
    orders, rest = halving_orders(n_member, n_band)
    units = unit_order(orders[group] + rest, n_member, n_band)
    rw = rows.shape[0] // (n_member * n_band)
    for core, ref in enumerate(out_refs):
        starts = [((core * (n_band // 2) + chip) * n_member + member) * rw for chip, member in units]
        ordered = jnp.concatenate([rows[i : i + rw] for i in starts], axis=0)
        ref[:, at : at + rows.shape[1]] = ordered.astype(BF)


def transpose_body(n_member, n_band, hidden_ref, mate_ref, other_ref, out_ref, turned):
    members, nodes, _ = hidden_ref.shape
    rim = mate_ref.shape[0] // members
    parts = []
    for m in range(members):
        parts.append(hidden_ref[m])
        parts.append(mate_ref[m * rim : (m + 1) * rim, :])
        parts.append(other_ref[m * rim : (m + 1) * rim, :])
    turned[...] = jnp.concatenate(parts, axis=0).astype(F32).T
    out_ref[...] = reorder(turned, n_member, n_band).astype(BF)


def select_heads(block):
    half = block.shape[0] // 2
    low = lax.broadcasted_iota(jnp.int32, (half, block.shape[1]), 1) < HEAD_DIM
    return jnp.where(low, block[:half], block[half:])


def soft_slope(v):
    return v * lax.rsqrt(v * v + SOFTENING * SOFTENING)


def value_body(n_member, n_band, *refs):
    recv_refs = refs[: n_member - 1]
    part_ref, base_ref, truth_ref, weight_ref, pt_ref, gate_ref, ext_ref = refs[n_member - 1 : n_member + 6]
    grad_ref, dm_ref, ng_ref, *out_refs = refs[n_member + 6 :]
    group_width = out_refs[0].shape[1]
    members, width, _ = dm_ref.shape
    ext = ng_ref.shape[0] // members
    channels = truth_ref.shape[0]
    total = members * n_member
    spread = (1.0 - (1.0 - ALPHA) / total) / (total * (total - 1))

    grad_ref[...] = jnp.zeros_like(grad_ref)
    own = [part_ref[m, 0:channels, :] for m in range(members)]
    sent_rows = -(-channels // 8) * 8
    others = []
    for ref in recv_refs:
        rows = ref[...].astype(F32)
        others += [rows[k * sent_rows : k * sent_rows + channels] for k in range(members)]
    for m in range(members):
        slopes = jnp.zeros_like(own[m])
        for k in range(members):
            if k != m:
                slopes = slopes + soft_slope(own[m] - own[k])
        for other in others:
            slopes = slopes + soft_slope(own[m] - other)
        gap = soft_slope(own[m] + base_ref[0:channels, :] - truth_ref[...])
        grad_ref[m, 0:channels, :] = (weight_ref[...] * (gap / total - spread * slopes)).astype(BF)
    for m in range(members):
        dm_ref[m] = mm(pt_ref[...], grad_ref[m]).astype(BF)
    for pair in range(width // LANES):
        cols = slice(pair * LANES, (pair + 1) * LANES)
        for m in range(members):
            result = mm(gate_ref[pair, m], dm_ref[m, cols, :], NT)
            ng_ref[m * ext : (m + 1) * ext, cols] = select_heads(result).astype(BF)
    store_group(mm(ext_ref[...], ng_ref[:, 0:group_width]), 0, n_member, n_band, 0, out_refs)


def key_body(
    n_member, n_band, width1, grad_ref, dm_ref, value_ref, slope_ref, q_ref, merged_ref, wo_ref, ext_ref, ngv_ref,
    ng_ref, *refs
):
    out_refs, turned = refs[:-1], refs[-1]
    members, ext, width = value_ref.shape
    scale = HEAD_DIM ** (-0.5)
    for pair in range(width // LANES):
        cols = slice(pair * LANES, (pair + 1) * LANES)
        for m in range(members):
            dgate = mm(split_heads(value_ref[m, :, cols]), dm_ref[m, cols, :])
            dscore = (dgate * slope_ref[pair, m].astype(F32)).astype(BF)
            keys = select_heads(mm(dscore, q_ref[:, cols])) * scale
            ng_ref[m * ext : (m + 1) * ext, cols] = keys.astype(BF)
    m_t = sum(mm(grad_ref[m], merged_ref[m], NT) for m in range(members))
    head_t = sum(mm(grad_ref[m], q_ref[...]) for m in range(members)) + mm(m_t.astype(BF), wo_ref[...])
    turned[...] = jnp.concatenate([m_t, head_t], axis=0).T
    pieces = [(ngv_ref, width1, width), (ng_ref, 0, width), (None, 0, 2 * LANES)]
    group, offset = 0, 0
    for ref, first, last in pieces:
        while first < last:
            outs = out_refs[2 * group : 2 * group + 2]
            take = min(last - first, outs[0].shape[1] - offset)
            if ref is None:
                rows = reorder(turned, n_member, n_band)
            else:
                rows = mm(ext_ref[...], ref[:, first : first + take])
            store_group(rows, group + 1, n_member, n_band, offset, outs)
            first, offset = first + take, offset + take
            if offset == outs[0].shape[1]:
                group, offset = group + 1, 0


def extended_grad_body(members, nodes, rim, ngk_ref, ngv_ref, kvw_ref, own_ref, mate_ref, other_ref):
    ext = nodes + 2 * rim
    width = kvw_ref.shape[0]
    rows = mm(ngk_ref[...], kvw_ref[:, 0:width], NT) + mm(ngv_ref[...], kvw_ref[:, width:], NT)
    for m in range(members):
        at = m * ext
        own_ref[m] = rows[at : at + nodes]
        mate_ref[m * rim : (m + 1) * rim, :] = rows[at + nodes : at + nodes + rim].astype(BF)
        other_ref[m * rim : (m + 1) * rim, :] = rows[at + nodes + rim : at + ext].astype(BF)


def hidden_body(own_ref, from_mate_ref, from_other_ref, halo_ref, out_ref):
    members, nodes, _ = own_ref.shape
    rim = halo_ref.shape[1]
    mate, other = [one_hot_rows(rows, nodes) for rows in halo_lists(halo_ref)]
    for m in range(members):
        rows = slice(m * rim, (m + 1) * rim)
        out_ref[m] = own_ref[m] + mm(mate, from_mate_ref[rows, :]) + mm(other, from_other_ref[rows, :])


def finish_body(devices, own_ref, arrived_ref, hp_ref, kv_ref, out_ref, head_ref):
    width = kv_ref.shape[1] // 2
    channels = hp_ref.shape[0]
    total = (own_ref[...] + arrived_ref[...].astype(F32)) * (1.0 / devices)
    kv_ref[:, width:] = total[:, 0:width]
    kv_ref[:, 0:width] = total[:, width : 2 * width]
    m_rows = total[:, 2 * width : 2 * width + channels]
    high = m_rows.astype(BF)
    low = (m_rows - high.astype(F32)).astype(BF)
    out_ref[...] = mm(high, hp_ref[...]) + mm(low, hp_ref[...])
    head_ref[...] = total[:, 2 * width + LANES : 2 * width + LANES + channels]


def add_up(*parts):
    return functools.reduce(lambda a, b: a + b, [p.astype(F32) for p in parts])


def swap(rows, axis, bit, count):
    return lax.ppermute(rows, axis, [(i, i ^ (1 << bit)) for i in range(count)])


def upper(terms):
    return [t[: t.shape[0] // 2] for t in terms]


def lower(terms):
    return [t[t.shape[0] // 2 :] for t in terms]


def shards(
    n_member, n_band,
    hidden, queries, kv_weight, out_weight, head_projection, initial_state, truth,
    latitude_weight, channel_loss_weight, sources, halo_rows,
):
    members, nodes, width = hidden.shape
    points = queries.shape[0]
    channels = head_projection.shape[1]
    rim = halo_rows.shape[1]
    ext = nodes + 2 * rim
    pairs = width // LANES
    devices = n_member * n_band
    rw = width // devices
    chips = n_band // 2
    send_rows = -(-channels // 8) * 8
    mates = [(i, i ^ 1) for i in range(n_band)]
    others = [(0, 0), (n_band - 1, n_band - 1)]
    others += [(i, i + 1 if i % 2 else i - 1) for i in range(1, n_band - 1)]

    own_hidden, halo, for_mate, for_other = call(
        pick_body,
        [sds(hidden.shape, BF), sds(halo_rows.shape, jnp.int32)] + [sds((members * rim, width), BF)] * 2,
        (hidden, halo_rows),
        [pltpu.SemaphoreType.DMA((2,))],
        hbm=(0, 1),
        flops=10**10,
    )
    mate = lax.ppermute(for_mate, "band", mates)
    other = lax.ppermute(for_other, "band", others)

    hp = head_projection.T
    own_kv, pt, p, base, weight = call(
        prepare_body,
        [
            sds((members * nodes, 2 * width), BF),
            sds((width, LANES), BF),
            sds((LANES, width), BF),
            sds((LANES, points), F32),
            sds((channels, points), F32),
        ],
        (
            own_hidden, out_weight, hp, queries, kv_weight, initial_state,
            channel_loss_weight[None, :], latitude_weight[None, :],
        ),
        [pltpu.VMEM((8, LANES), F32), pltpu.VMEM((LANES, width), F32)],
    )

    value, gates, slopes, merged, part, sent = call(
        functools.partial(forward_body, send_rows),
        [
            sds((members, ext, width), BF),
            sds((pairs, members, 2 * ext, points), BF),
            sds((pairs, members, 2 * ext, points), BF),
            sds((members, width, points), BF),
            sds((members, LANES, points), F32),
            sds((-(-members * send_rows // 16) * 16, points), BF),
        ],
        (mate, other, own_kv, kv_weight, queries, sources, p),
    )

    received = [
        lax.ppermute(sent, "member", [(i, i ^ s) for i in range(n_member)]) for s in range(n_member - 1, 0, -1)
    ]

    ext_t = call(
        functools.partial(transpose_body, n_member, n_band),
        sds((width, members * ext), BF),
        (own_hidden, mate, other),
        [pltpu.VMEM((width, members * ext), F32)],
    )

    extra = 2 * LANES
    third = (2 * width + extra) // LANES // GROUPS
    widths = [(third - 1) * LANES, third * LANES]
    widths.append(2 * width + extra - sum(widths))
    grad, dm, ng_value, send, keep = call(
        functools.partial(value_body, n_member, n_band),
        [sds((members, LANES, points), BF), sds((members, width, points), BF), sds((members * ext, width), BF)]
        + [sds((width // 2, widths[0]), BF)] * 2,
        (*received, part, base, truth, weight, pt, gates, ext_t),
    )
    groups = [[keep, swap(send, "band", 0, n_band)]]
    ng_key, *outs = call(
        functools.partial(key_body, n_member, n_band, widths[0]),
        [sds((members * ext, width), BF)] + [sds((width // 2, w), BF) for w in widths[1:] for _ in range(2)],
        (grad, dm, value, slopes, queries, merged, out_weight, ext_t, ng_value),
        [pltpu.VMEM((width, extra), F32)],
    )
    for i in range(GROUPS - 1):
        groups.append([outs[2 * i + 1], swap(outs[2 * i], "band", 0, n_band)])

    count = {"member": n_member, "band": n_band}
    turns, rest = halving_orders(n_member, n_band)
    for step in range(len(turns[0])):
        outgoing = [add_up(*upper(terms)).astype(BF) for terms in groups]
        if step == 0:
            outgoing[0], groups[1:] = lax.optimization_barrier((outgoing[0], groups[1:]))
            outgoing[1:] = [add_up(*upper(terms)).astype(BF) for terms in groups[1:]]
            outgoing, ng_key = lax.optimization_barrier((outgoing, ng_key))
            own_grad, back_mate, back_other = call(
                functools.partial(extended_grad_body, members, nodes, rim),
                [sds((members, nodes, width), F32)] + [sds((members * rim, width), BF)] * 2,
                (ng_key, ng_value, kv_weight),
            )
        arrived = [swap(out, *turn[step], count[turn[step][0]]) for out, turn in zip(outgoing, turns)]
        if step == 0:
            from_mate = lax.ppermute(back_mate, "band", mates)
            from_other = lax.ppermute(back_other, "band", others)
            arrived, from_mate, from_other = lax.optimization_barrier((arrived, from_mate, from_other))
        groups = [lower(terms) + [new] for terms, new in zip(groups, arrived)]
    hidden_grad = call(
        hidden_body,
        sds((members, nodes, width), F32),
        (own_grad, from_mate, from_other, halo),
    )
    terms = [jnp.concatenate([add_up(*group) for group in groups], axis=1)]
    for axis, bit in rest:
        arrived = swap(add_up(*upper(terms)).astype(BF), axis, bit, count[axis])
        terms = lower(terms) + [arrived]

    kv_grad, out_grad, head_grad = call(
        functools.partial(finish_body, devices),
        [sds((rw, 2 * width), F32), sds((rw, width), F32), sds((rw, channels), F32)],
        (add_up(*terms[:-1]), terms[-1], hp),
    )
    return hidden_grad, kv_grad, out_grad, head_grad


def solution(mesh):
    placed = (
        P("member", "band", None),
        P("band", None),
        P(),
        P(),
        P(),
        P(None, "band"),
        P(None, "band"),
        P("band"),
        P(),
        P(None, "band"),
        P("band", None),
    )
    return jax.shard_map(
        functools.partial(shards, mesh.shape["member"], mesh.shape["band"]),
        mesh=mesh,
        in_specs=placed,
        out_specs=(
            P("member", "band", None),
            P(("member", "band"), None),
            P(("member", "band"), None),
            P(("member", "band"), None),
        ),
        check_vma=False,
    )
```

```python
import functools

import jax
import jax.numpy as jnp
from jax import lax
from jax.experimental import pallas as pl
from jax.experimental.pallas import tpu as pltpu
from jax.sharding import PartitionSpec as P

HEAD_DIM = 64
LANES = 128
GROUPS = 3
ALPHA = 0.95
SOFTENING = 0.5
BF = jnp.bfloat16
F32 = jnp.float32
NN = (((1,), (0,)), ((), ()))
NT = (((1,), (1,)), ((), ()))
TN = (((0,), (0,)), ((), ()))


def mm(a, b, dims=NN):
    return lax.dot_general(a, b, dims, preferred_element_type=F32)


def call(body, out_shape, args, scratch=(), hbm=(), limit=24, flops=1):
    args = [pltpu.with_memory_space_constraint(x, pltpu.HBM) if i in hbm else x for i, x in enumerate(args)]
    return pl.pallas_call(
        body,
        out_shape=out_shape,
        in_specs=[
            pl.BlockSpec(memory_space=pltpu.HBM if i in hbm else pltpu.VMEM) for i in range(len(args))
        ],
        out_specs=jax.tree.map(lambda _: pl.BlockSpec(memory_space=pltpu.VMEM), out_shape),
        scratch_shapes=list(scratch),
        compiler_params=pltpu.CompilerParams(vmem_limit_bytes=limit * 1024 * 1024),
        cost_estimate=pl.CostEstimate(flops=flops, bytes_accessed=1, transcendentals=0),
    )(*args)


def sds(shape, dtype):
    return jax.ShapeDtypeStruct(shape, dtype)


def one_hot_rows(rows, node_count):
    nodes = lax.broadcasted_iota(jnp.int32, (node_count, rows.shape[1]), 0).astype(rows.dtype)
    return (nodes == rows).astype(F32).astype(BF)


def start_copies(pairs, sems):
    copies = [pltpu.make_async_copy(src, dst, sems.at[i]) for i, (src, dst) in enumerate(pairs)]
    for copy in copies:
        copy.start()
    return copies


def halo_lists(halo_ref):
    even = lax.axis_index("band") % 2 == 0
    down, up = halo_ref[0:1, :], halo_ref[1:2, :]
    return jnp.where(even, up, down), jnp.where(even, down, up)


def pick_body(hidden_hbm, halo_hbm, hidden_ref, halo_ref, mate_ref, other_ref, sems):
    for copy in start_copies([(hidden_hbm, hidden_ref), (halo_hbm, halo_ref)], sems):
        copy.wait()
    members, nodes, _ = hidden_ref.shape
    rim = halo_ref.shape[1]
    for rows, out_ref in zip(halo_lists(halo_ref), (mate_ref, other_ref)):
        hot = one_hot_rows(rows, nodes)
        for m in range(members):
            out_ref[m * rim : (m + 1) * rim, :] = mm(hot, hidden_ref[m], TN).astype(BF)


def prepare_body(
    hidden_ref, wo_ref, hp_ref, q_ref, kvw_ref, init_ref, chw_ref, lat_ref,
    kv_ref, pt_ref, p_ref, base_ref, weight_ref, chw_pad, hp_pad,
):
    channels = hp_ref.shape[0]
    hp_pad[...] = jnp.zeros_like(hp_pad)
    hp_pad[0:channels, :] = hp_ref[...].astype(F32)
    hp_t = hp_pad[...].astype(BF)
    chw_pad[:, 0:channels] = jnp.broadcast_to(chw_ref[...], (8, channels))
    weight_ref[...] = chw_pad[...].T[0:channels, 0:1] * lat_ref[...]
    base_ref[...] = mm(hp_t, q_ref[...], NT)
    base_ref[0:channels, :] = base_ref[0:channels, :] + init_ref[...]
    p = mm(hp_t, wo_ref[...], NT)
    p_ref[...] = p.astype(BF)
    pt_ref[...] = p.T.astype(BF)
    hidden = jnp.concatenate([hidden_ref[m] for m in range(hidden_ref.shape[0])], axis=0)
    kv_ref[...] = mm(hidden, kvw_ref[...]).astype(BF)


def split_heads(block):
    low = lax.broadcasted_iota(jnp.int32, block.shape, 1) < HEAD_DIM
    zero = jnp.zeros_like(block)
    return jnp.concatenate([jnp.where(low, block, zero), jnp.where(low, zero, block)], axis=0)


def forward_body(
    send_rows, mate_ref, other_ref, own_ref, kvw_ref, q_ref, src_ref, p_ref,
    value_ref, gate_ref, slope_ref, merged_ref, part_ref, send_ref,
):
    members, ext, width = value_ref.shape
    points = q_ref.shape[0]
    nodes = own_ref.shape[0] // members
    rim = mate_ref.shape[0] // members
    step = 2 * LANES
    halo_rows = jnp.concatenate([mate_ref[...], other_ref[...]], axis=0)

    def project(start):
        halo = mm(halo_rows, kvw_ref[:, start : start + step]).astype(BF)
        result = []
        for m in range(members):
            own = own_ref[m * nodes : (m + 1) * nodes, start : start + step]
            mate = halo[m * rim : (m + 1) * rim]
            other = halo[(members + m) * rim : (members + m + 1) * rim]
            result.append(jnp.concatenate([own, mate, other], axis=0))
        return result

    rows = lax.broadcasted_iota(jnp.int32, (ext, points), 0)
    src = src_ref[...]
    even = lax.axis_index("band") % 2 == 0
    shift = jnp.where(src >= nodes + rim, -rim, jnp.where(src >= nodes, rim, 0))
    src = src + jnp.where(even, shift, 0)
    mask = rows == src[0:1, :]
    for e in range(1, src.shape[0]):
        mask = mask | (rows == src[e : e + 1, :])
    half_mask = jnp.where(mask, 0.5, 0.0).astype(F32)
    half_mask = jnp.concatenate([half_mask, half_mask], axis=0)
    half_scale = 0.5 * HEAD_DIM ** (-0.5)
    low_rows = lax.broadcasted_iota(jnp.int32, (LANES, ext), 0) < HEAD_DIM

    keys, values = {}, {}

    def prepare(block):
        start = block * step
        for m, rows in enumerate(project(start)):
            keys[block, m] = rows
        for m, rows in enumerate(project(width + start)):
            values[block, m] = rows
            value_ref[m, :, start : start + step] = rows

    def scores(pair, m):
        block, at = pair * LANES // step, pair * LANES % step
        q = (q_ref[:, pair * LANES : (pair + 1) * LANES].astype(F32) * half_scale).astype(BF)
        return mm(split_heads(keys[block, m][:, at : at + LANES]), q, NT)

    tasks = [(pair, m) for pair in range(width // LANES) for m in range(members)]
    prepare(0)
    ahead = scores(*tasks[0])
    for i, (pair, m) in enumerate(tasks):
        block, at = pair * LANES // step, pair * LANES % step
        current = ahead
        if at == 0 and m == 0 and (block + 1) * step < width:
            prepare(block + 1)
        if i + 1 < len(tasks):
            ahead = scores(*tasks[i + 1])
        value_t = values[block, m][:, at : at + LANES].astype(F32).T
        zero = jnp.zeros_like(value_t)
        value_t = jnp.concatenate(
            [jnp.where(low_rows, value_t, zero), jnp.where(low_rows, zero, value_t)], axis=1
        ).astype(BF)
        gate = jnp.tanh(current) * half_mask + half_mask
        rounded = gate.astype(BF)
        gate_ref[pair, m] = rounded
        slope_ref[pair, m] = (gate - gate * gate).astype(BF)
        merged_ref[m, pair * LANES : (pair + 1) * LANES, :] = mm(value_t, rounded).astype(BF)
    sent = []
    for m in range(members):
        part = mm(p_ref[...], merged_ref[m])
        part_ref[m] = part
        sent.append(part[0:send_rows])
    filler = send_ref.shape[0] - members * send_rows
    if filler:
        sent.append(jnp.zeros((filler, points), F32))
    send_ref[...] = jnp.concatenate(sent, axis=0).astype(BF)


def halving_orders(n_member, n_band):
    chips = [("band", bit) for bit in range(1, n_band.bit_length() - 1)]
    member = [("member", bit) for bit in range(n_member.bit_length() - 1)]
    turn = chips + member[:1]
    return [turn[i:] + turn[:i] for i in range(GROUPS)], member[1:]


def unit_order(order, n_member, n_band):
    def key(unit):
        return [-((2 * unit[0] if axis == "band" else unit[1]) >> bit & 1) for axis, bit in order]

    return sorted([(c, m) for c in range(n_band // 2) for m in range(n_member)], key=key)


def destination_rows(member, band, n_member, n_band, rw):
    chip, core = band // 2, band % 2
    for rel_core in (1, 0):
        for rel_chip in range(n_band // 2):
            to_band = (chip ^ rel_chip) * 2 + (core ^ rel_core)
            for rel_member in range(n_member):
                yield pl.multiple_of(((member ^ rel_member) * n_band + to_band) * rw, rw)


def reorder(src_ref, n_member, n_band):
    rw = src_ref.shape[0] // (n_member * n_band)
    member, band = lax.axis_index("member"), lax.axis_index("band")
    starts = destination_rows(member, band, n_member, n_band, rw)
    return jnp.concatenate([src_ref[pl.ds(start, rw), :] for start in starts], axis=0)


def store_group(rows, group, n_member, n_band, at, out_refs):
    orders, rest = halving_orders(n_member, n_band)
    units = unit_order(orders[group] + rest, n_member, n_band)
    rw = rows.shape[0] // (n_member * n_band)
    for core, ref in enumerate(out_refs):
        starts = [((core * (n_band // 2) + chip) * n_member + member) * rw for chip, member in units]
        ordered = jnp.concatenate([rows[i : i + rw] for i in starts], axis=0)
        ref[:, at : at + rows.shape[1]] = ordered.astype(BF)


def transpose_body(n_member, n_band, hidden_ref, mate_ref, other_ref, out_ref, turned):
    members, nodes, _ = hidden_ref.shape
    rim = mate_ref.shape[0] // members
    parts = []
    for m in range(members):
        parts.append(hidden_ref[m])
        parts.append(mate_ref[m * rim : (m + 1) * rim, :])
        parts.append(other_ref[m * rim : (m + 1) * rim, :])
    turned[...] = jnp.concatenate(parts, axis=0).astype(F32).T
    out_ref[...] = reorder(turned, n_member, n_band).astype(BF)


def select_heads(block):
    half = block.shape[0] // 2
    low = lax.broadcasted_iota(jnp.int32, (half, block.shape[1]), 1) < HEAD_DIM
    return jnp.where(low, block[:half], block[half:])


def soft_slope(v):
    return v * lax.rsqrt(v * v + SOFTENING * SOFTENING)


def value_body(n_member, n_band, *refs):
    recv_refs = refs[: n_member - 1]
    part_ref, base_ref, truth_ref, weight_ref, pt_ref, gate_ref, ext_ref = refs[n_member - 1 : n_member + 6]
    grad_ref, dm_ref, ng_ref, *out_refs = refs[n_member + 6 :]
    group_width = out_refs[0].shape[1]
    members, width, _ = dm_ref.shape
    ext = ng_ref.shape[0] // members
    channels = truth_ref.shape[0]
    total = members * n_member
    spread = (1.0 - (1.0 - ALPHA) / total) / (total * (total - 1))

    grad_ref[...] = jnp.zeros_like(grad_ref)
    own = [part_ref[m, 0:channels, :] for m in range(members)]
    sent_rows = -(-channels // 8) * 8
    others = []
    for ref in recv_refs:
        rows = ref[...].astype(F32)
        others += [rows[k * sent_rows : k * sent_rows + channels] for k in range(members)]
    for m in range(members):
        slopes = jnp.zeros_like(own[m])
        for k in range(members):
            if k != m:
                slopes = slopes + soft_slope(own[m] - own[k])
        for other in others:
            slopes = slopes + soft_slope(own[m] - other)
        gap = soft_slope(own[m] + base_ref[0:channels, :] - truth_ref[...])
        grad_ref[m, 0:channels, :] = (weight_ref[...] * (gap / total - spread * slopes)).astype(BF)
    for m in range(members):
        dm_ref[m] = mm(pt_ref[...], grad_ref[m]).astype(BF)
    for pair in range(width // LANES):
        cols = slice(pair * LANES, (pair + 1) * LANES)
        for m in range(members):
            result = mm(gate_ref[pair, m], dm_ref[m, cols, :], NT)
            ng_ref[m * ext : (m + 1) * ext, cols] = select_heads(result).astype(BF)
    store_group(mm(ext_ref[...], ng_ref[:, 0:group_width]), 0, n_member, n_band, 0, out_refs)


def key_gradients(pairs, dm_ref, value_ref, slope_ref, q_ref, ng_ref):
    members, ext, _ = value_ref.shape
    scale = HEAD_DIM ** (-0.5)
    for place, pair in enumerate(pairs):
        cols = slice(pair * LANES, (pair + 1) * LANES)
        for m in range(members):
            dgate = mm(split_heads(value_ref[m, :, cols]), dm_ref[m, cols, :])
            dscore = (dgate * slope_ref[pair, m].astype(F32)).astype(BF)
            keys = select_heads(mm(dscore, q_ref[:, cols])) * scale
            ng_ref[m * ext : (m + 1) * ext, place * LANES : (place + 1) * LANES] = keys.astype(BF)


def first_keys_body(
    n_member, n_band, first_value, dm_ref, value_ref, slope_ref, q_ref, ext_ref, ngv_ref, ng_ref, *out_refs
):
    count = ng_ref.shape[1] // LANES
    rest = mm(ext_ref[...], ngv_ref[:, first_value:])
    store_group(rest, 1, n_member, n_band, 0, out_refs)
    key_gradients(range(count), dm_ref, value_ref, slope_ref, q_ref, ng_ref)
    store_group(mm(ext_ref[...], ng_ref[...]), 1, n_member, n_band, rest.shape[1], out_refs)


def last_keys_body(
    n_member, n_band, grad_ref, dm_ref, value_ref, slope_ref, q_ref, merged_ref, wo_ref, ext_ref, ng_ref, *refs
):
    out_refs, turned = refs[:-1], refs[-1]
    members, _, width = value_ref.shape
    count = ng_ref.shape[1] // LANES
    key_gradients(range(width // LANES - count, width // LANES), dm_ref, value_ref, slope_ref, q_ref, ng_ref)
    m_t = sum(mm(grad_ref[m], merged_ref[m], NT) for m in range(members))
    head_t = sum(mm(grad_ref[m], q_ref[...]) for m in range(members)) + mm(m_t.astype(BF), wo_ref[...])
    turned[...] = jnp.concatenate([m_t, head_t], axis=0).T
    store_group(mm(ext_ref[...], ng_ref[...]), 2, n_member, n_band, 0, out_refs)
    store_group(reorder(turned, n_member, n_band), 2, n_member, n_band, ng_ref.shape[1], out_refs)


def extended_grad_body(members, nodes, rim, first_ref, last_ref, ngv_ref, kvw_ref, own_ref, mate_ref, other_ref):
    ext = nodes + 2 * rim
    grads = jnp.concatenate([first_ref[...], last_ref[...], ngv_ref[...]], axis=1)
    rows = mm(grads, kvw_ref[...], NT)
    for m in range(members):
        at = m * ext
        own_ref[m] = rows[at : at + nodes]
        mate_ref[m * rim : (m + 1) * rim, :] = rows[at + nodes : at + nodes + rim].astype(BF)
        other_ref[m * rim : (m + 1) * rim, :] = rows[at + nodes + rim : at + ext].astype(BF)


def hidden_body(own_ref, from_mate_ref, from_other_ref, halo_ref, out_ref):
    members, nodes, _ = own_ref.shape
    rim = halo_ref.shape[1]
    mate, other = [one_hot_rows(rows, nodes) for rows in halo_lists(halo_ref)]
    for m in range(members):
        rows = slice(m * rim, (m + 1) * rim)
        out_ref[m] = own_ref[m] + mm(mate, from_mate_ref[rows, :]) + mm(other, from_other_ref[rows, :])


def finish_body(devices, own_ref, arrived_ref, hp_ref, kv_ref, out_ref, head_ref):
    width = kv_ref.shape[1] // 2
    channels = hp_ref.shape[0]
    total = (own_ref[...] + arrived_ref[...].astype(F32)) * (1.0 / devices)
    kv_ref[:, width:] = total[:, 0:width]
    kv_ref[:, 0:width] = total[:, width : 2 * width]
    m_rows = total[:, 2 * width : 2 * width + channels]
    high = m_rows.astype(BF)
    low = (m_rows - high.astype(F32)).astype(BF)
    out_ref[...] = mm(high, hp_ref[...]) + mm(low, hp_ref[...])
    head_ref[...] = total[:, 2 * width + LANES : 2 * width + LANES + channels]


def add_up(*parts):
    return functools.reduce(lambda a, b: a + b, [p.astype(F32) for p in parts])


def swap(rows, axis, bit, count):
    return lax.ppermute(rows, axis, [(i, i ^ (1 << bit)) for i in range(count)])


def upper(terms):
    return [t[: t.shape[0] // 2] for t in terms]


def lower(terms):
    return [t[t.shape[0] // 2 :] for t in terms]


def shards(
    n_member, n_band,
    hidden, queries, kv_weight, out_weight, head_projection, initial_state, truth,
    latitude_weight, channel_loss_weight, sources, halo_rows,
):
    members, nodes, width = hidden.shape
    points = queries.shape[0]
    channels = head_projection.shape[1]
    rim = halo_rows.shape[1]
    ext = nodes + 2 * rim
    pairs = width // LANES
    devices = n_member * n_band
    rw = width // devices
    chips = n_band // 2
    send_rows = -(-channels // 8) * 8
    mates = [(i, i ^ 1) for i in range(n_band)]
    others = [(i, (i + 1 if i % 2 else i - 1) % n_band) for i in range(n_band)]

    own_hidden, halo, for_mate, for_other = call(
        pick_body,
        [sds(hidden.shape, BF), sds(halo_rows.shape, jnp.int32)] + [sds((members * rim, width), BF)] * 2,
        (hidden, halo_rows),
        [pltpu.SemaphoreType.DMA((2,))],
        hbm=(0, 1),
        flops=10**10,
    )
    mate = lax.ppermute(for_mate, "band", mates)
    other = lax.ppermute(for_other, "band", others)

    hp = head_projection.T
    own_kv, pt, p, base, weight = call(
        prepare_body,
        [
            sds((members * nodes, 2 * width), BF),
            sds((width, LANES), BF),
            sds((LANES, width), BF),
            sds((LANES, points), F32),
            sds((channels, points), F32),
        ],
        (
            own_hidden, out_weight, hp, queries, kv_weight, initial_state,
            channel_loss_weight[None, :], latitude_weight[None, :],
        ),
        [pltpu.VMEM((8, LANES), F32), pltpu.VMEM((LANES, width), F32)],
    )

    value, gates, slopes, merged, part, sent = call(
        functools.partial(forward_body, send_rows),
        [
            sds((members, ext, width), BF),
            sds((pairs, members, 2 * ext, points), BF),
            sds((pairs, members, 2 * ext, points), BF),
            sds((members, width, points), BF),
            sds((members, LANES, points), F32),
            sds((-(-members * send_rows // 16) * 16, points), BF),
        ],
        (mate, other, own_kv, kv_weight, queries, sources, p),
    )

    received = [
        lax.ppermute(sent, "member", [(i, i ^ s) for i in range(n_member)]) for s in range(n_member - 1, 0, -1)
    ]

    ext_t = call(
        functools.partial(transpose_body, n_member, n_band),
        sds((width, members * ext), BF),
        (own_hidden, mate, other),
        [pltpu.VMEM((width, members * ext), F32)],
    )

    extra = 2 * LANES
    group_width = (2 * width + extra) // GROUPS
    first_keys = 2 * group_width - width
    group_shape = [sds((width // 2, group_width), BF)] * 2
    grad, dm, ng_value, send, keep = call(
        functools.partial(value_body, n_member, n_band),
        [sds((members, LANES, points), BF), sds((members, width, points), BF), sds((members * ext, width), BF)]
        + group_shape,
        (*received, part, base, truth, weight, pt, gates, ext_t),
    )
    groups = [[keep, swap(send, "band", 0, n_band)]]
    ng_first, send, keep = call(
        functools.partial(first_keys_body, n_member, n_band, group_width),
        [sds((members * ext, first_keys), BF)] + group_shape,
        (dm, value, slopes, queries, ext_t, ng_value),
    )
    groups.append([keep, swap(send, "band", 0, n_band)])
    ng_last, send, keep = call(
        functools.partial(last_keys_body, n_member, n_band),
        [sds((members * ext, width - first_keys), BF)] + group_shape,
        (grad, dm, value, slopes, queries, merged, out_weight, ext_t),
        [pltpu.VMEM((width, extra), F32)],
    )
    groups.append([keep, swap(send, "band", 0, n_band)])

    count = {"member": n_member, "band": n_band}
    turns, rest = halving_orders(n_member, n_band)
    steps = len(turns[0])
    for step in range(steps):
        outgoing = []
        for i in range(GROUPS):
            outgoing.append(add_up(*upper(groups[i])).astype(BF))
            if step == 0 and i + 1 < GROUPS:
                outgoing[i], groups[i + 1] = lax.optimization_barrier((outgoing[i], groups[i + 1]))
        if step == 0:
            outgoing, ng_last = lax.optimization_barrier((outgoing, ng_last))
            own_grad, back_mate, back_other = call(
                functools.partial(extended_grad_body, members, nodes, rim),
                [sds((members, nodes, width), F32)] + [sds((members * rim, width), BF)] * 2,
                (ng_first, ng_last, ng_value, kv_weight),
            )
        arrived = [swap(out, *turn[step], count[turn[step][0]]) for out, turn in zip(outgoing, turns)]
        if step == 0:
            arrived, back_mate, back_other = lax.optimization_barrier((arrived, back_mate, back_other))
        if step == steps - 1:
            from_mate = lax.ppermute(back_mate, "band", mates)
            from_other = lax.ppermute(back_other, "band", others)
            arrived, from_mate, from_other = lax.optimization_barrier((arrived, from_mate, from_other))
        groups = [lower(terms) + [new] for terms, new in zip(groups, arrived)]
    hidden_grad = call(
        hidden_body,
        sds((members, nodes, width), F32),
        (own_grad, from_mate, from_other, halo),
    )
    terms = [jnp.concatenate([add_up(*group) for group in groups], axis=1)]
    for axis, bit in rest:
        arrived = swap(add_up(*upper(terms)).astype(BF), axis, bit, count[axis])
        terms = lower(terms) + [arrived]

    kv_grad, out_grad, head_grad = call(
        functools.partial(finish_body, devices),
        [sds((rw, 2 * width), F32), sds((rw, width), F32), sds((rw, channels), F32)],
        (add_up(*terms[:-1]), terms[-1], hp),
    )
    return hidden_grad, kv_grad, out_grad, head_grad


def solution(mesh):
    placed = (
        P("member", "band", None),
        P("band", None),
        P(),
        P(),
        P(),
        P(None, "band"),
        P(None, "band"),
        P("band"),
        P(),
        P(None, "band"),
        P("band", None),
    )
    return jax.shard_map(
        functools.partial(shards, mesh.shape["member"], mesh.shape["band"]),
        mesh=mesh,
        in_specs=placed,
        out_specs=(
            P("member", "band", None),
            P(("member", "band"), None),
            P(("member", "band"), None),
            P(("member", "band"), None),
        ),
        check_vma=False,
    )
```

```python
import functools

import jax
import jax.numpy as jnp
from jax import lax
from jax.experimental import pallas as pl
from jax.experimental.pallas import tpu as pltpu
from jax.sharding import PartitionSpec as P

HEAD_DIM = 64
LANES = 128
GROUPS = 3
ALPHA = 0.95
SOFTENING = 0.5
BF = jnp.bfloat16
F32 = jnp.float32
NN = (((1,), (0,)), ((), ()))
NT = (((1,), (1,)), ((), ()))
TN = (((0,), (0,)), ((), ()))


def mm(a, b, dims=NN):
    return lax.dot_general(a, b, dims, preferred_element_type=F32)


def call(body, out_shape, args, scratch=(), hbm=(), limit=24, flops=1):
    args = [pltpu.with_memory_space_constraint(x, pltpu.HBM) if i in hbm else x for i, x in enumerate(args)]
    return pl.pallas_call(
        body,
        out_shape=out_shape,
        in_specs=[
            pl.BlockSpec(memory_space=pltpu.HBM if i in hbm else pltpu.VMEM) for i in range(len(args))
        ],
        out_specs=jax.tree.map(lambda _: pl.BlockSpec(memory_space=pltpu.VMEM), out_shape),
        scratch_shapes=list(scratch),
        compiler_params=pltpu.CompilerParams(vmem_limit_bytes=limit * 1024 * 1024),
        cost_estimate=pl.CostEstimate(flops=flops, bytes_accessed=1, transcendentals=0),
    )(*args)


def sds(shape, dtype):
    return jax.ShapeDtypeStruct(shape, dtype)


def one_hot_rows(rows, node_count):
    nodes = lax.broadcasted_iota(jnp.int32, (node_count, rows.shape[1]), 0).astype(rows.dtype)
    return (nodes == rows).astype(F32).astype(BF)


def start_copies(pairs, sems):
    copies = [pltpu.make_async_copy(src, dst, sems.at[i]) for i, (src, dst) in enumerate(pairs)]
    for copy in copies:
        copy.start()
    return copies


def halo_lists(halo_ref):
    even = lax.axis_index("band") % 2 == 0
    down, up = halo_ref[0:1, :], halo_ref[1:2, :]
    return jnp.where(even, up, down), jnp.where(even, down, up)


def pick_body(hidden_hbm, halo_hbm, hidden_ref, halo_ref, mate_ref, other_ref, sems):
    for copy in start_copies([(hidden_hbm, hidden_ref), (halo_hbm, halo_ref)], sems):
        copy.wait()
    members, nodes, _ = hidden_ref.shape
    rim = halo_ref.shape[1]
    for rows, out_ref in zip(halo_lists(halo_ref), (mate_ref, other_ref)):
        hot = one_hot_rows(rows, nodes)
        for m in range(members):
            out_ref[m * rim : (m + 1) * rim, :] = mm(hot, hidden_ref[m], TN).astype(BF)


def prepare_body(
    hidden_ref, wo_ref, hp_ref, q_ref, kvw_ref, init_ref, chw_ref, lat_ref,
    kv_ref, pt_ref, p_ref, base_ref, weight_ref, chw_pad, hp_pad,
):
    channels = hp_ref.shape[0]
    hp_pad[...] = jnp.zeros_like(hp_pad)
    hp_pad[0:channels, :] = hp_ref[...].astype(F32)
    hp_t = hp_pad[...].astype(BF)
    chw_pad[:, 0:channels] = jnp.broadcast_to(chw_ref[...], (8, channels))
    weight_ref[...] = chw_pad[...].T[0:channels, 0:1] * lat_ref[...]
    base_ref[...] = mm(hp_t, q_ref[...], NT)
    base_ref[0:channels, :] = base_ref[0:channels, :] + init_ref[...]
    p = mm(hp_t, wo_ref[...], NT)
    p_ref[...] = p.astype(BF)
    pt_ref[...] = p.T.astype(BF)
    hidden = jnp.concatenate([hidden_ref[m] for m in range(hidden_ref.shape[0])], axis=0)
    kv_ref[...] = mm(hidden, kvw_ref[...]).astype(BF)


def split_heads(block):
    low = lax.broadcasted_iota(jnp.int32, block.shape, 1) < HEAD_DIM
    zero = jnp.zeros_like(block)
    return jnp.concatenate([jnp.where(low, block, zero), jnp.where(low, zero, block)], axis=0)


def forward_body(
    send_rows, mate_ref, other_ref, own_ref, kvw_ref, q_ref, src_ref, p_ref,
    value_ref, gate_ref, slope_ref, merged_ref, part_ref, send_ref,
):
    members, ext, width = value_ref.shape
    points = q_ref.shape[0]
    nodes = own_ref.shape[0] // members
    rim = mate_ref.shape[0] // members
    step = 2 * LANES
    halo_rows = jnp.concatenate([mate_ref[...], other_ref[...]], axis=0)

    def project(start):
        halo = mm(halo_rows, kvw_ref[:, start : start + step]).astype(BF)
        result = []
        for m in range(members):
            own = own_ref[m * nodes : (m + 1) * nodes, start : start + step]
            mate = halo[m * rim : (m + 1) * rim]
            other = halo[(members + m) * rim : (members + m + 1) * rim]
            result.append(jnp.concatenate([own, mate, other], axis=0))
        return result

    rows = lax.broadcasted_iota(jnp.int32, (ext, points), 0)
    src = src_ref[...]
    even = lax.axis_index("band") % 2 == 0
    shift = jnp.where(src >= nodes + rim, -rim, jnp.where(src >= nodes, rim, 0))
    src = src + jnp.where(even, shift, 0)
    mask = rows == src[0:1, :]
    for e in range(1, src.shape[0]):
        mask = mask | (rows == src[e : e + 1, :])
    half_mask = jnp.where(mask, 0.5, 0.0).astype(F32)
    half_mask = jnp.concatenate([half_mask, half_mask], axis=0)
    half_scale = 0.5 * HEAD_DIM ** (-0.5)
    low_rows = lax.broadcasted_iota(jnp.int32, (LANES, ext), 0) < HEAD_DIM

    keys, values = {}, {}

    def prepare(block):
        start = block * step
        for m, rows in enumerate(project(start)):
            keys[block, m] = rows
        for m, rows in enumerate(project(width + start)):
            values[block, m] = rows
            value_ref[m, :, start : start + step] = rows

    def scores(pair, m):
        block, at = pair * LANES // step, pair * LANES % step
        q = (q_ref[:, pair * LANES : (pair + 1) * LANES].astype(F32) * half_scale).astype(BF)
        return mm(split_heads(keys[block, m][:, at : at + LANES]), q, NT)

    tasks = [(pair, m) for pair in range(width // LANES) for m in range(members)]
    prepare(0)
    ahead = scores(*tasks[0])
    for i, (pair, m) in enumerate(tasks):
        block, at = pair * LANES // step, pair * LANES % step
        current = ahead
        if at == 0 and m == 0 and (block + 1) * step < width:
            prepare(block + 1)
        if i + 1 < len(tasks):
            ahead = scores(*tasks[i + 1])
        value_t = values[block, m][:, at : at + LANES].astype(F32).T
        zero = jnp.zeros_like(value_t)
        value_t = jnp.concatenate(
            [jnp.where(low_rows, value_t, zero), jnp.where(low_rows, zero, value_t)], axis=1
        ).astype(BF)
        gate = jnp.tanh(current) * half_mask + half_mask
        rounded = gate.astype(BF)
        gate_ref[pair, m] = rounded
        slope_ref[pair, m] = (gate - gate * gate).astype(BF)
        merged_ref[m, pair * LANES : (pair + 1) * LANES, :] = mm(value_t, rounded).astype(BF)
    sent = []
    for m in range(members):
        part = mm(p_ref[...], merged_ref[m])
        part_ref[m] = part
        sent.append(part[0:send_rows])
    filler = send_ref.shape[0] - members * send_rows
    if filler:
        sent.append(jnp.zeros((filler, points), F32))
    send_ref[...] = jnp.concatenate(sent, axis=0).astype(BF)


def halving_orders(n_member, n_band):
    chips = [("band", bit) for bit in range(1, n_band.bit_length() - 1)]
    member = [("member", bit) for bit in range(n_member.bit_length() - 1)]
    turn = chips + member[:1]
    return [turn[i:] + turn[:i] for i in range(GROUPS)], member[1:]


def unit_order(order, n_member, n_band):
    def key(unit):
        return [-((2 * unit[0] if axis == "band" else unit[1]) >> bit & 1) for axis, bit in order]

    return sorted([(c, m) for c in range(n_band // 2) for m in range(n_member)], key=key)


def destination_rows(member, band, n_member, n_band, rw):
    chip, core = band // 2, band % 2
    for rel_core in (1, 0):
        for rel_chip in range(n_band // 2):
            to_band = (chip ^ rel_chip) * 2 + (core ^ rel_core)
            for rel_member in range(n_member):
                yield pl.multiple_of(((member ^ rel_member) * n_band + to_band) * rw, rw)


def reorder(src_ref, n_member, n_band):
    rw = src_ref.shape[0] // (n_member * n_band)
    member, band = lax.axis_index("member"), lax.axis_index("band")
    starts = destination_rows(member, band, n_member, n_band, rw)
    return jnp.concatenate([src_ref[pl.ds(start, rw), :] for start in starts], axis=0)


def store_group(rows, group, n_member, n_band, at, out_refs):
    orders, rest = halving_orders(n_member, n_band)
    units = unit_order(orders[group] + rest, n_member, n_band)
    rw = rows.shape[0] // (n_member * n_band)
    for core, ref in enumerate(out_refs):
        starts = [((core * (n_band // 2) + chip) * n_member + member) * rw for chip, member in units]
        ordered = jnp.concatenate([rows[i : i + rw] for i in starts], axis=0)
        ref[:, at : at + rows.shape[1]] = ordered.astype(BF)


def transpose_body(n_member, n_band, hidden_ref, mate_ref, other_ref, out_ref, turned):
    members, nodes, _ = hidden_ref.shape
    rim = mate_ref.shape[0] // members
    parts = []
    for m in range(members):
        parts.append(hidden_ref[m])
        parts.append(mate_ref[m * rim : (m + 1) * rim, :])
        parts.append(other_ref[m * rim : (m + 1) * rim, :])
    turned[...] = jnp.concatenate(parts, axis=0).astype(F32).T
    out_ref[...] = reorder(turned, n_member, n_band).astype(BF)


def select_heads(block):
    half = block.shape[0] // 2
    low = lax.broadcasted_iota(jnp.int32, (half, block.shape[1]), 1) < HEAD_DIM
    return jnp.where(low, block[:half], block[half:])


def soft_slope(v):
    return v * lax.rsqrt(v * v + SOFTENING * SOFTENING)


def value_body(n_member, n_band, *refs):
    recv_refs = refs[: n_member - 1]
    part_ref, base_ref, truth_ref, weight_ref, pt_ref, gate_ref, ext_ref = refs[n_member - 1 : n_member + 6]
    grad_ref, dm_ref, ng_ref, *out_refs = refs[n_member + 6 :]
    group_width = out_refs[0].shape[1]
    members, width, _ = dm_ref.shape
    ext = ng_ref.shape[0] // members
    channels = truth_ref.shape[0]
    total = members * n_member
    spread = (1.0 - (1.0 - ALPHA) / total) / (total * (total - 1))

    grad_ref[...] = jnp.zeros_like(grad_ref)
    own = [part_ref[m, 0:channels, :] for m in range(members)]
    sent_rows = -(-channels // 8) * 8
    others = []
    for ref in recv_refs:
        rows = ref[...].astype(F32)
        others += [rows[k * sent_rows : k * sent_rows + channels] for k in range(members)]
    for m in range(members):
        slopes = jnp.zeros_like(own[m])
        for k in range(members):
            if k != m:
                slopes = slopes + soft_slope(own[m] - own[k])
        for other in others:
            slopes = slopes + soft_slope(own[m] - other)
        gap = soft_slope(own[m] + base_ref[0:channels, :] - truth_ref[...])
        grad_ref[m, 0:channels, :] = (weight_ref[...] * (gap / total - spread * slopes)).astype(BF)
    for m in range(members):
        dm_ref[m] = mm(pt_ref[...], grad_ref[m]).astype(BF)
    for pair in range(width // LANES):
        cols = slice(pair * LANES, (pair + 1) * LANES)
        for m in range(members):
            result = mm(gate_ref[pair, m], dm_ref[m, cols, :], NT)
            ng_ref[m * ext : (m + 1) * ext, cols] = select_heads(result).astype(BF)
    store_group(mm(ext_ref[...], ng_ref[:, 0:group_width]), 0, n_member, n_band, 0, out_refs)


def key_gradients(pairs, dm_ref, value_ref, slope_ref, q_ref, ng_ref):
    members, ext, _ = value_ref.shape
    scale = HEAD_DIM ** (-0.5)
    for place, pair in enumerate(pairs):
        cols = slice(pair * LANES, (pair + 1) * LANES)
        for m in range(members):
            dgate = mm(split_heads(value_ref[m, :, cols]), dm_ref[m, cols, :])
            dscore = (dgate * slope_ref[pair, m].astype(F32)).astype(BF)
            keys = select_heads(mm(dscore, q_ref[:, cols])) * scale
            ng_ref[m * ext : (m + 1) * ext, place * LANES : (place + 1) * LANES] = keys.astype(BF)


def first_keys_body(
    n_member, n_band, first_value, dm_ref, value_ref, slope_ref, q_ref, ext_ref, ngv_ref, ng_ref, *out_refs
):
    count = ng_ref.shape[1] // LANES
    rest = mm(ext_ref[...], ngv_ref[:, first_value:])
    store_group(rest, 1, n_member, n_band, 0, out_refs)
    key_gradients(range(count), dm_ref, value_ref, slope_ref, q_ref, ng_ref)
    store_group(mm(ext_ref[...], ng_ref[...]), 1, n_member, n_band, rest.shape[1], out_refs)


def last_keys_body(
    n_member, n_band, grad_ref, dm_ref, value_ref, slope_ref, q_ref, merged_ref, wo_ref, ext_ref, ng_ref, *refs
):
    out_refs, turned = refs[:-1], refs[-1]
    members, _, width = value_ref.shape
    count = ng_ref.shape[1] // LANES
    key_gradients(range(width // LANES - count, width // LANES), dm_ref, value_ref, slope_ref, q_ref, ng_ref)
    m_t = sum(mm(grad_ref[m], merged_ref[m], NT) for m in range(members))
    head_t = sum(mm(grad_ref[m], q_ref[...]) for m in range(members)) + mm(m_t.astype(BF), wo_ref[...])
    turned[...] = jnp.concatenate([m_t, head_t], axis=0).T
    store_group(mm(ext_ref[...], ng_ref[...]), 2, n_member, n_band, 0, out_refs)
    store_group(reorder(turned, n_member, n_band), 2, n_member, n_band, ng_ref.shape[1], out_refs)


def extended_grad_body(members, nodes, rim, first_ref, last_ref, ngv_ref, kvw_ref, own_ref, mate_ref, other_ref):
    ext = nodes + 2 * rim
    grads = jnp.concatenate([first_ref[...], last_ref[...], ngv_ref[...]], axis=1)
    rows = mm(grads, kvw_ref[...], NT)
    for m in range(members):
        at = m * ext
        own_ref[m] = rows[at : at + nodes]
        mate_ref[m * rim : (m + 1) * rim, :] = rows[at + nodes : at + nodes + rim].astype(BF)
        other_ref[m * rim : (m + 1) * rim, :] = rows[at + nodes + rim : at + ext].astype(BF)


def hidden_body(own_ref, from_mate_ref, from_other_ref, halo_ref, out_ref):
    members, nodes, _ = own_ref.shape
    rim = halo_ref.shape[1]
    mate, other = [one_hot_rows(rows, nodes) for rows in halo_lists(halo_ref)]
    for m in range(members):
        rows = slice(m * rim, (m + 1) * rim)
        out_ref[m] = own_ref[m] + mm(mate, from_mate_ref[rows, :]) + mm(other, from_other_ref[rows, :])


def finish_body(devices, own_ref, arrived_ref, hp_ref, kv_ref, out_ref, head_ref):
    width = kv_ref.shape[1] // 2
    channels = hp_ref.shape[0]
    total = (own_ref[...] + arrived_ref[...].astype(F32)) * (1.0 / devices)
    kv_ref[:, width:] = total[:, 0:width]
    kv_ref[:, 0:width] = total[:, width : 2 * width]
    m_rows = total[:, 2 * width : 2 * width + channels]
    high = m_rows.astype(BF)
    low = (m_rows - high.astype(F32)).astype(BF)
    out_ref[...] = mm(high, hp_ref[...]) + mm(low, hp_ref[...])
    head_ref[...] = total[:, 2 * width + LANES : 2 * width + LANES + channels]


def add_up(*parts):
    return functools.reduce(lambda a, b: a + b, [p.astype(F32) for p in parts])


def swap(rows, axis, bit, count):
    return lax.ppermute(rows, axis, [(i, i ^ (1 << bit)) for i in range(count)])


def upper(terms):
    return [t[: t.shape[0] // 2] for t in terms]


def lower(terms):
    return [t[t.shape[0] // 2 :] for t in terms]


def shards(
    n_member, n_band,
    hidden, queries, kv_weight, out_weight, head_projection, initial_state, truth,
    latitude_weight, channel_loss_weight, sources, halo_rows,
):
    members, nodes, width = hidden.shape
    points = queries.shape[0]
    channels = head_projection.shape[1]
    rim = halo_rows.shape[1]
    ext = nodes + 2 * rim
    pairs = width // LANES
    devices = n_member * n_band
    rw = width // devices
    chips = n_band // 2
    send_rows = -(-channels // 8) * 8
    mates = [(i, i ^ 1) for i in range(n_band)]
    others = [(i, (i + 1 if i % 2 else i - 1) % n_band) for i in range(n_band)]

    own_hidden, halo, for_mate, for_other = call(
        pick_body,
        [sds(hidden.shape, BF), sds(halo_rows.shape, jnp.int32)] + [sds((members * rim, width), BF)] * 2,
        (hidden, halo_rows),
        [pltpu.SemaphoreType.DMA((2,))],
        hbm=(0, 1),
        flops=10**10,
    )
    mate = lax.ppermute(for_mate, "band", mates)
    other = lax.ppermute(for_other, "band", others)

    hp = head_projection.T
    own_kv, pt, p, base, weight = call(
        prepare_body,
        [
            sds((members * nodes, 2 * width), BF),
            sds((width, LANES), BF),
            sds((LANES, width), BF),
            sds((LANES, points), F32),
            sds((channels, points), F32),
        ],
        (
            own_hidden, out_weight, hp, queries, kv_weight, initial_state,
            channel_loss_weight[None, :], latitude_weight[None, :],
        ),
        [pltpu.VMEM((8, LANES), F32), pltpu.VMEM((LANES, width), F32)],
    )

    value, gates, slopes, merged, part, sent = call(
        functools.partial(forward_body, send_rows),
        [
            sds((members, ext, width), BF),
            sds((pairs, members, 2 * ext, points), BF),
            sds((pairs, members, 2 * ext, points), BF),
            sds((members, width, points), BF),
            sds((members, LANES, points), F32),
            sds((-(-members * send_rows // 16) * 16, points), BF),
        ],
        (mate, other, own_kv, kv_weight, queries, sources, p),
    )

    received = [
        lax.ppermute(sent, "member", [(i, i ^ s) for i in range(n_member)]) for s in range(n_member - 1, 0, -1)
    ]

    ext_t = call(
        functools.partial(transpose_body, n_member, n_band),
        sds((width, members * ext), BF),
        (own_hidden, mate, other),
        [pltpu.VMEM((width, members * ext), F32)],
    )

    extra = 2 * LANES
    group_width = (2 * width + extra) // GROUPS
    first_keys = 2 * group_width - width
    group_shape = [sds((width // 2, group_width), BF)] * 2
    grad, dm, ng_value, send, keep = call(
        functools.partial(value_body, n_member, n_band),
        [sds((members, LANES, points), BF), sds((members, width, points), BF), sds((members * ext, width), BF)]
        + group_shape,
        (*received, part, base, truth, weight, pt, gates, ext_t),
    )
    groups = [[keep, swap(send, "band", 0, n_band)]]
    ng_first, send, keep = call(
        functools.partial(first_keys_body, n_member, n_band, group_width),
        [sds((members * ext, first_keys), BF)] + group_shape,
        (dm, value, slopes, queries, ext_t, ng_value),
    )
    groups.append([keep, swap(send, "band", 0, n_band)])
    ng_last, send, keep = call(
        functools.partial(last_keys_body, n_member, n_band),
        [sds((members * ext, width - first_keys), BF)] + group_shape,
        (grad, dm, value, slopes, queries, merged, out_weight, ext_t),
        [pltpu.VMEM((width, extra), F32)],
    )
    groups.append([keep, swap(send, "band", 0, n_band)])

    count = {"member": n_member, "band": n_band}
    turns, rest = halving_orders(n_member, n_band)
    steps = len(turns[0])
    for step in range(steps):
        outgoing = []
        for i in range(GROUPS):
            outgoing.append(add_up(*upper(groups[i])).astype(BF))
            if step == 0 and i + 1 < GROUPS:
                outgoing[i], groups[i + 1] = lax.optimization_barrier((outgoing[i], groups[i + 1]))
        if step == 0:
            outgoing, ng_last = lax.optimization_barrier((outgoing, ng_last))
            own_grad, back_mate, back_other = call(
                functools.partial(extended_grad_body, members, nodes, rim),
                [sds((members, nodes, width), F32)] + [sds((members * rim, width), BF)] * 2,
                (ng_first, ng_last, ng_value, kv_weight),
            )
        arrived = [swap(out, *turn[step], count[turn[step][0]]) for out, turn in zip(outgoing, turns)]
        if step == 0:
            from_mate = lax.ppermute(back_mate, "band", mates)
            arrived, from_mate, back_other = lax.optimization_barrier((arrived, from_mate, back_other))
        if step == steps - 1:
            arrived, back_other = lax.optimization_barrier((arrived, back_other))
            from_other = lax.ppermute(back_other, "band", others)
        groups = [lower(terms) + [new] for terms, new in zip(groups, arrived)]
    hidden_grad = call(
        hidden_body,
        sds((members, nodes, width), F32),
        (own_grad, from_mate, from_other, halo),
    )
    terms = [jnp.concatenate([add_up(*group) for group in groups], axis=1)]
    for axis, bit in rest:
        arrived = swap(add_up(*upper(terms)).astype(BF), axis, bit, count[axis])
        terms = lower(terms) + [arrived]

    kv_grad, out_grad, head_grad = call(
        functools.partial(finish_body, devices),
        [sds((rw, 2 * width), F32), sds((rw, width), F32), sds((rw, channels), F32)],
        (add_up(*terms[:-1]), terms[-1], hp),
    )
    return hidden_grad, kv_grad, out_grad, head_grad


def solution(mesh):
    placed = (
        P("member", "band", None),
        P("band", None),
        P(),
        P(),
        P(),
        P(None, "band"),
        P(None, "band"),
        P("band"),
        P(),
        P(None, "band"),
        P("band", None),
    )
    return jax.shard_map(
        functools.partial(shards, mesh.shape["member"], mesh.shape["band"]),
        mesh=mesh,
        in_specs=placed,
        out_specs=(
            P("member", "band", None),
            P(("member", "band"), None),
            P(("member", "band"), None),
            P(("member", "band"), None),
        ),
        check_vma=False,
    )
```

```python
import functools

import jax
import jax.numpy as jnp
from jax import lax
from jax.experimental import pallas as pl
from jax.experimental.pallas import tpu as pltpu
from jax.sharding import PartitionSpec as P

HEAD_DIM = 64
LANES = 128
GROUPS = 3
ALPHA = 0.95
SOFTENING = 0.5
BF = jnp.bfloat16
F32 = jnp.float32
NN = (((1,), (0,)), ((), ()))
NT = (((1,), (1,)), ((), ()))
TN = (((0,), (0,)), ((), ()))


def mm(a, b, dims=NN):
    return lax.dot_general(a, b, dims, preferred_element_type=F32)


def call(body, out_shape, args, scratch=(), hbm=(), limit=24, flops=1):
    args = [pltpu.with_memory_space_constraint(x, pltpu.HBM) if i in hbm else x for i, x in enumerate(args)]
    return pl.pallas_call(
        body,
        out_shape=out_shape,
        in_specs=[
            pl.BlockSpec(memory_space=pltpu.HBM if i in hbm else pltpu.VMEM) for i in range(len(args))
        ],
        out_specs=jax.tree.map(lambda _: pl.BlockSpec(memory_space=pltpu.VMEM), out_shape),
        scratch_shapes=list(scratch),
        compiler_params=pltpu.CompilerParams(vmem_limit_bytes=limit * 1024 * 1024),
        cost_estimate=pl.CostEstimate(flops=flops, bytes_accessed=1, transcendentals=0),
    )(*args)


def sds(shape, dtype):
    return jax.ShapeDtypeStruct(shape, dtype)


def one_hot_rows(rows, node_count):
    nodes = lax.broadcasted_iota(jnp.int32, (node_count, rows.shape[1]), 0).astype(rows.dtype)
    return (nodes == rows).astype(F32).astype(BF)


def start_copies(pairs, sems):
    copies = [pltpu.make_async_copy(src, dst, sems.at[i]) for i, (src, dst) in enumerate(pairs)]
    for copy in copies:
        copy.start()
    return copies


def halo_lists(halo_ref):
    even = lax.axis_index("band") % 2 == 0
    down, up = halo_ref[0:1, :], halo_ref[1:2, :]
    return jnp.where(even, up, down), jnp.where(even, down, up)


def pick_body(hidden_hbm, halo_hbm, hidden_ref, halo_ref, mate_ref, other_ref, sems):
    for copy in start_copies([(hidden_hbm, hidden_ref), (halo_hbm, halo_ref)], sems):
        copy.wait()
    members, nodes, _ = hidden_ref.shape
    rim = halo_ref.shape[1]
    for rows, out_ref in zip(halo_lists(halo_ref), (mate_ref, other_ref)):
        hot = one_hot_rows(rows, nodes)
        for m in range(members):
            out_ref[m * rim : (m + 1) * rim, :] = mm(hot, hidden_ref[m], TN).astype(BF)


def split_heads(block):
    low = lax.broadcasted_iota(jnp.int32, block.shape, 1) < HEAD_DIM
    zero = jnp.zeros_like(block)
    return jnp.concatenate([jnp.where(low, block, zero), jnp.where(low, zero, block)], axis=0)


def half_mask_of(src, first, count):
    rows = lax.broadcasted_iota(jnp.int32, (count, src.shape[1]), 0) + first
    mask = rows == src[0:1, :]
    for e in range(1, src.shape[0]):
        mask = mask | (rows == src[e : e + 1, :])
    half = jnp.where(mask, 0.5, 0.0).astype(F32)
    return jnp.concatenate([half, half], axis=0)


def gate_rows(tasks, keys, values, q_ref, half_mask, gate_ref, slope_ref, store_merged):
    half_scale = 0.5 * HEAD_DIM ** (-0.5)

    def scores(pair, m):
        q = (q_ref[:, pair * LANES : (pair + 1) * LANES].astype(F32) * half_scale).astype(BF)
        return mm(split_heads(keys(pair, m)), q, NT)

    ahead = scores(*tasks[0])
    for i, (pair, m) in enumerate(tasks):
        current = ahead
        if i + 1 < len(tasks):
            ahead = scores(*tasks[i + 1])
        turned = split_heads(values(pair, m)).astype(F32).T.astype(BF)
        gate = jnp.tanh(current) * half_mask + half_mask
        rounded = gate.astype(BF)
        gate_ref[pair, m] = rounded
        slope_ref[pair, m] = (gate - gate * gate).astype(BF)
        store_merged(pair, m, mm(turned, rounded))


def tasks_of(width, members):
    return [(pair, m) for pair in range(width // LANES) for m in range(members)]


def own_body(
    hidden_ref, wo_ref, hp_ref, q_ref, kvw_ref, init_ref, chw_ref, lat_ref, src_ref,
    value_ref, gate_ref, slope_ref, merged_ref, pt_ref, p_ref, base_ref, weight_ref, chw_pad, hp_pad,
):
    channels = hp_ref.shape[0]
    members, nodes, width = hidden_ref.shape
    hidden = jnp.concatenate([hidden_ref[m] for m in range(members)], axis=0)
    rows = mm(hidden, kvw_ref[...]).astype(BF)

    def part(pair, m, first):
        at = first + pair * LANES
        return rows[m * nodes : (m + 1) * nodes, at : at + LANES]

    def store_merged(pair, m, result):
        merged_ref[m, pair * LANES : (pair + 1) * LANES, :] = result

    for m in range(members):
        value_ref[m] = rows[m * nodes : (m + 1) * nodes, width:]
    gate_rows(
        tasks_of(width, members),
        lambda pair, m: part(pair, m, 0),
        lambda pair, m: part(pair, m, width),
        q_ref, half_mask_of(src_ref[...], 0, nodes), gate_ref, slope_ref, store_merged,
    )
    hp_pad[...] = jnp.zeros_like(hp_pad)
    hp_pad[0:channels, :] = hp_ref[...].astype(F32)
    hp_t = hp_pad[...].astype(BF)
    chw_pad[:, 0:channels] = jnp.broadcast_to(chw_ref[...], (8, channels))
    weight_ref[...] = chw_pad[...].T[0:channels, 0:1] * lat_ref[...]
    base_ref[...] = mm(hp_t, q_ref[...], NT)
    base_ref[0:channels, :] = base_ref[0:channels, :] + init_ref[...]
    p = mm(hp_t, wo_ref[...], NT)
    p_ref[...] = p.astype(BF)
    pt_ref[...] = p.T.astype(BF)


def halo_body(
    send_rows, nodes, other_ref, mate_ref, own_ref, kvw_ref, q_ref, src_ref, p_ref,
    value_ref, gate_ref, slope_ref, merged_ref, part_ref, send_ref,
):
    members, count, width = value_ref.shape
    points = q_ref.shape[0]
    rim = count // 2
    step = 2 * LANES
    halo_rows = jnp.concatenate([mate_ref[...], other_ref[...]], axis=0)

    src = src_ref[...]
    even = lax.axis_index("band") % 2 == 0
    shift = jnp.where(src >= nodes + rim, -rim, jnp.where(src >= nodes, rim, 0))
    src = src + jnp.where(even, shift, 0)
    held = {}

    def rows(pair, m, first):
        start = first + pair * LANES // step * step
        if start not in held:
            held[start] = mm(halo_rows, kvw_ref[:, start : start + step]).astype(BF)
        at = pair * LANES % step
        block = held[start][:, at : at + LANES]
        mate = block[m * rim : (m + 1) * rim]
        other = block[(members + m) * rim : (members + m + 1) * rim]
        return jnp.concatenate([mate, other], axis=0)

    def values(pair, m):
        result = rows(pair, m, width)
        value_ref[m, :, pair * LANES : (pair + 1) * LANES] = result
        return result

    def store_merged(pair, m, result):
        cols = slice(pair * LANES, (pair + 1) * LANES)
        merged_ref[m, cols, :] = (own_ref[m, cols, :] + result).astype(BF)

    gate_rows(
        tasks_of(width, members), lambda pair, m: rows(pair, m, 0), values,
        q_ref, half_mask_of(src, nodes, count), gate_ref, slope_ref, store_merged,
    )
    sent = []
    for m in range(members):
        part = mm(p_ref[...], merged_ref[m])
        part_ref[m] = part
        sent.append(part[0:send_rows])
    filler = send_ref.shape[0] - members * send_rows
    if filler:
        sent.append(jnp.zeros((filler, points), F32))
    send_ref[...] = jnp.concatenate(sent, axis=0).astype(BF)


def halving_orders(n_member, n_band):
    chips = [("band", bit) for bit in range(1, n_band.bit_length() - 1)]
    member = [("member", bit) for bit in range(n_member.bit_length() - 1)]
    turn = chips + member[:1]
    return [turn[i:] + turn[:i] for i in range(GROUPS)], member[1:]


def unit_order(order, n_member, n_band):
    def key(unit):
        return [-((2 * unit[0] if axis == "band" else unit[1]) >> bit & 1) for axis, bit in order]

    return sorted([(c, m) for c in range(n_band // 2) for m in range(n_member)], key=key)


def destination_rows(member, band, n_member, n_band, rw):
    chip, core = band // 2, band % 2
    for rel_core in (1, 0):
        for rel_chip in range(n_band // 2):
            to_band = (chip ^ rel_chip) * 2 + (core ^ rel_core)
            for rel_member in range(n_member):
                yield pl.multiple_of(((member ^ rel_member) * n_band + to_band) * rw, rw)


def reorder(src_ref, n_member, n_band):
    rw = src_ref.shape[0] // (n_member * n_band)
    member, band = lax.axis_index("member"), lax.axis_index("band")
    starts = destination_rows(member, band, n_member, n_band, rw)
    return jnp.concatenate([src_ref[pl.ds(start, rw), :] for start in starts], axis=0)


def store_group(rows, group, n_member, n_band, at, out_refs):
    orders, rest = halving_orders(n_member, n_band)
    units = unit_order(orders[group] + rest, n_member, n_band)
    rw = rows.shape[0] // (n_member * n_band)
    for core, ref in enumerate(out_refs):
        starts = [((core * (n_band // 2) + chip) * n_member + member) * rw for chip, member in units]
        ordered = jnp.concatenate([rows[i : i + rw] for i in starts], axis=0)
        ref[:, at : at + rows.shape[1]] = ordered.astype(BF)


def transpose_body(n_member, n_band, hidden_ref, mate_ref, other_ref, out_ref, turned):
    members, nodes, _ = hidden_ref.shape
    rim = mate_ref.shape[0] // members
    parts = []
    for m in range(members):
        parts.append(hidden_ref[m])
        parts.append(mate_ref[m * rim : (m + 1) * rim, :])
        parts.append(other_ref[m * rim : (m + 1) * rim, :])
    turned[...] = jnp.concatenate(parts, axis=0).astype(F32).T
    out_ref[...] = reorder(turned, n_member, n_band).astype(BF)


def select_heads(block):
    half = block.shape[0] // 2
    low = lax.broadcasted_iota(jnp.int32, (half, block.shape[1]), 1) < HEAD_DIM
    return jnp.where(low, block[:half], block[half:])


def joined(refs, pair, m):
    return jnp.concatenate([ref[pair, m] for ref in refs], axis=0)


def select_rows(block, own):
    return jnp.concatenate([select_heads(block[: 2 * own]), select_heads(block[2 * own :])], axis=0)


def soft_slope(v):
    return v * lax.rsqrt(v * v + SOFTENING * SOFTENING)


def value_body(n_member, n_band, *refs):
    recv_refs = refs[: n_member - 1]
    part_ref, base_ref, truth_ref, weight_ref, pt_ref, *gate_refs, ext_ref = refs[n_member - 1 : n_member + 7]
    grad_ref, dm_ref, ng_ref, *out_refs = refs[n_member + 7 :]
    own_rows = gate_refs[0].shape[2] // 2
    group_width = out_refs[0].shape[1]
    members, width, _ = dm_ref.shape
    ext = ng_ref.shape[0] // members
    channels = truth_ref.shape[0]
    total = members * n_member
    spread = (1.0 - (1.0 - ALPHA) / total) / (total * (total - 1))

    grad_ref[...] = jnp.zeros_like(grad_ref)
    own = [part_ref[m, 0:channels, :] for m in range(members)]
    sent_rows = -(-channels // 8) * 8
    others = []
    for ref in recv_refs:
        rows = ref[...].astype(F32)
        others += [rows[k * sent_rows : k * sent_rows + channels] for k in range(members)]
    for m in range(members):
        slopes = jnp.zeros_like(own[m])
        for k in range(members):
            if k != m:
                slopes = slopes + soft_slope(own[m] - own[k])
        for other in others:
            slopes = slopes + soft_slope(own[m] - other)
        gap = soft_slope(own[m] + base_ref[0:channels, :] - truth_ref[...])
        grad_ref[m, 0:channels, :] = (weight_ref[...] * (gap / total - spread * slopes)).astype(BF)
    for m in range(members):
        dm_ref[m] = mm(pt_ref[...], grad_ref[m]).astype(BF)
    for pair in range(width // LANES):
        cols = slice(pair * LANES, (pair + 1) * LANES)
        for m in range(members):
            result = mm(joined(gate_refs, pair, m), dm_ref[m, cols, :], NT)
            ng_ref[m * ext : (m + 1) * ext, cols] = select_rows(result, own_rows).astype(BF)
    store_group(mm(ext_ref[...], ng_ref[:, 0:group_width]), 0, n_member, n_band, 0, out_refs)


def key_gradients(pairs, dm_ref, value_refs, slope_refs, q_ref, ng_ref):
    members = dm_ref.shape[0]
    ext = ng_ref.shape[0] // members
    scale = HEAD_DIM ** (-0.5)
    for place, pair in enumerate(pairs):
        cols = slice(pair * LANES, (pair + 1) * LANES)
        for m in range(members):
            value = jnp.concatenate([split_heads(ref[m, :, cols]) for ref in value_refs], axis=0)
            dgate = mm(value, dm_ref[m, cols, :])
            dscore = (dgate * joined(slope_refs, pair, m).astype(F32)).astype(BF)
            keys = select_rows(mm(dscore, q_ref[:, cols]), value_refs[0].shape[1]) * scale
            ng_ref[m * ext : (m + 1) * ext, place * LANES : (place + 1) * LANES] = keys.astype(BF)


def first_keys_body(
    n_member, n_band, first_value, dm_ref, own_value_ref, halo_value_ref, own_slope_ref, halo_slope_ref,
    q_ref, ext_ref, ngv_ref, ng_ref, *out_refs
):
    count = ng_ref.shape[1] // LANES
    rest = mm(ext_ref[...], ngv_ref[:, first_value:])
    store_group(rest, 1, n_member, n_band, 0, out_refs)
    value_refs, slope_refs = (own_value_ref, halo_value_ref), (own_slope_ref, halo_slope_ref)
    key_gradients(range(count), dm_ref, value_refs, slope_refs, q_ref, ng_ref)
    store_group(mm(ext_ref[...], ng_ref[...]), 1, n_member, n_band, rest.shape[1], out_refs)


def last_keys_body(
    n_member, n_band, grad_ref, dm_ref, own_value_ref, halo_value_ref, own_slope_ref, halo_slope_ref,
    q_ref, merged_ref, wo_ref, ext_ref, ng_ref, *refs
):
    out_refs, turned = refs[:-1], refs[-1]
    members, width, _ = dm_ref.shape
    count = ng_ref.shape[1] // LANES
    value_refs, slope_refs = (own_value_ref, halo_value_ref), (own_slope_ref, halo_slope_ref)
    key_gradients(range(width // LANES - count, width // LANES), dm_ref, value_refs, slope_refs, q_ref, ng_ref)
    m_t = sum(mm(grad_ref[m], merged_ref[m], NT) for m in range(members))
    head_t = sum(mm(grad_ref[m], q_ref[...]) for m in range(members)) + mm(m_t.astype(BF), wo_ref[...])
    turned[...] = jnp.concatenate([m_t, head_t], axis=0).T
    store_group(mm(ext_ref[...], ng_ref[...]), 2, n_member, n_band, 0, out_refs)
    store_group(reorder(turned, n_member, n_band), 2, n_member, n_band, ng_ref.shape[1], out_refs)


def extended_grad_body(members, nodes, rim, first_ref, last_ref, ngv_ref, kvw_ref, own_ref, mate_ref, other_ref):
    ext = nodes + 2 * rim
    grads = jnp.concatenate([first_ref[...], last_ref[...], ngv_ref[...]], axis=1)
    rows = mm(grads, kvw_ref[...], NT)
    for m in range(members):
        at = m * ext
        own_ref[m] = rows[at : at + nodes]
        mate_ref[m * rim : (m + 1) * rim, :] = rows[at + nodes : at + nodes + rim].astype(BF)
        other_ref[m * rim : (m + 1) * rim, :] = rows[at + nodes + rim : at + ext].astype(BF)


def hidden_body(own_ref, from_mate_ref, from_other_ref, halo_ref, out_ref):
    members, nodes, _ = own_ref.shape
    rim = halo_ref.shape[1]
    mate, other = [one_hot_rows(rows, nodes) for rows in halo_lists(halo_ref)]
    for m in range(members):
        rows = slice(m * rim, (m + 1) * rim)
        out_ref[m] = own_ref[m] + mm(mate, from_mate_ref[rows, :]) + mm(other, from_other_ref[rows, :])


def finish_body(devices, own_ref, arrived_ref, hp_ref, kv_ref, out_ref, head_ref):
    width = kv_ref.shape[1] // 2
    channels = hp_ref.shape[0]
    total = (own_ref[...] + arrived_ref[...].astype(F32)) * (1.0 / devices)
    kv_ref[:, width:] = total[:, 0:width]
    kv_ref[:, 0:width] = total[:, width : 2 * width]
    m_rows = total[:, 2 * width : 2 * width + channels]
    high = m_rows.astype(BF)
    low = (m_rows - high.astype(F32)).astype(BF)
    out_ref[...] = mm(high, hp_ref[...]) + mm(low, hp_ref[...])
    head_ref[...] = total[:, 2 * width + LANES : 2 * width + LANES + channels]


def add_up(*parts):
    return functools.reduce(lambda a, b: a + b, [p.astype(F32) for p in parts])


def swap(rows, axis, bit, count):
    return lax.ppermute(rows, axis, [(i, i ^ (1 << bit)) for i in range(count)])


def upper(terms):
    return [t[: t.shape[0] // 2] for t in terms]


def lower(terms):
    return [t[t.shape[0] // 2 :] for t in terms]


def shards(
    n_member, n_band,
    hidden, queries, kv_weight, out_weight, head_projection, initial_state, truth,
    latitude_weight, channel_loss_weight, sources, halo_rows,
):
    members, nodes, width = hidden.shape
    points = queries.shape[0]
    channels = head_projection.shape[1]
    rim = halo_rows.shape[1]
    ext = nodes + 2 * rim
    pairs = width // LANES
    devices = n_member * n_band
    rw = width // devices
    chips = n_band // 2
    send_rows = -(-channels // 8) * 8
    mates = [(i, i ^ 1) for i in range(n_band)]
    others = [(i, (i + 1 if i % 2 else i - 1) % n_band) for i in range(n_band)]

    own_hidden, halo, for_mate, for_other = call(
        pick_body,
        [sds(hidden.shape, BF), sds(halo_rows.shape, jnp.int32)] + [sds((members * rim, width), BF)] * 2,
        (hidden, halo_rows),
        [pltpu.SemaphoreType.DMA((2,))],
        hbm=(0, 1),
        flops=10**10,
    )
    other = lax.ppermute(for_other, "band", others)
    mate = lax.ppermute(for_mate, "band", mates)

    hp = head_projection.T

    def gate_shapes(rows):
        return [sds((members, rows, width), BF)] + [sds((pairs, members, 2 * rows, points), BF)] * 2

    own_value, own_gates, own_slopes, own_merged, pt, p, base, weight = call(
        own_body,
        gate_shapes(nodes)
        + [
            sds((members, width, points), F32),
            sds((width, LANES), BF),
            sds((LANES, width), BF),
            sds((LANES, points), F32),
            sds((channels, points), F32),
        ],
        (
            own_hidden, out_weight, hp, queries, kv_weight, initial_state,
            channel_loss_weight[None, :], latitude_weight[None, :], sources,
        ),
        [pltpu.VMEM((8, LANES), F32), pltpu.VMEM((LANES, width), F32)],
    )

    halo_value, halo_gates, halo_slopes, merged, part, sent = call(
        functools.partial(halo_body, send_rows, nodes),
        gate_shapes(2 * rim)
        + [
            sds((members, width, points), BF),
            sds((members, LANES, points), F32),
            sds((-(-members * send_rows // 16) * 16, points), BF),
        ],
        (other, mate, own_merged, kv_weight, queries, sources, p),
    )

    received = [
        lax.ppermute(sent, "member", [(i, i ^ s) for i in range(n_member)]) for s in range(n_member - 1, 0, -1)
    ]

    ext_t = call(
        functools.partial(transpose_body, n_member, n_band),
        sds((width, members * ext), BF),
        (own_hidden, mate, other),
        [pltpu.VMEM((width, members * ext), F32)],
    )

    extra = 2 * LANES
    group_width = (2 * width + extra) // GROUPS
    first_keys = 2 * group_width - width
    group_shape = [sds((width // 2, group_width), BF)] * 2
    grad, dm, ng_value, send, keep = call(
        functools.partial(value_body, n_member, n_band),
        [sds((members, LANES, points), BF), sds((members, width, points), BF), sds((members * ext, width), BF)]
        + group_shape,
        (*received, part, base, truth, weight, pt, own_gates, halo_gates, ext_t),
    )
    groups = [[keep, swap(send, "band", 0, n_band)]]
    ng_first, send, keep = call(
        functools.partial(first_keys_body, n_member, n_band, group_width),
        [sds((members * ext, first_keys), BF)] + group_shape,
        (dm, own_value, halo_value, own_slopes, halo_slopes, queries, ext_t, ng_value),
    )
    groups.append([keep, swap(send, "band", 0, n_band)])
    ng_last, send, keep = call(
        functools.partial(last_keys_body, n_member, n_band),
        [sds((members * ext, width - first_keys), BF)] + group_shape,
        (grad, dm, own_value, halo_value, own_slopes, halo_slopes, queries, merged, out_weight, ext_t),
        [pltpu.VMEM((width, extra), F32)],
    )
    groups.append([keep, swap(send, "band", 0, n_band)])

    count = {"member": n_member, "band": n_band}
    turns, rest = halving_orders(n_member, n_band)
    steps = len(turns[0])
    for step in range(steps):
        outgoing = []
        for i in range(GROUPS):
            outgoing.append(add_up(*upper(groups[i])).astype(BF))
            if step == 0 and i + 1 < GROUPS:
                outgoing[i], groups[i + 1] = lax.optimization_barrier((outgoing[i], groups[i + 1]))
        if step == 0:
            outgoing, ng_last = lax.optimization_barrier((outgoing, ng_last))
            own_grad, back_mate, back_other = call(
                functools.partial(extended_grad_body, members, nodes, rim),
                [sds((members, nodes, width), F32)] + [sds((members * rim, width), BF)] * 2,
                (ng_first, ng_last, ng_value, kv_weight),
            )
        arrived = [swap(out, *turn[step], count[turn[step][0]]) for out, turn in zip(outgoing, turns)]
        if step == 0:
            from_mate = lax.ppermute(back_mate, "band", mates)
            arrived, from_mate, back_other = lax.optimization_barrier((arrived, from_mate, back_other))
        if step == steps - 1:
            arrived, back_other = lax.optimization_barrier((arrived, back_other))
            from_other = lax.ppermute(back_other, "band", others)
        groups = [lower(terms) + [new] for terms, new in zip(groups, arrived)]
    terms = [jnp.concatenate([add_up(*group) for group in groups], axis=1)]
    for axis, bit in rest:
        arrived = swap(add_up(*upper(terms)).astype(BF), axis, bit, count[axis])
        terms = lower(terms) + [arrived]

    kv_grad, out_grad, head_grad = call(
        functools.partial(finish_body, devices),
        [sds((rw, 2 * width), F32), sds((rw, width), F32), sds((rw, channels), F32)],
        (add_up(*terms[:-1]), terms[-1], hp),
    )
    kv_grad, from_other = lax.optimization_barrier((kv_grad, from_other))
    hidden_grad = call(
        hidden_body,
        sds((members, nodes, width), F32),
        (own_grad, from_mate, from_other, halo),
    )
    return hidden_grad, kv_grad, out_grad, head_grad


def solution(mesh):
    placed = (
        P("member", "band", None),
        P("band", None),
        P(),
        P(),
        P(),
        P(None, "band"),
        P(None, "band"),
        P("band"),
        P(),
        P(None, "band"),
        P("band", None),
    )
    return jax.shard_map(
        functools.partial(shards, mesh.shape["member"], mesh.shape["band"]),
        mesh=mesh,
        in_specs=placed,
        out_specs=(
            P("member", "band", None),
            P(("member", "band"), None),
            P(("member", "band"), None),
            P(("member", "band"), None),
        ),
        check_vma=False,
    )
```

```python
import functools

import jax
import jax.numpy as jnp
from jax import lax
from jax.experimental import pallas as pl
from jax.experimental.pallas import tpu as pltpu
from jax.sharding import PartitionSpec as P

HEAD_DIM = 64
LANES = 128
GROUPS = 3
ALPHA = 0.95
SOFTENING = 0.5
BF = jnp.bfloat16
F32 = jnp.float32
NN = (((1,), (0,)), ((), ()))
NT = (((1,), (1,)), ((), ()))
TN = (((0,), (0,)), ((), ()))


def mm(a, b, dims=NN):
    return lax.dot_general(a, b, dims, preferred_element_type=F32)


def call(body, out_shape, args, scratch=(), hbm=(), limit=24, flops=1):
    args = [pltpu.with_memory_space_constraint(x, pltpu.HBM) if i in hbm else x for i, x in enumerate(args)]
    return pl.pallas_call(
        body,
        out_shape=out_shape,
        in_specs=[
            pl.BlockSpec(memory_space=pltpu.HBM if i in hbm else pltpu.VMEM) for i in range(len(args))
        ],
        out_specs=jax.tree.map(lambda _: pl.BlockSpec(memory_space=pltpu.VMEM), out_shape),
        scratch_shapes=list(scratch),
        compiler_params=pltpu.CompilerParams(vmem_limit_bytes=limit * 1024 * 1024),
        cost_estimate=pl.CostEstimate(flops=flops, bytes_accessed=1, transcendentals=0),
    )(*args)


def sds(shape, dtype):
    return jax.ShapeDtypeStruct(shape, dtype)


def one_hot_rows(rows, node_count):
    nodes = lax.broadcasted_iota(jnp.int32, (node_count, rows.shape[1]), 0).astype(rows.dtype)
    return (nodes == rows).astype(F32).astype(BF)


def start_copies(pairs, sems):
    copies = [pltpu.make_async_copy(src, dst, sems.at[i]) for i, (src, dst) in enumerate(pairs)]
    for copy in copies:
        copy.start()
    return copies


def halo_lists(halo_ref):
    even = lax.axis_index("band") % 2 == 0
    down, up = halo_ref[0:1, :], halo_ref[1:2, :]
    return jnp.where(even, up, down), jnp.where(even, down, up)


def pick_body(hidden_hbm, halo_hbm, hidden_ref, halo_ref, mate_ref, other_ref, sems):
    for copy in start_copies([(hidden_hbm, hidden_ref), (halo_hbm, halo_ref)], sems):
        copy.wait()
    members, nodes, _ = hidden_ref.shape
    rim = halo_ref.shape[1]
    for rows, out_ref in zip(halo_lists(halo_ref), (mate_ref, other_ref)):
        hot = one_hot_rows(rows, nodes)
        for m in range(members):
            out_ref[m * rim : (m + 1) * rim, :] = mm(hot, hidden_ref[m], TN).astype(BF)


def split_heads(block):
    low = lax.broadcasted_iota(jnp.int32, block.shape, 1) < HEAD_DIM
    zero = jnp.zeros_like(block)
    return jnp.concatenate([jnp.where(low, block, zero), jnp.where(low, zero, block)], axis=0)


def half_mask_of(src, first, count):
    rows = lax.broadcasted_iota(jnp.int32, (count, src.shape[1]), 0) + first
    mask = rows == src[0:1, :]
    for e in range(1, src.shape[0]):
        mask = mask | (rows == src[e : e + 1, :])
    half = jnp.where(mask, 0.5, 0.0).astype(F32)
    return jnp.concatenate([half, half], axis=0)


def gate_rows(tasks, keys, values, q_ref, half_mask, gate_ref, slope_ref, store_merged, prefetch=None):
    half_scale = 0.5 * HEAD_DIM ** (-0.5)

    def scores(pair, m):
        q = (q_ref[:, pair * LANES : (pair + 1) * LANES].astype(F32) * half_scale).astype(BF)
        return mm(split_heads(keys(pair, m)), q, NT)

    ahead = scores(*tasks[0])
    for i, (pair, m) in enumerate(tasks):
        current = ahead
        if prefetch is not None:
            prefetch(pair)
        if i + 1 < len(tasks):
            ahead = scores(*tasks[i + 1])
        turned = split_heads(values(pair, m)).astype(F32).T.astype(BF)
        gate = jnp.tanh(current) * half_mask + half_mask
        rounded = gate.astype(BF)
        gate_ref[pair, m] = rounded
        slope_ref[pair, m] = (gate - gate * gate).astype(BF)
        store_merged(pair, m, mm(turned, rounded))


def tasks_of(width, members):
    return [(pair, m) for pair in range(width // LANES) for m in range(members)]


def own_body(
    hidden_ref, wo_ref, hp_ref, q_ref, kvw_ref, init_ref, chw_ref, lat_ref, src_ref,
    value_ref, gate_ref, slope_ref, merged_ref, pt_ref, p_ref, base_ref, weight_ref, chw_pad, hp_pad,
):
    channels = hp_ref.shape[0]
    members, nodes, width = hidden_ref.shape
    hidden = jnp.concatenate([hidden_ref[m] for m in range(members)], axis=0)
    rows = mm(hidden, kvw_ref[...]).astype(BF)

    def part(pair, m, first):
        at = first + pair * LANES
        return rows[m * nodes : (m + 1) * nodes, at : at + LANES]

    def store_merged(pair, m, result):
        merged_ref[m, pair * LANES : (pair + 1) * LANES, :] = result

    for m in range(members):
        value_ref[m] = rows[m * nodes : (m + 1) * nodes, width:]
    gate_rows(
        tasks_of(width, members),
        lambda pair, m: part(pair, m, 0),
        lambda pair, m: part(pair, m, width),
        q_ref, half_mask_of(src_ref[...], 0, nodes), gate_ref, slope_ref, store_merged,
    )
    hp_pad[...] = jnp.zeros_like(hp_pad)
    hp_pad[0:channels, :] = hp_ref[...].astype(F32)
    hp_t = hp_pad[...].astype(BF)
    chw_pad[:, 0:channels] = jnp.broadcast_to(chw_ref[...], (8, channels))
    weight_ref[...] = chw_pad[...].T[0:channels, 0:1] * lat_ref[...]
    base_ref[...] = mm(hp_t, q_ref[...], NT)
    base_ref[0:channels, :] = base_ref[0:channels, :] + init_ref[...]
    p = mm(hp_t, wo_ref[...], NT)
    p_ref[...] = p.astype(BF)
    pt_ref[...] = p.T.astype(BF)


def halo_body(
    send_rows, nodes, other_ref, mate_ref, own_ref, kvw_ref, q_ref, src_ref, p_ref,
    value_ref, gate_ref, slope_ref, merged_ref, part_ref, send_ref,
):
    members, count, width = value_ref.shape
    points = q_ref.shape[0]
    rim = count // 2
    step = 2 * LANES
    halo_rows = jnp.concatenate([mate_ref[...], other_ref[...]], axis=0)

    src = src_ref[...]
    even = lax.axis_index("band") % 2 == 0
    shift = jnp.where(src >= nodes + rim, -rim, jnp.where(src >= nodes, rim, 0))
    src = src + jnp.where(even, shift, 0)
    held = {}

    def prefetch(pair):
        start = (pair * LANES // step + 1) * step
        for first in (0, width):
            if start < width and first + start not in held:
                held[first + start] = mm(halo_rows, kvw_ref[:, first + start : first + start + step]).astype(BF)

    prefetch(-1)

    def rows(pair, m, first):
        at = pair * LANES % step
        block = held[first + pair * LANES - at][:, at : at + LANES]
        mate = block[m * rim : (m + 1) * rim]
        other = block[(members + m) * rim : (members + m + 1) * rim]
        return jnp.concatenate([mate, other], axis=0)

    def values(pair, m):
        result = rows(pair, m, width)
        value_ref[m, :, pair * LANES : (pair + 1) * LANES] = result
        return result

    def store_merged(pair, m, result):
        cols = slice(pair * LANES, (pair + 1) * LANES)
        merged_ref[m, cols, :] = (own_ref[m, cols, :] + result).astype(BF)

    gate_rows(
        tasks_of(width, members), lambda pair, m: rows(pair, m, 0), values,
        q_ref, half_mask_of(src, nodes, count), gate_ref, slope_ref, store_merged, prefetch,
    )
    sent = []
    for m in range(members):
        part = mm(p_ref[...], merged_ref[m])
        part_ref[m] = part
        sent.append(part[0:send_rows])
    filler = send_ref.shape[0] - members * send_rows
    if filler:
        sent.append(jnp.zeros((filler, points), F32))
    send_ref[...] = jnp.concatenate(sent, axis=0).astype(BF)


def halving_orders(n_member, n_band):
    chips = [("band", bit) for bit in range(1, n_band.bit_length() - 1)]
    member = [("member", bit) for bit in range(n_member.bit_length() - 1)]
    turn = chips + member[:1]
    return [turn[i:] + turn[:i] for i in range(GROUPS)], member[1:]


def unit_order(order, n_member, n_band):
    def key(unit):
        return [-((2 * unit[0] if axis == "band" else unit[1]) >> bit & 1) for axis, bit in order]

    return sorted([(c, m) for c in range(n_band // 2) for m in range(n_member)], key=key)


def destination_rows(member, band, n_member, n_band, rw):
    chip, core = band // 2, band % 2
    for rel_core in (1, 0):
        for rel_chip in range(n_band // 2):
            to_band = (chip ^ rel_chip) * 2 + (core ^ rel_core)
            for rel_member in range(n_member):
                yield pl.multiple_of(((member ^ rel_member) * n_band + to_band) * rw, rw)


def reorder(src_ref, n_member, n_band):
    rw = src_ref.shape[0] // (n_member * n_band)
    member, band = lax.axis_index("member"), lax.axis_index("band")
    starts = destination_rows(member, band, n_member, n_band, rw)
    return jnp.concatenate([src_ref[pl.ds(start, rw), :] for start in starts], axis=0)


def store_group(rows, group, n_member, n_band, at, out_refs):
    orders, rest = halving_orders(n_member, n_band)
    units = unit_order(orders[group] + rest, n_member, n_band)
    rw = rows.shape[0] // (n_member * n_band)
    for core, ref in enumerate(out_refs):
        starts = [((core * (n_band // 2) + chip) * n_member + member) * rw for chip, member in units]
        ordered = jnp.concatenate([rows[i : i + rw] for i in starts], axis=0)
        ref[:, at : at + rows.shape[1]] = ordered.astype(BF)


def transpose_body(n_member, n_band, hidden_ref, mate_ref, other_ref, out_ref, turned):
    members, nodes, _ = hidden_ref.shape
    rim = mate_ref.shape[0] // members
    parts = []
    for m in range(members):
        parts.append(hidden_ref[m])
        parts.append(mate_ref[m * rim : (m + 1) * rim, :])
        parts.append(other_ref[m * rim : (m + 1) * rim, :])
    turned[...] = jnp.concatenate(parts, axis=0).astype(F32).T
    out_ref[...] = reorder(turned, n_member, n_band).astype(BF)


def select_heads(block):
    half = block.shape[0] // 2
    low = lax.broadcasted_iota(jnp.int32, (half, block.shape[1]), 1) < HEAD_DIM
    return jnp.where(low, block[:half], block[half:])


def joined(refs, pair, m):
    return jnp.concatenate([ref[pair, m] for ref in refs], axis=0)


def select_rows(block, own):
    return jnp.concatenate([select_heads(block[: 2 * own]), select_heads(block[2 * own :])], axis=0)


def soft_slope(v):
    return v * lax.rsqrt(v * v + SOFTENING * SOFTENING)


def value_body(n_member, n_band, *refs):
    recv_refs = refs[: n_member - 1]
    part_ref, base_ref, truth_ref, weight_ref, pt_ref, *gate_refs, ext_ref = refs[n_member - 1 : n_member + 7]
    grad_ref, dm_ref, ng_ref, *out_refs = refs[n_member + 7 :]
    own_rows = gate_refs[0].shape[2] // 2
    group_width = out_refs[0].shape[1]
    members, width, _ = dm_ref.shape
    ext = ng_ref.shape[0] // members
    channels = truth_ref.shape[0]
    total = members * n_member
    spread = (1.0 - (1.0 - ALPHA) / total) / (total * (total - 1))

    grad_ref[...] = jnp.zeros_like(grad_ref)
    own = [part_ref[m, 0:channels, :] for m in range(members)]
    sent_rows = -(-channels // 8) * 8
    others = []
    for ref in recv_refs:
        rows = ref[...].astype(F32)
        others += [rows[k * sent_rows : k * sent_rows + channels] for k in range(members)]
    for m in range(members):
        slopes = jnp.zeros_like(own[m])
        for k in range(members):
            if k != m:
                slopes = slopes + soft_slope(own[m] - own[k])
        for other in others:
            slopes = slopes + soft_slope(own[m] - other)
        gap = soft_slope(own[m] + base_ref[0:channels, :] - truth_ref[...])
        grad_ref[m, 0:channels, :] = (weight_ref[...] * (gap / total - spread * slopes)).astype(BF)
    for m in range(members):
        dm_ref[m] = mm(pt_ref[...], grad_ref[m]).astype(BF)
    for pair in range(width // LANES):
        cols = slice(pair * LANES, (pair + 1) * LANES)
        for m in range(members):
            result = mm(joined(gate_refs, pair, m), dm_ref[m, cols, :], NT)
            ng_ref[m * ext : (m + 1) * ext, cols] = select_rows(result, own_rows).astype(BF)
    store_group(mm(ext_ref[...], ng_ref[:, 0:group_width]), 0, n_member, n_band, 0, out_refs)


def key_gradients(pairs, dm_ref, value_refs, slope_refs, q_ref, ng_ref):
    members = dm_ref.shape[0]
    ext = ng_ref.shape[0] // members
    scale = HEAD_DIM ** (-0.5)
    for place, pair in enumerate(pairs):
        cols = slice(pair * LANES, (pair + 1) * LANES)
        for m in range(members):
            value = jnp.concatenate([split_heads(ref[m, :, cols]) for ref in value_refs], axis=0)
            dgate = mm(value, dm_ref[m, cols, :])
            dscore = (dgate * joined(slope_refs, pair, m).astype(F32)).astype(BF)
            keys = select_rows(mm(dscore, q_ref[:, cols]), value_refs[0].shape[1]) * scale
            ng_ref[m * ext : (m + 1) * ext, place * LANES : (place + 1) * LANES] = keys.astype(BF)


def first_keys_body(
    n_member, n_band, first_value, dm_ref, own_value_ref, halo_value_ref, own_slope_ref, halo_slope_ref,
    q_ref, ext_ref, ngv_ref, ng_ref, *out_refs
):
    count = ng_ref.shape[1] // LANES
    rest = mm(ext_ref[...], ngv_ref[:, first_value:])
    store_group(rest, 1, n_member, n_band, 0, out_refs)
    value_refs, slope_refs = (own_value_ref, halo_value_ref), (own_slope_ref, halo_slope_ref)
    key_gradients(range(count), dm_ref, value_refs, slope_refs, q_ref, ng_ref)
    store_group(mm(ext_ref[...], ng_ref[...]), 1, n_member, n_band, rest.shape[1], out_refs)


def last_keys_body(
    n_member, n_band, grad_ref, dm_ref, own_value_ref, halo_value_ref, own_slope_ref, halo_slope_ref,
    q_ref, merged_ref, wo_ref, ext_ref, ng_ref, *refs
):
    out_refs, turned = refs[:-1], refs[-1]
    members, width, _ = dm_ref.shape
    count = ng_ref.shape[1] // LANES
    value_refs, slope_refs = (own_value_ref, halo_value_ref), (own_slope_ref, halo_slope_ref)
    key_gradients(range(width // LANES - count, width // LANES), dm_ref, value_refs, slope_refs, q_ref, ng_ref)
    m_t = sum(mm(grad_ref[m], merged_ref[m], NT) for m in range(members))
    head_t = sum(mm(grad_ref[m], q_ref[...]) for m in range(members)) + mm(m_t.astype(BF), wo_ref[...])
    turned[...] = jnp.concatenate([m_t, head_t], axis=0).T
    store_group(mm(ext_ref[...], ng_ref[...]), 2, n_member, n_band, 0, out_refs)
    store_group(reorder(turned, n_member, n_band), 2, n_member, n_band, ng_ref.shape[1], out_refs)


def extended_grad_body(members, nodes, rim, first_ref, last_ref, ngv_ref, kvw_ref, own_ref, mate_ref, other_ref):
    ext = nodes + 2 * rim
    grads = jnp.concatenate([first_ref[...], last_ref[...], ngv_ref[...]], axis=1)
    rows = mm(grads, kvw_ref[...], NT)
    for m in range(members):
        at = m * ext
        own_ref[m] = rows[at : at + nodes]
        mate_ref[m * rim : (m + 1) * rim, :] = rows[at + nodes : at + nodes + rim].astype(BF)
        other_ref[m * rim : (m + 1) * rim, :] = rows[at + nodes + rim : at + ext].astype(BF)


def hidden_body(own_ref, from_mate_ref, from_other_ref, halo_ref, out_ref):
    members, nodes, _ = own_ref.shape
    rim = halo_ref.shape[1]
    mate, other = [one_hot_rows(rows, nodes) for rows in halo_lists(halo_ref)]
    for m in range(members):
        rows = slice(m * rim, (m + 1) * rim)
        out_ref[m] = own_ref[m] + mm(mate, from_mate_ref[rows, :]) + mm(other, from_other_ref[rows, :])


def finish_body(devices, own_ref, arrived_ref, hp_ref, kv_ref, out_ref, head_ref):
    width = kv_ref.shape[1] // 2
    channels = hp_ref.shape[0]
    total = (own_ref[...] + arrived_ref[...].astype(F32)) * (1.0 / devices)
    kv_ref[:, width:] = total[:, 0:width]
    kv_ref[:, 0:width] = total[:, width : 2 * width]
    m_rows = total[:, 2 * width : 2 * width + channels]
    high = m_rows.astype(BF)
    low = (m_rows - high.astype(F32)).astype(BF)
    out_ref[...] = mm(high, hp_ref[...]) + mm(low, hp_ref[...])
    head_ref[...] = total[:, 2 * width + LANES : 2 * width + LANES + channels]


def add_up(*parts):
    return functools.reduce(lambda a, b: a + b, [p.astype(F32) for p in parts])


def swap(rows, axis, bit, count):
    return lax.ppermute(rows, axis, [(i, i ^ (1 << bit)) for i in range(count)])


def upper(terms):
    return [t[: t.shape[0] // 2] for t in terms]


def lower(terms):
    return [t[t.shape[0] // 2 :] for t in terms]


def shards(
    n_member, n_band,
    hidden, queries, kv_weight, out_weight, head_projection, initial_state, truth,
    latitude_weight, channel_loss_weight, sources, halo_rows,
):
    members, nodes, width = hidden.shape
    points = queries.shape[0]
    channels = head_projection.shape[1]
    rim = halo_rows.shape[1]
    ext = nodes + 2 * rim
    pairs = width // LANES
    devices = n_member * n_band
    rw = width // devices
    chips = n_band // 2
    send_rows = -(-channels // 8) * 8
    mates = [(i, i ^ 1) for i in range(n_band)]
    others = [(i, (i + 1 if i % 2 else i - 1) % n_band) for i in range(n_band)]

    own_hidden, halo, for_mate, for_other = call(
        pick_body,
        [sds(hidden.shape, BF), sds(halo_rows.shape, jnp.int32)] + [sds((members * rim, width), BF)] * 2,
        (hidden, halo_rows),
        [pltpu.SemaphoreType.DMA((2,))],
        hbm=(0, 1),
        flops=10**10,
    )
    other = lax.ppermute(for_other, "band", others)
    mate = lax.ppermute(for_mate, "band", mates)

    hp = head_projection.T

    def gate_shapes(rows):
        return [sds((members, rows, width), BF)] + [sds((pairs, members, 2 * rows, points), BF)] * 2

    own_value, own_gates, own_slopes, own_merged, pt, p, base, weight = call(
        own_body,
        gate_shapes(nodes)
        + [
            sds((members, width, points), F32),
            sds((width, LANES), BF),
            sds((LANES, width), BF),
            sds((LANES, points), F32),
            sds((channels, points), F32),
        ],
        (
            own_hidden, out_weight, hp, queries, kv_weight, initial_state,
            channel_loss_weight[None, :], latitude_weight[None, :], sources,
        ),
        [pltpu.VMEM((8, LANES), F32), pltpu.VMEM((LANES, width), F32)],
    )

    halo_value, halo_gates, halo_slopes, merged, part, sent = call(
        functools.partial(halo_body, send_rows, nodes),
        gate_shapes(2 * rim)
        + [
            sds((members, width, points), BF),
            sds((members, LANES, points), F32),
            sds((-(-members * send_rows // 16) * 16, points), BF),
        ],
        (other, mate, own_merged, kv_weight, queries, sources, p),
    )

    received = [
        lax.ppermute(sent, "member", [(i, i ^ s) for i in range(n_member)]) for s in range(n_member - 1, 0, -1)
    ]

    ext_t = call(
        functools.partial(transpose_body, n_member, n_band),
        sds((width, members * ext), BF),
        (own_hidden, mate, other),
        [pltpu.VMEM((width, members * ext), F32)],
    )

    extra = 2 * LANES
    group_width = (2 * width + extra) // GROUPS
    first_keys = 2 * group_width - width
    group_shape = [sds((width // 2, group_width), BF)] * 2
    grad, dm, ng_value, send, keep = call(
        functools.partial(value_body, n_member, n_band),
        [sds((members, LANES, points), BF), sds((members, width, points), BF), sds((members * ext, width), BF)]
        + group_shape,
        (*received, part, base, truth, weight, pt, own_gates, halo_gates, ext_t),
    )
    groups = [[keep, swap(send, "band", 0, n_band)]]
    ng_first, send, keep = call(
        functools.partial(first_keys_body, n_member, n_band, group_width),
        [sds((members * ext, first_keys), BF)] + group_shape,
        (dm, own_value, halo_value, own_slopes, halo_slopes, queries, ext_t, ng_value),
    )
    groups.append([keep, swap(send, "band", 0, n_band)])
    ng_last, send, keep = call(
        functools.partial(last_keys_body, n_member, n_band),
        [sds((members * ext, width - first_keys), BF)] + group_shape,
        (grad, dm, own_value, halo_value, own_slopes, halo_slopes, queries, merged, out_weight, ext_t),
        [pltpu.VMEM((width, extra), F32)],
    )
    groups.append([keep, swap(send, "band", 0, n_band)])

    count = {"member": n_member, "band": n_band}
    turns, rest = halving_orders(n_member, n_band)
    steps = len(turns[0])
    for step in range(steps):
        outgoing = []
        for i in range(GROUPS):
            outgoing.append(add_up(*upper(groups[i])).astype(BF))
            if step == 0 and i + 1 < GROUPS:
                outgoing[i], groups[i + 1] = lax.optimization_barrier((outgoing[i], groups[i + 1]))
        if step == 0:
            outgoing, ng_last = lax.optimization_barrier((outgoing, ng_last))
            own_grad, back_mate, back_other = call(
                functools.partial(extended_grad_body, members, nodes, rim),
                [sds((members, nodes, width), F32)] + [sds((members * rim, width), BF)] * 2,
                (ng_first, ng_last, ng_value, kv_weight),
            )
        if step == steps - 1:
            outgoing[0], back_other = lax.optimization_barrier((outgoing[0], back_other))
            from_other = lax.ppermute(back_other, "band", others)
        arrived = [swap(out, *turn[step], count[turn[step][0]]) for out, turn in zip(outgoing, turns)]
        if step == 0:
            from_mate = lax.ppermute(back_mate, "band", mates)
            arrived, from_mate, back_other = lax.optimization_barrier((arrived, from_mate, back_other))
        if step == steps - 1:
            arrived, from_other = lax.optimization_barrier((arrived, from_other))
        groups = [lower(terms) + [new] for terms, new in zip(groups, arrived)]
    terms = [jnp.concatenate([add_up(*group) for group in groups], axis=1)]
    for axis, bit in rest:
        arrived = swap(add_up(*upper(terms)).astype(BF), axis, bit, count[axis])
        terms = lower(terms) + [arrived]

    kv_grad, out_grad, head_grad = call(
        functools.partial(finish_body, devices),
        [sds((rw, 2 * width), F32), sds((rw, width), F32), sds((rw, channels), F32)],
        (add_up(*terms[:-1]), terms[-1], hp),
    )
    hidden_grad = call(
        hidden_body,
        sds((members, nodes, width), F32),
        (own_grad, from_mate, from_other, halo),
    )
    return hidden_grad, kv_grad, out_grad, head_grad


def solution(mesh):
    placed = (
        P("member", "band", None),
        P("band", None),
        P(),
        P(),
        P(),
        P(None, "band"),
        P(None, "band"),
        P("band"),
        P(),
        P(None, "band"),
        P("band", None),
    )
    return jax.shard_map(
        functools.partial(shards, mesh.shape["member"], mesh.shape["band"]),
        mesh=mesh,
        in_specs=placed,
        out_specs=(
            P("member", "band", None),
            P(("member", "band"), None),
            P(("member", "band"), None),
            P(("member", "band"), None),
        ),
        check_vma=False,
    )
```

```python
import functools

import jax
import jax.numpy as jnp
from jax import lax
from jax.experimental import pallas as pl
from jax.experimental.pallas import tpu as pltpu
from jax.sharding import PartitionSpec as P

HEAD_DIM = 64
LANES = 128
GROUPS = 3
ALPHA = 0.95
SOFTENING = 0.5
BF = jnp.bfloat16
F32 = jnp.float32
NN = (((1,), (0,)), ((), ()))
NT = (((1,), (1,)), ((), ()))
TN = (((0,), (0,)), ((), ()))


def mm(a, b, dims=NN):
    return lax.dot_general(a, b, dims, preferred_element_type=F32)


def call(body, out_shape, args, scratch=(), hbm=(), limit=24, flops=1):
    args = [pltpu.with_memory_space_constraint(x, pltpu.HBM) if i in hbm else x for i, x in enumerate(args)]
    return pl.pallas_call(
        body,
        out_shape=out_shape,
        in_specs=[
            pl.BlockSpec(memory_space=pltpu.HBM if i in hbm else pltpu.VMEM) for i in range(len(args))
        ],
        out_specs=jax.tree.map(lambda _: pl.BlockSpec(memory_space=pltpu.VMEM), out_shape),
        scratch_shapes=list(scratch),
        compiler_params=pltpu.CompilerParams(vmem_limit_bytes=limit * 1024 * 1024),
        cost_estimate=pl.CostEstimate(flops=flops, bytes_accessed=1, transcendentals=0),
    )(*args)


def sds(shape, dtype):
    return jax.ShapeDtypeStruct(shape, dtype)


def one_hot_rows(rows, node_count):
    nodes = lax.broadcasted_iota(jnp.int32, (node_count, rows.shape[1]), 0).astype(rows.dtype)
    return (nodes == rows).astype(F32).astype(BF)


def start_copies(pairs, sems):
    copies = [pltpu.make_async_copy(src, dst, sems.at[i]) for i, (src, dst) in enumerate(pairs)]
    for copy in copies:
        copy.start()
    return copies


def halo_lists(halo_ref):
    even = lax.axis_index("band") % 2 == 0
    down, up = halo_ref[0:1, :], halo_ref[1:2, :]
    return jnp.where(even, up, down), jnp.where(even, down, up)


def pick_body(hidden_hbm, halo_hbm, hidden_ref, halo_ref, mate_ref, other_ref, sems):
    for copy in start_copies([(hidden_hbm, hidden_ref), (halo_hbm, halo_ref)], sems):
        copy.wait()
    members, nodes, _ = hidden_ref.shape
    rim = halo_ref.shape[1]
    for rows, out_ref in zip(halo_lists(halo_ref), (mate_ref, other_ref)):
        hot = one_hot_rows(rows, nodes)
        for m in range(members):
            out_ref[m * rim : (m + 1) * rim, :] = mm(hot, hidden_ref[m], TN).astype(BF)


def split_heads(block):
    low = lax.broadcasted_iota(jnp.int32, block.shape, 1) < HEAD_DIM
    zero = jnp.zeros_like(block)
    return jnp.concatenate([jnp.where(low, block, zero), jnp.where(low, zero, block)], axis=0)


def half_mask_of(src, first, count):
    rows = lax.broadcasted_iota(jnp.int32, (count, src.shape[1]), 0) + first
    mask = rows == src[0:1, :]
    for e in range(1, src.shape[0]):
        mask = mask | (rows == src[e : e + 1, :])
    half = jnp.where(mask, 0.5, 0.0).astype(F32)
    return jnp.concatenate([half, half], axis=0)


def gate_rows(tasks, keys, values, qt_ref, half_mask, gate_ref, slope_ref, store_merged, prefetch=None):
    def scores(pair, m):
        return mm(split_heads(keys(pair, m)), qt_ref[pair * LANES : (pair + 1) * LANES, :])

    ahead = scores(*tasks[0])
    for i, (pair, m) in enumerate(tasks):
        current = ahead
        if prefetch is not None:
            prefetch(pair)
        if i + 1 < len(tasks):
            ahead = scores(*tasks[i + 1])
        turned = split_heads(values(pair, m)).astype(F32).T.astype(BF)
        gate = jnp.tanh(current) * half_mask + half_mask
        rounded = gate.astype(BF)
        gate_ref[pair, m] = rounded
        slope_ref[pair, m] = (gate - gate * gate).astype(BF)
        store_merged(pair, m, mm(turned, rounded))


def tasks_of(width, members):
    return [(pair, m) for pair in range(width // LANES) for m in range(members)]


def own_body(
    hidden_ref, wo_ref, hp_ref, q_ref, kvw_ref, init_ref, chw_ref, lat_ref, src_ref,
    value_ref, gate_ref, slope_ref, merged_ref, qt_ref, pt_ref, p_ref, base_ref, weight_ref, chw_pad, hp_pad,
):
    channels = hp_ref.shape[0]
    members, nodes, width = hidden_ref.shape
    half_scale = 0.5 * HEAD_DIM ** (-0.5)
    qt_ref[...] = (q_ref[...].astype(F32) * half_scale).T.astype(BF)
    hidden = jnp.concatenate([hidden_ref[m] for m in range(members)], axis=0)
    rows = mm(hidden, kvw_ref[...]).astype(BF)

    def part(pair, m, first):
        at = first + pair * LANES
        return rows[m * nodes : (m + 1) * nodes, at : at + LANES]

    def store_merged(pair, m, result):
        merged_ref[m, pair * LANES : (pair + 1) * LANES, :] = result

    for m in range(members):
        value_ref[m] = rows[m * nodes : (m + 1) * nodes, width:]
    gate_rows(
        tasks_of(width, members),
        lambda pair, m: part(pair, m, 0),
        lambda pair, m: part(pair, m, width),
        qt_ref, half_mask_of(src_ref[...], 0, nodes), gate_ref, slope_ref, store_merged,
    )
    hp_pad[...] = jnp.zeros_like(hp_pad)
    hp_pad[0:channels, :] = hp_ref[...].astype(F32)
    hp_t = hp_pad[...].astype(BF)
    chw_pad[:, 0:channels] = jnp.broadcast_to(chw_ref[...], (8, channels))
    weight_ref[...] = chw_pad[...].T[0:channels, 0:1] * lat_ref[...]
    base_ref[...] = mm(hp_t, q_ref[...], NT)
    base_ref[0:channels, :] = base_ref[0:channels, :] + init_ref[...]
    p = mm(hp_t, wo_ref[...], NT)
    p_ref[...] = p.astype(BF)
    pt_ref[...] = p.T.astype(BF)


def halo_body(
    send_rows, nodes, other_ref, mate_ref, own_ref, kvw_ref, qt_ref, src_ref, p_ref,
    value_ref, gate_ref, slope_ref, merged_ref, part_ref, send_ref,
):
    members, count, width = value_ref.shape
    points = qt_ref.shape[1]
    rim = count // 2
    step = 2 * LANES
    halo_rows = jnp.concatenate([mate_ref[...], other_ref[...]], axis=0)

    src = src_ref[...]
    even = lax.axis_index("band") % 2 == 0
    shift = jnp.where(src >= nodes + rim, -rim, jnp.where(src >= nodes, rim, 0))
    src = src + jnp.where(even, shift, 0)
    held = {}

    def prefetch(pair):
        start = (pair * LANES // step + 1) * step
        for first in (0, width):
            if start < width and first + start not in held:
                held[first + start] = mm(halo_rows, kvw_ref[:, first + start : first + start + step]).astype(BF)

    prefetch(-1)

    def rows(pair, m, first):
        at = pair * LANES % step
        block = held[first + pair * LANES - at][:, at : at + LANES]
        mate = block[m * rim : (m + 1) * rim]
        other = block[(members + m) * rim : (members + m + 1) * rim]
        return jnp.concatenate([mate, other], axis=0)

    def values(pair, m):
        result = rows(pair, m, width)
        value_ref[m, :, pair * LANES : (pair + 1) * LANES] = result
        return result

    def store_merged(pair, m, result):
        cols = slice(pair * LANES, (pair + 1) * LANES)
        merged_ref[m, cols, :] = (own_ref[m, cols, :] + result).astype(BF)

    gate_rows(
        tasks_of(width, members), lambda pair, m: rows(pair, m, 0), values,
        qt_ref, half_mask_of(src, nodes, count), gate_ref, slope_ref, store_merged, prefetch,
    )
    sent = []
    for m in range(members):
        part = mm(p_ref[...], merged_ref[m])
        part_ref[m] = part
        sent.append(part[0:send_rows])
    filler = send_ref.shape[0] - members * send_rows
    if filler:
        sent.append(jnp.zeros((filler, points), F32))
    send_ref[...] = jnp.concatenate(sent, axis=0).astype(BF)


def halving_orders(n_member, n_band):
    chips = [("band", bit) for bit in range(1, n_band.bit_length() - 1)]
    member = [("member", bit) for bit in range(n_member.bit_length() - 1)]
    turn = chips + member[:1]
    return [turn[i:] + turn[:i] for i in range(GROUPS)], member[1:]


def unit_order(order, n_member, n_band):
    def key(unit):
        return [-((2 * unit[0] if axis == "band" else unit[1]) >> bit & 1) for axis, bit in order]

    return sorted([(c, m) for c in range(n_band // 2) for m in range(n_member)], key=key)


def destination_rows(member, band, n_member, n_band, rw):
    chip, core = band // 2, band % 2
    for rel_core in (1, 0):
        for rel_chip in range(n_band // 2):
            to_band = (chip ^ rel_chip) * 2 + (core ^ rel_core)
            for rel_member in range(n_member):
                yield pl.multiple_of(((member ^ rel_member) * n_band + to_band) * rw, rw)


def reorder(src_ref, n_member, n_band):
    rw = src_ref.shape[0] // (n_member * n_band)
    member, band = lax.axis_index("member"), lax.axis_index("band")
    starts = destination_rows(member, band, n_member, n_band, rw)
    return jnp.concatenate([src_ref[pl.ds(start, rw), :] for start in starts], axis=0)


def store_group(rows, group, n_member, n_band, at, out_refs):
    orders, rest = halving_orders(n_member, n_band)
    units = unit_order(orders[group] + rest, n_member, n_band)
    rw = rows.shape[0] // (n_member * n_band)
    for core, ref in enumerate(out_refs):
        starts = [((core * (n_band // 2) + chip) * n_member + member) * rw for chip, member in units]
        ordered = jnp.concatenate([rows[i : i + rw] for i in starts], axis=0)
        ref[:, at : at + rows.shape[1]] = ordered.astype(BF)


def transpose_body(n_member, n_band, hidden_ref, mate_ref, other_ref, out_ref, turned):
    members, nodes, _ = hidden_ref.shape
    rim = mate_ref.shape[0] // members
    parts = []
    for m in range(members):
        parts.append(hidden_ref[m])
        parts.append(mate_ref[m * rim : (m + 1) * rim, :])
        parts.append(other_ref[m * rim : (m + 1) * rim, :])
    turned[...] = jnp.concatenate(parts, axis=0).astype(F32).T
    out_ref[...] = reorder(turned, n_member, n_band).astype(BF)


def select_heads(block):
    half = block.shape[0] // 2
    low = lax.broadcasted_iota(jnp.int32, (half, block.shape[1]), 1) < HEAD_DIM
    return jnp.where(low, block[:half], block[half:])


def joined(refs, pair, m):
    return jnp.concatenate([ref[pair, m] for ref in refs], axis=0)


def select_rows(block, own):
    return jnp.concatenate([select_heads(block[: 2 * own]), select_heads(block[2 * own :])], axis=0)


def soft_slope(v):
    return v * lax.rsqrt(v * v + SOFTENING * SOFTENING)


def value_body(n_member, n_band, *refs):
    recv_refs = refs[: n_member - 1]
    part_ref, base_ref, truth_ref, weight_ref, p_ref, *gate_refs, ext_ref = refs[n_member - 1 : n_member + 7]
    grad_ref, ng_ref, *out_refs = refs[n_member + 7 :]
    own_rows = gate_refs[0].shape[2] // 2
    members, width = grad_ref.shape[0], p_ref.shape[1]
    ext = ng_ref.shape[0] // members
    channels = truth_ref.shape[0]
    total = members * n_member
    spread = (1.0 - (1.0 - ALPHA) / total) / (total * (total - 1))

    grad_ref[...] = jnp.zeros_like(grad_ref)
    own = [part_ref[m, 0:channels, :] for m in range(members)]
    sent_rows = -(-channels // 8) * 8
    others = []
    for ref in recv_refs:
        rows = ref[...].astype(F32)
        others += [rows[k * sent_rows : k * sent_rows + channels] for k in range(members)]
    for m in range(members):
        slopes = jnp.zeros_like(own[m])
        for k in range(members):
            if k != m:
                slopes = slopes + soft_slope(own[m] - own[k])
        for other in others:
            slopes = slopes + soft_slope(own[m] - other)
        gap = soft_slope(own[m] + base_ref[0:channels, :] - truth_ref[...])
        grad_ref[m, 0:channels, :] = (weight_ref[...] * (gap / total - spread * slopes)).astype(BF)
    dm = [mm(grad_ref[m].astype(F32).T.astype(BF), p_ref[...]).astype(BF) for m in range(members)]
    for pair in range(width // LANES):
        cols = slice(pair * LANES, (pair + 1) * LANES)
        for m in range(members):
            result = mm(joined(gate_refs, pair, m), dm[m][:, cols])
            ng_ref[m * ext : (m + 1) * ext, cols] = select_rows(result, own_rows).astype(BF)
    group_width = out_refs[0].shape[1]
    store_group(mm(ext_ref[...], ng_ref[:, 0:group_width]), 0, n_member, n_band, 0, out_refs)


def key_gradients(pairs, grad_ref, pt_ref, value_refs, slope_refs, q_ref, ng_ref):
    members = grad_ref.shape[0]
    ext = ng_ref.shape[0] // members
    own_rows = value_refs[0].shape[1]
    scale = HEAD_DIM ** (-0.5)
    tasks = [(place, pair, m) for place, pair in enumerate(pairs) for m in range(members)]
    first, count = pairs[0] * LANES, len(pairs) * LANES
    dm = [mm(pt_ref[first : first + count, :], grad_ref[m]).astype(BF) for m in range(members)]

    def gate_gradients(place, pair, m):
        cols = slice(pair * LANES, (pair + 1) * LANES)
        value = jnp.concatenate([split_heads(ref[m, :, cols]) for ref in value_refs], axis=0)
        return mm(value, dm[m][place * LANES : (place + 1) * LANES])

    ahead = gate_gradients(*tasks[0])
    for i, (place, pair, m) in enumerate(tasks):
        current = ahead
        if i + 1 < len(tasks):
            ahead = gate_gradients(*tasks[i + 1])
        dscore = (current * joined(slope_refs, pair, m).astype(F32)).astype(BF)
        keys = select_rows(mm(dscore, q_ref[:, pair * LANES : (pair + 1) * LANES]), own_rows) * scale
        ng_ref[m * ext : (m + 1) * ext, place * LANES : (place + 1) * LANES] = keys.astype(BF)


def first_keys_body(
    n_member, n_band, first_value, grad_ref, pt_ref, own_value_ref, halo_value_ref, own_slope_ref,
    halo_slope_ref, q_ref, ext_ref, ngv_ref, ng_ref, *out_refs
):
    count = ng_ref.shape[1] // LANES
    rest = mm(ext_ref[...], ngv_ref[:, first_value:])
    store_group(rest, 1, n_member, n_band, 0, out_refs)
    value_refs, slope_refs = (own_value_ref, halo_value_ref), (own_slope_ref, halo_slope_ref)
    key_gradients(range(count), grad_ref, pt_ref, value_refs, slope_refs, q_ref, ng_ref)
    store_group(mm(ext_ref[...], ng_ref[...]), 1, n_member, n_band, rest.shape[1], out_refs)


def last_keys_body(
    n_member, n_band, grad_ref, pt_ref, own_value_ref, halo_value_ref, own_slope_ref, halo_slope_ref,
    q_ref, merged_ref, wo_ref, ext_ref, ng_ref, *refs
):
    out_refs, turned = refs[:-1], refs[-1]
    members, width, _ = merged_ref.shape
    pairs = range((width - ng_ref.shape[1]) // LANES, width // LANES)
    value_refs, slope_refs = (own_value_ref, halo_value_ref), (own_slope_ref, halo_slope_ref)
    key_gradients(pairs, grad_ref, pt_ref, value_refs, slope_refs, q_ref, ng_ref)
    m_t = sum(mm(grad_ref[m], merged_ref[m], NT) for m in range(members))
    head_t = sum(mm(grad_ref[m], q_ref[...]) for m in range(members)) + mm(m_t.astype(BF), wo_ref[...])
    turned[...] = jnp.concatenate([m_t, head_t], axis=0).T
    store_group(mm(ext_ref[...], ng_ref[...]), 2, n_member, n_band, 0, out_refs)
    store_group(reorder(turned, n_member, n_band), 2, n_member, n_band, ng_ref.shape[1], out_refs)


def extended_grad_body(members, nodes, rim, first_ref, last_ref, ngv_ref, kvw_ref, own_ref, mate_ref, other_ref):
    ext = nodes + 2 * rim
    grads = jnp.concatenate([first_ref[...], last_ref[...], ngv_ref[...]], axis=1)
    rows = mm(grads, kvw_ref[...], NT)
    for m in range(members):
        at = m * ext
        own_ref[m] = rows[at : at + nodes]
        mate_ref[m * rim : (m + 1) * rim, :] = rows[at + nodes : at + nodes + rim].astype(BF)
        other_ref[m * rim : (m + 1) * rim, :] = rows[at + nodes + rim : at + ext].astype(BF)


def hidden_body(own_ref, from_mate_ref, from_other_ref, halo_ref, out_ref):
    members, nodes, _ = own_ref.shape
    rim = halo_ref.shape[1]
    mate, other = [one_hot_rows(rows, nodes) for rows in halo_lists(halo_ref)]
    for m in range(members):
        rows = slice(m * rim, (m + 1) * rim)
        out_ref[m] = own_ref[m] + mm(mate, from_mate_ref[rows, :]) + mm(other, from_other_ref[rows, :])


def finish_body(devices, own_ref, arrived_ref, hp_ref, kv_ref, out_ref, head_ref):
    width = kv_ref.shape[1] // 2
    channels = hp_ref.shape[0]
    total = (own_ref[...] + arrived_ref[...].astype(F32)) * (1.0 / devices)
    kv_ref[:, width:] = total[:, 0:width]
    kv_ref[:, 0:width] = total[:, width : 2 * width]
    m_rows = total[:, 2 * width : 2 * width + channels]
    high = m_rows.astype(BF)
    low = (m_rows - high.astype(F32)).astype(BF)
    out_ref[...] = mm(high, hp_ref[...]) + mm(low, hp_ref[...])
    head_ref[...] = total[:, 2 * width + LANES : 2 * width + LANES + channels]


def add_up(*parts):
    return functools.reduce(lambda a, b: a + b, [p.astype(F32) for p in parts])


def swap(rows, axis, bit, count):
    return lax.ppermute(rows, axis, [(i, i ^ (1 << bit)) for i in range(count)])


def upper(terms):
    return [t[: t.shape[0] // 2] for t in terms]


def lower(terms):
    return [t[t.shape[0] // 2 :] for t in terms]


def shards(
    n_member, n_band,
    hidden, queries, kv_weight, out_weight, head_projection, initial_state, truth,
    latitude_weight, channel_loss_weight, sources, halo_rows,
):
    members, nodes, width = hidden.shape
    points = queries.shape[0]
    channels = head_projection.shape[1]
    rim = halo_rows.shape[1]
    ext = nodes + 2 * rim
    pairs = width // LANES
    devices = n_member * n_band
    rw = width // devices
    chips = n_band // 2
    send_rows = -(-channels // 8) * 8
    mates = [(i, i ^ 1) for i in range(n_band)]
    others = [(i, (i + 1 if i % 2 else i - 1) % n_band) for i in range(n_band)]

    own_hidden, halo, for_mate, for_other = call(
        pick_body,
        [sds(hidden.shape, BF), sds(halo_rows.shape, jnp.int32)] + [sds((members * rim, width), BF)] * 2,
        (hidden, halo_rows),
        [pltpu.SemaphoreType.DMA((2,))],
        hbm=(0, 1),
        flops=10**10,
    )
    other = lax.ppermute(for_other, "band", others)
    mate = lax.ppermute(for_mate, "band", mates)

    hp = head_projection.T

    def gate_shapes(rows):
        return [sds((members, rows, width), BF)] + [sds((pairs, members, 2 * rows, points), BF)] * 2

    own_value, own_gates, own_slopes, own_merged, qt, pt, p, base, weight = call(
        own_body,
        gate_shapes(nodes)
        + [
            sds((members, width, points), F32),
            sds((width, points), BF),
            sds((width, LANES), BF),
            sds((LANES, width), BF),
            sds((LANES, points), F32),
            sds((channels, points), F32),
        ],
        (
            own_hidden, out_weight, hp, queries, kv_weight, initial_state,
            channel_loss_weight[None, :], latitude_weight[None, :], sources,
        ),
        [pltpu.VMEM((8, LANES), F32), pltpu.VMEM((LANES, width), F32)],
    )

    halo_value, halo_gates, halo_slopes, merged, part, sent = call(
        functools.partial(halo_body, send_rows, nodes),
        gate_shapes(2 * rim)
        + [
            sds((members, width, points), BF),
            sds((members, LANES, points), F32),
            sds((-(-members * send_rows // 16) * 16, points), BF),
        ],
        (other, mate, own_merged, kv_weight, qt, sources, p),
    )

    received = [
        lax.ppermute(sent, "member", [(i, i ^ s) for i in range(n_member)]) for s in range(n_member - 1, 0, -1)
    ]

    ext_t = call(
        functools.partial(transpose_body, n_member, n_band),
        sds((width, members * ext), BF),
        (own_hidden, mate, other),
        [pltpu.VMEM((width, members * ext), F32)],
    )

    extra = 2 * LANES
    group_width = (2 * width + extra) // GROUPS
    first_keys = 2 * group_width - width
    group_shape = [sds((width // 2, group_width), BF)] * 2
    grad, ng_value, send, keep = call(
        functools.partial(value_body, n_member, n_band),
        [sds((members, LANES, points), BF), sds((members * ext, width), BF)]
        + group_shape,
        (*received, part, base, truth, weight, p, own_gates, halo_gates, ext_t),
    )
    groups = [[keep, swap(send, "band", 0, n_band)]]
    ng_first, send, keep = call(
        functools.partial(first_keys_body, n_member, n_band, group_width),
        [sds((members * ext, first_keys), BF)] + group_shape,
        (grad, pt, own_value, halo_value, own_slopes, halo_slopes, queries, ext_t, ng_value),
    )
    groups.append([keep, swap(send, "band", 0, n_band)])
    ng_last, send, keep = call(
        functools.partial(last_keys_body, n_member, n_band),
        [sds((members * ext, width - first_keys), BF)] + group_shape,
        (grad, pt, own_value, halo_value, own_slopes, halo_slopes, queries, merged, out_weight, ext_t),
        [pltpu.VMEM((width, extra), F32)],
    )
    groups.append([keep, swap(send, "band", 0, n_band)])

    count = {"member": n_member, "band": n_band}
    turns, rest = halving_orders(n_member, n_band)
    steps = len(turns[0])
    for step in range(steps):
        outgoing = []
        for i in range(GROUPS):
            outgoing.append(add_up(*upper(groups[i])).astype(BF))
            if step == 0 and i + 1 < GROUPS:
                outgoing[i], groups[i + 1] = lax.optimization_barrier((outgoing[i], groups[i + 1]))
        if step == 0:
            outgoing, ng_last = lax.optimization_barrier((outgoing, ng_last))
            own_grad, back_mate, back_other = call(
                functools.partial(extended_grad_body, members, nodes, rim),
                [sds((members, nodes, width), F32)] + [sds((members * rim, width), BF)] * 2,
                (ng_first, ng_last, ng_value, kv_weight),
            )
        arrived = [swap(out, *turn[step], count[turn[step][0]]) for out, turn in zip(outgoing, turns)]
        if step == 0:
            from_mate = lax.ppermute(back_mate, "band", mates)
            arrived, from_mate, back_other = lax.optimization_barrier((arrived, from_mate, back_other))
        if step == steps - 1:
            arrived, back_other = lax.optimization_barrier((arrived, back_other))
            from_other = lax.ppermute(back_other, "band", others)
        groups = [lower(terms) + [new] for terms, new in zip(groups, arrived)]
    terms = [jnp.concatenate([add_up(*group) for group in groups], axis=1)]
    for axis, bit in rest:
        arrived = swap(add_up(*upper(terms)).astype(BF), axis, bit, count[axis])
        terms = lower(terms) + [arrived]

    kv_grad, out_grad, head_grad = call(
        functools.partial(finish_body, devices),
        [sds((rw, 2 * width), F32), sds((rw, width), F32), sds((rw, channels), F32)],
        (add_up(*terms[:-1]), terms[-1], hp),
    )
    kv_grad, from_other = lax.optimization_barrier((kv_grad, from_other))
    hidden_grad = call(
        hidden_body,
        sds((members, nodes, width), F32),
        (own_grad, from_mate, from_other, halo),
    )
    return hidden_grad, kv_grad, out_grad, head_grad


def solution(mesh):
    placed = (
        P("member", "band", None),
        P("band", None),
        P(),
        P(),
        P(),
        P(None, "band"),
        P(None, "band"),
        P("band"),
        P(),
        P(None, "band"),
        P("band", None),
    )
    return jax.shard_map(
        functools.partial(shards, mesh.shape["member"], mesh.shape["band"]),
        mesh=mesh,
        in_specs=placed,
        out_specs=(
            P("member", "band", None),
            P(("member", "band"), None),
            P(("member", "band"), None),
            P(("member", "band"), None),
        ),
        check_vma=False,
    )
```

```python
import functools

import jax
import jax.numpy as jnp
from jax import lax
from jax.experimental import pallas as pl
from jax.experimental.pallas import tpu as pltpu
from jax.sharding import PartitionSpec as P

HEAD_DIM = 64
LANES = 128
GROUPS = 3
ALPHA = 0.95
SOFTENING = 0.5
BF = jnp.bfloat16
F32 = jnp.float32
NN = (((1,), (0,)), ((), ()))
NT = (((1,), (1,)), ((), ()))
TN = (((0,), (0,)), ((), ()))


def mm(a, b, dims=NN):
    return lax.dot_general(a, b, dims, preferred_element_type=F32)


def call(body, out_shape, args, scratch=(), hbm=(), limit=24, flops=1):
    args = [pltpu.with_memory_space_constraint(x, pltpu.HBM) if i in hbm else x for i, x in enumerate(args)]
    return pl.pallas_call(
        body,
        out_shape=out_shape,
        in_specs=[
            pl.BlockSpec(memory_space=pltpu.HBM if i in hbm else pltpu.VMEM) for i in range(len(args))
        ],
        out_specs=jax.tree.map(lambda _: pl.BlockSpec(memory_space=pltpu.VMEM), out_shape),
        scratch_shapes=list(scratch),
        compiler_params=pltpu.CompilerParams(vmem_limit_bytes=limit * 1024 * 1024),
        cost_estimate=pl.CostEstimate(flops=flops, bytes_accessed=1, transcendentals=0),
    )(*args)


def sds(shape, dtype):
    return jax.ShapeDtypeStruct(shape, dtype)


def one_hot_rows(rows, node_count):
    nodes = lax.broadcasted_iota(jnp.int32, (node_count, rows.shape[1]), 0).astype(rows.dtype)
    return (nodes == rows).astype(F32).astype(BF)


def start_copies(pairs, sems):
    copies = [pltpu.make_async_copy(src, dst, sems.at[i]) for i, (src, dst) in enumerate(pairs)]
    for copy in copies:
        copy.start()
    return copies


def halo_lists(halo_ref):
    even = lax.axis_index("band") % 2 == 0
    down, up = halo_ref[0:1, :], halo_ref[1:2, :]
    return jnp.where(even, up, down), jnp.where(even, down, up)


def pick_body(hidden_hbm, halo_hbm, hidden_ref, halo_ref, mate_ref, other_ref, sems):
    for copy in start_copies([(hidden_hbm, hidden_ref), (halo_hbm, halo_ref)], sems):
        copy.wait()
    members, nodes, _ = hidden_ref.shape
    rim = halo_ref.shape[1]
    for rows, out_ref in zip(halo_lists(halo_ref), (mate_ref, other_ref)):
        hot = one_hot_rows(rows, nodes)
        for m in range(members):
            out_ref[m * rim : (m + 1) * rim, :] = mm(hot, hidden_ref[m], TN).astype(BF)


def split_heads(block):
    low = lax.broadcasted_iota(jnp.int32, block.shape, 1) < HEAD_DIM
    zero = jnp.zeros_like(block)
    return jnp.concatenate([jnp.where(low, block, zero), jnp.where(low, zero, block)], axis=0)


def half_mask_of(src, first, count):
    rows = lax.broadcasted_iota(jnp.int32, (count, src.shape[1]), 0) + first
    mask = rows == src[0:1, :]
    for e in range(1, src.shape[0]):
        mask = mask | (rows == src[e : e + 1, :])
    half = jnp.where(mask, 0.5, 0.0).astype(F32)
    return jnp.concatenate([half, half], axis=0)


def gate_rows(tasks, keys, values, qt_ref, half_mask, gate_ref, slope_ref, store_merged, prefetch=None):
    def scores(pair, m):
        return mm(split_heads(keys(pair, m)), qt_ref[pair * LANES : (pair + 1) * LANES, :])

    ahead = scores(*tasks[0])
    for i, (pair, m) in enumerate(tasks):
        current = ahead
        if prefetch is not None:
            prefetch(pair)
        if i + 1 < len(tasks):
            ahead = scores(*tasks[i + 1])
        turned = split_heads(values(pair, m)).astype(F32).T.astype(BF)
        gate = jnp.tanh(current) * half_mask + half_mask
        rounded = gate.astype(BF)
        gate_ref[pair, m] = rounded
        slope_ref[pair, m] = (gate - gate * gate).astype(BF)
        store_merged(pair, m, mm(turned, rounded))


def tasks_of(width, members):
    return [(pair, m) for pair in range(width // LANES) for m in range(members)]


def own_body(
    hidden_ref, wo_ref, hp_ref, q_ref, kvw_ref, init_ref, chw_ref, lat_ref, src_ref,
    value_ref, gate_ref, slope_ref, merged_ref, qt_ref, pt_ref, p_ref, base_ref, weight_ref, chw_pad, hp_pad,
):
    channels = hp_ref.shape[0]
    members, nodes, width = hidden_ref.shape
    half_scale = 0.5 * HEAD_DIM ** (-0.5)
    qt_ref[...] = (q_ref[...].astype(F32) * half_scale).T.astype(BF)
    hidden = jnp.concatenate([hidden_ref[m] for m in range(members)], axis=0)
    rows = mm(hidden, kvw_ref[...]).astype(BF)

    def part(pair, m, first):
        at = first + pair * LANES
        return rows[m * nodes : (m + 1) * nodes, at : at + LANES]

    def store_merged(pair, m, result):
        merged_ref[m, pair * LANES : (pair + 1) * LANES, :] = result

    for m in range(members):
        value_ref[m] = rows[m * nodes : (m + 1) * nodes, width:]
    gate_rows(
        tasks_of(width, members),
        lambda pair, m: part(pair, m, 0),
        lambda pair, m: part(pair, m, width),
        qt_ref, half_mask_of(src_ref[...], 0, nodes), gate_ref, slope_ref, store_merged,
    )
    hp_pad[...] = jnp.zeros_like(hp_pad)
    hp_pad[0:channels, :] = hp_ref[...].astype(F32)
    hp_t = hp_pad[...].astype(BF)
    chw_pad[:, 0:channels] = jnp.broadcast_to(chw_ref[...], (8, channels))
    weight_ref[...] = chw_pad[...].T[0:channels, 0:1] * lat_ref[...]
    base_ref[...] = mm(hp_t, q_ref[...], NT)
    base_ref[0:channels, :] = base_ref[0:channels, :] + init_ref[...]
    p = mm(hp_t, wo_ref[...], NT)
    p_ref[...] = p.astype(BF)
    pt_ref[...] = p.T.astype(BF)


def halo_body(
    channels, nodes, other_ref, mate_ref, own_ref, kvw_ref, qt_ref, src_ref, p_ref,
    value_ref, gate_ref, slope_ref, merged_ref, part_ref, send_ref,
):
    members, count, width = value_ref.shape
    points = qt_ref.shape[1]
    rim = count // 2
    step = 2 * LANES
    halo_rows = jnp.concatenate([mate_ref[...], other_ref[...]], axis=0)

    src = src_ref[...]
    even = lax.axis_index("band") % 2 == 0
    shift = jnp.where(src >= nodes + rim, -rim, jnp.where(src >= nodes, rim, 0))
    src = src + jnp.where(even, shift, 0)
    held = {}

    def prefetch(pair):
        start = (pair * LANES // step + 1) * step
        for first in (0, width):
            if start < width and first + start not in held:
                held[first + start] = mm(halo_rows, kvw_ref[:, first + start : first + start + step]).astype(BF)

    prefetch(-1)

    def rows(pair, m, first):
        at = pair * LANES % step
        block = held[first + pair * LANES - at][:, at : at + LANES]
        mate = block[m * rim : (m + 1) * rim]
        other = block[(members + m) * rim : (members + m + 1) * rim]
        return jnp.concatenate([mate, other], axis=0)

    def values(pair, m):
        result = rows(pair, m, width)
        value_ref[m, :, pair * LANES : (pair + 1) * LANES] = result
        return result

    def store_merged(pair, m, result):
        cols = slice(pair * LANES, (pair + 1) * LANES)
        merged_ref[m, cols, :] = (own_ref[m, cols, :] + result).astype(BF)

    gate_rows(
        tasks_of(width, members), lambda pair, m: rows(pair, m, 0), values,
        qt_ref, half_mask_of(src, nodes, count), gate_ref, slope_ref, store_merged, prefetch,
    )
    sent = []
    for m in range(members):
        part = mm(p_ref[...], merged_ref[m])
        part_ref[m] = part
        sent.append(part[0:channels])
    send_ref[...] = jnp.concatenate(sent, axis=0).astype(BF)


def halving_orders(n_member, n_band):
    chips = [("band", bit) for bit in range(1, n_band.bit_length() - 1)]
    member = [("member", bit) for bit in range(n_member.bit_length() - 1)]
    turn = chips + member[:1]
    return [turn[i:] + turn[:i] for i in range(GROUPS)], member[1:]


def unit_order(order, n_member, n_band):
    def key(unit):
        return [-((2 * unit[0] if axis == "band" else unit[1]) >> bit & 1) for axis, bit in order]

    return sorted([(c, m) for c in range(n_band // 2) for m in range(n_member)], key=key)


def destination_rows(member, band, n_member, n_band, rw):
    chip, core = band // 2, band % 2
    for rel_core in (1, 0):
        for rel_chip in range(n_band // 2):
            to_band = (chip ^ rel_chip) * 2 + (core ^ rel_core)
            for rel_member in range(n_member):
                yield pl.multiple_of(((member ^ rel_member) * n_band + to_band) * rw, rw)


def reorder(src_ref, n_member, n_band):
    rw = src_ref.shape[0] // (n_member * n_band)
    member, band = lax.axis_index("member"), lax.axis_index("band")
    starts = destination_rows(member, band, n_member, n_band, rw)
    return jnp.concatenate([src_ref[pl.ds(start, rw), :] for start in starts], axis=0)


def store_group(rows, group, n_member, n_band, at, out_refs):
    orders, rest = halving_orders(n_member, n_band)
    units = unit_order(orders[group] + rest, n_member, n_band)
    rw = rows.shape[0] // (n_member * n_band)
    for core, ref in enumerate(out_refs):
        starts = [((core * (n_band // 2) + chip) * n_member + member) * rw for chip, member in units]
        ordered = jnp.concatenate([rows[i : i + rw] for i in starts], axis=0)
        ref[:, at : at + rows.shape[1]] = ordered.astype(BF)


def transpose_body(n_member, n_band, hidden_ref, mate_ref, other_ref, out_ref, turned):
    members, nodes, _ = hidden_ref.shape
    rim = mate_ref.shape[0] // members
    parts = []
    for m in range(members):
        parts.append(hidden_ref[m])
        parts.append(mate_ref[m * rim : (m + 1) * rim, :])
        parts.append(other_ref[m * rim : (m + 1) * rim, :])
    turned[...] = jnp.concatenate(parts, axis=0).astype(F32).T
    out_ref[...] = reorder(turned, n_member, n_band).astype(BF)


def select_heads(block):
    half = block.shape[0] // 2
    low = lax.broadcasted_iota(jnp.int32, (half, block.shape[1]), 1) < HEAD_DIM
    return jnp.where(low, block[:half], block[half:])


def joined(refs, pair, m):
    return jnp.concatenate([ref[pair, m] for ref in refs], axis=0)


def select_rows(block, own):
    return jnp.concatenate([select_heads(block[: 2 * own]), select_heads(block[2 * own :])], axis=0)


def soft_slope(v):
    return v * lax.rsqrt(v * v + SOFTENING * SOFTENING)


def value_body(n_member, n_band, *refs):
    recv_refs = refs[: n_member - 1]
    part_ref, base_ref, truth_ref, weight_ref, p_ref, *gate_refs, ext_ref = refs[n_member - 1 : n_member + 7]
    grad_ref, ng_ref, *out_refs = refs[n_member + 7 :]
    own_rows = gate_refs[0].shape[2] // 2
    members, width = grad_ref.shape[0], p_ref.shape[1]
    ext = ng_ref.shape[0] // members
    channels = truth_ref.shape[0]
    total = members * n_member
    spread = (1.0 - (1.0 - ALPHA) / total) / (total * (total - 1))

    grad_ref[...] = jnp.zeros_like(grad_ref)
    own = [part_ref[m, 0:channels, :] for m in range(members)]
    others = []
    for ref in recv_refs:
        rows = ref[...].astype(F32)
        others += [rows[k * channels : (k + 1) * channels] for k in range(members)]
    for m in range(members):
        slopes = jnp.zeros_like(own[m])
        for k in range(members):
            if k != m:
                slopes = slopes + soft_slope(own[m] - own[k])
        for other in others:
            slopes = slopes + soft_slope(own[m] - other)
        gap = soft_slope(own[m] + base_ref[0:channels, :] - truth_ref[...])
        grad_ref[m, 0:channels, :] = (weight_ref[...] * (gap / total - spread * slopes)).astype(BF)
    dm = [mm(grad_ref[m].astype(F32).T.astype(BF), p_ref[...]).astype(BF) for m in range(members)]
    for pair in range(width // LANES):
        cols = slice(pair * LANES, (pair + 1) * LANES)
        for m in range(members):
            result = mm(joined(gate_refs, pair, m), dm[m][:, cols])
            ng_ref[m * ext : (m + 1) * ext, cols] = select_rows(result, own_rows).astype(BF)
    group_width = out_refs[0].shape[1]
    store_group(mm(ext_ref[...], ng_ref[:, 0:group_width]), 0, n_member, n_band, 0, out_refs)


def key_gradients(pairs, grad_ref, pt_ref, value_refs, slope_refs, q_ref, ng_ref):
    members = grad_ref.shape[0]
    ext = ng_ref.shape[0] // members
    own_rows = value_refs[0].shape[1]
    scale = HEAD_DIM ** (-0.5)
    tasks = [(place, pair, m) for place, pair in enumerate(pairs) for m in range(members)]
    first, count = pairs[0] * LANES, len(pairs) * LANES
    dm = [mm(pt_ref[first : first + count, :], grad_ref[m]).astype(BF) for m in range(members)]

    def gate_gradients(place, pair, m):
        cols = slice(pair * LANES, (pair + 1) * LANES)
        value = jnp.concatenate([split_heads(ref[m, :, cols]) for ref in value_refs], axis=0)
        return mm(value, dm[m][place * LANES : (place + 1) * LANES])

    ahead = gate_gradients(*tasks[0])
    for i, (place, pair, m) in enumerate(tasks):
        current = ahead
        if i + 1 < len(tasks):
            ahead = gate_gradients(*tasks[i + 1])
        dscore = (current * joined(slope_refs, pair, m).astype(F32)).astype(BF)
        keys = select_rows(mm(dscore, q_ref[:, pair * LANES : (pair + 1) * LANES]), own_rows) * scale
        ng_ref[m * ext : (m + 1) * ext, place * LANES : (place + 1) * LANES] = keys.astype(BF)


def first_keys_body(
    n_member, n_band, first_value, grad_ref, pt_ref, own_value_ref, halo_value_ref, own_slope_ref,
    halo_slope_ref, q_ref, ext_ref, ngv_ref, ng_ref, *out_refs
):
    count = ng_ref.shape[1] // LANES
    rest = mm(ext_ref[...], ngv_ref[:, first_value:])
    store_group(rest, 1, n_member, n_band, 0, out_refs)
    value_refs, slope_refs = (own_value_ref, halo_value_ref), (own_slope_ref, halo_slope_ref)
    key_gradients(range(count), grad_ref, pt_ref, value_refs, slope_refs, q_ref, ng_ref)
    store_group(mm(ext_ref[...], ng_ref[...]), 1, n_member, n_band, rest.shape[1], out_refs)


def last_keys_body(
    n_member, n_band, grad_ref, pt_ref, own_value_ref, halo_value_ref, own_slope_ref, halo_slope_ref,
    q_ref, merged_ref, wo_ref, ext_ref, ng_ref, *refs
):
    out_refs, turned = refs[:-1], refs[-1]
    members, width, _ = merged_ref.shape
    pairs = range((width - ng_ref.shape[1]) // LANES, width // LANES)
    value_refs, slope_refs = (own_value_ref, halo_value_ref), (own_slope_ref, halo_slope_ref)
    key_gradients(pairs, grad_ref, pt_ref, value_refs, slope_refs, q_ref, ng_ref)
    m_t = sum(mm(grad_ref[m], merged_ref[m], NT) for m in range(members))
    head_t = sum(mm(grad_ref[m], q_ref[...]) for m in range(members)) + mm(m_t.astype(BF), wo_ref[...])
    turned[...] = jnp.concatenate([m_t, head_t], axis=0).T
    store_group(mm(ext_ref[...], ng_ref[...]), 2, n_member, n_band, 0, out_refs)
    store_group(reorder(turned, n_member, n_band), 2, n_member, n_band, ng_ref.shape[1], out_refs)


def extended_grad_body(members, nodes, rim, first_ref, last_ref, ngv_ref, kvw_ref, own_ref, mate_ref, other_ref):
    ext = nodes + 2 * rim
    grads = jnp.concatenate([first_ref[...], last_ref[...], ngv_ref[...]], axis=1)
    rows = mm(grads, kvw_ref[...], NT)
    for m in range(members):
        at = m * ext
        own_ref[m] = rows[at : at + nodes]
        mate_ref[m * rim : (m + 1) * rim, :] = rows[at + nodes : at + nodes + rim].astype(BF)
        other_ref[m * rim : (m + 1) * rim, :] = rows[at + nodes + rim : at + ext].astype(BF)


def finish_body(
    devices, own_hidden_ref, mate_ref, other_ref, halo_ref, own_ref, arrived_ref, hp_ref,
    hidden_ref, kv_ref, out_ref, head_ref,
):
    members, nodes, _ = own_hidden_ref.shape
    rim = halo_ref.shape[1]
    mate, other = [one_hot_rows(rows, nodes) for rows in halo_lists(halo_ref)]
    for m in range(members):
        rows = slice(m * rim, (m + 1) * rim)
        back = mm(mate, mate_ref[rows, :]) + mm(other, other_ref[rows, :])
        hidden_ref[m] = own_hidden_ref[m] + back
    width = kv_ref.shape[1] // 2
    channels = hp_ref.shape[0]
    total = (own_ref[...] + arrived_ref[...].astype(F32)) * (1.0 / devices)
    kv_ref[:, width:] = total[:, 0:width]
    kv_ref[:, 0:width] = total[:, width : 2 * width]
    m_rows = total[:, 2 * width : 2 * width + channels]
    high = m_rows.astype(BF)
    low = (m_rows - high.astype(F32)).astype(BF)
    out_ref[...] = mm(high, hp_ref[...]) + mm(low, hp_ref[...])
    head_ref[...] = total[:, 2 * width + LANES : 2 * width + LANES + channels]


def add_up(*parts):
    return functools.reduce(lambda a, b: a + b, [p.astype(F32) for p in parts])


def swap(rows, axis, bit, count):
    return lax.ppermute(rows, axis, [(i, i ^ (1 << bit)) for i in range(count)])


def upper(terms):
    return [t[: t.shape[0] // 2] for t in terms]


def lower(terms):
    return [t[t.shape[0] // 2 :] for t in terms]


def shards(
    n_member, n_band,
    hidden, queries, kv_weight, out_weight, head_projection, initial_state, truth,
    latitude_weight, channel_loss_weight, sources, halo_rows,
):
    members, nodes, width = hidden.shape
    points = queries.shape[0]
    channels = head_projection.shape[1]
    rim = halo_rows.shape[1]
    ext = nodes + 2 * rim
    pairs = width // LANES
    devices = n_member * n_band
    rw = width // devices
    chips = n_band // 2
    mates = [(i, i ^ 1) for i in range(n_band)]
    others = [(i, (i + 1 if i % 2 else i - 1) % n_band) for i in range(n_band)]

    own_hidden, halo, for_mate, for_other = call(
        pick_body,
        [sds(hidden.shape, BF), sds(halo_rows.shape, jnp.int32)] + [sds((members * rim, width), BF)] * 2,
        (hidden, halo_rows),
        [pltpu.SemaphoreType.DMA((2,))],
        hbm=(0, 1),
        flops=10**10,
    )
    other = lax.ppermute(for_other, "band", others)
    mate = lax.ppermute(for_mate, "band", mates)

    hp = head_projection.T

    def gate_shapes(rows):
        return [sds((members, rows, width), BF)] + [sds((pairs, members, 2 * rows, points), BF)] * 2

    own_value, own_gates, own_slopes, own_merged, qt, pt, p, base, weight = call(
        own_body,
        gate_shapes(nodes)
        + [
            sds((members, width, points), F32),
            sds((width, points), BF),
            sds((width, LANES), BF),
            sds((LANES, width), BF),
            sds((LANES, points), F32),
            sds((channels, points), F32),
        ],
        (
            own_hidden, out_weight, hp, queries, kv_weight, initial_state,
            channel_loss_weight[None, :], latitude_weight[None, :], sources,
        ),
        [pltpu.VMEM((8, LANES), F32), pltpu.VMEM((LANES, width), F32)],
    )

    halo_value, halo_gates, halo_slopes, merged, part, sent = call(
        functools.partial(halo_body, channels, nodes),
        gate_shapes(2 * rim)
        + [
            sds((members, width, points), BF),
            sds((members, LANES, points), F32),
            sds((members * channels, points), BF),
        ],
        (other, mate, own_merged, kv_weight, qt, sources, p),
    )

    received = [
        lax.ppermute(sent, "member", [(i, i ^ s) for i in range(n_member)]) for s in range(n_member - 1, 0, -1)
    ]

    ext_t = call(
        functools.partial(transpose_body, n_member, n_band),
        sds((width, members * ext), BF),
        (own_hidden, mate, other),
        [pltpu.VMEM((width, members * ext), F32)],
    )

    extra = 2 * LANES
    group_width = (2 * width + extra) // GROUPS
    first_keys = 2 * group_width - width
    group_shape = [sds((width // 2, group_width), BF)] * 2
    grad, ng_value, send, keep = call(
        functools.partial(value_body, n_member, n_band),
        [sds((members, LANES, points), BF), sds((members * ext, width), BF)]
        + group_shape,
        (*received, part, base, truth, weight, p, own_gates, halo_gates, ext_t),
    )
    groups = [[keep, swap(send, "band", 0, n_band)]]
    ng_first, send, keep = call(
        functools.partial(first_keys_body, n_member, n_band, group_width),
        [sds((members * ext, first_keys), BF)] + group_shape,
        (grad, pt, own_value, halo_value, own_slopes, halo_slopes, queries, ext_t, ng_value),
    )
    groups.append([keep, swap(send, "band", 0, n_band)])
    ng_last, send, keep = call(
        functools.partial(last_keys_body, n_member, n_band),
        [sds((members * ext, width - first_keys), BF)] + group_shape,
        (grad, pt, own_value, halo_value, own_slopes, halo_slopes, queries, merged, out_weight, ext_t),
        [pltpu.VMEM((width, extra), F32)],
    )
    groups.append([keep, swap(send, "band", 0, n_band)])

    count = {"member": n_member, "band": n_band}
    turns, rest = halving_orders(n_member, n_band)
    steps = len(turns[0])
    for step in range(steps):
        outgoing = []
        for i in range(GROUPS):
            outgoing.append(add_up(*upper(groups[i])).astype(BF))
            if step == 0 and i + 1 < GROUPS:
                outgoing[i], groups[i + 1] = lax.optimization_barrier((outgoing[i], groups[i + 1]))
        if step == 0:
            outgoing, ng_last = lax.optimization_barrier((outgoing, ng_last))
            own_grad, back_mate, back_other = call(
                functools.partial(extended_grad_body, members, nodes, rim),
                [sds((members, nodes, width), F32)] + [sds((members * rim, width), BF)] * 2,
                (ng_first, ng_last, ng_value, kv_weight),
            )
        arrived = [swap(out, *turn[step], count[turn[step][0]]) for out, turn in zip(outgoing, turns)]
        if step == 0:
            from_mate = lax.ppermute(back_mate, "band", mates)
            arrived, from_mate, back_other = lax.optimization_barrier((arrived, from_mate, back_other))
        if step == steps - 1:
            arrived, back_other = lax.optimization_barrier((arrived, back_other))
            from_other = lax.ppermute(back_other, "band", others)
        groups = [lower(terms) + [new] for terms, new in zip(groups, arrived)]
    terms = [jnp.concatenate([add_up(*group) for group in groups], axis=1)]
    for axis, bit in rest:
        arrived = swap(add_up(*upper(terms)).astype(BF), axis, bit, count[axis])
        terms = lower(terms) + [arrived]

    return call(
        functools.partial(finish_body, devices),
        [
            sds((members, nodes, width), F32),
            sds((rw, 2 * width), F32),
            sds((rw, width), F32),
            sds((rw, channels), F32),
        ],
        (own_grad, from_mate, from_other, halo, add_up(*terms[:-1]), terms[-1], hp),
    )


def solution(mesh):
    placed = (
        P("member", "band", None),
        P("band", None),
        P(),
        P(),
        P(),
        P(None, "band"),
        P(None, "band"),
        P("band"),
        P(),
        P(None, "band"),
        P("band", None),
    )
    return jax.shard_map(
        functools.partial(shards, mesh.shape["member"], mesh.shape["band"]),
        mesh=mesh,
        in_specs=placed,
        out_specs=(
            P("member", "band", None),
            P(("member", "band"), None),
            P(("member", "band"), None),
            P(("member", "band"), None),
        ),
        check_vma=False,
    )
```

```python
import functools

import jax
import jax.numpy as jnp
from jax import lax
from jax.experimental import pallas as pl
from jax.experimental.pallas import tpu as pltpu
from jax.sharding import PartitionSpec as P

HEAD_DIM = 64
LANES = 128
GROUPS = 3
ALPHA = 0.95
SOFTENING = 0.5
BF = jnp.bfloat16
F32 = jnp.float32
NN = (((1,), (0,)), ((), ()))
NT = (((1,), (1,)), ((), ()))
TN = (((0,), (0,)), ((), ()))


def mm(a, b, dims=NN):
    return lax.dot_general(a, b, dims, preferred_element_type=F32)


def call(body, out_shape, args, scratch=(), hbm=(), limit=24, flops=1):
    args = [pltpu.with_memory_space_constraint(x, pltpu.HBM) if i in hbm else x for i, x in enumerate(args)]
    return pl.pallas_call(
        body,
        out_shape=out_shape,
        in_specs=[
            pl.BlockSpec(memory_space=pltpu.HBM if i in hbm else pltpu.VMEM) for i in range(len(args))
        ],
        out_specs=jax.tree.map(lambda _: pl.BlockSpec(memory_space=pltpu.VMEM), out_shape),
        scratch_shapes=list(scratch),
        compiler_params=pltpu.CompilerParams(vmem_limit_bytes=limit * 1024 * 1024),
        cost_estimate=pl.CostEstimate(flops=flops, bytes_accessed=1, transcendentals=0),
    )(*args)


def sds(shape, dtype):
    return jax.ShapeDtypeStruct(shape, dtype)


def one_hot_rows(rows, node_count):
    nodes = lax.broadcasted_iota(jnp.int32, (node_count, rows.shape[1]), 0).astype(rows.dtype)
    return (nodes == rows).astype(F32).astype(BF)


def start_copies(pairs, sems):
    copies = [pltpu.make_async_copy(src, dst, sems.at[i]) for i, (src, dst) in enumerate(pairs)]
    for copy in copies:
        copy.start()
    return copies


def halo_lists(halo_ref):
    even = lax.axis_index("band") % 2 == 0
    down, up = halo_ref[0:1, :], halo_ref[1:2, :]
    return jnp.where(even, up, down), jnp.where(even, down, up)


def pick_body(hidden_hbm, halo_hbm, hidden_ref, halo_ref, mate_ref, other_ref, sems):
    for copy in start_copies([(hidden_hbm, hidden_ref), (halo_hbm, halo_ref)], sems):
        copy.wait()
    members, nodes, _ = hidden_ref.shape
    rim = halo_ref.shape[1]
    for rows, out_ref in zip(halo_lists(halo_ref), (mate_ref, other_ref)):
        hot = one_hot_rows(rows, nodes)
        for m in range(members):
            out_ref[m * rim : (m + 1) * rim, :] = mm(hot, hidden_ref[m], TN).astype(BF)


def split_heads(block):
    low = lax.broadcasted_iota(jnp.int32, block.shape, 1) < HEAD_DIM
    zero = jnp.zeros_like(block)
    return jnp.concatenate([jnp.where(low, block, zero), jnp.where(low, zero, block)], axis=0)


def half_mask_of(src, first, count):
    rows = lax.broadcasted_iota(jnp.int32, (count, src.shape[1]), 0) + first
    mask = rows == src[0:1, :]
    for e in range(1, src.shape[0]):
        mask = mask | (rows == src[e : e + 1, :])
    half = jnp.where(mask, 0.5, 0.0).astype(F32)
    return jnp.concatenate([half, half], axis=0)


def gate_rows(tasks, keys, values, qt_ref, half_mask, gate_ref, slope_ref, store_merged, prefetch=None):
    def scores(pair, m):
        return mm(split_heads(keys(pair, m)), qt_ref[pair * LANES : (pair + 1) * LANES, :])

    ahead = scores(*tasks[0])
    for i, (pair, m) in enumerate(tasks):
        current = ahead
        if prefetch is not None:
            prefetch(pair)
        if i + 1 < len(tasks):
            ahead = scores(*tasks[i + 1])
        turned = split_heads(values(pair, m)).astype(F32).T.astype(BF)
        gate = jnp.tanh(current) * half_mask + half_mask
        rounded = gate.astype(BF)
        gate_ref[pair, m] = rounded
        slope_ref[pair, m] = (gate - gate * gate).astype(BF)
        store_merged(pair, m, mm(turned, rounded))


def tasks_of(width, members):
    return [(pair, m) for pair in range(width // LANES) for m in range(members)]


def own_body(
    hidden_ref, wo_ref, hp_ref, q_ref, kvw_ref, init_ref, chw_ref, lat_ref, src_ref,
    value_ref, gate_ref, slope_ref, merged_ref, qt_ref, pt_ref, p_ref, base_ref, weight_ref, chw_pad, hp_pad,
):
    channels = hp_ref.shape[0]
    members, nodes, width = hidden_ref.shape
    half_scale = 0.5 * HEAD_DIM ** (-0.5)
    qt_ref[...] = (q_ref[...].astype(F32) * half_scale).T.astype(BF)
    hidden = jnp.concatenate([hidden_ref[m] for m in range(members)], axis=0)
    rows = mm(hidden, kvw_ref[...]).astype(BF)

    def part(pair, m, first):
        at = first + pair * LANES
        return rows[m * nodes : (m + 1) * nodes, at : at + LANES]

    def store_merged(pair, m, result):
        merged_ref[m, pair * LANES : (pair + 1) * LANES, :] = result

    for m in range(members):
        value_ref[m] = rows[m * nodes : (m + 1) * nodes, width:]
    gate_rows(
        tasks_of(width, members),
        lambda pair, m: part(pair, m, 0),
        lambda pair, m: part(pair, m, width),
        qt_ref, half_mask_of(src_ref[...], 0, nodes), gate_ref, slope_ref, store_merged,
    )
    hp_pad[...] = jnp.zeros_like(hp_pad)
    hp_pad[0:channels, :] = hp_ref[...].astype(F32)
    hp_t = hp_pad[...].astype(BF)
    chw_pad[:, 0:channels] = jnp.broadcast_to(chw_ref[...], (8, channels))
    weight_ref[...] = chw_pad[...].T[0:channels, 0:1] * lat_ref[...]
    base_ref[...] = mm(hp_t, q_ref[...], NT)
    base_ref[0:channels, :] = base_ref[0:channels, :] + init_ref[...]
    p = mm(hp_t, wo_ref[...], NT)
    p_ref[...] = p.astype(BF)
    pt_ref[...] = p.T.astype(BF)


def halo_body(
    channels, nodes, other_ref, mate_ref, own_ref, kvw_ref, qt_ref, src_ref, p_ref,
    value_ref, gate_ref, slope_ref, merged_ref, part_ref, send_ref,
):
    members, count, width = value_ref.shape
    points = qt_ref.shape[1]
    rim = count // 2
    step = 2 * LANES
    halo_rows = jnp.concatenate([mate_ref[...], other_ref[...]], axis=0)

    src = src_ref[...]
    even = lax.axis_index("band") % 2 == 0
    shift = jnp.where(src >= nodes + rim, -rim, jnp.where(src >= nodes, rim, 0))
    src = src + jnp.where(even, shift, 0)
    held = {}

    def prefetch(pair):
        start = (pair * LANES // step + 1) * step
        for first in (0, width):
            if start < width and first + start not in held:
                held[first + start] = mm(halo_rows, kvw_ref[:, first + start : first + start + step]).astype(BF)

    prefetch(-1)

    def rows(pair, m, first):
        at = pair * LANES % step
        block = held[first + pair * LANES - at][:, at : at + LANES]
        mate = block[m * rim : (m + 1) * rim]
        other = block[(members + m) * rim : (members + m + 1) * rim]
        return jnp.concatenate([mate, other], axis=0)

    def values(pair, m):
        result = rows(pair, m, width)
        value_ref[m, :, pair * LANES : (pair + 1) * LANES] = result
        return result

    def store_merged(pair, m, result):
        cols = slice(pair * LANES, (pair + 1) * LANES)
        merged_ref[m, cols, :] = (own_ref[m, cols, :] + result).astype(BF)

    gate_rows(
        tasks_of(width, members), lambda pair, m: rows(pair, m, 0), values,
        qt_ref, half_mask_of(src, nodes, count), gate_ref, slope_ref, store_merged, prefetch,
    )
    sent = []
    for m in range(members):
        part = mm(p_ref[...], merged_ref[m])
        part_ref[m] = part
        sent.append(part[0:channels])
    send_ref[...] = jnp.concatenate(sent, axis=0).astype(BF)


def halving_orders(n_member, n_band):
    chips = [("band", bit) for bit in range(1, n_band.bit_length() - 1)]
    member = [("member", bit) for bit in range(n_member.bit_length() - 1)]
    turn = chips + member[:1]
    return [turn[i:] + turn[:i] for i in range(GROUPS)], member[1:]


def unit_order(order, n_member, n_band):
    def key(unit):
        return [-((2 * unit[0] if axis == "band" else unit[1]) >> bit & 1) for axis, bit in order]

    return sorted([(c, m) for c in range(n_band // 2) for m in range(n_member)], key=key)


def destination_rows(member, band, n_member, n_band, rw):
    chip, core = band // 2, band % 2
    for rel_core in (1, 0):
        for rel_chip in range(n_band // 2):
            to_band = (chip ^ rel_chip) * 2 + (core ^ rel_core)
            for rel_member in range(n_member):
                yield pl.multiple_of(((member ^ rel_member) * n_band + to_band) * rw, rw)


def reorder(src_ref, n_member, n_band):
    rw = src_ref.shape[0] // (n_member * n_band)
    member, band = lax.axis_index("member"), lax.axis_index("band")
    starts = destination_rows(member, band, n_member, n_band, rw)
    return jnp.concatenate([src_ref[pl.ds(start, rw), :] for start in starts], axis=0)


def store_group(rows, group, n_member, n_band, at, out_refs):
    orders, rest = halving_orders(n_member, n_band)
    units = unit_order(orders[group] + rest, n_member, n_band)
    rw = rows.shape[0] // (n_member * n_band)
    for core, ref in enumerate(out_refs):
        starts = [((core * (n_band // 2) + chip) * n_member + member) * rw for chip, member in units]
        ordered = jnp.concatenate([rows[i : i + rw] for i in starts], axis=0)
        ref[:, at : at + rows.shape[1]] = ordered.astype(BF)


def transpose_body(n_member, n_band, hidden_ref, mate_ref, other_ref, out_ref, turned):
    members, nodes, _ = hidden_ref.shape
    rim = mate_ref.shape[0] // members
    parts = []
    for m in range(members):
        parts.append(hidden_ref[m])
        parts.append(mate_ref[m * rim : (m + 1) * rim, :])
        parts.append(other_ref[m * rim : (m + 1) * rim, :])
    turned[...] = jnp.concatenate(parts, axis=0).astype(F32).T
    out_ref[...] = reorder(turned, n_member, n_band).astype(BF)


def select_heads(block):
    half = block.shape[0] // 2
    low = lax.broadcasted_iota(jnp.int32, (half, block.shape[1]), 1) < HEAD_DIM
    return jnp.where(low, block[:half], block[half:])


def joined(refs, pair, m):
    return jnp.concatenate([ref[pair, m] for ref in refs], axis=0)


def select_rows(block, own):
    return jnp.concatenate([select_heads(block[: 2 * own]), select_heads(block[2 * own :])], axis=0)


def soft_slope(v):
    return v * lax.rsqrt(v * v + SOFTENING * SOFTENING)


def value_body(n_member, n_band, *refs):
    recv_refs = refs[: n_member - 1]
    part_ref, base_ref, truth_ref, weight_ref, p_ref, *gate_refs, ext_ref = refs[n_member - 1 : n_member + 7]
    grad_ref, ng_ref, *out_refs = refs[n_member + 7 :]
    own_rows = gate_refs[0].shape[2] // 2
    members, width = grad_ref.shape[0], p_ref.shape[1]
    ext = ng_ref.shape[0] // members
    channels = truth_ref.shape[0]
    total = members * n_member
    spread = (1.0 - (1.0 - ALPHA) / total) / (total * (total - 1))

    grad_ref[...] = jnp.zeros_like(grad_ref)
    own = [part_ref[m, 0:channels, :] for m in range(members)]
    others = []
    for ref in recv_refs:
        rows = ref[...].astype(F32)
        others += [rows[k * channels : (k + 1) * channels] for k in range(members)]
    for m in range(members):
        slopes = jnp.zeros_like(own[m])
        for k in range(members):
            if k != m:
                slopes = slopes + soft_slope(own[m] - own[k])
        for other in others:
            slopes = slopes + soft_slope(own[m] - other)
        gap = soft_slope(own[m] + base_ref[0:channels, :] - truth_ref[...])
        grad_ref[m, 0:channels, :] = (weight_ref[...] * (gap / total - spread * slopes)).astype(BF)
    dm = [mm(grad_ref[m].astype(F32).T.astype(BF), p_ref[...]).astype(BF) for m in range(members)]
    for pair in range(width // LANES):
        cols = slice(pair * LANES, (pair + 1) * LANES)
        for m in range(members):
            result = mm(joined(gate_refs, pair, m), dm[m][:, cols])
            ng_ref[m * ext : (m + 1) * ext, cols] = select_rows(result, own_rows).astype(BF)
    group_width = out_refs[0].shape[1]
    store_group(mm(ext_ref[...], ng_ref[:, 0:group_width]), 0, n_member, n_band, 0, out_refs)


def key_gradients(pairs, grad_ref, pt_ref, value_refs, slope_refs, q_ref, ng_ref):
    members = grad_ref.shape[0]
    ext = ng_ref.shape[0] // members
    own_rows = value_refs[0].shape[1]
    scale = HEAD_DIM ** (-0.5)
    tasks = [(place, pair, m) for place, pair in enumerate(pairs) for m in range(members)]
    first, count = pairs[0] * LANES, len(pairs) * LANES
    dm = [mm(pt_ref[first : first + count, :], grad_ref[m]).astype(BF) for m in range(members)]

    def gate_gradients(place, pair, m):
        cols = slice(pair * LANES, (pair + 1) * LANES)
        value = jnp.concatenate([split_heads(ref[m, :, cols]) for ref in value_refs], axis=0)
        return mm(value, dm[m][place * LANES : (place + 1) * LANES])

    ahead = gate_gradients(*tasks[0])
    for i, (place, pair, m) in enumerate(tasks):
        current = ahead
        if i + 1 < len(tasks):
            ahead = gate_gradients(*tasks[i + 1])
        dscore = (current * joined(slope_refs, pair, m).astype(F32)).astype(BF)
        keys = select_rows(mm(dscore, q_ref[:, pair * LANES : (pair + 1) * LANES]), own_rows) * scale
        ng_ref[m * ext : (m + 1) * ext, place * LANES : (place + 1) * LANES] = keys.astype(BF)


def first_keys_body(
    n_member, n_band, first_value, grad_ref, pt_ref, own_value_ref, halo_value_ref, own_slope_ref,
    halo_slope_ref, q_ref, ext_ref, ngv_ref, ng_ref, *out_refs
):
    count = ng_ref.shape[1] // LANES
    rest = mm(ext_ref[...], ngv_ref[:, first_value:])
    store_group(rest, 1, n_member, n_band, 0, out_refs)
    value_refs, slope_refs = (own_value_ref, halo_value_ref), (own_slope_ref, halo_slope_ref)
    key_gradients(range(count), grad_ref, pt_ref, value_refs, slope_refs, q_ref, ng_ref)
    store_group(mm(ext_ref[...], ng_ref[...]), 1, n_member, n_band, rest.shape[1], out_refs)


def last_keys_body(
    n_member, n_band, grad_ref, pt_ref, own_value_ref, halo_value_ref, own_slope_ref, halo_slope_ref,
    q_ref, merged_ref, wo_ref, ext_ref, ng_ref, *refs
):
    out_refs, turned = refs[:-1], refs[-1]
    members, width, _ = merged_ref.shape
    pairs = range((width - ng_ref.shape[1]) // LANES, width // LANES)
    value_refs, slope_refs = (own_value_ref, halo_value_ref), (own_slope_ref, halo_slope_ref)
    key_gradients(pairs, grad_ref, pt_ref, value_refs, slope_refs, q_ref, ng_ref)
    m_t = sum(mm(grad_ref[m], merged_ref[m], NT) for m in range(members))
    head_t = sum(mm(grad_ref[m], q_ref[...]) for m in range(members)) + mm(m_t.astype(BF), wo_ref[...])
    turned[...] = jnp.concatenate([m_t, head_t], axis=0).T
    store_group(mm(ext_ref[...], ng_ref[...]), 2, n_member, n_band, 0, out_refs)
    store_group(reorder(turned, n_member, n_band), 2, n_member, n_band, ng_ref.shape[1], out_refs)


def extended_grad_body(members, nodes, rim, first_ref, last_ref, ngv_ref, kvw_ref, own_ref, back_ref):
    ext = nodes + 2 * rim
    grads = jnp.concatenate([first_ref[...], last_ref[...], ngv_ref[...]], axis=1)
    rows = mm(grads, kvw_ref[...], NT)
    for m in range(members):
        at = m * ext
        own_ref[m] = rows[at : at + nodes]
        for side in range(2):
            first = (side * members + m) * rim
            start = at + nodes + side * rim
            back_ref[first : first + rim, :] = rows[start : start + rim].astype(BF)


def finish_body(
    devices, own_hidden_ref, mate_ref, other_ref, halo_ref, own_ref, arrived_ref, hp_ref,
    hidden_ref, kv_ref, out_ref, head_ref,
):
    members, nodes, _ = own_hidden_ref.shape
    rim = halo_ref.shape[1]
    mate, other = [one_hot_rows(rows, nodes) for rows in halo_lists(halo_ref)]
    for m in range(members):
        rows = slice(m * rim, (m + 1) * rim)
        back = mm(mate, mate_ref[rows, :]) + mm(other, other_ref[rows, :])
        hidden_ref[m] = own_hidden_ref[m] + back
    width = kv_ref.shape[1] // 2
    channels = hp_ref.shape[0]
    total = (own_ref[...] + arrived_ref[...].astype(F32)) * (1.0 / devices)
    kv_ref[:, width:] = total[:, 0:width]
    kv_ref[:, 0:width] = total[:, width : 2 * width]
    m_rows = total[:, 2 * width : 2 * width + channels]
    high = m_rows.astype(BF)
    low = (m_rows - high.astype(F32)).astype(BF)
    out_ref[...] = mm(high, hp_ref[...]) + mm(low, hp_ref[...])
    head_ref[...] = total[:, 2 * width + LANES : 2 * width + LANES + channels]


def add_up(*parts):
    return functools.reduce(lambda a, b: a + b, [p.astype(F32) for p in parts])


def swap(rows, axis, bit, count):
    return lax.ppermute(rows, axis, [(i, i ^ (1 << bit)) for i in range(count)])


def upper(terms):
    return [t[: t.shape[0] // 2] for t in terms]


def lower(terms):
    return [t[t.shape[0] // 2 :] for t in terms]


def shards(
    n_member, n_band,
    hidden, queries, kv_weight, out_weight, head_projection, initial_state, truth,
    latitude_weight, channel_loss_weight, sources, halo_rows,
):
    members, nodes, width = hidden.shape
    points = queries.shape[0]
    channels = head_projection.shape[1]
    rim = halo_rows.shape[1]
    ext = nodes + 2 * rim
    pairs = width // LANES
    devices = n_member * n_band
    rw = width // devices
    chips = n_band // 2
    mates = [(i, i ^ 1) for i in range(n_band)]
    others = [(i, (i + 1 if i % 2 else i - 1) % n_band) for i in range(n_band)]

    own_hidden, halo, for_mate, for_other = call(
        pick_body,
        [sds(hidden.shape, BF), sds(halo_rows.shape, jnp.int32)] + [sds((members * rim, width), BF)] * 2,
        (hidden, halo_rows),
        [pltpu.SemaphoreType.DMA((2,))],
        hbm=(0, 1),
        flops=10**10,
    )
    other = lax.ppermute(for_other, "band", others)
    mate = lax.ppermute(for_mate, "band", mates)

    hp = head_projection.T

    def gate_shapes(rows):
        return [sds((members, rows, width), BF)] + [sds((pairs, members, 2 * rows, points), BF)] * 2

    own_value, own_gates, own_slopes, own_merged, qt, pt, p, base, weight = call(
        own_body,
        gate_shapes(nodes)
        + [
            sds((members, width, points), F32),
            sds((width, points), BF),
            sds((width, LANES), BF),
            sds((LANES, width), BF),
            sds((LANES, points), F32),
            sds((channels, points), F32),
        ],
        (
            own_hidden, out_weight, hp, queries, kv_weight, initial_state,
            channel_loss_weight[None, :], latitude_weight[None, :], sources,
        ),
        [pltpu.VMEM((8, LANES), F32), pltpu.VMEM((LANES, width), F32)],
    )

    halo_value, halo_gates, halo_slopes, merged, part, sent = call(
        functools.partial(halo_body, channels, nodes),
        gate_shapes(2 * rim)
        + [
            sds((members, width, points), BF),
            sds((members, LANES, points), F32),
            sds((members * channels, points), BF),
        ],
        (other, mate, own_merged, kv_weight, qt, sources, p),
    )

    received = [
        lax.ppermute(sent, "member", [(i, i ^ s) for i in range(n_member)]) for s in range(n_member - 1, 0, -1)
    ]

    ext_t = call(
        functools.partial(transpose_body, n_member, n_band),
        sds((width, members * ext), BF),
        (own_hidden, mate, other),
        [pltpu.VMEM((width, members * ext), F32)],
    )

    extra = 2 * LANES
    group_width = (2 * width + extra) // GROUPS
    first_keys = 2 * group_width - width
    group_shape = [sds((width // 2, group_width), BF)] * 2
    grad, ng_value, send, keep = call(
        functools.partial(value_body, n_member, n_band),
        [sds((members, LANES, points), BF), sds((members * ext, width), BF)]
        + group_shape,
        (*received, part, base, truth, weight, p, own_gates, halo_gates, ext_t),
    )
    groups = [[keep, swap(send, "band", 0, n_band)]]
    ng_first, send, keep = call(
        functools.partial(first_keys_body, n_member, n_band, group_width),
        [sds((members * ext, first_keys), BF)] + group_shape,
        (grad, pt, own_value, halo_value, own_slopes, halo_slopes, queries, ext_t, ng_value),
    )
    groups.append([keep, swap(send, "band", 0, n_band)])
    ng_last, send, keep = call(
        functools.partial(last_keys_body, n_member, n_band),
        [sds((members * ext, width - first_keys), BF)] + group_shape,
        (grad, pt, own_value, halo_value, own_slopes, halo_slopes, queries, merged, out_weight, ext_t),
        [pltpu.VMEM((width, extra), F32)],
    )
    groups.append([keep, swap(send, "band", 0, n_band)])

    count = {"member": n_member, "band": n_band}
    turns, rest = halving_orders(n_member, n_band)
    steps = len(turns[0])
    for step in range(steps):
        outgoing = []
        for i in range(GROUPS):
            outgoing.append(add_up(*upper(groups[i])).astype(BF))
            if step == 0 and i + 1 < GROUPS:
                outgoing[i], groups[i + 1] = lax.optimization_barrier((outgoing[i], groups[i + 1]))
        if step == 0:
            outgoing, ng_last = lax.optimization_barrier((outgoing, ng_last))
            own_grad, back = call(
                functools.partial(extended_grad_body, members, nodes, rim),
                [sds((members, nodes, width), F32), sds((2 * members * rim, width), BF)],
                (ng_first, ng_last, ng_value, kv_weight),
            )
        arrived = [swap(out, *turn[step], count[turn[step][0]]) for out, turn in zip(outgoing, turns)]
        if step == 0:
            from_mate = lax.ppermute(back, "band", mates)
            arrived, from_mate = lax.optimization_barrier((arrived, from_mate))
        if step == steps - 1:
            onward = lower([from_mate])[0]
            arrived, onward = lax.optimization_barrier((arrived, onward))
            chips_on = [(i, (i + 2 - i % 2 * 4) % n_band) for i in range(n_band)]
            from_other = lax.ppermute(onward, "band", chips_on)
        groups = [lower(terms) + [new] for terms, new in zip(groups, arrived)]
    terms = [jnp.concatenate([add_up(*group) for group in groups], axis=1)]
    for axis, bit in rest:
        arrived = swap(add_up(*upper(terms)).astype(BF), axis, bit, count[axis])
        terms = lower(terms) + [arrived]

    return call(
        functools.partial(finish_body, devices),
        [
            sds((members, nodes, width), F32),
            sds((rw, 2 * width), F32),
            sds((rw, width), F32),
            sds((rw, channels), F32),
        ],
        (own_grad, from_mate, from_other, halo, add_up(*terms[:-1]), terms[-1], hp),
    )


def solution(mesh):
    placed = (
        P("member", "band", None),
        P("band", None),
        P(),
        P(),
        P(),
        P(None, "band"),
        P(None, "band"),
        P("band"),
        P(),
        P(None, "band"),
        P("band", None),
    )
    return jax.shard_map(
        functools.partial(shards, mesh.shape["member"], mesh.shape["band"]),
        mesh=mesh,
        in_specs=placed,
        out_specs=(
            P("member", "band", None),
            P(("member", "band"), None),
            P(("member", "band"), None),
            P(("member", "band"), None),
        ),
        check_vma=False,
    )
```

```python
import functools

import jax
import jax.numpy as jnp
from jax import lax
from jax.experimental import pallas as pl
from jax.experimental.pallas import tpu as pltpu
from jax.sharding import PartitionSpec as P

HEAD_DIM = 64
LANES = 128
GROUPS = 3
ALPHA = 0.95
SOFTENING = 0.5
BF = jnp.bfloat16
F32 = jnp.float32
NN = (((1,), (0,)), ((), ()))
NT = (((1,), (1,)), ((), ()))
TN = (((0,), (0,)), ((), ()))


def mm(a, b, dims=NN):
    return lax.dot_general(a, b, dims, preferred_element_type=F32)


def call(body, out_shape, args, scratch=(), hbm=(), limit=24, flops=1):
    args = [pltpu.with_memory_space_constraint(x, pltpu.HBM) if i in hbm else x for i, x in enumerate(args)]
    return pl.pallas_call(
        body,
        out_shape=out_shape,
        in_specs=[
            pl.BlockSpec(memory_space=pltpu.HBM if i in hbm else pltpu.VMEM) for i in range(len(args))
        ],
        out_specs=jax.tree.map(lambda _: pl.BlockSpec(memory_space=pltpu.VMEM), out_shape),
        scratch_shapes=list(scratch),
        compiler_params=pltpu.CompilerParams(vmem_limit_bytes=limit * 1024 * 1024),
        cost_estimate=pl.CostEstimate(flops=flops, bytes_accessed=1, transcendentals=0),
    )(*args)


def sds(shape, dtype):
    return jax.ShapeDtypeStruct(shape, dtype)


def one_hot_rows(rows, node_count):
    nodes = lax.broadcasted_iota(jnp.int32, (node_count, rows.shape[1]), 0).astype(rows.dtype)
    return (nodes == rows).astype(F32).astype(BF)


def start_copies(pairs, sems):
    copies = [pltpu.make_async_copy(src, dst, sems.at[i]) for i, (src, dst) in enumerate(pairs)]
    for copy in copies:
        copy.start()
    return copies


def halo_lists(halo_ref):
    even = lax.axis_index("band") % 2 == 0
    down, up = halo_ref[0:1, :], halo_ref[1:2, :]
    return jnp.where(even, up, down), jnp.where(even, down, up)


def pick_body(hidden_hbm, halo_hbm, hidden_ref, halo_ref, mate_ref, other_ref, sems):
    for copy in start_copies([(hidden_hbm, hidden_ref), (halo_hbm, halo_ref)], sems):
        copy.wait()
    members, nodes, _ = hidden_ref.shape
    rim = halo_ref.shape[1]
    for rows, out_ref in zip(halo_lists(halo_ref), (mate_ref, other_ref)):
        hot = one_hot_rows(rows, nodes)
        for m in range(members):
            out_ref[m * rim : (m + 1) * rim, :] = mm(hot, hidden_ref[m], TN).astype(BF)


def split_heads(block):
    low = lax.broadcasted_iota(jnp.int32, block.shape, 1) < HEAD_DIM
    zero = jnp.zeros_like(block)
    return jnp.concatenate([jnp.where(low, block, zero), jnp.where(low, zero, block)], axis=0)


def half_mask_of(src, first, count):
    rows = lax.broadcasted_iota(jnp.int32, (count, src.shape[1]), 0) + first
    mask = rows == src[0:1, :]
    for e in range(1, src.shape[0]):
        mask = mask | (rows == src[e : e + 1, :])
    half = jnp.where(mask, 0.5, 0.0).astype(F32)
    return jnp.concatenate([half, half], axis=0)


def gate_rows(tasks, keys, values, qt_ref, half_mask, gate_ref, slope_ref, store_merged, prefetch=None):
    def scores(pair, m):
        return mm(split_heads(keys(pair, m)), qt_ref[pair * LANES : (pair + 1) * LANES, :])

    ahead = scores(*tasks[0])
    for i, (pair, m) in enumerate(tasks):
        current = ahead
        if prefetch is not None:
            prefetch(pair)
        if i + 1 < len(tasks):
            ahead = scores(*tasks[i + 1])
        turned = split_heads(values(pair, m)).astype(F32).T.astype(BF)
        gate = jnp.tanh(current) * half_mask + half_mask
        rounded = gate.astype(BF)
        gate_ref[pair, m] = rounded
        slope_ref[pair, m] = (gate - gate * gate).astype(BF)
        store_merged(pair, m, mm(turned, rounded))


def tasks_of(width, members):
    return [(pair, m) for pair in range(width // LANES) for m in range(members)]


def own_body(
    hidden_ref, wo_ref, hp_ref, q_ref, kvw_ref, init_ref, chw_ref, lat_ref, src_ref,
    value_ref, gate_ref, slope_ref, merged_ref, qt_ref, pt_ref, p_ref, base_ref, weight_ref, chw_pad, hp_pad,
):
    channels = hp_ref.shape[0]
    members, nodes, width = hidden_ref.shape
    half_scale = 0.5 * HEAD_DIM ** (-0.5)
    qt_ref[...] = (q_ref[...].astype(F32) * half_scale).T.astype(BF)
    hidden = jnp.concatenate([hidden_ref[m] for m in range(members)], axis=0)
    rows = mm(hidden, kvw_ref[...]).astype(BF)

    def part(pair, m, first):
        at = first + pair * LANES
        return rows[m * nodes : (m + 1) * nodes, at : at + LANES]

    def store_merged(pair, m, result):
        merged_ref[m, pair * LANES : (pair + 1) * LANES, :] = result

    for m in range(members):
        value_ref[m] = rows[m * nodes : (m + 1) * nodes, width:]
    gate_rows(
        tasks_of(width, members),
        lambda pair, m: part(pair, m, 0),
        lambda pair, m: part(pair, m, width),
        qt_ref, half_mask_of(src_ref[...], 0, nodes), gate_ref, slope_ref, store_merged,
    )
    hp_pad[...] = jnp.zeros_like(hp_pad)
    hp_pad[0:channels, :] = hp_ref[...].astype(F32)
    hp_t = hp_pad[...].astype(BF)
    chw_pad[:, 0:channels] = jnp.broadcast_to(chw_ref[...], (8, channels))
    weight_ref[...] = chw_pad[...].T[0:channels, 0:1] * lat_ref[...]
    base_ref[...] = mm(hp_t, q_ref[...], NT)
    base_ref[0:channels, :] = base_ref[0:channels, :] + init_ref[...]
    p = mm(hp_t, wo_ref[...], NT)
    p_ref[...] = p.astype(BF)
    pt_ref[...] = p.T.astype(BF)


def halo_body(
    channels, nodes, other_ref, mate_ref, own_ref, kvw_ref, qt_ref, src_ref, p_ref,
    value_ref, gate_ref, slope_ref, merged_ref, part_ref, send_ref,
):
    members, count, width = value_ref.shape
    points = qt_ref.shape[1]
    rim = count // 2
    step = 2 * LANES
    halo_rows = jnp.concatenate([mate_ref[...], other_ref[...]], axis=0)

    src = src_ref[...]
    even = lax.axis_index("band") % 2 == 0
    shift = jnp.where(src >= nodes + rim, -rim, jnp.where(src >= nodes, rim, 0))
    src = src + jnp.where(even, shift, 0)
    held = {}

    def prefetch(pair):
        start = (pair * LANES // step + 1) * step
        for first in (0, width):
            if start < width and first + start not in held:
                held[first + start] = mm(halo_rows, kvw_ref[:, first + start : first + start + step]).astype(BF)

    prefetch(-1)

    def rows(pair, m, first):
        at = pair * LANES % step
        block = held[first + pair * LANES - at][:, at : at + LANES]
        mate = block[m * rim : (m + 1) * rim]
        other = block[(members + m) * rim : (members + m + 1) * rim]
        return jnp.concatenate([mate, other], axis=0)

    def values(pair, m):
        result = rows(pair, m, width)
        value_ref[m, :, pair * LANES : (pair + 1) * LANES] = result
        return result

    def store_merged(pair, m, result):
        cols = slice(pair * LANES, (pair + 1) * LANES)
        merged_ref[m, cols, :] = (own_ref[m, cols, :] + result).astype(BF)

    gate_rows(
        tasks_of(width, members), lambda pair, m: rows(pair, m, 0), values,
        qt_ref, half_mask_of(src, nodes, count), gate_ref, slope_ref, store_merged, prefetch,
    )
    sent = []
    for m in range(members):
        part = mm(p_ref[...], merged_ref[m])
        part_ref[m] = part
        sent.append(part[0:channels])
    send_ref[...] = jnp.concatenate(sent, axis=0).astype(BF)


def halving_orders(n_member, n_band):
    chips = [("band", bit) for bit in range(1, n_band.bit_length() - 1)]
    member = [("member", bit) for bit in range(n_member.bit_length() - 1)]
    turn = chips + member[:1]
    return [turn[i:] + turn[:i] for i in range(GROUPS)], member[1:]


def unit_order(order, n_member, n_band):
    def key(unit):
        return [-((2 * unit[0] if axis == "band" else unit[1]) >> bit & 1) for axis, bit in order]

    return sorted([(c, m) for c in range(n_band // 2) for m in range(n_member)], key=key)


def destination_rows(member, band, n_member, n_band, rw):
    chip, core = band // 2, band % 2
    for rel_core in (1, 0):
        for rel_chip in range(n_band // 2):
            to_band = (chip ^ rel_chip) * 2 + (core ^ rel_core)
            for rel_member in range(n_member):
                yield pl.multiple_of(((member ^ rel_member) * n_band + to_band) * rw, rw)


def reorder(src_ref, n_member, n_band):
    rw = src_ref.shape[0] // (n_member * n_band)
    member, band = lax.axis_index("member"), lax.axis_index("band")
    starts = destination_rows(member, band, n_member, n_band, rw)
    return jnp.concatenate([src_ref[pl.ds(start, rw), :] for start in starts], axis=0)


def store_group(rows, group, n_member, n_band, at, out_refs):
    orders, rest = halving_orders(n_member, n_band)
    units = unit_order(orders[group] + rest, n_member, n_band)
    rw = rows.shape[0] // (n_member * n_band)
    for core, ref in enumerate(out_refs):
        starts = [((core * (n_band // 2) + chip) * n_member + member) * rw for chip, member in units]
        ordered = jnp.concatenate([rows[i : i + rw] for i in starts], axis=0)
        ref[:, at : at + rows.shape[1]] = ordered.astype(BF)


def transpose_body(n_member, n_band, hidden_ref, mate_ref, other_ref, out_ref, turned):
    members, nodes, _ = hidden_ref.shape
    rim = mate_ref.shape[0] // members
    parts = []
    for m in range(members):
        parts.append(hidden_ref[m])
        parts.append(mate_ref[m * rim : (m + 1) * rim, :])
        parts.append(other_ref[m * rim : (m + 1) * rim, :])
    turned[...] = jnp.concatenate(parts, axis=0).astype(F32).T
    out_ref[...] = reorder(turned, n_member, n_band).astype(BF)


def select_heads(block):
    half = block.shape[0] // 2
    low = lax.broadcasted_iota(jnp.int32, (half, block.shape[1]), 1) < HEAD_DIM
    return jnp.where(low, block[:half], block[half:])


def joined(refs, pair, m):
    return jnp.concatenate([ref[pair, m] for ref in refs], axis=0)


def select_rows(block, own):
    return jnp.concatenate([select_heads(block[: 2 * own]), select_heads(block[2 * own :])], axis=0)


def soft_slope(v):
    return v * lax.rsqrt(v * v + SOFTENING * SOFTENING)


def value_body(n_member, n_band, *refs):
    recv_refs = refs[: n_member - 1]
    part_ref, base_ref, truth_ref, weight_ref, p_ref, *gate_refs, ext_ref = refs[n_member - 1 : n_member + 7]
    grad_ref, ng_ref, *out_refs = refs[n_member + 7 :]
    own_rows = gate_refs[0].shape[2] // 2
    members, width = grad_ref.shape[0], p_ref.shape[1]
    ext = ng_ref.shape[0] // members
    channels = truth_ref.shape[0]
    total = members * n_member
    spread = (1.0 - (1.0 - ALPHA) / total) / (total * (total - 1))

    grad_ref[...] = jnp.zeros_like(grad_ref)
    own = [part_ref[m, 0:channels, :] for m in range(members)]
    others = []
    for ref in recv_refs:
        rows = ref[...].astype(F32)
        others += [rows[k * channels : (k + 1) * channels] for k in range(members)]
    for m in range(members):
        slopes = jnp.zeros_like(own[m])
        for k in range(members):
            if k != m:
                slopes = slopes + soft_slope(own[m] - own[k])
        for other in others:
            slopes = slopes + soft_slope(own[m] - other)
        gap = soft_slope(own[m] + base_ref[0:channels, :] - truth_ref[...])
        grad_ref[m, 0:channels, :] = (weight_ref[...] * (gap / total - spread * slopes)).astype(BF)
    dm = [mm(grad_ref[m].astype(F32).T.astype(BF), p_ref[...]).astype(BF) for m in range(members)]
    for pair in range(width // LANES):
        cols = slice(pair * LANES, (pair + 1) * LANES)
        for m in range(members):
            result = mm(joined(gate_refs, pair, m), dm[m][:, cols])
            ng_ref[m * ext : (m + 1) * ext, cols] = select_rows(result, own_rows).astype(BF)
    group_width = out_refs[0].shape[1]
    store_group(mm(ext_ref[...], ng_ref[:, 0:group_width]), 0, n_member, n_band, 0, out_refs)


def key_gradients(pairs, grad_ref, pt_ref, value_refs, slope_refs, q_ref, ng_ref):
    members = grad_ref.shape[0]
    ext = ng_ref.shape[0] // members
    own_rows = value_refs[0].shape[1]
    scale = HEAD_DIM ** (-0.5)
    tasks = [(place, pair, m) for place, pair in enumerate(pairs) for m in range(members)]
    first, count = pairs[0] * LANES, len(pairs) * LANES
    dm = [mm(pt_ref[first : first + count, :], grad_ref[m]).astype(BF) for m in range(members)]

    def gate_gradients(place, pair, m):
        cols = slice(pair * LANES, (pair + 1) * LANES)
        value = jnp.concatenate([split_heads(ref[m, :, cols]) for ref in value_refs], axis=0)
        return mm(value, dm[m][place * LANES : (place + 1) * LANES])

    ahead = gate_gradients(*tasks[0])
    for i, (place, pair, m) in enumerate(tasks):
        current = ahead
        if i + 1 < len(tasks):
            ahead = gate_gradients(*tasks[i + 1])
        dscore = (current * joined(slope_refs, pair, m).astype(F32)).astype(BF)
        keys = select_rows(mm(dscore, q_ref[:, pair * LANES : (pair + 1) * LANES]), own_rows) * scale
        ng_ref[m * ext : (m + 1) * ext, place * LANES : (place + 1) * LANES] = keys.astype(BF)


def first_keys_body(
    n_member, n_band, first_value, grad_ref, pt_ref, own_value_ref, halo_value_ref, own_slope_ref,
    halo_slope_ref, q_ref, ext_ref, ngv_ref, ng_ref, *out_refs
):
    count = ng_ref.shape[1] // LANES
    rest = mm(ext_ref[...], ngv_ref[:, first_value:])
    store_group(rest, 1, n_member, n_band, 0, out_refs)
    value_refs, slope_refs = (own_value_ref, halo_value_ref), (own_slope_ref, halo_slope_ref)
    key_gradients(range(count), grad_ref, pt_ref, value_refs, slope_refs, q_ref, ng_ref)
    store_group(mm(ext_ref[...], ng_ref[...]), 1, n_member, n_band, rest.shape[1], out_refs)


def last_keys_body(
    n_member, n_band, grad_ref, pt_ref, own_value_ref, halo_value_ref, own_slope_ref, halo_slope_ref,
    q_ref, merged_ref, wo_ref, ext_ref, ng_ref, *refs
):
    out_refs, turned = refs[:-1], refs[-1]
    members, width, _ = merged_ref.shape
    pairs = range((width - ng_ref.shape[1]) // LANES, width // LANES)
    value_refs, slope_refs = (own_value_ref, halo_value_ref), (own_slope_ref, halo_slope_ref)
    key_gradients(pairs, grad_ref, pt_ref, value_refs, slope_refs, q_ref, ng_ref)
    m_t = sum(mm(grad_ref[m], merged_ref[m], NT) for m in range(members))
    head_t = sum(mm(grad_ref[m], q_ref[...]) for m in range(members)) + mm(m_t.astype(BF), wo_ref[...])
    turned[...] = jnp.concatenate([m_t, head_t], axis=0).T
    store_group(mm(ext_ref[...], ng_ref[...]), 2, n_member, n_band, 0, out_refs)
    store_group(reorder(turned, n_member, n_band), 2, n_member, n_band, ng_ref.shape[1], out_refs)


def extended_grad_body(members, nodes, rim, first_ref, last_ref, ngv_ref, kvw_ref, own_ref, back_ref):
    ext = nodes + 2 * rim
    grads = jnp.concatenate([first_ref[...], last_ref[...], ngv_ref[...]], axis=1)
    rows = mm(grads, kvw_ref[...], NT)
    for m in range(members):
        at = m * ext
        own_ref[m] = rows[at : at + nodes]
        for side in range(2):
            first = (side * members + m) * rim
            start = at + nodes + side * rim
            back_ref[first : first + rim, :] = rows[start : start + rim].astype(BF)


def finish_body(
    devices, own_hidden_ref, mate_ref, other_ref, halo_ref, hp_ref, late_ref, late_arrived_ref, early_ref,
    early_arrived_ref, hidden_ref, kv_ref, out_ref, head_ref,
):
    members, nodes, _ = own_hidden_ref.shape
    rim = halo_ref.shape[1]
    mate, other = [one_hot_rows(rows, nodes) for rows in halo_lists(halo_ref)]
    for m in range(members):
        rows = slice(m * rim, (m + 1) * rim)
        back = mm(mate, mate_ref[rows, :]) + mm(other, other_ref[rows, :])
        hidden_ref[m] = own_hidden_ref[m] + back
    width = kv_ref.shape[1] // 2
    channels = hp_ref.shape[0]
    late = late_ref[...] + late_arrived_ref[...].astype(F32)
    early = early_ref[...] + early_arrived_ref[...].astype(F32)
    total = jnp.concatenate([late, early], axis=1) * (1.0 / devices)
    kv_ref[:, width:] = total[:, 0:width]
    kv_ref[:, 0:width] = total[:, width : 2 * width]
    m_rows = total[:, 2 * width : 2 * width + channels]
    high = m_rows.astype(BF)
    low = (m_rows - high.astype(F32)).astype(BF)
    out_ref[...] = mm(high, hp_ref[...]) + mm(low, hp_ref[...])
    head_ref[...] = total[:, 2 * width + LANES : 2 * width + LANES + channels]


def add_up(*parts):
    return functools.reduce(lambda a, b: a + b, [p.astype(F32) for p in parts])


def swap(rows, axis, bit, count):
    return lax.ppermute(rows, axis, [(i, i ^ (1 << bit)) for i in range(count)])


def upper(terms):
    return [t[: t.shape[0] // 2] for t in terms]


def lower(terms):
    return [t[t.shape[0] // 2 :] for t in terms]


def shards(
    n_member, n_band,
    hidden, queries, kv_weight, out_weight, head_projection, initial_state, truth,
    latitude_weight, channel_loss_weight, sources, halo_rows,
):
    members, nodes, width = hidden.shape
    points = queries.shape[0]
    channels = head_projection.shape[1]
    rim = halo_rows.shape[1]
    ext = nodes + 2 * rim
    pairs = width // LANES
    devices = n_member * n_band
    rw = width // devices
    chips = n_band // 2
    mates = [(i, i ^ 1) for i in range(n_band)]
    others = [(i, (i + 1 if i % 2 else i - 1) % n_band) for i in range(n_band)]

    own_hidden, halo, for_mate, for_other = call(
        pick_body,
        [sds(hidden.shape, BF), sds(halo_rows.shape, jnp.int32)] + [sds((members * rim, width), BF)] * 2,
        (hidden, halo_rows),
        [pltpu.SemaphoreType.DMA((2,))],
        hbm=(0, 1),
        flops=10**10,
    )
    other = lax.ppermute(for_other, "band", others)
    mate = lax.ppermute(for_mate, "band", mates)

    hp = head_projection.T

    def gate_shapes(rows):
        return [sds((members, rows, width), BF)] + [sds((pairs, members, 2 * rows, points), BF)] * 2

    own_value, own_gates, own_slopes, own_merged, qt, pt, p, base, weight = call(
        own_body,
        gate_shapes(nodes)
        + [
            sds((members, width, points), F32),
            sds((width, points), BF),
            sds((width, LANES), BF),
            sds((LANES, width), BF),
            sds((LANES, points), F32),
            sds((channels, points), F32),
        ],
        (
            own_hidden, out_weight, hp, queries, kv_weight, initial_state,
            channel_loss_weight[None, :], latitude_weight[None, :], sources,
        ),
        [pltpu.VMEM((8, LANES), F32), pltpu.VMEM((LANES, width), F32)],
    )

    halo_value, halo_gates, halo_slopes, merged, part, sent = call(
        functools.partial(halo_body, channels, nodes),
        gate_shapes(2 * rim)
        + [
            sds((members, width, points), BF),
            sds((members, LANES, points), F32),
            sds((members * channels, points), BF),
        ],
        (other, mate, own_merged, kv_weight, qt, sources, p),
    )

    received = [
        lax.ppermute(sent, "member", [(i, i ^ s) for i in range(n_member)]) for s in range(n_member - 1, 0, -1)
    ]

    ext_t = call(
        functools.partial(transpose_body, n_member, n_band),
        sds((width, members * ext), BF),
        (own_hidden, mate, other),
        [pltpu.VMEM((width, members * ext), F32)],
    )

    extra = 2 * LANES
    group_width = (2 * width + extra) // GROUPS
    first_keys = 2 * group_width - width
    group_shape = [sds((width // 2, group_width), BF)] * 2
    grad, ng_value, send, keep = call(
        functools.partial(value_body, n_member, n_band),
        [sds((members, LANES, points), BF), sds((members * ext, width), BF)]
        + group_shape,
        (*received, part, base, truth, weight, p, own_gates, halo_gates, ext_t),
    )
    groups = [[keep, swap(send, "band", 0, n_band)]]
    ng_first, send, keep = call(
        functools.partial(first_keys_body, n_member, n_band, group_width),
        [sds((members * ext, first_keys), BF)] + group_shape,
        (grad, pt, own_value, halo_value, own_slopes, halo_slopes, queries, ext_t, ng_value),
    )
    groups.append([keep, swap(send, "band", 0, n_band)])
    ng_last, send, keep = call(
        functools.partial(last_keys_body, n_member, n_band),
        [sds((members * ext, width - first_keys), BF)] + group_shape,
        (grad, pt, own_value, halo_value, own_slopes, halo_slopes, queries, merged, out_weight, ext_t),
        [pltpu.VMEM((width, extra), F32)],
    )
    groups.append([keep, swap(send, "band", 0, n_band)])

    count = {"member": n_member, "band": n_band}
    turns, rest = halving_orders(n_member, n_band)
    steps = len(turns[0])
    for step in range(steps):
        outgoing = []
        for i in range(GROUPS):
            outgoing.append(add_up(*upper(groups[i])).astype(BF))
            if step == 0 and i + 1 < GROUPS:
                outgoing[i], groups[i + 1] = lax.optimization_barrier((outgoing[i], groups[i + 1]))
        if step == 0:
            outgoing, ng_last = lax.optimization_barrier((outgoing, ng_last))
            own_grad, back = call(
                functools.partial(extended_grad_body, members, nodes, rim),
                [sds((members, nodes, width), F32), sds((2 * members * rim, width), BF)],
                (ng_first, ng_last, ng_value, kv_weight),
            )
        arrived = [swap(out, *turn[step], count[turn[step][0]]) for out, turn in zip(outgoing, turns)]
        if step == 0:
            from_mate = lax.ppermute(back, "band", mates)
            arrived, from_mate = lax.optimization_barrier((arrived, from_mate))
        groups = [lower(terms) + [new] for terms, new in zip(groups, arrived)]
    late = [add_up(*groups[0])]
    early = [jnp.concatenate([add_up(*group) for group in groups[1:]], axis=1)]
    onward = lower([from_mate])[0]
    early, onward = lax.optimization_barrier((early, onward))
    from_other = lax.ppermute(onward, "band", [(i, (i + 2 - i % 2 * 4) % n_band) for i in range(n_band)])
    for axis, bit in rest:
        arrived = swap(add_up(*upper(early)).astype(BF), axis, bit, count[axis])
        early = lower(early) + [arrived]
        outgoing = add_up(*upper(late)).astype(BF)
        arrived, outgoing = lax.optimization_barrier((arrived, outgoing))
        early[-1] = arrived
        late = lower(late) + [swap(outgoing, axis, bit, count[axis])]

    return call(
        functools.partial(finish_body, devices),
        [
            sds((members, nodes, width), F32),
            sds((rw, 2 * width), F32),
            sds((rw, width), F32),
            sds((rw, channels), F32),
        ],
        (
            own_grad, from_mate, from_other, halo, hp,
            add_up(*late[:-1]), late[-1], add_up(*early[:-1]), early[-1],
        ),
    )


def solution(mesh):
    placed = (
        P("member", "band", None),
        P("band", None),
        P(),
        P(),
        P(),
        P(None, "band"),
        P(None, "band"),
        P("band"),
        P(),
        P(None, "band"),
        P("band", None),
    )
    return jax.shard_map(
        functools.partial(shards, mesh.shape["member"], mesh.shape["band"]),
        mesh=mesh,
        in_specs=placed,
        out_specs=(
            P("member", "band", None),
            P(("member", "band"), None),
            P(("member", "band"), None),
            P(("member", "band"), None),
        ),
        check_vma=False,
    )
```

```python
import functools

import jax
import jax.numpy as jnp
from jax import lax
from jax.experimental import pallas as pl
from jax.experimental.pallas import tpu as pltpu
from jax.sharding import PartitionSpec as P

HEAD_DIM = 64
LANES = 128
GROUPS = 3
ALPHA = 0.95
SOFTENING = 0.5
BF = jnp.bfloat16
F32 = jnp.float32
NN = (((1,), (0,)), ((), ()))
NT = (((1,), (1,)), ((), ()))
TN = (((0,), (0,)), ((), ()))


def mm(a, b, dims=NN):
    return lax.dot_general(a, b, dims, preferred_element_type=F32)


def call(body, out_shape, args, scratch=(), hbm=(), limit=24, flops=1):
    args = [pltpu.with_memory_space_constraint(x, pltpu.HBM) if i in hbm else x for i, x in enumerate(args)]
    return pl.pallas_call(
        body,
        out_shape=out_shape,
        in_specs=[
            pl.BlockSpec(memory_space=pltpu.HBM if i in hbm else pltpu.VMEM) for i in range(len(args))
        ],
        out_specs=jax.tree.map(lambda _: pl.BlockSpec(memory_space=pltpu.VMEM), out_shape),
        scratch_shapes=list(scratch),
        compiler_params=pltpu.CompilerParams(vmem_limit_bytes=limit * 1024 * 1024),
        cost_estimate=pl.CostEstimate(flops=flops, bytes_accessed=1, transcendentals=0),
    )(*args)


def sds(shape, dtype):
    return jax.ShapeDtypeStruct(shape, dtype)


def one_hot_rows(rows, node_count):
    nodes = lax.broadcasted_iota(jnp.int32, (node_count, rows.shape[1]), 0).astype(rows.dtype)
    return (nodes == rows).astype(F32).astype(BF)


def start_copies(pairs, sems):
    copies = [pltpu.make_async_copy(src, dst, sems.at[i]) for i, (src, dst) in enumerate(pairs)]
    for copy in copies:
        copy.start()
    return copies


def halo_lists(halo_ref):
    even = lax.axis_index("band") % 2 == 0
    down, up = halo_ref[0:1, :], halo_ref[1:2, :]
    return jnp.where(even, up, down), jnp.where(even, down, up)


def pick_body(hidden_hbm, halo_hbm, hidden_ref, halo_ref, mate_ref, other_ref, sems):
    for copy in start_copies([(hidden_hbm, hidden_ref), (halo_hbm, halo_ref)], sems):
        copy.wait()
    members, nodes, _ = hidden_ref.shape
    rim = halo_ref.shape[1]
    for rows, out_ref in zip(halo_lists(halo_ref), (mate_ref, other_ref)):
        hot = one_hot_rows(rows, nodes)
        for m in range(members):
            out_ref[m * rim : (m + 1) * rim, :] = mm(hot, hidden_ref[m], TN).astype(BF)


def split_heads(block):
    low = lax.broadcasted_iota(jnp.int32, block.shape, 1) < HEAD_DIM
    zero = jnp.zeros_like(block)
    return jnp.concatenate([jnp.where(low, block, zero), jnp.where(low, zero, block)], axis=0)


def half_mask_of(src, first, count):
    rows = lax.broadcasted_iota(jnp.int32, (count, src.shape[1]), 0) + first
    mask = rows == src[0:1, :]
    for e in range(1, src.shape[0]):
        mask = mask | (rows == src[e : e + 1, :])
    half = jnp.where(mask, 0.5, 0.0).astype(F32)
    return jnp.concatenate([half, half], axis=0)


def gate_rows(tasks, keys, values, qt_ref, half_mask, gate_ref, slope_ref, store_merged, prefetch=None):
    def scores(pair, m):
        return mm(split_heads(keys(pair, m)), qt_ref[pair * LANES : (pair + 1) * LANES, :])

    ahead = scores(*tasks[0])
    for i, (pair, m) in enumerate(tasks):
        current = ahead
        if prefetch is not None:
            prefetch(pair)
        if i + 1 < len(tasks):
            ahead = scores(*tasks[i + 1])
        turned = split_heads(values(pair, m)).astype(F32).T.astype(BF)
        gate = jnp.tanh(current) * half_mask + half_mask
        rounded = gate.astype(BF)
        gate_ref[pair, m] = rounded
        slope_ref[pair, m] = (gate - gate * gate).astype(BF)
        store_merged(pair, m, mm(turned, rounded))


def tasks_of(width, members):
    return [(pair, m) for pair in range(width // LANES) for m in range(members)]


def own_body(
    hidden_ref, wo_ref, hp_ref, q_ref, kvw_ref, init_ref, chw_ref, lat_ref, src_ref,
    value_ref, gate_ref, slope_ref, merged_ref, qt_ref, pt_ref, p_ref, base_ref, weight_ref, chw_pad, hp_pad,
):
    channels = hp_ref.shape[0]
    members, nodes, width = hidden_ref.shape
    half_scale = 0.5 * HEAD_DIM ** (-0.5)
    qt_ref[...] = (q_ref[...].astype(F32) * half_scale).T.astype(BF)
    hidden = jnp.concatenate([hidden_ref[m] for m in range(members)], axis=0)
    rows = mm(hidden, kvw_ref[...]).astype(BF)

    def part(pair, m, first):
        at = first + pair * LANES
        return rows[m * nodes : (m + 1) * nodes, at : at + LANES]

    def store_merged(pair, m, result):
        merged_ref[m, pair * LANES : (pair + 1) * LANES, :] = result

    for m in range(members):
        value_ref[m] = rows[m * nodes : (m + 1) * nodes, width:]
    gate_rows(
        tasks_of(width, members),
        lambda pair, m: part(pair, m, 0),
        lambda pair, m: part(pair, m, width),
        qt_ref, half_mask_of(src_ref[...], 0, nodes), gate_ref, slope_ref, store_merged,
    )
    hp_pad[...] = jnp.zeros_like(hp_pad)
    hp_pad[0:channels, :] = hp_ref[...].astype(F32)
    hp_t = hp_pad[...].astype(BF)
    chw_pad[:, 0:channels] = jnp.broadcast_to(chw_ref[...], (8, channels))
    weight_ref[...] = chw_pad[...].T[0:channels, 0:1] * lat_ref[...]
    base_ref[...] = mm(hp_t, q_ref[...], NT)
    base_ref[0:channels, :] = base_ref[0:channels, :] + init_ref[...]
    p = mm(hp_t, wo_ref[...], NT)
    p_ref[...] = p.astype(BF)
    pt_ref[...] = p.T.astype(BF)


def halo_body(
    channels, nodes, other_ref, mate_ref, own_ref, kvw_ref, qt_ref, src_ref, p_ref,
    value_ref, gate_ref, slope_ref, merged_ref, part_ref, send_ref,
):
    members, count, width = value_ref.shape
    points = qt_ref.shape[1]
    rim = count // 2
    step = 2 * LANES
    halo_rows = jnp.concatenate([mate_ref[...], other_ref[...]], axis=0)

    src = src_ref[...]
    even = lax.axis_index("band") % 2 == 0
    shift = jnp.where(src >= nodes + rim, -rim, jnp.where(src >= nodes, rim, 0))
    src = src + jnp.where(even, shift, 0)
    held = {}

    def prefetch(pair):
        start = (pair * LANES // step + 1) * step
        for first in (0, width):
            if start < width and first + start not in held:
                held[first + start] = mm(halo_rows, kvw_ref[:, first + start : first + start + step]).astype(BF)

    prefetch(-1)

    def rows(pair, m, first):
        at = pair * LANES % step
        block = held[first + pair * LANES - at][:, at : at + LANES]
        mate = block[m * rim : (m + 1) * rim]
        other = block[(members + m) * rim : (members + m + 1) * rim]
        return jnp.concatenate([mate, other], axis=0)

    def values(pair, m):
        result = rows(pair, m, width)
        value_ref[m, :, pair * LANES : (pair + 1) * LANES] = result
        return result

    def store_merged(pair, m, result):
        cols = slice(pair * LANES, (pair + 1) * LANES)
        merged_ref[m, cols, :] = (own_ref[m, cols, :] + result).astype(BF)

    gate_rows(
        tasks_of(width, members), lambda pair, m: rows(pair, m, 0), values,
        qt_ref, half_mask_of(src, nodes, count), gate_ref, slope_ref, store_merged, prefetch,
    )
    sent = []
    for m in range(members):
        part = mm(p_ref[...], merged_ref[m])
        part_ref[m] = part
        sent.append(part[0:channels])
    send_ref[...] = jnp.concatenate(sent, axis=0).astype(BF)


def halving_orders(n_member, n_band):
    chips = [("band", bit) for bit in range(1, n_band.bit_length() - 1)]
    member = [("member", bit) for bit in range(n_member.bit_length() - 1)]
    turn = chips + member[:1]
    return [turn[i:] + turn[:i] for i in range(GROUPS)], member[1:]


def unit_order(order, n_member, n_band):
    def key(unit):
        return [-((2 * unit[0] if axis == "band" else unit[1]) >> bit & 1) for axis, bit in order]

    return sorted([(c, m) for c in range(n_band // 2) for m in range(n_member)], key=key)


def destination_rows(member, band, n_member, n_band, rw):
    chip, core = band // 2, band % 2
    for rel_core in (1, 0):
        for rel_chip in range(n_band // 2):
            to_band = (chip ^ rel_chip) * 2 + (core ^ rel_core)
            for rel_member in range(n_member):
                yield pl.multiple_of(((member ^ rel_member) * n_band + to_band) * rw, rw)


def reorder(src_ref, n_member, n_band):
    rw = src_ref.shape[0] // (n_member * n_band)
    member, band = lax.axis_index("member"), lax.axis_index("band")
    starts = destination_rows(member, band, n_member, n_band, rw)
    return jnp.concatenate([src_ref[pl.ds(start, rw), :] for start in starts], axis=0)


def store_group(rows, group, n_member, n_band, at, out_refs):
    orders, rest = halving_orders(n_member, n_band)
    units = unit_order(orders[group] + rest, n_member, n_band)
    rw = rows.shape[0] // (n_member * n_band)
    for core, ref in enumerate(out_refs):
        starts = [((core * (n_band // 2) + chip) * n_member + member) * rw for chip, member in units]
        ordered = jnp.concatenate([rows[i : i + rw] for i in starts], axis=0)
        ref[:, at : at + rows.shape[1]] = ordered.astype(BF)


def transpose_body(n_member, n_band, hidden_ref, mate_ref, other_ref, out_ref, turned):
    members, nodes, _ = hidden_ref.shape
    rim = mate_ref.shape[0] // members
    parts = []
    for m in range(members):
        parts.append(hidden_ref[m])
        parts.append(mate_ref[m * rim : (m + 1) * rim, :])
        parts.append(other_ref[m * rim : (m + 1) * rim, :])
    turned[...] = jnp.concatenate(parts, axis=0).astype(F32).T
    out_ref[...] = reorder(turned, n_member, n_band).astype(BF)


def select_heads(block):
    half = block.shape[0] // 2
    low = lax.broadcasted_iota(jnp.int32, (half, block.shape[1]), 1) < HEAD_DIM
    return jnp.where(low, block[:half], block[half:])


def joined(refs, pair, m):
    return jnp.concatenate([ref[pair, m] for ref in refs], axis=0)


def select_rows(block, own):
    return jnp.concatenate([select_heads(block[: 2 * own]), select_heads(block[2 * own :])], axis=0)


def soft_slope(v):
    return v * lax.rsqrt(v * v + SOFTENING * SOFTENING)


def value_body(n_member, n_band, *refs):
    recv_refs = refs[: n_member - 1]
    part_ref, base_ref, truth_ref, weight_ref, p_ref, *gate_refs, ext_ref = refs[n_member - 1 : n_member + 7]
    grad_ref, ng_ref, *out_refs = refs[n_member + 7 :]
    own_rows = gate_refs[0].shape[2] // 2
    members, width = grad_ref.shape[0], p_ref.shape[1]
    ext = ng_ref.shape[0] // members
    channels = truth_ref.shape[0]
    total = members * n_member
    spread = (1.0 - (1.0 - ALPHA) / total) / (total * (total - 1))

    grad_ref[...] = jnp.zeros_like(grad_ref)
    own = [part_ref[m, 0:channels, :] for m in range(members)]
    others = []
    for ref in recv_refs:
        rows = ref[...].astype(F32)
        others += [rows[k * channels : (k + 1) * channels] for k in range(members)]
    for m in range(members):
        slopes = jnp.zeros_like(own[m])
        for k in range(members):
            if k != m:
                slopes = slopes + soft_slope(own[m] - own[k])
        for other in others:
            slopes = slopes + soft_slope(own[m] - other)
        gap = soft_slope(own[m] + base_ref[0:channels, :] - truth_ref[...])
        grad_ref[m, 0:channels, :] = (weight_ref[...] * (gap / total - spread * slopes)).astype(BF)
    dm = [mm(grad_ref[m].astype(F32).T.astype(BF), p_ref[...]).astype(BF) for m in range(members)]
    for pair in range(width // LANES):
        cols = slice(pair * LANES, (pair + 1) * LANES)
        for m in range(members):
            result = mm(joined(gate_refs, pair, m), dm[m][:, cols])
            ng_ref[m * ext : (m + 1) * ext, cols] = select_rows(result, own_rows).astype(BF)
    group_width = out_refs[0].shape[1]
    store_group(mm(ext_ref[...], ng_ref[:, 0:group_width]), 0, n_member, n_band, 0, out_refs)


def key_gradients(pairs, grad_ref, pt_ref, value_refs, slope_refs, q_ref, ng_ref):
    members = grad_ref.shape[0]
    ext = ng_ref.shape[0] // members
    own_rows = value_refs[0].shape[1]
    scale = HEAD_DIM ** (-0.5)
    tasks = [(place, pair, m) for place, pair in enumerate(pairs) for m in range(members)]
    first, count = pairs[0] * LANES, len(pairs) * LANES
    dm = [mm(pt_ref[first : first + count, :], grad_ref[m]).astype(BF) for m in range(members)]

    def gate_gradients(place, pair, m):
        cols = slice(pair * LANES, (pair + 1) * LANES)
        value = jnp.concatenate([split_heads(ref[m, :, cols]) for ref in value_refs], axis=0)
        return mm(value, dm[m][place * LANES : (place + 1) * LANES])

    ahead = gate_gradients(*tasks[0])
    for i, (place, pair, m) in enumerate(tasks):
        current = ahead
        if i + 1 < len(tasks):
            ahead = gate_gradients(*tasks[i + 1])
        dscore = (current * joined(slope_refs, pair, m).astype(F32)).astype(BF)
        keys = select_rows(mm(dscore, q_ref[:, pair * LANES : (pair + 1) * LANES]), own_rows) * scale
        ng_ref[m * ext : (m + 1) * ext, place * LANES : (place + 1) * LANES] = keys.astype(BF)


def first_keys_body(
    n_member, n_band, first_value, grad_ref, pt_ref, own_value_ref, halo_value_ref, own_slope_ref,
    halo_slope_ref, q_ref, ext_ref, ngv_ref, ng_ref, *out_refs
):
    count = ng_ref.shape[1] // LANES
    rest = mm(ext_ref[...], ngv_ref[:, first_value:])
    store_group(rest, 1, n_member, n_band, 0, out_refs)
    value_refs, slope_refs = (own_value_ref, halo_value_ref), (own_slope_ref, halo_slope_ref)
    key_gradients(range(count), grad_ref, pt_ref, value_refs, slope_refs, q_ref, ng_ref)
    store_group(mm(ext_ref[...], ng_ref[...]), 1, n_member, n_band, rest.shape[1], out_refs)


def last_keys_body(
    n_member, n_band, grad_ref, pt_ref, own_value_ref, halo_value_ref, own_slope_ref, halo_slope_ref,
    q_ref, merged_ref, wo_ref, ext_ref, ng_ref, *refs
):
    out_refs, turned = refs[:-1], refs[-1]
    members, width, _ = merged_ref.shape
    pairs = range((width - ng_ref.shape[1]) // LANES, width // LANES)
    value_refs, slope_refs = (own_value_ref, halo_value_ref), (own_slope_ref, halo_slope_ref)
    key_gradients(pairs, grad_ref, pt_ref, value_refs, slope_refs, q_ref, ng_ref)
    m_t = sum(mm(grad_ref[m], merged_ref[m], NT) for m in range(members))
    head_t = sum(mm(grad_ref[m], q_ref[...]) for m in range(members)) + mm(m_t.astype(BF), wo_ref[...])
    turned[...] = jnp.concatenate([m_t, head_t], axis=0).T
    store_group(mm(ext_ref[...], ng_ref[...]), 2, n_member, n_band, 0, out_refs)
    store_group(reorder(turned, n_member, n_band), 2, n_member, n_band, ng_ref.shape[1], out_refs)


def extended_grad_body(members, nodes, rim, first_ref, last_ref, ngv_ref, kvw_ref, own_ref, back_ref):
    ext = nodes + 2 * rim
    grads = jnp.concatenate([first_ref[...], last_ref[...], ngv_ref[...]], axis=1)
    rows = mm(grads, kvw_ref[...], NT)
    for m in range(members):
        at = m * ext
        own_ref[m] = rows[at : at + nodes]
        for side in range(2):
            first = (side * members + m) * rim
            start = at + nodes + side * rim
            back_ref[first : first + rim, :] = rows[start : start + rim].astype(BF)


def finish_body(
    devices, own_hidden_ref, mate_ref, other_ref, halo_ref, own_ref, arrived_ref, hp_ref,
    hidden_ref, kv_ref, out_ref, head_ref,
):
    members, nodes, _ = own_hidden_ref.shape
    rim = halo_ref.shape[1]
    mate, other = [one_hot_rows(rows, nodes) for rows in halo_lists(halo_ref)]
    for m in range(members):
        rows = slice(m * rim, (m + 1) * rim)
        back = mm(mate, mate_ref[rows, :]) + mm(other, other_ref[rows, :])
        hidden_ref[m] = own_hidden_ref[m] + back
    width = kv_ref.shape[1] // 2
    channels = hp_ref.shape[0]
    total = (own_ref[...] + arrived_ref[...].astype(F32)) * (1.0 / devices)
    kv_ref[:, width:] = total[:, 0:width]
    kv_ref[:, 0:width] = total[:, width : 2 * width]
    m_rows = total[:, 2 * width : 2 * width + channels]
    high = m_rows.astype(BF)
    low = (m_rows - high.astype(F32)).astype(BF)
    out_ref[...] = mm(high, hp_ref[...]) + mm(low, hp_ref[...])
    head_ref[...] = total[:, 2 * width + LANES : 2 * width + LANES + channels]


def add_up(*parts):
    return functools.reduce(lambda a, b: a + b, [p.astype(F32) for p in parts])


def swap(rows, axis, bit, count):
    return lax.ppermute(rows, axis, [(i, i ^ (1 << bit)) for i in range(count)])


def upper(terms):
    return [t[: t.shape[0] // 2] for t in terms]


def lower(terms):
    return [t[t.shape[0] // 2 :] for t in terms]


def shards(
    n_member, n_band,
    hidden, queries, kv_weight, out_weight, head_projection, initial_state, truth,
    latitude_weight, channel_loss_weight, sources, halo_rows,
):
    members, nodes, width = hidden.shape
    points = queries.shape[0]
    channels = head_projection.shape[1]
    rim = halo_rows.shape[1]
    ext = nodes + 2 * rim
    pairs = width // LANES
    devices = n_member * n_band
    rw = width // devices
    chips = n_band // 2
    mates = [(i, i ^ 1) for i in range(n_band)]
    others = [(i, (i + 1 if i % 2 else i - 1) % n_band) for i in range(n_band)]

    own_hidden, halo, for_mate, for_other = call(
        pick_body,
        [sds(hidden.shape, BF), sds(halo_rows.shape, jnp.int32)] + [sds((members * rim, width), BF)] * 2,
        (hidden, halo_rows),
        [pltpu.SemaphoreType.DMA((2,))],
        hbm=(0, 1),
        flops=10**10,
    )
    other = lax.ppermute(for_other, "band", others)
    mate = lax.ppermute(for_mate, "band", mates)

    hp = head_projection.T

    def gate_shapes(rows):
        return [sds((members, rows, width), BF)] + [sds((pairs, members, 2 * rows, points), BF)] * 2

    own_value, own_gates, own_slopes, own_merged, qt, pt, p, base, weight = call(
        own_body,
        gate_shapes(nodes)
        + [
            sds((members, width, points), F32),
            sds((width, points), BF),
            sds((width, LANES), BF),
            sds((LANES, width), BF),
            sds((LANES, points), F32),
            sds((channels, points), F32),
        ],
        (
            own_hidden, out_weight, hp, queries, kv_weight, initial_state,
            channel_loss_weight[None, :], latitude_weight[None, :], sources,
        ),
        [pltpu.VMEM((8, LANES), F32), pltpu.VMEM((LANES, width), F32)],
    )

    halo_value, halo_gates, halo_slopes, merged, part, sent = call(
        functools.partial(halo_body, channels, nodes),
        gate_shapes(2 * rim)
        + [
            sds((members, width, points), BF),
            sds((members, LANES, points), F32),
            sds((members * channels, points), BF),
        ],
        (other, mate, own_merged, kv_weight, qt, sources, p),
    )

    received = [
        lax.ppermute(sent, "member", [(i, i ^ s) for i in range(n_member)]) for s in range(n_member - 1, 0, -1)
    ]

    ext_t = call(
        functools.partial(transpose_body, n_member, n_band),
        sds((width, members * ext), BF),
        (own_hidden, mate, other),
        [pltpu.VMEM((width, members * ext), F32)],
    )

    extra = 2 * LANES
    group_width = (2 * width + extra) // GROUPS
    first_keys = 2 * group_width - width
    group_shape = [sds((width // 2, group_width), BF)] * 2
    grad, ng_value, send, keep = call(
        functools.partial(value_body, n_member, n_band),
        [sds((members, LANES, points), BF), sds((members * ext, width), BF)]
        + group_shape,
        (*received, part, base, truth, weight, p, own_gates, halo_gates, ext_t),
    )
    groups = [[keep, swap(send, "band", 0, n_band)]]
    ng_first, send, keep = call(
        functools.partial(first_keys_body, n_member, n_band, group_width),
        [sds((members * ext, first_keys), BF)] + group_shape,
        (grad, pt, own_value, halo_value, own_slopes, halo_slopes, queries, ext_t, ng_value),
    )
    groups.append([keep, swap(send, "band", 0, n_band)])
    ng_last, send, keep = call(
        functools.partial(last_keys_body, n_member, n_band),
        [sds((members * ext, width - first_keys), BF)] + group_shape,
        (grad, pt, own_value, halo_value, own_slopes, halo_slopes, queries, merged, out_weight, ext_t),
        [pltpu.VMEM((width, extra), F32)],
    )
    groups.append([keep, swap(send, "band", 0, n_band)])

    count = {"member": n_member, "band": n_band}
    turns, rest = halving_orders(n_member, n_band)
    steps = len(turns[0])
    for step in range(steps):
        outgoing = []
        for i in range(GROUPS):
            outgoing.append(add_up(*upper(groups[i])).astype(BF))
            if step <= 1 and i + 1 < GROUPS:
                outgoing[i], groups[i + 1] = lax.optimization_barrier((outgoing[i], groups[i + 1]))
        if step == 0:
            outgoing, ng_last = lax.optimization_barrier((outgoing, ng_last))
            own_grad, back = call(
                functools.partial(extended_grad_body, members, nodes, rim),
                [sds((members, nodes, width), F32), sds((2 * members * rim, width), BF)],
                (ng_first, ng_last, ng_value, kv_weight),
            )
        arrived = [swap(out, *turn[step], count[turn[step][0]]) for out, turn in zip(outgoing, turns)]
        if step == 0:
            from_mate = lax.ppermute(back, "band", mates)
            arrived[-1], from_mate = lax.optimization_barrier((arrived[-1], from_mate))
        if step == steps - 1:
            onward = lower([from_mate])[0]
            arrived, onward = lax.optimization_barrier((arrived, onward))
            chips_on = [(i, (i + 2 - i % 2 * 4) % n_band) for i in range(n_band)]
            from_other = lax.ppermute(onward, "band", chips_on)
        groups = [lower(terms) + [new] for terms, new in zip(groups, arrived)]
    terms = [jnp.concatenate([add_up(*group) for group in groups], axis=1)]
    for axis, bit in rest:
        arrived = swap(add_up(*upper(terms)).astype(BF), axis, bit, count[axis])
        terms = lower(terms) + [arrived]

    return call(
        functools.partial(finish_body, devices),
        [
            sds((members, nodes, width), F32),
            sds((rw, 2 * width), F32),
            sds((rw, width), F32),
            sds((rw, channels), F32),
        ],
        (own_grad, from_mate, from_other, halo, add_up(*terms[:-1]), terms[-1], hp),
    )


def solution(mesh):
    placed = (
        P("member", "band", None),
        P("band", None),
        P(),
        P(),
        P(),
        P(None, "band"),
        P(None, "band"),
        P("band"),
        P(),
        P(None, "band"),
        P("band", None),
    )
    return jax.shard_map(
        functools.partial(shards, mesh.shape["member"], mesh.shape["band"]),
        mesh=mesh,
        in_specs=placed,
        out_specs=(
            P("member", "band", None),
            P(("member", "band"), None),
            P(("member", "band"), None),
            P(("member", "band"), None),
        ),
        check_vma=False,
    )
```

```python
import functools

import jax
import jax.numpy as jnp
from jax import lax
from jax.experimental import pallas as pl
from jax.experimental.pallas import tpu as pltpu
from jax.sharding import PartitionSpec as P

HEAD_DIM = 64
LANES = 128
GROUPS = 3
ALPHA = 0.95
SOFTENING = 0.5
BF = jnp.bfloat16
F32 = jnp.float32
NN = (((1,), (0,)), ((), ()))
NT = (((1,), (1,)), ((), ()))
TN = (((0,), (0,)), ((), ()))


def mm(a, b, dims=NN):
    return lax.dot_general(a, b, dims, preferred_element_type=F32)


def call(body, out_shape, args, scratch=(), hbm=(), limit=24, flops=1):
    args = [pltpu.with_memory_space_constraint(x, pltpu.HBM) if i in hbm else x for i, x in enumerate(args)]
    return pl.pallas_call(
        body,
        out_shape=out_shape,
        in_specs=[
            pl.BlockSpec(memory_space=pltpu.HBM if i in hbm else pltpu.VMEM) for i in range(len(args))
        ],
        out_specs=jax.tree.map(lambda _: pl.BlockSpec(memory_space=pltpu.VMEM), out_shape),
        scratch_shapes=list(scratch),
        compiler_params=pltpu.CompilerParams(vmem_limit_bytes=limit * 1024 * 1024),
        cost_estimate=pl.CostEstimate(flops=flops, bytes_accessed=1, transcendentals=0),
    )(*args)


def sds(shape, dtype):
    return jax.ShapeDtypeStruct(shape, dtype)


def one_hot_rows(rows, node_count):
    nodes = lax.broadcasted_iota(jnp.int32, (node_count, rows.shape[1]), 0).astype(rows.dtype)
    return (nodes == rows).astype(F32).astype(BF)


def start_copies(pairs, sems):
    copies = [pltpu.make_async_copy(src, dst, sems.at[i]) for i, (src, dst) in enumerate(pairs)]
    for copy in copies:
        copy.start()
    return copies


def halo_lists(halo_ref):
    even = lax.axis_index("band") % 2 == 0
    down, up = halo_ref[0:1, :], halo_ref[1:2, :]
    return jnp.where(even, up, down), jnp.where(even, down, up)


def pick_body(hidden_hbm, halo_hbm, hidden_ref, halo_ref, mate_ref, other_ref, sems):
    for copy in start_copies([(hidden_hbm, hidden_ref), (halo_hbm, halo_ref)], sems):
        copy.wait()
    members, nodes, _ = hidden_ref.shape
    rim = halo_ref.shape[1]
    for rows, out_ref in zip(halo_lists(halo_ref), (mate_ref, other_ref)):
        hot = one_hot_rows(rows, nodes)
        for m in range(members):
            out_ref[m * rim : (m + 1) * rim, :] = mm(hot, hidden_ref[m], TN).astype(BF)


def split_heads(block):
    low = lax.broadcasted_iota(jnp.int32, block.shape, 1) < HEAD_DIM
    zero = jnp.zeros_like(block)
    return jnp.concatenate([jnp.where(low, block, zero), jnp.where(low, zero, block)], axis=0)


def half_mask_of(src, first, count):
    rows = lax.broadcasted_iota(jnp.int32, (count, src.shape[1]), 0) + first
    mask = rows == src[0:1, :]
    for e in range(1, src.shape[0]):
        mask = mask | (rows == src[e : e + 1, :])
    half = jnp.where(mask, 0.5, 0.0).astype(F32)
    return jnp.concatenate([half, half], axis=0)


def gate_rows(tasks, keys, values, qt_ref, half_mask, gate_ref, slope_ref, store_merged, prefetch=None):
    def scores(pair, m):
        return mm(split_heads(keys(pair, m)), qt_ref[pair * LANES : (pair + 1) * LANES, :])

    ahead = scores(*tasks[0])
    for i, (pair, m) in enumerate(tasks):
        current = ahead
        if prefetch is not None:
            prefetch(pair)
        if i + 1 < len(tasks):
            ahead = scores(*tasks[i + 1])
        turned = split_heads(values(pair, m)).astype(F32).T.astype(BF)
        gate = jnp.tanh(current) * half_mask + half_mask
        rounded = gate.astype(BF)
        gate_ref[pair, m] = rounded
        slope_ref[pair, m] = (gate - gate * gate).astype(BF)
        store_merged(pair, m, mm(turned, rounded))


def tasks_of(width, members):
    return [(pair, m) for pair in range(width // LANES) for m in range(members)]


def own_body(
    hidden_ref, wo_ref, hp_ref, q_ref, kvw_ref, init_ref, chw_ref, lat_ref, src_ref,
    value_ref, gate_ref, slope_ref, merged_ref, qt_ref, pt_ref, p_ref, base_ref, weight_ref, chw_pad, hp_pad,
):
    channels = hp_ref.shape[0]
    members, nodes, width = hidden_ref.shape
    half_scale = 0.5 * HEAD_DIM ** (-0.5)
    qt_ref[...] = (q_ref[...].astype(F32) * half_scale).T.astype(BF)
    hidden = jnp.concatenate([hidden_ref[m] for m in range(members)], axis=0)
    rows = mm(hidden, kvw_ref[...]).astype(BF)

    def part(pair, m, first):
        at = first + pair * LANES
        return rows[m * nodes : (m + 1) * nodes, at : at + LANES]

    def store_merged(pair, m, result):
        merged_ref[m, pair * LANES : (pair + 1) * LANES, :] = result

    for m in range(members):
        value_ref[m] = rows[m * nodes : (m + 1) * nodes, width:]
    gate_rows(
        tasks_of(width, members),
        lambda pair, m: part(pair, m, 0),
        lambda pair, m: part(pair, m, width),
        qt_ref, half_mask_of(src_ref[...], 0, nodes), gate_ref, slope_ref, store_merged,
    )
    hp_pad[...] = jnp.zeros_like(hp_pad)
    hp_pad[0:channels, :] = hp_ref[...].astype(F32)
    hp_t = hp_pad[...].astype(BF)
    chw_pad[:, 0:channels] = jnp.broadcast_to(chw_ref[...], (8, channels))
    weight_ref[...] = chw_pad[...].T[0:channels, 0:1] * lat_ref[...]
    base_ref[...] = mm(hp_t, q_ref[...], NT)
    base_ref[0:channels, :] = base_ref[0:channels, :] + init_ref[...]
    p = mm(hp_t, wo_ref[...], NT)
    p_ref[...] = p.astype(BF)
    pt_ref[...] = p.T.astype(BF)


def halo_body(
    channels, nodes, other_ref, mate_ref, own_ref, kvw_ref, qt_ref, src_ref, p_ref,
    value_ref, gate_ref, slope_ref, merged_ref, part_ref, send_ref,
):
    members, count, width = value_ref.shape
    points = qt_ref.shape[1]
    rim = count // 2
    step = 2 * LANES
    halo_rows = jnp.concatenate([mate_ref[...], other_ref[...]], axis=0)

    src = src_ref[...]
    even = lax.axis_index("band") % 2 == 0
    shift = jnp.where(src >= nodes + rim, -rim, jnp.where(src >= nodes, rim, 0))
    src = src + jnp.where(even, shift, 0)
    held = {}

    def prefetch(pair):
        start = (pair * LANES // step + 1) * step
        for first in (0, width):
            if start < width and first + start not in held:
                held[first + start] = mm(halo_rows, kvw_ref[:, first + start : first + start + step]).astype(BF)

    prefetch(-1)

    def rows(pair, m, first):
        at = pair * LANES % step
        block = held[first + pair * LANES - at][:, at : at + LANES]
        mate = block[m * rim : (m + 1) * rim]
        other = block[(members + m) * rim : (members + m + 1) * rim]
        return jnp.concatenate([mate, other], axis=0)

    def values(pair, m):
        result = rows(pair, m, width)
        value_ref[m, :, pair * LANES : (pair + 1) * LANES] = result
        return result

    def store_merged(pair, m, result):
        cols = slice(pair * LANES, (pair + 1) * LANES)
        merged_ref[m, cols, :] = (own_ref[m, cols, :] + result).astype(BF)

    gate_rows(
        tasks_of(width, members), lambda pair, m: rows(pair, m, 0), values,
        qt_ref, half_mask_of(src, nodes, count), gate_ref, slope_ref, store_merged, prefetch,
    )
    sent = []
    for m in range(members):
        part = mm(p_ref[...], merged_ref[m])
        part_ref[m] = part
        sent.append(part[0:channels])
    send_ref[...] = jnp.concatenate(sent, axis=0).astype(BF)


def halving_orders(n_member, n_band):
    chips = [("band", bit) for bit in range(1, n_band.bit_length() - 1)]
    member = [("member", bit) for bit in range(n_member.bit_length() - 1)]
    turn = chips + member[:1]
    return [turn[i:] + turn[:i] for i in range(GROUPS)], member[1:]


def unit_order(order, n_member, n_band):
    def key(unit):
        return [-((2 * unit[0] if axis == "band" else unit[1]) >> bit & 1) for axis, bit in order]

    return sorted([(c, m) for c in range(n_band // 2) for m in range(n_member)], key=key)


def destination_rows(member, band, n_member, n_band, rw):
    chip, core = band // 2, band % 2
    for rel_core in (1, 0):
        for rel_chip in range(n_band // 2):
            to_band = (chip ^ rel_chip) * 2 + (core ^ rel_core)
            for rel_member in range(n_member):
                yield pl.multiple_of(((member ^ rel_member) * n_band + to_band) * rw, rw)


def reorder(src_ref, n_member, n_band):
    rw = src_ref.shape[0] // (n_member * n_band)
    member, band = lax.axis_index("member"), lax.axis_index("band")
    starts = destination_rows(member, band, n_member, n_band, rw)
    return jnp.concatenate([src_ref[pl.ds(start, rw), :] for start in starts], axis=0)


def store_group(rows, group, n_member, n_band, at, out_refs):
    orders, rest = halving_orders(n_member, n_band)
    units = unit_order(orders[group] + rest, n_member, n_band)
    rw = rows.shape[0] // (n_member * n_band)
    for core, ref in enumerate(out_refs):
        starts = [((core * (n_band // 2) + chip) * n_member + member) * rw for chip, member in units]
        ordered = jnp.concatenate([rows[i : i + rw] for i in starts], axis=0)
        ref[:, at : at + rows.shape[1]] = ordered.astype(BF)


def transpose_body(n_member, n_band, hidden_ref, mate_ref, other_ref, out_ref, turned):
    members, nodes, _ = hidden_ref.shape
    rim = mate_ref.shape[0] // members
    parts = []
    for m in range(members):
        parts.append(hidden_ref[m])
        parts.append(mate_ref[m * rim : (m + 1) * rim, :])
        parts.append(other_ref[m * rim : (m + 1) * rim, :])
    turned[...] = jnp.concatenate(parts, axis=0).astype(F32).T
    out_ref[...] = reorder(turned, n_member, n_band).astype(BF)


def select_heads(block):
    half = block.shape[0] // 2
    low = lax.broadcasted_iota(jnp.int32, (half, block.shape[1]), 1) < HEAD_DIM
    return jnp.where(low, block[:half], block[half:])


def joined(refs, pair, m):
    return jnp.concatenate([ref[pair, m] for ref in refs], axis=0)


def select_rows(block, own):
    return jnp.concatenate([select_heads(block[: 2 * own]), select_heads(block[2 * own :])], axis=0)


def soft_slope(v):
    return v * lax.rsqrt(v * v + SOFTENING * SOFTENING)


def value_body(n_member, n_band, *refs):
    recv_refs = refs[: n_member - 1]
    part_ref, base_ref, truth_ref, weight_ref, p_ref, *gate_refs, ext_ref = refs[n_member - 1 : n_member + 7]
    grad_ref, ng_ref, *out_refs = refs[n_member + 7 :]
    own_rows = gate_refs[0].shape[2] // 2
    members, width = grad_ref.shape[0], p_ref.shape[1]
    ext = ng_ref.shape[0] // members
    channels = truth_ref.shape[0]
    total = members * n_member
    spread = (1.0 - (1.0 - ALPHA) / total) / (total * (total - 1))

    grad_ref[...] = jnp.zeros_like(grad_ref)
    own = [part_ref[m, 0:channels, :] for m in range(members)]
    others = []
    for ref in recv_refs:
        rows = ref[...].astype(F32)
        others += [rows[k * channels : (k + 1) * channels] for k in range(members)]
    for m in range(members):
        slopes = jnp.zeros_like(own[m])
        for k in range(members):
            if k != m:
                slopes = slopes + soft_slope(own[m] - own[k])
        for other in others:
            slopes = slopes + soft_slope(own[m] - other)
        gap = soft_slope(own[m] + base_ref[0:channels, :] - truth_ref[...])
        grad_ref[m, 0:channels, :] = (weight_ref[...] * (gap / total - spread * slopes)).astype(BF)
    dm = [mm(grad_ref[m].astype(F32).T.astype(BF), p_ref[...]).astype(BF) for m in range(members)]
    for pair in range(width // LANES):
        cols = slice(pair * LANES, (pair + 1) * LANES)
        for m in range(members):
            result = mm(joined(gate_refs, pair, m), dm[m][:, cols])
            ng_ref[m * ext : (m + 1) * ext, cols] = select_rows(result, own_rows).astype(BF)
    group_width = out_refs[0].shape[1]
    store_group(mm(ext_ref[...], ng_ref[:, 0:group_width]), 0, n_member, n_band, 0, out_refs)


def key_gradients(pairs, grad_ref, pt_ref, value_refs, slope_refs, q_ref, ng_ref):
    members = grad_ref.shape[0]
    ext = ng_ref.shape[0] // members
    own_rows = value_refs[0].shape[1]
    scale = HEAD_DIM ** (-0.5)
    tasks = [(place, pair, m) for place, pair in enumerate(pairs) for m in range(members)]
    first, count = pairs[0] * LANES, len(pairs) * LANES
    dm = [mm(pt_ref[first : first + count, :], grad_ref[m]).astype(BF) for m in range(members)]

    def gate_gradients(place, pair, m):
        cols = slice(pair * LANES, (pair + 1) * LANES)
        value = jnp.concatenate([split_heads(ref[m, :, cols]) for ref in value_refs], axis=0)
        return mm(value, dm[m][place * LANES : (place + 1) * LANES])

    ahead = gate_gradients(*tasks[0])
    for i, (place, pair, m) in enumerate(tasks):
        current = ahead
        if i + 1 < len(tasks):
            ahead = gate_gradients(*tasks[i + 1])
        dscore = (current * joined(slope_refs, pair, m).astype(F32)).astype(BF)
        keys = select_rows(mm(dscore, q_ref[:, pair * LANES : (pair + 1) * LANES]), own_rows) * scale
        ng_ref[m * ext : (m + 1) * ext, place * LANES : (place + 1) * LANES] = keys.astype(BF)


def first_keys_body(
    n_member, n_band, first_value, grad_ref, pt_ref, own_value_ref, halo_value_ref, own_slope_ref,
    halo_slope_ref, q_ref, ext_ref, ngv_ref, ng_ref, *out_refs
):
    count = ng_ref.shape[1] // LANES
    rest = mm(ext_ref[...], ngv_ref[:, first_value:])
    store_group(rest, 1, n_member, n_band, 0, out_refs)
    value_refs, slope_refs = (own_value_ref, halo_value_ref), (own_slope_ref, halo_slope_ref)
    key_gradients(range(count), grad_ref, pt_ref, value_refs, slope_refs, q_ref, ng_ref)
    store_group(mm(ext_ref[...], ng_ref[...]), 1, n_member, n_band, rest.shape[1], out_refs)


def last_keys_body(
    n_member, n_band, grad_ref, pt_ref, own_value_ref, halo_value_ref, own_slope_ref, halo_slope_ref,
    q_ref, ext_ref, ng_ref, *out_refs
):
    width = q_ref.shape[1]
    pairs = range((width - ng_ref.shape[1]) // LANES, width // LANES)
    value_refs, slope_refs = (own_value_ref, halo_value_ref), (own_slope_ref, halo_slope_ref)
    key_gradients(pairs, grad_ref, pt_ref, value_refs, slope_refs, q_ref, ng_ref)
    store_group(mm(ext_ref[...], ng_ref[...]), 2, n_member, n_band, 0, out_refs)


def small_body(n_member, n_band, grad_ref, q_ref, merged_ref, wo_ref, *refs):
    out_refs, turned = refs[:-1], refs[-1]
    members = grad_ref.shape[0]
    m_t = sum(mm(grad_ref[m], merged_ref[m], NT) for m in range(members))
    head_t = sum(mm(grad_ref[m], q_ref[...]) for m in range(members)) + mm(m_t.astype(BF), wo_ref[...])
    turned[...] = jnp.concatenate([m_t, head_t], axis=0).T
    store_group(reorder(turned, n_member, n_band), 2, n_member, n_band, 0, out_refs)


def extended_grad_body(members, nodes, rim, first_ref, last_ref, ngv_ref, kvw_ref, own_ref, back_ref):
    ext = nodes + 2 * rim
    grads = jnp.concatenate([first_ref[...], last_ref[...], ngv_ref[...]], axis=1)
    rows = mm(grads, kvw_ref[...], NT)
    for m in range(members):
        at = m * ext
        own_ref[m] = rows[at : at + nodes]
        for side in range(2):
            first = (side * members + m) * rim
            start = at + nodes + side * rim
            back_ref[first : first + rim, :] = rows[start : start + rim].astype(BF)


def finish_body(
    devices, own_hidden_ref, mate_ref, other_ref, halo_ref, own_ref, arrived_ref, hp_ref,
    hidden_ref, kv_ref, out_ref, head_ref,
):
    members, nodes, _ = own_hidden_ref.shape
    rim = halo_ref.shape[1]
    mate, other = [one_hot_rows(rows, nodes) for rows in halo_lists(halo_ref)]
    for m in range(members):
        rows = slice(m * rim, (m + 1) * rim)
        back = mm(mate, mate_ref[rows, :]) + mm(other, other_ref[rows, :])
        hidden_ref[m] = own_hidden_ref[m] + back
    width = kv_ref.shape[1] // 2
    channels = hp_ref.shape[0]
    total = (own_ref[...] + arrived_ref[...].astype(F32)) * (1.0 / devices)
    kv_ref[:, width:] = total[:, 0:width]
    kv_ref[:, 0:width] = total[:, width : 2 * width]
    m_rows = total[:, 2 * width : 2 * width + channels]
    high = m_rows.astype(BF)
    low = (m_rows - high.astype(F32)).astype(BF)
    out_ref[...] = mm(high, hp_ref[...]) + mm(low, hp_ref[...])
    head_ref[...] = total[:, 2 * width + LANES : 2 * width + LANES + channels]


def add_up(*parts):
    return functools.reduce(lambda a, b: a + b, [p.astype(F32) for p in parts])


def swap(rows, axis, bit, count):
    return lax.ppermute(rows, axis, [(i, i ^ (1 << bit)) for i in range(count)])


def upper(terms):
    return [t[: t.shape[0] // 2] for t in terms]


def lower(terms):
    return [t[t.shape[0] // 2 :] for t in terms]


def summed(pieces, half):
    return jnp.concatenate([add_up(*half(terms)) for terms in pieces], axis=1)


def remaining(pieces):
    return lower(pieces[0]) if len(pieces) == 1 else [summed(pieces, lower)]


def shards(
    n_member, n_band,
    hidden, queries, kv_weight, out_weight, head_projection, initial_state, truth,
    latitude_weight, channel_loss_weight, sources, halo_rows,
):
    members, nodes, width = hidden.shape
    points = queries.shape[0]
    channels = head_projection.shape[1]
    rim = halo_rows.shape[1]
    ext = nodes + 2 * rim
    pairs = width // LANES
    devices = n_member * n_band
    rw = width // devices
    chips = n_band // 2
    mates = [(i, i ^ 1) for i in range(n_band)]
    others = [(i, (i + 1 if i % 2 else i - 1) % n_band) for i in range(n_band)]

    own_hidden, halo, for_mate, for_other = call(
        pick_body,
        [sds(hidden.shape, BF), sds(halo_rows.shape, jnp.int32)] + [sds((members * rim, width), BF)] * 2,
        (hidden, halo_rows),
        [pltpu.SemaphoreType.DMA((2,))],
        hbm=(0, 1),
        flops=10**10,
    )
    other = lax.ppermute(for_other, "band", others)
    mate = lax.ppermute(for_mate, "band", mates)

    hp = head_projection.T

    def gate_shapes(rows):
        return [sds((members, rows, width), BF)] + [sds((pairs, members, 2 * rows, points), BF)] * 2

    own_value, own_gates, own_slopes, own_merged, qt, pt, p, base, weight = call(
        own_body,
        gate_shapes(nodes)
        + [
            sds((members, width, points), F32),
            sds((width, points), BF),
            sds((width, LANES), BF),
            sds((LANES, width), BF),
            sds((LANES, points), F32),
            sds((channels, points), F32),
        ],
        (
            own_hidden, out_weight, hp, queries, kv_weight, initial_state,
            channel_loss_weight[None, :], latitude_weight[None, :], sources,
        ),
        [pltpu.VMEM((8, LANES), F32), pltpu.VMEM((LANES, width), F32)],
    )

    halo_value, halo_gates, halo_slopes, merged, part, sent = call(
        functools.partial(halo_body, channels, nodes),
        gate_shapes(2 * rim)
        + [
            sds((members, width, points), BF),
            sds((members, LANES, points), F32),
            sds((members * channels, points), BF),
        ],
        (other, mate, own_merged, kv_weight, qt, sources, p),
    )

    received = [
        lax.ppermute(sent, "member", [(i, i ^ s) for i in range(n_member)]) for s in range(n_member - 1, 0, -1)
    ]

    ext_t = call(
        functools.partial(transpose_body, n_member, n_band),
        sds((width, members * ext), BF),
        (own_hidden, mate, other),
        [pltpu.VMEM((width, members * ext), F32)],
    )

    extra = 2 * LANES
    group_width = (2 * width + extra) // GROUPS
    first_keys = 2 * group_width - width
    group_shape = [sds((width // 2, group_width), BF)] * 2
    grad, ng_value, send, keep = call(
        functools.partial(value_body, n_member, n_band),
        [sds((members, LANES, points), BF), sds((members * ext, width), BF)]
        + group_shape,
        (*received, part, base, truth, weight, p, own_gates, halo_gates, ext_t),
    )
    groups = [[[keep, swap(send, "band", 0, n_band)]]]
    ng_first, send, keep = call(
        functools.partial(first_keys_body, n_member, n_band, group_width),
        [sds((members * ext, first_keys), BF)] + group_shape,
        (grad, pt, own_value, halo_value, own_slopes, halo_slopes, queries, ext_t, ng_value),
    )
    groups.append([[keep, swap(send, "band", 0, n_band)]])
    last_keys = width - first_keys
    ng_last, send, keep = call(
        functools.partial(last_keys_body, n_member, n_band),
        [sds((members * ext, last_keys), BF)] + [sds((width // 2, last_keys), BF)] * 2,
        (grad, pt, own_value, halo_value, own_slopes, halo_slopes, queries, ext_t),
    )
    groups.append([[keep, swap(send, "band", 0, n_band)]])
    send, keep = call(
        functools.partial(small_body, n_member, n_band),
        [sds((width // 2, extra), BF)] * 2,
        (grad, queries, merged, out_weight),
        [pltpu.VMEM((width, extra), F32)],
    )
    groups[-1].append([keep, swap(send, "band", 0, n_band)])

    count = {"member": n_member, "band": n_band}
    turns, rest = halving_orders(n_member, n_band)
    steps = len(turns[0])
    for step in range(steps):
        outgoing = []
        for i in range(GROUPS):
            outgoing.append(summed(groups[i], upper).astype(BF))
            if step <= 1 and i + 1 < GROUPS:
                outgoing[i], groups[i + 1] = lax.optimization_barrier((outgoing[i], groups[i + 1]))
        if step == 0:
            outgoing, ng_last = lax.optimization_barrier((outgoing, ng_last))
            own_grad, back = call(
                functools.partial(extended_grad_body, members, nodes, rim),
                [sds((members, nodes, width), F32), sds((2 * members * rim, width), BF)],
                (ng_first, ng_last, ng_value, kv_weight),
            )
        arrived = [swap(out, *turn[step], count[turn[step][0]]) for out, turn in zip(outgoing, turns)]
        if step == 0:
            from_mate = lax.ppermute(back, "band", mates)
            arrived[-1], from_mate = lax.optimization_barrier((arrived[-1], from_mate))
        if step == steps - 1:
            onward = lower([from_mate])[0]
            arrived, onward = lax.optimization_barrier((arrived, onward))
            chips_on = [(i, (i + 2 - i % 2 * 4) % n_band) for i in range(n_band)]
            from_other = lax.ppermute(onward, "band", chips_on)
        groups = [[remaining(pieces) + [new]] for pieces, new in zip(groups, arrived)]
    terms = [jnp.concatenate([add_up(*group[0]) for group in groups], axis=1)]
    for axis, bit in rest:
        arrived = swap(add_up(*upper(terms)).astype(BF), axis, bit, count[axis])
        terms = lower(terms) + [arrived]

    return call(
        functools.partial(finish_body, devices),
        [
            sds((members, nodes, width), F32),
            sds((rw, 2 * width), F32),
            sds((rw, width), F32),
            sds((rw, channels), F32),
        ],
        (own_grad, from_mate, from_other, halo, add_up(*terms[:-1]), terms[-1], hp),
    )


def solution(mesh):
    placed = (
        P("member", "band", None),
        P("band", None),
        P(),
        P(),
        P(),
        P(None, "band"),
        P(None, "band"),
        P("band"),
        P(),
        P(None, "band"),
        P("band", None),
    )
    return jax.shard_map(
        functools.partial(shards, mesh.shape["member"], mesh.shape["band"]),
        mesh=mesh,
        in_specs=placed,
        out_specs=(
            P("member", "band", None),
            P(("member", "band"), None),
            P(("member", "band"), None),
            P(("member", "band"), None),
        ),
        check_vma=False,
    )
```

```python
import functools

import jax
import jax.numpy as jnp
from jax import lax
from jax.experimental import pallas as pl
from jax.experimental.pallas import tpu as pltpu
from jax.sharding import PartitionSpec as P

HEAD_DIM = 64
LANES = 128
GROUPS = 3
ALPHA = 0.95
SOFTENING = 0.5
BF = jnp.bfloat16
F32 = jnp.float32
NN = (((1,), (0,)), ((), ()))
NT = (((1,), (1,)), ((), ()))
TN = (((0,), (0,)), ((), ()))


def mm(a, b, dims=NN):
    return lax.dot_general(a, b, dims, preferred_element_type=F32)


def call(body, out_shape, args, scratch=(), hbm=(), limit=24, flops=1):
    args = [pltpu.with_memory_space_constraint(x, pltpu.HBM) if i in hbm else x for i, x in enumerate(args)]
    return pl.pallas_call(
        body,
        out_shape=out_shape,
        in_specs=[
            pl.BlockSpec(memory_space=pltpu.HBM if i in hbm else pltpu.VMEM) for i in range(len(args))
        ],
        out_specs=jax.tree.map(lambda _: pl.BlockSpec(memory_space=pltpu.VMEM), out_shape),
        scratch_shapes=list(scratch),
        compiler_params=pltpu.CompilerParams(vmem_limit_bytes=limit * 1024 * 1024),
        cost_estimate=pl.CostEstimate(flops=flops, bytes_accessed=1, transcendentals=0),
    )(*args)


def sds(shape, dtype):
    return jax.ShapeDtypeStruct(shape, dtype)


def one_hot_rows(rows, node_count):
    nodes = lax.broadcasted_iota(jnp.int32, (node_count, rows.shape[1]), 0).astype(rows.dtype)
    return (nodes == rows).astype(F32).astype(BF)


def start_copies(pairs, sems):
    copies = [pltpu.make_async_copy(src, dst, sems.at[i]) for i, (src, dst) in enumerate(pairs)]
    for copy in copies:
        copy.start()
    return copies


def halo_lists(halo_ref):
    even = lax.axis_index("band") % 2 == 0
    down, up = halo_ref[0:1, :], halo_ref[1:2, :]
    return jnp.where(even, up, down), jnp.where(even, down, up)


def pick_body(hidden_hbm, halo_hbm, hidden_ref, halo_ref, mate_ref, other_ref, sems):
    for copy in start_copies([(hidden_hbm, hidden_ref), (halo_hbm, halo_ref)], sems):
        copy.wait()
    members, nodes, _ = hidden_ref.shape
    rim = halo_ref.shape[1]
    for rows, out_ref in zip(halo_lists(halo_ref), (mate_ref, other_ref)):
        hot = one_hot_rows(rows, nodes)
        for m in range(members):
            out_ref[m * rim : (m + 1) * rim, :] = mm(hot, hidden_ref[m], TN).astype(BF)


def split_heads(block):
    low = lax.broadcasted_iota(jnp.int32, block.shape, 1) < HEAD_DIM
    zero = jnp.zeros_like(block)
    return jnp.concatenate([jnp.where(low, block, zero), jnp.where(low, zero, block)], axis=0)


def half_mask_of(src, first, count):
    rows = lax.broadcasted_iota(jnp.int32, (count, src.shape[1]), 0) + first
    mask = rows == src[0:1, :]
    for e in range(1, src.shape[0]):
        mask = mask | (rows == src[e : e + 1, :])
    half = jnp.where(mask, 0.5, 0.0).astype(F32)
    return jnp.concatenate([half, half], axis=0)


def gate_rows(tasks, keys, values, qt_ref, half_mask, gate_ref, slope_ref, store_merged, prefetch=None):
    def scores(pair, m):
        return mm(split_heads(keys(pair, m)), qt_ref[pair * LANES : (pair + 1) * LANES, :])

    ahead = scores(*tasks[0])
    for i, (pair, m) in enumerate(tasks):
        current = ahead
        if prefetch is not None:
            prefetch(pair)
        if i + 1 < len(tasks):
            ahead = scores(*tasks[i + 1])
        turned = split_heads(values(pair, m)).astype(F32).T.astype(BF)
        gate = jnp.tanh(current) * half_mask + half_mask
        rounded = gate.astype(BF)
        gate_ref[pair, m] = rounded
        slope_ref[pair, m] = (gate - gate * gate).astype(BF)
        store_merged(pair, m, mm(turned, rounded))


def tasks_of(width, members):
    return [(pair, m) for pair in range(width // LANES) for m in range(members)]


def own_body(
    hidden_ref, wo_ref, hp_ref, q_ref, kvw_ref, init_ref, chw_ref, lat_ref, src_ref,
    value_ref, gate_ref, slope_ref, merged_ref, qt_ref, pt_ref, p_ref, base_ref, weight_ref, chw_pad, hp_pad,
):
    channels = hp_ref.shape[0]
    members, nodes, width = hidden_ref.shape
    half_scale = 0.5 * HEAD_DIM ** (-0.5)
    qt_ref[...] = (q_ref[...].astype(F32) * half_scale).T.astype(BF)
    hidden = jnp.concatenate([hidden_ref[m] for m in range(members)], axis=0)
    rows = mm(hidden, kvw_ref[...]).astype(BF)

    def part(pair, m, first):
        at = first + pair * LANES
        return rows[m * nodes : (m + 1) * nodes, at : at + LANES]

    def store_merged(pair, m, result):
        merged_ref[m, pair * LANES : (pair + 1) * LANES, :] = result

    for m in range(members):
        value_ref[m] = rows[m * nodes : (m + 1) * nodes, width:]
    gate_rows(
        tasks_of(width, members),
        lambda pair, m: part(pair, m, 0),
        lambda pair, m: part(pair, m, width),
        qt_ref, half_mask_of(src_ref[...], 0, nodes), gate_ref, slope_ref, store_merged,
    )
    hp_pad[...] = jnp.zeros_like(hp_pad)
    hp_pad[0:channels, :] = hp_ref[...].astype(F32)
    hp_t = hp_pad[...].astype(BF)
    chw_pad[:, 0:channels] = jnp.broadcast_to(chw_ref[...], (8, channels))
    weight_ref[...] = chw_pad[...].T[0:channels, 0:1] * lat_ref[...]
    base_ref[...] = mm(hp_t, q_ref[...], NT)
    base_ref[0:channels, :] = base_ref[0:channels, :] + init_ref[...]
    p = mm(hp_t, wo_ref[...], NT)
    p_ref[...] = p.astype(BF)
    pt_ref[...] = p.T.astype(BF)


def halo_body(
    channels, nodes, other_ref, mate_ref, own_ref, kvw_ref, qt_ref, src_ref, p_ref,
    value_ref, gate_ref, slope_ref, merged_ref, part_ref, send_ref,
):
    members, count, width = value_ref.shape
    points = qt_ref.shape[1]
    rim = count // 2
    step = 2 * LANES
    halo_rows = jnp.concatenate([mate_ref[...], other_ref[...]], axis=0)

    src = src_ref[...]
    even = lax.axis_index("band") % 2 == 0
    shift = jnp.where(src >= nodes + rim, -rim, jnp.where(src >= nodes, rim, 0))
    src = src + jnp.where(even, shift, 0)
    held = {}

    def prefetch(pair):
        start = (pair * LANES // step + 1) * step
        for first in (0, width):
            if start < width and first + start not in held:
                held[first + start] = mm(halo_rows, kvw_ref[:, first + start : first + start + step]).astype(BF)

    prefetch(-1)

    def rows(pair, m, first):
        at = pair * LANES % step
        block = held[first + pair * LANES - at][:, at : at + LANES]
        mate = block[m * rim : (m + 1) * rim]
        other = block[(members + m) * rim : (members + m + 1) * rim]
        return jnp.concatenate([mate, other], axis=0)

    def values(pair, m):
        result = rows(pair, m, width)
        value_ref[m, :, pair * LANES : (pair + 1) * LANES] = result
        return result

    def store_merged(pair, m, result):
        cols = slice(pair * LANES, (pair + 1) * LANES)
        merged_ref[m, cols, :] = (own_ref[m, cols, :] + result).astype(BF)

    gate_rows(
        tasks_of(width, members), lambda pair, m: rows(pair, m, 0), values,
        qt_ref, half_mask_of(src, nodes, count), gate_ref, slope_ref, store_merged, prefetch,
    )
    sent = []
    for m in range(members):
        part = mm(p_ref[...], merged_ref[m])
        part_ref[m] = part
        sent.append(part[0:channels])
    send_ref[...] = jnp.concatenate(sent, axis=0).astype(BF)


def halving_orders(n_member, n_band):
    chips = [("band", bit) for bit in range(1, n_band.bit_length() - 1)]
    member = [("member", bit) for bit in range(n_member.bit_length() - 1)]
    turn = chips + member[:1]
    return [turn[i:] + turn[:i] for i in range(GROUPS)], member[1:]


def unit_order(order, n_member, n_band):
    def key(unit):
        return [-((2 * unit[0] if axis == "band" else unit[1]) >> bit & 1) for axis, bit in order]

    return sorted([(c, m) for c in range(n_band // 2) for m in range(n_member)], key=key)


def destination_rows(member, band, n_member, n_band, rw):
    chip, core = band // 2, band % 2
    for rel_core in (1, 0):
        for rel_chip in range(n_band // 2):
            to_band = (chip ^ rel_chip) * 2 + (core ^ rel_core)
            for rel_member in range(n_member):
                yield pl.multiple_of(((member ^ rel_member) * n_band + to_band) * rw, rw)


def reorder(src_ref, n_member, n_band):
    rw = src_ref.shape[0] // (n_member * n_band)
    member, band = lax.axis_index("member"), lax.axis_index("band")
    starts = destination_rows(member, band, n_member, n_band, rw)
    return jnp.concatenate([src_ref[pl.ds(start, rw), :] for start in starts], axis=0)


def store_group(rows, group, n_member, n_band, at, out_refs):
    orders, rest = halving_orders(n_member, n_band)
    units = unit_order(orders[group] + rest, n_member, n_band)
    rw = rows.shape[0] // (n_member * n_band)
    for core, ref in enumerate(out_refs):
        starts = [((core * (n_band // 2) + chip) * n_member + member) * rw for chip, member in units]
        ordered = jnp.concatenate([rows[i : i + rw] for i in starts], axis=0)
        ref[:, at : at + rows.shape[1]] = ordered.astype(BF)


def transpose_body(n_member, n_band, hidden_ref, mate_ref, other_ref, out_ref, turned):
    members, nodes, _ = hidden_ref.shape
    rim = mate_ref.shape[0] // members
    parts = []
    for m in range(members):
        parts.append(hidden_ref[m])
        parts.append(mate_ref[m * rim : (m + 1) * rim, :])
        parts.append(other_ref[m * rim : (m + 1) * rim, :])
    turned[...] = jnp.concatenate(parts, axis=0).astype(F32).T
    out_ref[...] = reorder(turned, n_member, n_band).astype(BF)


def select_heads(block):
    half = block.shape[0] // 2
    low = lax.broadcasted_iota(jnp.int32, (half, block.shape[1]), 1) < HEAD_DIM
    return jnp.where(low, block[:half], block[half:])


def joined(refs, pair, m):
    return jnp.concatenate([ref[pair, m] for ref in refs], axis=0)


def select_rows(block, own):
    return jnp.concatenate([select_heads(block[: 2 * own]), select_heads(block[2 * own :])], axis=0)


def soft_slope(v):
    return v * lax.rsqrt(v * v + SOFTENING * SOFTENING)


def value_body(n_member, n_band, *refs):
    recv_refs = refs[: n_member - 1]
    part_ref, base_ref, truth_ref, weight_ref, p_ref, *gate_refs, ext_ref = refs[n_member - 1 : n_member + 7]
    grad_ref, ng_ref, *out_refs = refs[n_member + 7 :]
    own_rows = gate_refs[0].shape[2] // 2
    members, width = grad_ref.shape[0], p_ref.shape[1]
    ext = ng_ref.shape[0] // members
    channels = truth_ref.shape[0]
    total = members * n_member
    spread = (1.0 - (1.0 - ALPHA) / total) / (total * (total - 1))

    grad_ref[...] = jnp.zeros_like(grad_ref)
    own = [part_ref[m, 0:channels, :] for m in range(members)]
    others = []
    for ref in recv_refs:
        rows = ref[...].astype(F32)
        others += [rows[k * channels : (k + 1) * channels] for k in range(members)]
    for m in range(members):
        slopes = jnp.zeros_like(own[m])
        for k in range(members):
            if k != m:
                slopes = slopes + soft_slope(own[m] - own[k])
        for other in others:
            slopes = slopes + soft_slope(own[m] - other)
        gap = soft_slope(own[m] + base_ref[0:channels, :] - truth_ref[...])
        grad_ref[m, 0:channels, :] = (weight_ref[...] * (gap / total - spread * slopes)).astype(BF)
    dm = [mm(grad_ref[m].astype(F32).T.astype(BF), p_ref[...]).astype(BF) for m in range(members)]
    for pair in range(width // LANES):
        cols = slice(pair * LANES, (pair + 1) * LANES)
        for m in range(members):
            result = mm(joined(gate_refs, pair, m), dm[m][:, cols])
            ng_ref[m * ext : (m + 1) * ext, cols] = select_rows(result, own_rows).astype(BF)
    group_width = out_refs[0].shape[1]
    store_group(mm(ext_ref[...], ng_ref[:, 0:group_width]), 0, n_member, n_band, 0, out_refs)


def key_gradients(pairs, grad_ref, pt_ref, value_refs, slope_refs, q_ref, ng_ref):
    members = grad_ref.shape[0]
    ext = ng_ref.shape[0] // members
    own_rows = value_refs[0].shape[1]
    scale = HEAD_DIM ** (-0.5)
    tasks = [(place, pair, m) for place, pair in enumerate(pairs) for m in range(members)]
    first, count = pairs[0] * LANES, len(pairs) * LANES
    dm = [mm(pt_ref[first : first + count, :], grad_ref[m]).astype(BF) for m in range(members)]

    def gate_gradients(place, pair, m):
        cols = slice(pair * LANES, (pair + 1) * LANES)
        value = jnp.concatenate([split_heads(ref[m, :, cols]) for ref in value_refs], axis=0)
        return mm(value, dm[m][place * LANES : (place + 1) * LANES])

    ahead = gate_gradients(*tasks[0])
    for i, (place, pair, m) in enumerate(tasks):
        current = ahead
        if i + 1 < len(tasks):
            ahead = gate_gradients(*tasks[i + 1])
        dscore = (current * joined(slope_refs, pair, m).astype(F32)).astype(BF)
        keys = select_rows(mm(dscore, q_ref[:, pair * LANES : (pair + 1) * LANES]), own_rows) * scale
        ng_ref[m * ext : (m + 1) * ext, place * LANES : (place + 1) * LANES] = keys.astype(BF)


def first_keys_body(
    n_member, n_band, first_value, grad_ref, pt_ref, own_value_ref, halo_value_ref, own_slope_ref,
    halo_slope_ref, q_ref, ext_ref, ngv_ref, ng_ref, *out_refs
):
    count = ng_ref.shape[1] // LANES
    rest = mm(ext_ref[...], ngv_ref[:, first_value:])
    store_group(rest, 1, n_member, n_band, 0, out_refs)
    value_refs, slope_refs = (own_value_ref, halo_value_ref), (own_slope_ref, halo_slope_ref)
    key_gradients(range(count), grad_ref, pt_ref, value_refs, slope_refs, q_ref, ng_ref)
    store_group(mm(ext_ref[...], ng_ref[...]), 1, n_member, n_band, rest.shape[1], out_refs)


def last_keys_body(
    n_member, n_band, grad_ref, pt_ref, own_value_ref, halo_value_ref, own_slope_ref, halo_slope_ref,
    q_ref, merged_ref, wo_ref, ext_ref, ng_ref, *refs
):
    out_refs, turned = refs[:-1], refs[-1]
    members, width, _ = merged_ref.shape
    pairs = range((width - ng_ref.shape[1]) // LANES, width // LANES)
    value_refs, slope_refs = (own_value_ref, halo_value_ref), (own_slope_ref, halo_slope_ref)
    key_gradients(pairs, grad_ref, pt_ref, value_refs, slope_refs, q_ref, ng_ref)
    m_t = sum(mm(grad_ref[m], merged_ref[m], NT) for m in range(members))
    head_t = sum(mm(grad_ref[m], q_ref[...]) for m in range(members)) + mm(m_t.astype(BF), wo_ref[...])
    turned[...] = jnp.concatenate([m_t, head_t], axis=0).T
    store_group(mm(ext_ref[...], ng_ref[...]), 2, n_member, n_band, 0, out_refs)
    store_group(reorder(turned, n_member, n_band), 2, n_member, n_band, ng_ref.shape[1], out_refs)


def extended_grad_body(members, nodes, rim, first_ref, last_ref, ngv_ref, kvw_ref, own_ref, back_ref):
    ext = nodes + 2 * rim
    grads = jnp.concatenate([first_ref[...], last_ref[...], ngv_ref[...]], axis=1)
    rows = mm(grads, kvw_ref[...], NT)
    for m in range(members):
        at = m * ext
        own_ref[m] = rows[at : at + nodes]
        for side in range(2):
            first = (side * members + m) * rim
            start = at + nodes + side * rim
            back_ref[first : first + rim, :] = rows[start : start + rim].astype(BF)


def finish_body(
    devices, own_hidden_ref, mate_ref, other_ref, halo_ref, own_ref, arrived_ref, hp_ref,
    hidden_ref, kv_ref, out_ref, head_ref,
):
    members, nodes, _ = own_hidden_ref.shape
    rim = halo_ref.shape[1]
    mate, other = [one_hot_rows(rows, nodes) for rows in halo_lists(halo_ref)]
    for m in range(members):
        rows = slice(m * rim, (m + 1) * rim)
        back = mm(mate, mate_ref[rows, :]) + mm(other, other_ref[rows, :])
        hidden_ref[m] = own_hidden_ref[m] + back
    width = kv_ref.shape[1] // 2
    channels = hp_ref.shape[0]
    total = (own_ref[...] + arrived_ref[...].astype(F32)) * (1.0 / devices)
    kv_ref[:, width:] = total[:, 0:width]
    kv_ref[:, 0:width] = total[:, width : 2 * width]
    m_rows = total[:, 2 * width : 2 * width + channels]
    high = m_rows.astype(BF)
    low = (m_rows - high.astype(F32)).astype(BF)
    out_ref[...] = mm(high, hp_ref[...]) + mm(low, hp_ref[...])
    head_ref[...] = total[:, 2 * width + LANES : 2 * width + LANES + channels]


def add_up(*parts):
    return functools.reduce(lambda a, b: a + b, [p.astype(F32) for p in parts])


def swap(rows, axis, bit, count):
    return lax.ppermute(rows, axis, [(i, i ^ (1 << bit)) for i in range(count)])


def upper(terms):
    return [t[: t.shape[0] // 2] for t in terms]


def lower(terms):
    return [t[t.shape[0] // 2 :] for t in terms]


def shards(
    n_member, n_band,
    hidden, queries, kv_weight, out_weight, head_projection, initial_state, truth,
    latitude_weight, channel_loss_weight, sources, halo_rows,
):
    members, nodes, width = hidden.shape
    points = queries.shape[0]
    channels = head_projection.shape[1]
    rim = halo_rows.shape[1]
    ext = nodes + 2 * rim
    pairs = width // LANES
    devices = n_member * n_band
    rw = width // devices
    chips = n_band // 2
    mates = [(i, i ^ 1) for i in range(n_band)]
    others = [(i, (i + 1 if i % 2 else i - 1) % n_band) for i in range(n_band)]

    own_hidden, halo, for_mate, for_other = call(
        pick_body,
        [sds(hidden.shape, BF), sds(halo_rows.shape, jnp.int32)] + [sds((members * rim, width), BF)] * 2,
        (hidden, halo_rows),
        [pltpu.SemaphoreType.DMA((2,))],
        hbm=(0, 1),
        flops=10**10,
    )
    other = lax.ppermute(for_other, "band", others)
    mate = lax.ppermute(for_mate, "band", mates)

    hp = head_projection.T

    def gate_shapes(rows):
        return [sds((members, rows, width), BF)] + [sds((pairs, members, 2 * rows, points), BF)] * 2

    own_value, own_gates, own_slopes, own_merged, qt, pt, p, base, weight = call(
        own_body,
        gate_shapes(nodes)
        + [
            sds((members, width, points), F32),
            sds((width, points), BF),
            sds((width, LANES), BF),
            sds((LANES, width), BF),
            sds((LANES, points), F32),
            sds((channels, points), F32),
        ],
        (
            own_hidden, out_weight, hp, queries, kv_weight, initial_state,
            channel_loss_weight[None, :], latitude_weight[None, :], sources,
        ),
        [pltpu.VMEM((8, LANES), F32), pltpu.VMEM((LANES, width), F32)],
    )

    halo_value, halo_gates, halo_slopes, merged, part, sent = call(
        functools.partial(halo_body, channels, nodes),
        gate_shapes(2 * rim)
        + [
            sds((members, width, points), BF),
            sds((members, LANES, points), F32),
            sds((members * channels, points), BF),
        ],
        (other, mate, own_merged, kv_weight, qt, sources, p),
    )

    received = [
        lax.ppermute(sent, "member", [(i, i ^ s) for i in range(n_member)]) for s in range(n_member - 1, 0, -1)
    ]

    ext_t = call(
        functools.partial(transpose_body, n_member, n_band),
        sds((width, members * ext), BF),
        (own_hidden, mate, other),
        [pltpu.VMEM((width, members * ext), F32)],
    )

    extra = 2 * LANES
    group_width = (2 * width + extra) // GROUPS
    first_keys = 2 * group_width - width
    group_shape = [sds((width // 2, group_width), BF)] * 2
    grad, ng_value, send, keep = call(
        functools.partial(value_body, n_member, n_band),
        [sds((members, LANES, points), BF), sds((members * ext, width), BF)]
        + group_shape,
        (*received, part, base, truth, weight, p, own_gates, halo_gates, ext_t),
    )
    groups = [[keep, swap(send, "band", 0, n_band)]]
    ng_first, send, keep = call(
        functools.partial(first_keys_body, n_member, n_band, group_width),
        [sds((members * ext, first_keys), BF)] + group_shape,
        (grad, pt, own_value, halo_value, own_slopes, halo_slopes, queries, ext_t, ng_value),
    )
    groups.append([keep, swap(send, "band", 0, n_band)])
    ng_last, send, keep = call(
        functools.partial(last_keys_body, n_member, n_band),
        [sds((members * ext, width - first_keys), BF)] + group_shape,
        (grad, pt, own_value, halo_value, own_slopes, halo_slopes, queries, merged, out_weight, ext_t),
        [pltpu.VMEM((width, extra), F32)],
    )
    groups.append([keep, swap(send, "band", 0, n_band)])

    count = {"member": n_member, "band": n_band}
    turns, rest = halving_orders(n_member, n_band)
    steps = len(turns[0])
    for step in range(steps):
        outgoing = []
        for i in range(GROUPS):
            outgoing.append(add_up(*upper(groups[i])).astype(BF))
            if step == 0 and i + 1 < GROUPS:
                outgoing[i], groups[i + 1] = lax.optimization_barrier((outgoing[i], groups[i + 1]))
        if step == 0:
            outgoing, ng_last = lax.optimization_barrier((outgoing, ng_last))
            own_grad, back = call(
                functools.partial(extended_grad_body, members, nodes, rim),
                [sds((members, nodes, width), F32), sds((2 * members * rim, width), BF)],
                (ng_first, ng_last, ng_value, kv_weight),
            )
        if step == steps - 1:
            onward = lower([from_mate])[0]
            outgoing[0], onward = lax.optimization_barrier((outgoing[0], onward))
            chips_on = [(i, (i + 2 - i % 2 * 4) % n_band) for i in range(n_band)]
            from_other = lax.ppermute(onward, "band", chips_on)
        arrived = [swap(out, *turn[step], count[turn[step][0]]) for out, turn in zip(outgoing, turns)]
        if step == 0:
            from_mate = lax.ppermute(back, "band", mates)
            arrived, from_mate = lax.optimization_barrier((arrived, from_mate))
        if step == steps - 1:
            arrived, from_other = lax.optimization_barrier((arrived, from_other))
        groups = [lower(terms) + [new] for terms, new in zip(groups, arrived)]
    terms = [jnp.concatenate([add_up(*group) for group in groups], axis=1)]
    for axis, bit in rest:
        arrived = swap(add_up(*upper(terms)).astype(BF), axis, bit, count[axis])
        terms = lower(terms) + [arrived]

    return call(
        functools.partial(finish_body, devices),
        [
            sds((members, nodes, width), F32),
            sds((rw, 2 * width), F32),
            sds((rw, width), F32),
            sds((rw, channels), F32),
        ],
        (own_grad, from_mate, from_other, halo, add_up(*terms[:-1]), terms[-1], hp),
    )


def solution(mesh):
    placed = (
        P("member", "band", None),
        P("band", None),
        P(),
        P(),
        P(),
        P(None, "band"),
        P(None, "band"),
        P("band"),
        P(),
        P(None, "band"),
        P("band", None),
    )
    return jax.shard_map(
        functools.partial(shards, mesh.shape["member"], mesh.shape["band"]),
        mesh=mesh,
        in_specs=placed,
        out_specs=(
            P("member", "band", None),
            P(("member", "band"), None),
            P(("member", "band"), None),
            P(("member", "band"), None),
        ),
        check_vma=False,
    )
```

```python
import functools

import jax
import jax.numpy as jnp
from jax import lax
from jax.experimental import pallas as pl
from jax.experimental.pallas import tpu as pltpu
from jax.sharding import PartitionSpec as P

HEAD_DIM = 64
LANES = 128
GROUPS = 3
ALPHA = 0.95
SOFTENING = 0.5
BF = jnp.bfloat16
F32 = jnp.float32
NN = (((1,), (0,)), ((), ()))
NT = (((1,), (1,)), ((), ()))
TN = (((0,), (0,)), ((), ()))


def mm(a, b, dims=NN):
    return lax.dot_general(a, b, dims, preferred_element_type=F32)


def call(body, out_shape, args, scratch=(), hbm=(), limit=24, flops=1):
    args = [pltpu.with_memory_space_constraint(x, pltpu.HBM) if i in hbm else x for i, x in enumerate(args)]
    return pl.pallas_call(
        body,
        out_shape=out_shape,
        in_specs=[
            pl.BlockSpec(memory_space=pltpu.HBM if i in hbm else pltpu.VMEM) for i in range(len(args))
        ],
        out_specs=jax.tree.map(lambda _: pl.BlockSpec(memory_space=pltpu.VMEM), out_shape),
        scratch_shapes=list(scratch),
        compiler_params=pltpu.CompilerParams(vmem_limit_bytes=limit * 1024 * 1024),
        cost_estimate=pl.CostEstimate(flops=flops, bytes_accessed=1, transcendentals=0),
    )(*args)


def sds(shape, dtype):
    return jax.ShapeDtypeStruct(shape, dtype)


def one_hot_rows(rows, node_count):
    nodes = lax.broadcasted_iota(jnp.int32, (node_count, rows.shape[1]), 0).astype(rows.dtype)
    return (nodes == rows).astype(F32).astype(BF)


def start_copies(pairs, sems):
    copies = [pltpu.make_async_copy(src, dst, sems.at[i]) for i, (src, dst) in enumerate(pairs)]
    for copy in copies:
        copy.start()
    return copies


def halo_lists(halo_ref):
    even = lax.axis_index("band") % 2 == 0
    down, up = halo_ref[0:1, :], halo_ref[1:2, :]
    return jnp.where(even, up, down), jnp.where(even, down, up)


def pick_body(hidden_hbm, halo_hbm, hidden_ref, halo_ref, mate_ref, other_ref, sems):
    for copy in start_copies([(hidden_hbm, hidden_ref), (halo_hbm, halo_ref)], sems):
        copy.wait()
    members, nodes, _ = hidden_ref.shape
    rim = halo_ref.shape[1]
    for rows, out_ref in zip(halo_lists(halo_ref), (mate_ref, other_ref)):
        hot = one_hot_rows(rows, nodes)
        for m in range(members):
            out_ref[m * rim : (m + 1) * rim, :] = mm(hot, hidden_ref[m], TN).astype(BF)


def split_heads(block):
    low = lax.broadcasted_iota(jnp.int32, block.shape, 1) < HEAD_DIM
    zero = jnp.zeros_like(block)
    return jnp.concatenate([jnp.where(low, block, zero), jnp.where(low, zero, block)], axis=0)


def half_mask_of(src, first, count):
    rows = lax.broadcasted_iota(jnp.int32, (count, src.shape[1]), 0) + first
    mask = rows == src[0:1, :]
    for e in range(1, src.shape[0]):
        mask = mask | (rows == src[e : e + 1, :])
    half = jnp.where(mask, 0.5, 0.0).astype(F32)
    return jnp.concatenate([half, half], axis=0)


def gate_rows(tasks, keys, values, qt_ref, half_mask, gate_ref, slope_ref, store_merged, prefetch=None):
    def scores(pair, m):
        return mm(split_heads(keys(pair, m)), qt_ref[pair * LANES : (pair + 1) * LANES, :])

    ahead = scores(*tasks[0])
    for i, (pair, m) in enumerate(tasks):
        current = ahead
        if prefetch is not None:
            prefetch(pair)
        if i + 1 < len(tasks):
            ahead = scores(*tasks[i + 1])
        turned = split_heads(values(pair, m)).astype(F32).T.astype(BF)
        gate = jnp.tanh(current) * half_mask + half_mask
        rounded = gate.astype(BF)
        gate_ref[pair, m] = rounded
        slope_ref[pair, m] = (gate - gate * gate).astype(BF)
        store_merged(pair, m, mm(turned, rounded))


def tasks_of(width, members):
    return [(pair, m) for pair in range(width // LANES) for m in range(members)]


def own_body(
    hidden_ref, wo_ref, hp_ref, q_ref, kvw_ref, init_ref, chw_ref, lat_ref, src_ref,
    value_ref, gate_ref, slope_ref, merged_ref, qt_ref, pt_ref, p_ref, base_ref, weight_ref, chw_pad, hp_pad,
):
    channels = hp_ref.shape[0]
    members, nodes, width = hidden_ref.shape
    half_scale = 0.5 * HEAD_DIM ** (-0.5)
    qt_ref[...] = (q_ref[...].astype(F32) * half_scale).T.astype(BF)
    hidden = jnp.concatenate([hidden_ref[m] for m in range(members)], axis=0)
    rows = mm(hidden, kvw_ref[...]).astype(BF)

    def part(pair, m, first):
        at = first + pair * LANES
        return rows[m * nodes : (m + 1) * nodes, at : at + LANES]

    def store_merged(pair, m, result):
        merged_ref[m, pair * LANES : (pair + 1) * LANES, :] = result

    for m in range(members):
        value_ref[m] = rows[m * nodes : (m + 1) * nodes, width:]
    gate_rows(
        tasks_of(width, members),
        lambda pair, m: part(pair, m, 0),
        lambda pair, m: part(pair, m, width),
        qt_ref, half_mask_of(src_ref[...], 0, nodes), gate_ref, slope_ref, store_merged,
    )
    hp_pad[...] = jnp.zeros_like(hp_pad)
    hp_pad[0:channels, :] = hp_ref[...].astype(F32)
    hp_t = hp_pad[...].astype(BF)
    chw_pad[:, 0:channels] = jnp.broadcast_to(chw_ref[...], (8, channels))
    weight_ref[...] = chw_pad[...].T[0:channels, 0:1] * lat_ref[...]
    base_ref[...] = mm(hp_t, q_ref[...], NT)
    base_ref[0:channels, :] = base_ref[0:channels, :] + init_ref[...]
    p = mm(hp_t, wo_ref[...], NT)
    p_ref[...] = p.astype(BF)
    pt_ref[...] = p.T.astype(BF)


def halo_body(
    channels, nodes, other_ref, mate_ref, own_ref, kvw_ref, qt_ref, src_ref, p_ref,
    value_ref, gate_ref, slope_ref, merged_ref, part_ref, send_ref,
):
    members, count, width = value_ref.shape
    points = qt_ref.shape[1]
    rim = count // 2
    step = 2 * LANES
    halo_rows = jnp.concatenate([mate_ref[...], other_ref[...]], axis=0)

    src = src_ref[...]
    even = lax.axis_index("band") % 2 == 0
    shift = jnp.where(src >= nodes + rim, -rim, jnp.where(src >= nodes, rim, 0))
    src = src + jnp.where(even, shift, 0)
    held = {}

    def prefetch(pair):
        start = (pair * LANES // step + 1) * step
        for first in (0, width):
            if start < width and first + start not in held:
                held[first + start] = mm(halo_rows, kvw_ref[:, first + start : first + start + step]).astype(BF)

    prefetch(-1)

    def rows(pair, m, first):
        at = pair * LANES % step
        block = held[first + pair * LANES - at][:, at : at + LANES]
        mate = block[m * rim : (m + 1) * rim]
        other = block[(members + m) * rim : (members + m + 1) * rim]
        return jnp.concatenate([mate, other], axis=0)

    def values(pair, m):
        result = rows(pair, m, width)
        value_ref[m, :, pair * LANES : (pair + 1) * LANES] = result
        return result

    def store_merged(pair, m, result):
        cols = slice(pair * LANES, (pair + 1) * LANES)
        merged_ref[m, cols, :] = (own_ref[m, cols, :] + result).astype(BF)

    gate_rows(
        tasks_of(width, members), lambda pair, m: rows(pair, m, 0), values,
        qt_ref, half_mask_of(src, nodes, count), gate_ref, slope_ref, store_merged, prefetch,
    )
    sent = []
    for m in range(members):
        part = mm(p_ref[...], merged_ref[m])
        part_ref[m] = part
        sent.append(part[0:channels])
    send_ref[...] = jnp.concatenate(sent, axis=0).astype(BF)


def halving_orders(n_member, n_band):
    chips = [("band", bit) for bit in range(1, n_band.bit_length() - 1)]
    member = [("member", bit) for bit in range(n_member.bit_length() - 1)]
    turn = chips + member[:1]
    return [turn[i:] + turn[:i] for i in range(GROUPS)], member[1:]


def unit_order(order, n_member, n_band):
    def key(unit):
        return [-((2 * unit[0] if axis == "band" else unit[1]) >> bit & 1) for axis, bit in order]

    return sorted([(c, m) for c in range(n_band // 2) for m in range(n_member)], key=key)


def destination_rows(member, band, n_member, n_band, rw):
    chip, core = band // 2, band % 2
    for rel_core in (1, 0):
        for rel_chip in range(n_band // 2):
            to_band = (chip ^ rel_chip) * 2 + (core ^ rel_core)
            for rel_member in range(n_member):
                yield pl.multiple_of(((member ^ rel_member) * n_band + to_band) * rw, rw)


def reorder(src_ref, n_member, n_band):
    rw = src_ref.shape[0] // (n_member * n_band)
    member, band = lax.axis_index("member"), lax.axis_index("band")
    starts = destination_rows(member, band, n_member, n_band, rw)
    return jnp.concatenate([src_ref[pl.ds(start, rw), :] for start in starts], axis=0)


def store_group(rows, group, n_member, n_band, at, out_refs):
    orders, rest = halving_orders(n_member, n_band)
    units = unit_order(orders[group] + rest, n_member, n_band)
    rw = rows.shape[0] // (n_member * n_band)
    for core, ref in enumerate(out_refs):
        starts = [((core * (n_band // 2) + chip) * n_member + member) * rw for chip, member in units]
        ordered = jnp.concatenate([rows[i : i + rw] for i in starts], axis=0)
        ref[:, at : at + rows.shape[1]] = ordered.astype(BF)


def transpose_body(n_member, n_band, hidden_ref, mate_ref, other_ref, out_ref, turned):
    members, nodes, _ = hidden_ref.shape
    rim = mate_ref.shape[0] // members
    parts = []
    for m in range(members):
        parts.append(hidden_ref[m])
        parts.append(mate_ref[m * rim : (m + 1) * rim, :])
        parts.append(other_ref[m * rim : (m + 1) * rim, :])
    turned[...] = jnp.concatenate(parts, axis=0).astype(F32).T
    out_ref[...] = reorder(turned, n_member, n_band).astype(BF)


def select_heads(block):
    half = block.shape[0] // 2
    low = lax.broadcasted_iota(jnp.int32, (half, block.shape[1]), 1) < HEAD_DIM
    return jnp.where(low, block[:half], block[half:])


def joined(refs, pair, m):
    return jnp.concatenate([ref[pair, m] for ref in refs], axis=0)


def select_rows(block, own):
    return jnp.concatenate([select_heads(block[: 2 * own]), select_heads(block[2 * own :])], axis=0)


def soft_slope(v):
    return v * lax.rsqrt(v * v + SOFTENING * SOFTENING)


def value_body(n_member, n_band, *refs):
    recv_refs = refs[: n_member - 1]
    part_ref, base_ref, truth_ref, weight_ref, p_ref, *gate_refs, ext_ref = refs[n_member - 1 : n_member + 7]
    grad_ref, ng_ref, *out_refs = refs[n_member + 7 :]
    own_rows = gate_refs[0].shape[2] // 2
    members, width = grad_ref.shape[0], p_ref.shape[1]
    ext = ng_ref.shape[0] // members
    channels = truth_ref.shape[0]
    total = members * n_member
    spread = (1.0 - (1.0 - ALPHA) / total) / (total * (total - 1))

    grad_ref[...] = jnp.zeros_like(grad_ref)
    own = [part_ref[m, 0:channels, :] for m in range(members)]
    others = []
    for ref in recv_refs:
        rows = ref[...].astype(F32)
        others += [rows[k * channels : (k + 1) * channels] for k in range(members)]
    for m in range(members):
        slopes = jnp.zeros_like(own[m])
        for k in range(members):
            if k != m:
                slopes = slopes + soft_slope(own[m] - own[k])
        for other in others:
            slopes = slopes + soft_slope(own[m] - other)
        gap = soft_slope(own[m] + base_ref[0:channels, :] - truth_ref[...])
        grad_ref[m, 0:channels, :] = (weight_ref[...] * (gap / total - spread * slopes)).astype(BF)
    dm = [mm(grad_ref[m].astype(F32).T.astype(BF), p_ref[...]).astype(BF) for m in range(members)]
    for pair in range(width // LANES):
        cols = slice(pair * LANES, (pair + 1) * LANES)
        for m in range(members):
            result = mm(joined(gate_refs, pair, m), dm[m][:, cols])
            ng_ref[m * ext : (m + 1) * ext, cols] = select_rows(result, own_rows).astype(BF)
    group_width = out_refs[0].shape[1]
    store_group(mm(ext_ref[...], ng_ref[:, 0:group_width]), 0, n_member, n_band, 0, out_refs)


def key_gradients(pairs, grad_ref, pt_ref, value_refs, slope_refs, q_ref, ng_ref):
    members = grad_ref.shape[0]
    ext = ng_ref.shape[0] // members
    own_rows = value_refs[0].shape[1]
    scale = HEAD_DIM ** (-0.5)
    tasks = [(place, pair, m) for place, pair in enumerate(pairs) for m in range(members)]
    first, count = pairs[0] * LANES, len(pairs) * LANES
    dm = [mm(pt_ref[first : first + count, :], grad_ref[m]).astype(BF) for m in range(members)]

    def gate_gradients(place, pair, m):
        cols = slice(pair * LANES, (pair + 1) * LANES)
        value = jnp.concatenate([split_heads(ref[m, :, cols]) for ref in value_refs], axis=0)
        return mm(value, dm[m][place * LANES : (place + 1) * LANES])

    ahead = gate_gradients(*tasks[0])
    for i, (place, pair, m) in enumerate(tasks):
        current = ahead
        if i + 1 < len(tasks):
            ahead = gate_gradients(*tasks[i + 1])
        dscore = (current * joined(slope_refs, pair, m).astype(F32)).astype(BF)
        keys = select_rows(mm(dscore, q_ref[:, pair * LANES : (pair + 1) * LANES]), own_rows) * scale
        ng_ref[m * ext : (m + 1) * ext, place * LANES : (place + 1) * LANES] = keys.astype(BF)


def first_keys_body(
    n_member, n_band, first_value, grad_ref, pt_ref, own_value_ref, halo_value_ref, own_slope_ref,
    halo_slope_ref, q_ref, ext_ref, ngv_ref, ng_ref, *out_refs
):
    count = ng_ref.shape[1] // LANES
    rest = mm(ext_ref[...], ngv_ref[:, first_value:])
    store_group(rest, 1, n_member, n_band, 0, out_refs)
    value_refs, slope_refs = (own_value_ref, halo_value_ref), (own_slope_ref, halo_slope_ref)
    key_gradients(range(count), grad_ref, pt_ref, value_refs, slope_refs, q_ref, ng_ref)
    store_group(mm(ext_ref[...], ng_ref[...]), 1, n_member, n_band, rest.shape[1], out_refs)


def last_keys_body(
    n_member, n_band, grad_ref, pt_ref, own_value_ref, halo_value_ref, own_slope_ref, halo_slope_ref,
    q_ref, merged_ref, wo_ref, ext_ref, ng_ref, *refs
):
    out_refs, turned = refs[:-1], refs[-1]
    members, width, _ = merged_ref.shape
    pairs = range((width - ng_ref.shape[1]) // LANES, width // LANES)
    value_refs, slope_refs = (own_value_ref, halo_value_ref), (own_slope_ref, halo_slope_ref)
    key_gradients(pairs, grad_ref, pt_ref, value_refs, slope_refs, q_ref, ng_ref)
    m_t = sum(mm(grad_ref[m], merged_ref[m], NT) for m in range(members))
    head_t = sum(mm(grad_ref[m], q_ref[...]) for m in range(members)) + mm(m_t.astype(BF), wo_ref[...])
    turned[...] = jnp.concatenate([m_t, head_t], axis=0).T
    store_group(mm(ext_ref[...], ng_ref[...]), 2, n_member, n_band, 0, out_refs)
    store_group(reorder(turned, n_member, n_band), 2, n_member, n_band, ng_ref.shape[1], out_refs)


def extended_grad_body(members, nodes, rim, first_ref, last_ref, ngv_ref, kvw_ref, own_ref, back_ref):
    ext = nodes + 2 * rim
    grads = jnp.concatenate([first_ref[...], last_ref[...], ngv_ref[...]], axis=1)
    rows = mm(grads, kvw_ref[...], NT)
    for m in range(members):
        at = m * ext
        own_ref[m] = rows[at : at + nodes]
        for side in range(2):
            first = (side * members + m) * rim
            start = at + nodes + side * rim
            back_ref[first : first + rim, :] = rows[start : start + rim].astype(BF)


def finish_body(
    devices, own_hidden_ref, mate_ref, other_ref, halo_ref, own_ref, arrived_ref, hp_ref,
    hidden_ref, kv_ref, out_ref, head_ref,
):
    members, nodes, _ = own_hidden_ref.shape
    rim = halo_ref.shape[1]
    mate, other = [one_hot_rows(rows, nodes) for rows in halo_lists(halo_ref)]
    for m in range(members):
        rows = slice(m * rim, (m + 1) * rim)
        back = mm(mate, mate_ref[rows, :]) + mm(other, other_ref[rows, :])
        hidden_ref[m] = own_hidden_ref[m] + back
    width = kv_ref.shape[1] // 2
    channels = hp_ref.shape[0]
    total = (own_ref[...] + arrived_ref[...].astype(F32)) * (1.0 / devices)
    kv_ref[:, width:] = total[:, 0:width]
    kv_ref[:, 0:width] = total[:, width : 2 * width]
    m_rows = total[:, 2 * width : 2 * width + channels]
    high = m_rows.astype(BF)
    low = (m_rows - high.astype(F32)).astype(BF)
    out_ref[...] = mm(high, hp_ref[...]) + mm(low, hp_ref[...])
    head_ref[...] = total[:, 2 * width + LANES : 2 * width + LANES + channels]


def add_up(*parts):
    return functools.reduce(lambda a, b: a + b, [p.astype(F32) for p in parts])


def swap(rows, axis, bit, count):
    return lax.ppermute(rows, axis, [(i, i ^ (1 << bit)) for i in range(count)])


def upper(terms):
    return [t[: t.shape[0] // 2] for t in terms]


def lower(terms):
    return [t[t.shape[0] // 2 :] for t in terms]


def shards(
    n_member, n_band,
    hidden, queries, kv_weight, out_weight, head_projection, initial_state, truth,
    latitude_weight, channel_loss_weight, sources, halo_rows,
):
    members, nodes, width = hidden.shape
    points = queries.shape[0]
    channels = head_projection.shape[1]
    rim = halo_rows.shape[1]
    ext = nodes + 2 * rim
    pairs = width // LANES
    devices = n_member * n_band
    rw = width // devices
    chips = n_band // 2
    mates = [(i, i ^ 1) for i in range(n_band)]
    others = [(i, (i + 1 if i % 2 else i - 1) % n_band) for i in range(n_band)]

    own_hidden, halo, for_mate, for_other = call(
        pick_body,
        [sds(hidden.shape, BF), sds(halo_rows.shape, jnp.int32)] + [sds((members * rim, width), BF)] * 2,
        (hidden, halo_rows),
        [pltpu.SemaphoreType.DMA((2,))],
        hbm=(0, 1),
        flops=10**10,
    )
    other = lax.ppermute(for_other, "band", others)
    mate = lax.ppermute(for_mate, "band", mates)

    hp = head_projection.T

    def gate_shapes(rows):
        return [sds((members, rows, width), BF)] + [sds((pairs, members, 2 * rows, points), BF)] * 2

    own_value, own_gates, own_slopes, own_merged, qt, pt, p, base, weight = call(
        own_body,
        gate_shapes(nodes)
        + [
            sds((members, width, points), F32),
            sds((width, points), BF),
            sds((width, LANES), BF),
            sds((LANES, width), BF),
            sds((LANES, points), F32),
            sds((channels, points), F32),
        ],
        (
            own_hidden, out_weight, hp, queries, kv_weight, initial_state,
            channel_loss_weight[None, :], latitude_weight[None, :], sources,
        ),
        [pltpu.VMEM((8, LANES), F32), pltpu.VMEM((LANES, width), F32)],
    )

    halo_value, halo_gates, halo_slopes, merged, part, sent = call(
        functools.partial(halo_body, channels, nodes),
        gate_shapes(2 * rim)
        + [
            sds((members, width, points), BF),
            sds((members, LANES, points), F32),
            sds((members * channels, points), BF),
        ],
        (other, mate, own_merged, kv_weight, qt, sources, p),
    )

    received = [
        lax.ppermute(sent, "member", [(i, i ^ s) for i in range(n_member)]) for s in range(n_member - 1, 0, -1)
    ]

    ext_t = call(
        functools.partial(transpose_body, n_member, n_band),
        sds((width, members * ext), BF),
        (own_hidden, mate, other),
        [pltpu.VMEM((width, members * ext), F32)],
    )

    extra = 2 * LANES
    group_width = (2 * width + extra) // GROUPS
    widths = [group_width, group_width - LANES, group_width + LANES]
    first_keys = widths[0] + widths[1] - width
    group_shapes = [[sds((width // 2, w), BF)] * 2 for w in widths]
    grad, ng_value, send, keep = call(
        functools.partial(value_body, n_member, n_band),
        [sds((members, LANES, points), BF), sds((members * ext, width), BF)]
        + group_shapes[0],
        (*received, part, base, truth, weight, p, own_gates, halo_gates, ext_t),
    )
    groups = [[keep, swap(send, "band", 0, n_band)]]
    ng_first, send, keep = call(
        functools.partial(first_keys_body, n_member, n_band, group_width),
        [sds((members * ext, first_keys), BF)] + group_shapes[1],
        (grad, pt, own_value, halo_value, own_slopes, halo_slopes, queries, ext_t, ng_value),
    )
    groups.append([keep, swap(send, "band", 0, n_band)])
    ng_last, send, keep = call(
        functools.partial(last_keys_body, n_member, n_band),
        [sds((members * ext, width - first_keys), BF)] + group_shapes[2],
        (grad, pt, own_value, halo_value, own_slopes, halo_slopes, queries, merged, out_weight, ext_t),
        [pltpu.VMEM((width, extra), F32)],
    )
    groups.append([keep, swap(send, "band", 0, n_band)])

    count = {"member": n_member, "band": n_band}
    turns, rest = halving_orders(n_member, n_band)
    steps = len(turns[0])
    for step in range(steps):
        outgoing = []
        for i in range(GROUPS):
            outgoing.append(add_up(*upper(groups[i])).astype(BF))
            if step == 0 and i + 1 < GROUPS:
                outgoing[i], groups[i + 1] = lax.optimization_barrier((outgoing[i], groups[i + 1]))
        if step == 0:
            outgoing, ng_last = lax.optimization_barrier((outgoing, ng_last))
            own_grad, back = call(
                functools.partial(extended_grad_body, members, nodes, rim),
                [sds((members, nodes, width), F32), sds((2 * members * rim, width), BF)],
                (ng_first, ng_last, ng_value, kv_weight),
            )
        arrived = [swap(out, *turn[step], count[turn[step][0]]) for out, turn in zip(outgoing, turns)]
        if step == 0:
            from_mate = lax.ppermute(back, "band", mates)
            arrived, from_mate = lax.optimization_barrier((arrived, from_mate))
        if step == steps - 1:
            onward = lower([from_mate])[0]
            arrived, onward = lax.optimization_barrier((arrived, onward))
            chips_on = [(i, (i + 2 - i % 2 * 4) % n_band) for i in range(n_band)]
            from_other = lax.ppermute(onward, "band", chips_on)
        groups = [lower(terms) + [new] for terms, new in zip(groups, arrived)]
    terms = [jnp.concatenate([add_up(*group) for group in groups], axis=1)]
    for axis, bit in rest:
        arrived = swap(add_up(*upper(terms)).astype(BF), axis, bit, count[axis])
        terms = lower(terms) + [arrived]

    return call(
        functools.partial(finish_body, devices),
        [
            sds((members, nodes, width), F32),
            sds((rw, 2 * width), F32),
            sds((rw, width), F32),
            sds((rw, channels), F32),
        ],
        (own_grad, from_mate, from_other, halo, add_up(*terms[:-1]), terms[-1], hp),
    )


def solution(mesh):
    placed = (
        P("member", "band", None),
        P("band", None),
        P(),
        P(),
        P(),
        P(None, "band"),
        P(None, "band"),
        P("band"),
        P(),
        P(None, "band"),
        P("band", None),
    )
    return jax.shard_map(
        functools.partial(shards, mesh.shape["member"], mesh.shape["band"]),
        mesh=mesh,
        in_specs=placed,
        out_specs=(
            P("member", "band", None),
            P(("member", "band"), None),
            P(("member", "band"), None),
            P(("member", "band"), None),
        ),
        check_vma=False,
    )
```
